32 devices in a mesh: dp: 4 (over z), mp: 8 (over y, x, core).
Axes of the slice: x: 2, y: 2, z: 4, core: 2. Of those that a mesh axis runs over, the one named last changes fastest.
Arguments:
- inputs: bfloat16 [8, 1024, 2048], P('dp'), may hold values from -6 to 6
- positions: int32 [8, 1024], P('dp'), may hold values from 0 to 1023, as said below
- cotangent: bfloat16 [8, 1024, 2048], P('dp'), may hold values from -6 to 6
- w_attend_in: float32 [2048, 3, 2048], P('dp', None, 'mp'), may hold values from -0.125 to 0.125
- w_attend_out: float32 [2048, 2048], P('dp', 'mp'), may hold values from -1.5 to 1.5
- w_expand: float32 [2048, 2, 5632], P('dp', None, 'mp'), may hold values from -0.125 to 0.125
- w_reduce: float32 [2048, 5632], P('dp', 'mp'), may hold values from -0.078125 to 0.078125
- norm_params: float32 [2, 2048], replicated, may hold values from -0.8 to 1.2, as said below
- attend_bias: float32 [3, 2048], P(None, 'mp'), may hold values from -3 to 3
- moment_attend_in: float32 [2048, 3, 2048], P('dp', None, 'mp'), may hold values from -640 to 640
- moment_attend_out: float32 [2048, 2048], P('dp', 'mp'), may hold values from -56 to 56
- moment_expand: float32 [2048, 2, 5632], P('dp', None, 'mp'), may hold values from -160 to 160
- moment_reduce: float32 [2048, 5632], P('dp', 'mp'), may hold values from -320 to 320
- moment_norm: float32 [2, 2048], replicated, may hold values from -1024 to 1024
- moment_bias: float32 [3, 2048], P(None, 'mp'), may hold values from -512 to 512
- average_attend_in: float32 [2048, 3, 2048], P('dp', None, 'mp'), may hold values from -0.125 to 0.125
- average_attend_out: float32 [2048, 2048], P('dp', 'mp'), may hold values from -1.5 to 1.5
- average_expand: float32 [2048, 2, 5632], P('dp', None, 'mp'), may hold values from -0.125 to 0.125
- average_reduce: float32 [2048, 5632], P('dp', 'mp'), may hold values from -0.078125 to 0.078125
- average_norm: float32 [2, 2048], replicated, may hold values from -0.8 to 1.2, as said below
- average_bias: float32 [3, 2048], P(None, 'mp'), may hold values from -3 to 3
Outputs:
- output: bfloat16 [8, 1024, 2048], P('dp')
- input_grad: float32 [8, 1024, 2048], P('dp')
- grad_attend_in: float32 [2048, 3, 2048], P('dp', None, 'mp')
- grad_attend_out: float32 [2048, 2048], P('dp', 'mp')
- grad_expand: float32 [2048, 2, 5632], P('dp', None, 'mp')
- grad_reduce: float32 [2048, 5632], P('dp', 'mp')
- grad_norm: float32 [2, 2048], replicated
- grad_bias: float32 [3, 2048], P(None, 'mp')
- new_attend_in: float32 [2048, 3, 2048], P('dp', None, 'mp')
- new_attend_out: float32 [2048, 2048], P('dp', 'mp')
- new_expand: float32 [2048, 2, 5632], P('dp', None, 'mp')
- new_reduce: float32 [2048, 5632], P('dp', 'mp')
- new_norm: float32 [2, 2048], replicated
- new_bias: float32 [3, 2048], P(None, 'mp')
- new_moment_attend_in: float32 [2048, 3, 2048], P('dp', None, 'mp')
- new_moment_attend_out: float32 [2048, 2048], P('dp', 'mp')
- new_moment_expand: float32 [2048, 2, 5632], P('dp', None, 'mp')
- new_moment_reduce: float32 [2048, 5632], P('dp', 'mp')
- new_moment_norm: float32 [2, 2048], replicated
- new_moment_bias: float32 [3, 2048], P(None, 'mp')
- new_average_attend_in: float32 [2048, 3, 2048], P('dp', None, 'mp')
- new_average_attend_out: float32 [2048, 2048], P('dp', 'mp')
- new_average_expand: float32 [2048, 2, 5632], P('dp', None, 'mp')
- new_average_reduce: float32 [2048, 5632], P('dp', 'mp')
- new_average_norm: float32 [2, 2048], replicated
- new_average_bias: float32 [3, 2048], P(None, 'mp')
The draws below stay inside these ranges and needn't reach their ends.
Inputs may be any that keep to these rules, and one draw needn't show every extreme that they name: `positions`: A position counts the tokens since the start of its document in the sequence; every sequence starts a document at its first token, the first sequence of the batch is one whole document, and in the others further documents begin at random places. `norm_params`: row 0 lies near one, row 1 near zero. `average_norm`: row 0 lies near one, row 1 near zero.
All inputs are finite; a program needn't handle non-finite values.
Results may differ from the reference program's by a relative error of at most 0.012.
Values may be sent and summed in bfloat16 or wider, within the bound.
No kernel may reach another device: no remote copies, remote signals or barrier semaphores. Data moves between devices by JAX's collectives and lax.ppermute only.
A program may use at most 256 MiB of HBM per device.

```python
import jax
import jax.numpy as jnp
from jax import lax

H = 32
HD = 64
ROT = 16
FF = 5632
D = 2048
SEQ = 1024
BATCH = 8


def draw_positions(key, part):
    spacing = max(2, SEQ // 8)
    marks = jax.random.randint(jax.random.fold_in(key, 5), (BATCH, SEQ), 0, spacing) == 0
    later = (jnp.arange(BATCH, dtype=jnp.int32) > 0)[:, None]
    marks = jnp.logical_and(marks, later)
    places = jnp.arange(SEQ, dtype=jnp.int32)
    starts = lax.cummax(jnp.where(marks, places[None, :], 0), axis=1)
    return (places[None, :] - starts).astype(jnp.int32)


def norm_rows(key):
    gain_key, shift_key = jax.random.split(key)
    gain = 1.0 + 0.1 * jnp.clip(jax.random.normal(gain_key, (D,), jnp.float32), -2.0, 2.0)
    shift = 0.3 * jnp.clip(jax.random.normal(shift_key, (D,), jnp.float32), -2.6, 2.6)
    return jnp.stack([gain, shift]).astype(jnp.float32)


def draw_norm_params(key, part):
    return norm_rows(jax.random.fold_in(key, 11))


def draw_average_norm(key, part):
    return norm_rows(jax.random.fold_in(key, 23))


def shard_levels(own_key, dims, cuts, smallest, high):
    level = 1.0
    for dim, parts in cuts:
        heights = jax.random.uniform(jax.random.fold_in(jax.random.fold_in(own_key, 6), dim), (parts,), jnp.float32, smallest / len(cuts), high / len(cuts))
        level = level * jnp.repeat(jnp.exp(heights), dims[dim] // parts).reshape((-1,) + (1,) * (len(dims) - 1 - dim))
    return level


def bell_draw(rng, dims, scale, bound, cuts=(), kind=jnp.bfloat16):
    values = jax.random.normal(rng, dims, jnp.float32) * scale
    if len(cuts) > 0:
        values = shard_levels(rng, dims, cuts, -0.22, 0.18) * values
    return jnp.clip(values, min=-bound, max=bound).astype(kind)


def setup_inputs(seed: int = 0) -> dict:
    key_of = jax.random.split(jax.random.key(seed), 22)
    inputs = bell_draw(key_of[0], (BATCH, SEQ, D), 1.0, 6.0, ((0, 4),))
    positions = draw_positions(jax.random.fold_in(key_of[21], 71), 0)
    cotangent = bell_draw(key_of[2], (BATCH, SEQ, D), 1.0, 6.0, ((0, 4),))
    w_attend_in = bell_draw(key_of[3], (D, 3, D), D ** -0.5, 0.125, ((0, 4), (2, 8)), jnp.float32)
    w_attend_out = bell_draw(key_of[4], (D, D), (max(1, D * 8 // SEQ)) ** -0.5, 1.5, ((0, 4), (1, 8)), jnp.float32)
    w_expand = bell_draw(key_of[5], (D, 2, FF), D ** -0.5, 0.125, ((0, 4), (2, 8)), jnp.float32)
    w_reduce = bell_draw(key_of[6], (D, FF), FF ** -0.5, 0.078125, ((0, 4), (1, 8)), jnp.float32)
    norm_params = draw_norm_params(jax.random.fold_in(key_of[21], 71), 0)
    attend_bias = bell_draw(key_of[8], (3, D), 0.5, 3.0, ((1, 8),), jnp.float32)
    moment_attend_in = bell_draw(key_of[9], (D, 3, D), (1.1 * (BATCH * SEQ) ** 0.5), 640.0, ((0, 4), (2, 8)), jnp.float32)
    moment_attend_out = bell_draw(key_of[10], (D, D), (0.1 * (BATCH * SEQ) ** 0.5), 56.0, ((0, 4), (1, 8)), jnp.float32)
    moment_expand = bell_draw(key_of[11], (D, 2, FF), (0.3 * (BATCH * SEQ) ** 0.5), 160.0, ((0, 4), (2, 8)), jnp.float32)
    moment_reduce = bell_draw(key_of[12], (D, FF), (0.65 * (BATCH * SEQ) ** 0.5), 320.0, ((0, 4), (1, 8)), jnp.float32)
    moment_norm = bell_draw(key_of[13], (2, D), (1.9 * (BATCH * SEQ) ** 0.5), 1024.0, (), jnp.float32)
    moment_bias = bell_draw(key_of[14], (3, D), (1.0 * (BATCH * SEQ) ** 0.5), 512.0, ((1, 8),), jnp.float32)
    average_attend_in = bell_draw(key_of[15], (D, 3, D), D ** -0.5, 0.125, ((0, 4), (2, 8)), jnp.float32)
    average_attend_out = bell_draw(key_of[16], (D, D), (max(1, D * 8 // SEQ)) ** -0.5, 1.5, ((0, 4), (1, 8)), jnp.float32)
    average_expand = bell_draw(key_of[17], (D, 2, FF), D ** -0.5, 0.125, ((0, 4), (2, 8)), jnp.float32)
    average_reduce = bell_draw(key_of[18], (D, FF), FF ** -0.5, 0.078125, ((0, 4), (1, 8)), jnp.float32)
    average_norm = draw_average_norm(jax.random.fold_in(key_of[21], 71), 0)
    average_bias = bell_draw(key_of[20], (3, D), 0.5, 3.0, ((1, 8),), jnp.float32)
    return {"inputs": inputs, "positions": positions, "cotangent": cotangent, "w_attend_in": w_attend_in, "w_attend_out": w_attend_out, "w_expand": w_expand, "w_reduce": w_reduce, "norm_params": norm_params, "attend_bias": attend_bias, "moment_attend_in": moment_attend_in, "moment_attend_out": moment_attend_out, "moment_expand": moment_expand, "moment_reduce": moment_reduce, "moment_norm": moment_norm, "moment_bias": moment_bias, "average_attend_in": average_attend_in, "average_attend_out": average_attend_out, "average_expand": average_expand, "average_reduce": average_reduce, "average_norm": average_norm, "average_bias": average_bias}


@jax.custom_vjp
def low(v):
    return lax.optimization_barrier(v.astype(jnp.bfloat16)).astype(jnp.float32)

@jax.custom_vjp
def low_back(v):
    return v

def low_keep(v):
    return (low(v), None)

def low_pass(kept, grad):
    return (grad,)

def back_keep(v):
    return (v, None)

def back_low(kept, grad):
    return (low(grad),)
low.defvjp(low_keep, low_pass)
low_back.defvjp(back_keep, back_low)
epsilon = 1e-05
decay_moment = 0.9
decay_average = 0.9
masked_score = -1e+30
highest = lax.Precision.HIGHEST

def rotate(values, cosine, sine):
    half = cosine.shape[-1]
    first = values[..., :half]
    second = values[..., half:2 * half]
    return jnp.concatenate([first * cosine - second * sine, second * cosine + first * sine, values[..., 2 * half:]], axis=-1)

def attention(queries, keys, values):
    length = queries.shape[0]
    block = min(512, length)
    count = length // block
    scale = HD ** (-0.5)
    columns = jnp.arange(length, dtype=jnp.int32)

    def one_block(start):
        query_block = lax.dynamic_slice_in_dim(queries, start, block, 0)
        scores = low_back(jnp.einsum('qhd,khd->hqk', query_block, keys, precision=highest) * scale)
        allowed = columns[None, :] <= (start + jnp.arange(block, dtype=jnp.int32))[:, None]
        probs = low(jax.nn.softmax(jnp.where(allowed[None], scores, masked_score), axis=-1))
        return jnp.einsum('hqk,khd->qhd', probs, values, precision=highest)
    starts = jnp.arange(count, dtype=jnp.int32) * block
    blocks = lax.map(jax.checkpoint(one_block), starts)
    return blocks.reshape(length, queries.shape[1], queries.shape[2])

def layer(tokens, params, cosine, sine):
    weight_in, weight_out, weight_expand, weight_reduce, norm_params, attend_bias = params
    length = tokens.shape[0]
    centre = lax.optimization_barrier(jnp.mean(tokens, axis=-1, keepdims=True))
    centred = tokens - centre
    normal = centred * lax.rsqrt(lax.optimization_barrier(jnp.mean(centred * centred, axis=-1, keepdims=True)) + epsilon)
    hidden = low(normal * norm_params[0] + norm_params[1])
    mixed = jnp.dot(hidden, low(weight_in).reshape(D, 3 * D), precision=highest) + attend_bias.reshape(3 * D)
    mixed = low_back(mixed).reshape(length, 3, H, HD)
    queries = low(rotate(mixed[:, 0], cosine, sine))
    keys = low(rotate(mixed[:, 1], cosine, sine))
    values = low(mixed[:, 2])
    context = attention(queries, keys, values).reshape(length, D)
    context = low_back(low(context))
    attended = jnp.dot(context, low(weight_out).T, precision=highest)
    gates = low_back(jnp.dot(hidden, low(weight_expand).reshape(D, 2 * FF), precision=highest)).reshape(length, 2, FF)
    active = low(jax.nn.silu(gates[:, 0]) * gates[:, 1])
    expanded = jnp.dot(active, low(weight_reduce).T, precision=highest)
    return tokens + attended + expanded

def advance(weight, grad, moment, average, rate):
    moment_new = decay_moment * moment + grad
    weight_new = weight - rate * (grad + decay_moment * moment_new)
    average_new = decay_average * average + (1.0 - decay_average) * weight_new
    return (weight_new, moment_new, average_new)

def reference(inputs, positions, cotangent, w_attend_in, w_attend_out, w_expand, w_reduce, norm_params, attend_bias, moment_attend_in, moment_attend_out, moment_expand, moment_reduce, moment_norm, moment_bias, average_attend_in, average_attend_out, average_expand, average_reduce, average_norm, average_bias):
    params = (w_attend_in, w_attend_out, w_expand, w_reduce, norm_params, attend_bias)
    frequency = 10000.0 ** (-(jnp.arange(ROT // 2, dtype=jnp.float32) * 2.0 / ROT))

    def one_sequence(totals, pieces):
        tokens, places, cot_seq = pieces
        angles = places.astype(jnp.float32)[:, None] * frequency[None, :]
        cosine = jnp.cos(angles)[:, None, :]
        sine = jnp.sin(angles)[:, None, :]
        result, pullback = jax.vjp(lambda rows_in, weights: layer(rows_in, weights, cosine, sine), tokens.astype(jnp.float32), params)
        grad_rows, weight_grads = pullback(cot_seq.astype(jnp.float32))
        totals = jax.tree.map(jnp.add, totals, weight_grads)
        return (totals, (result.astype(jnp.bfloat16), grad_rows))
    zeros = jax.tree.map(jnp.zeros_like, params)
    grads, (output, input_grad) = lax.scan(one_sequence, zeros, (inputs, positions, cotangent))
    grad_in, grad_out, grad_expand, grad_reduce, grad_norm, grad_bias = grads
    total_tokens = BATCH * SEQ
    new_in, moment_in_new, average_in_new = advance(w_attend_in, grad_in, moment_attend_in, average_attend_in, 0.5 / (D * total_tokens) ** 0.5)
    new_out, moment_out_new, average_out_new = advance(w_attend_out, grad_out, moment_attend_out, average_attend_out, 1.8 / (D * BATCH) ** 0.5)
    new_expand, moment_expand_new, average_expand_new = advance(w_expand, grad_expand, moment_expand, average_expand, 1.6 / (D * total_tokens) ** 0.5)
    new_reduce, moment_reduce_new, average_reduce_new = advance(w_reduce, grad_reduce, moment_reduce, average_reduce, 0.77 / (FF * total_tokens) ** 0.5)
    new_norm, moment_norm_new, average_norm_new = advance(norm_params, grad_norm, moment_norm, average_norm, 0.06 / total_tokens ** 0.5)
    new_bias, moment_bias_new, average_bias_new = advance(attend_bias, grad_bias, moment_bias, average_bias, 0.25 / total_tokens ** 0.5)
    return (output, input_grad, grad_in, grad_out, grad_expand, grad_reduce, grad_norm, grad_bias, new_in, new_out, new_expand, new_reduce, new_norm, new_bias, moment_in_new, moment_out_new, moment_expand_new, moment_reduce_new, moment_norm_new, moment_bias_new, average_in_new, average_out_new, average_expand_new, average_reduce_new, average_norm_new, average_bias_new)
```

```python
import functools
import math

import jax
import jax.numpy as jnp
from jax import lax
from jax.experimental import pallas as pl
from jax.experimental.pallas import tpu as pltpu
from jax.sharding import PartitionSpec as P

HD = 64
ROT = 16
FF = 5632

epsilon = 1e-05
decay_moment = 0.9
decay_average = 0.9
masked_score = -1e30

low = jnp.bfloat16
full = jnp.float32
vmem_limit = 60 << 20


def dot_nt(left, right):
    return lax.dot_general(left, right, (((1,), (1,)), ((), ())), preferred_element_type=full)


def dot_nn(left, right):
    return lax.dot_general(left, right, (((1,), (0,)), ((), ())), preferred_element_type=full)


def dot_tn(left, right):
    return lax.dot_general(left, right, (((0,), (0,)), ((), ())), preferred_element_type=full)


def params(**more):
    return pltpu.CompilerParams(vmem_limit_bytes=vmem_limit, **more)


def cost(flops, moved, trans=0):
    return pl.CostEstimate(flops=int(flops), bytes_accessed=int(moved), transcendentals=int(trans))


def shape(dims, kind):
    return jax.ShapeDtypeStruct(dims, kind)


def advance(weight, grad, moment, average, rate):
    moment_new = decay_moment * moment + grad
    weight_new = weight - rate * (grad + decay_moment * moment_new)
    average_new = decay_average * average + (1.0 - decay_average) * weight_new
    return (weight_new, moment_new, average_new)


def gather_hops(shard):
    n = lax.axis_size("dp")
    rights, lefts = [], []
    right = left = shard
    for k in range(1, n):
        right = lax.ppermute(right, "dp", [(a, a + 1) for a in range(k - 1, n - 1)])
        left = lax.ppermute(left, "dp", [(a, a - 1) for a in range(1, n - k + 1)])
        right, left = yield right, left
        yield
        rights.append(right)
        lefts.append(left)
    yield [shard] + rights + lefts


def scatter_hops(slots):
    n = lax.axis_size("dp")
    right = left = None
    for k in range(1, n):
        to_right, to_left = slots[n - k], slots[k]
        if k > 1:
            to_right = (to_right.astype(full) + right.astype(full)).astype(low)
            to_left = (to_left.astype(full) + left.astype(full)).astype(low)
        right = lax.ppermute(to_right, "dp", [(a, a + 1) for a in range(k)])
        left = lax.ppermute(to_left, "dp", [(a, a - 1) for a in range(n - 1, n - 1 - k, -1)])
        right, left = yield right, left
        yield
    yield slots[0] + right.astype(full) + left.astype(full)


def swap(value, mask, axis="mp"):
    n = lax.axis_size(axis)
    return lax.ppermute(value, axis, [(a, a ^ mask) for a in range(n)])


def small_sum(value, axis):
    n = lax.axis_size(axis)
    if n & (n - 1):
        return lax.psum(value, axis)
    mask = 1
    while mask < n:
        value = value + swap(value, mask, axis)
        mask *= 2
    return value


def norm_kernel(x_ref, p_ref, o_ref):
    x = x_ref[...].astype(full)
    centred = x - jnp.mean(x, axis=-1, keepdims=True)
    inv = lax.rsqrt(jnp.mean(centred * centred, axis=-1, keepdims=True) + epsilon)
    o_ref[...] = (centred * inv * p_ref[0:1] + p_ref[1:2]).astype(low)


def layer_norm(rows, norm_params):
    count, width = rows.shape
    block = min(256, count)
    return pl.pallas_call(
        norm_kernel,
        grid=(count // block,),
        in_specs=[
            pl.BlockSpec((block, width), lambda i: (i, 0)),
            pl.BlockSpec((2, width), lambda i: (0, 0)),
        ],
        out_specs=pl.BlockSpec((block, width), lambda i: (i, 0)),
        out_shape=shape((count, width), low),
        compiler_params=params(),
        cost_estimate=cost(8 * count * width, 4 * count * width),
        name="layer_norm",
    )(rows, norm_params)


def fetch(n, me, pieces, target_of, sems, action):
    def run(source, index, sem):
        copy = pltpu.make_async_copy(source, target_of(index), sem)
        if action == "start":
            copy.start()
        else:
            copy.wait()

    if len(pieces) == 1:
        for j in range(n):
            run(pieces[0].at[j], j, sems.at[j])
        return
    run(pieces[0], me, sems.at[0])
    for k in range(1, n):

        @pl.when(me >= k)
        def _(k=k):
            run(pieces[k], me - k, sems.at[k])

        @pl.when(me + k < n)
        def _(k=k):
            run(pieces[n - 1 + k], me + k, sems.at[n - 1 + k])


def gates_of(w_ref, h, c):
    units = w_ref.shape[1]
    both = dot_nt(w_ref[0:2].reshape(2 * units, w_ref.shape[2]), h)
    gate, upper = both[:units], both[units:]
    active_grad = dot_nt(w_ref[2], c)
    sigmoid = jax.nn.sigmoid(gate)
    swish = gate * sigmoid
    active = (swish * upper).astype(low)
    gate_grad = active_grad * upper * sigmoid * (1.0 + gate * (1.0 - sigmoid))
    return active, jnp.concatenate([gate_grad, active_grad * swish], axis=0).astype(low)


def add_grads(acc, step, active, gates_grad, h, c):
    units = active.shape[0]

    @pl.when(step == 0)
    def _():
        acc[: 2 * units] = dot_nn(gates_grad, h)
        acc[2 * units :] = dot_nn(active, c)

    @pl.when(step > 0)
    def _():
        acc[: 2 * units] += dot_nn(gates_grad, h)
        acc[2 * units :] += dot_nn(active, c)


def store_grads(n, acc, out_ref):
    piece = out_ref.shape[2]
    for j in range(n):
        out_ref[j] = acc[:, j * piece : (j + 1) * piece].astype(low)


def wide_target(w_ref, piece):
    return lambda index: w_ref.at[:, :, pl.ds(pl.multiple_of(index * piece, piece), piece)]


def feed_kernel(n, count, steps, me_ref, *refs):
    pieces = refs[:count]
    h_ref, c_ref, act_ref, grad_ref, w_ref, out_ref, acc, sems = refs[count:]
    step = pl.program_id(0)
    target_of = wide_target(w_ref, out_ref.shape[2])

    @pl.when(step == 0)
    def _():
        fetch(n, me_ref[0], pieces, target_of, sems, "start")
        fetch(n, me_ref[0], pieces, target_of, sems, "wait")

    h = h_ref[...]
    c = c_ref[...]
    active, gates_grad = gates_of(w_ref, h, c)
    act_ref[...] = active
    grad_ref[...] = gates_grad
    add_grads(acc, step, active, gates_grad, h, c)

    @pl.when(step == steps - 1)
    def _():
        store_grads(n, acc, out_ref)


def feed_chunk(n, me, pieces, hidden, cot):
    rows, width = hidden.shape
    units, piece = pieces[0].shape[-2:]
    count = len(pieces)
    block = min(512, rows)
    steps = rows // block
    row_spec = pl.BlockSpec((block, width), lambda i, m: (i, 0))
    return pl.pallas_call(
        functools.partial(feed_kernel, n, count, steps),
        grid_spec=pltpu.PrefetchScalarGridSpec(
            num_scalar_prefetch=1,
            grid=(steps,),
            in_specs=[pl.BlockSpec(memory_space=pl.ANY)] * count + [row_spec, row_spec],
            out_specs=[
                pl.BlockSpec((units, block), lambda i, m: (0, i)),
                pl.BlockSpec((2 * units, block), lambda i, m: (0, i)),
                pl.BlockSpec((3, units, width), lambda i, m: (0, 0, 0)),
                pl.BlockSpec((n, 3 * units, piece), lambda i, m: (0, 0, 0)),
            ],
            scratch_shapes=[
                pltpu.VMEM((3 * units, width), full),
                pltpu.SemaphoreType.DMA((2 * n - 1,)),
            ],
        ),
        out_shape=[
            shape((units, rows), low),
            shape((2 * units, rows), low),
            shape((3, units, width), low),
            shape((n, 3 * units, piece), low),
        ],
        compiler_params=params(),
        cost_estimate=cost(
            12 * rows * width * units, 4 * rows * width + 20 * units * width, rows * units
        ),
        name="feed_chunk",
    )(me, *pieces, hidden, cot)


def last_kernel(n, count, split, info_ref, *refs):
    pieces = refs[:count]
    h_ref, c_ref, hid_ref, out_ref = refs[count : count + 4]
    w_ref, sems = refs[-2:]
    act_ref, grad_ref = refs[-4:-2]
    parts = refs[count + 4 : -4]
    target_of = wide_target(w_ref, w_ref.shape[2] // n)
    step = pl.program_id(0)

    @pl.when(step == 0)
    def _():
        fetch(n, info_ref[3], pieces, target_of, sems, "start")
        fetch(n, info_ref[3], pieces, target_of, sems, "wait")

    active, gates_grad = gates_of(w_ref, h_ref[...], c_ref[...])
    act_ref[...] = active
    grad_ref[...] = gates_grad
    joined = w_ref[0:2].reshape(gates_grad.shape[0], w_ref.shape[2])
    hid = (hid_ref[...].astype(full) + dot_tn(gates_grad, joined)).astype(low)
    out = (out_ref[...].astype(full) + dot_tn(active, w_ref[2])).astype(low)
    if not split:
        parts[0][...] = hid
        parts[1][...] = out
        return
    sub = hid.shape[0] // 4
    high = jnp.where(step % 2 == 0, info_ref[1], info_ref[2])
    small = jnp.where(step % 2 == 0, info_ref[2], info_ref[1])
    for half in range(2):

        @pl.when(step // 2 == half)
        def _(half=half):
            for ref, value in ((parts[2 * half], hid), (parts[2 * half + 1], out)):
                for i in range(4):
                    at = ((i // 2) ^ high) * 2 + ((i % 2) ^ small)
                    place = pl.ds(pl.multiple_of(at * sub, sub), sub)
                    ref[place, :] = value[i * sub : (i + 1) * sub]


def feed_last(n, info, split, pieces, hidden, cot, hid_early, out_early):
    rows, width = hidden.shape
    units = pieces[0].shape[-2]
    count = len(pieces)
    if split:
        block, steps = rows // 4, 4
        place = lambda i, m: (m[0] ^ (1 - i // 2)) * 2 + i % 2
        part_specs = [pl.BlockSpec((block, width), lambda i, m: (jnp.minimum(i, 1), 0))] * 2
        part_specs += [pl.BlockSpec((block, width), lambda i, m: (jnp.maximum(i, 2) - 2, 0))] * 2
        part_shapes = [shape((rows // 2, width), low)] * 4
    else:
        block = min(256, rows)
        steps = rows // block
        place = lambda i, m: i
        part_specs = [pl.BlockSpec((block, width), lambda i, m: (i, 0))] * 2
        part_shapes = [shape((rows, width), low)] * 2
    row_spec = pl.BlockSpec((block, width), lambda i, m: (place(i, m), 0))
    return pl.pallas_call(
        functools.partial(last_kernel, n, count, split),
        grid_spec=pltpu.PrefetchScalarGridSpec(
            num_scalar_prefetch=1,
            grid=(steps,),
            in_specs=[pl.BlockSpec(memory_space=pl.ANY)] * count + [row_spec] * 4,
            out_specs=part_specs
            + [
                pl.BlockSpec((units, block), lambda i, m: (0, place(i, m))),
                pl.BlockSpec((2 * units, block), lambda i, m: (0, place(i, m))),
            ],
            scratch_shapes=[
                pltpu.VMEM((3, units, width), low),
                pltpu.SemaphoreType.DMA((2 * n - 1,)),
            ],
        ),
        out_shape=part_shapes + [shape((units, rows), low), shape((2 * units, rows), low)],
        compiler_params=params(),
        cost_estimate=cost(12 * rows * width * units, 12 * rows * width, rows * units),
        name="feed_last",
    )(info, *pieces, hidden, cot, hid_early, out_early)


def feed_grads_kernel(n, steps, h_ref, c_ref, act_ref, grad_ref, out_ref, acc):
    step = pl.program_id(0)
    add_grads(acc, step, act_ref[...], grad_ref[...], h_ref[...], c_ref[...])

    @pl.when(step == steps - 1)
    def _():
        store_grads(n, acc, out_ref)


def feed_grads(n, hidden, cot, active, gates_grad):
    rows, width = hidden.shape
    units = active.shape[0]
    piece = width // n
    block = min(512, rows)
    steps = rows // block
    row_spec = pl.BlockSpec((block, width), lambda i: (i, 0))
    return pl.pallas_call(
        functools.partial(feed_grads_kernel, n, steps),
        grid=(steps,),
        in_specs=[
            row_spec,
            row_spec,
            pl.BlockSpec((units, block), lambda i: (0, i)),
            pl.BlockSpec((2 * units, block), lambda i: (0, i)),
        ],
        out_specs=pl.BlockSpec((n, 3 * units, piece), lambda i: (0, 0, 0)),
        out_shape=shape((n, 3 * units, piece), low),
        scratch_shapes=[pltpu.VMEM((3 * units, width), full)],
        compiler_params=params(),
        cost_estimate=cost(6 * rows * width * units, 4 * rows * width + 12 * units * width),
        name="feed_grads",
    )(hidden, cot, active, gates_grad)


def turn(values, cosine, sine, half):
    cols = values.shape[1]
    lane = lax.broadcasted_iota(jnp.int32, (1, cols), 1) % HD
    other = jnp.where(
        lane < half, pltpu.roll(values, cols - half, 1), pltpu.roll(values, half, 1)
    )
    repeat = cols // cosine.shape[1]
    if repeat > 1:
        cosine = jnp.concatenate([cosine] * repeat, axis=1)
        sine = jnp.concatenate([sine] * repeat, axis=1)
    return values * cosine + other * sine


def project_kernel(n, count, me_ref, *refs):
    pieces = refs[:count]
    h_ref, c_ref, cos_ref, sin_ref, bias_ref, q_ref, k_ref, v_ref, o_ref, w_ref, sems = refs[
        count:
    ]
    piece = pieces[0].shape[-2]

    def target_of(index):
        return w_ref.at[:, pl.ds(pl.multiple_of(index * piece, piece), piece), :]

    @pl.when(pl.program_id(0) == 0)
    def _():
        fetch(n, me_ref[0], pieces, target_of, sems, "start")
        fetch(n, me_ref[0], pieces, target_of, sems, "wait")

    h = h_ref[...]
    cosine, sine = cos_ref[...], sin_ref[...]
    half = ROT // 2
    q_ref[...] = turn(dot_nn(h, w_ref[0]) + bias_ref[0:1], cosine, sine, half).astype(low)
    k_ref[...] = turn(dot_nn(h, w_ref[1]) + bias_ref[1:2], cosine, sine, half).astype(low)
    v_ref[...] = (dot_nn(h, w_ref[2]) + bias_ref[2:3]).astype(low)
    o_ref[...] = dot_nn(c_ref[...], w_ref[3]).astype(low)


def project(n, me, pieces, hidden, cot, cosine, sine, bias):
    rows, width = hidden.shape
    piece, cols = pieces[0].shape[-2:]
    count = len(pieces)
    block = min(512, rows)
    row_spec = pl.BlockSpec((block, width), lambda i, m: (i, 0))
    angle_spec = pl.BlockSpec((block, 128), lambda i, m: (i, 0))
    out_spec = pl.BlockSpec((block, cols), lambda i, m: (i, 0))
    return pl.pallas_call(
        functools.partial(project_kernel, n, count),
        grid_spec=pltpu.PrefetchScalarGridSpec(
            num_scalar_prefetch=1,
            grid=(rows // block,),
            in_specs=[pl.BlockSpec(memory_space=pl.ANY)] * count
            + [row_spec, row_spec, angle_spec, angle_spec]
            + [pl.BlockSpec((3, cols), lambda i, m: (0, 0))],
            out_specs=[out_spec] * 4 + [pl.BlockSpec((4, width, cols), lambda i, m: (0, 0, 0))],
            scratch_shapes=[pltpu.SemaphoreType.DMA((2 * n - 1,))],
        ),
        out_shape=[shape((rows, cols), low)] * 4 + [shape((4, width, cols), low)],
        compiler_params=params(),
        cost_estimate=cost(8 * rows * width * cols, 4 * rows * width + 16 * width * cols),
        name="project",
    )(me, *pieces, hidden, cot, cosine, sine, bias)


def attend_kernel(block, q_ref, k_ref, v_ref, o_ref, cos_ref, sin_ref, ctx_ref, mg_ref, bias_ref, dq, dk, dv):
    length, lanes = q_ref.shape
    scale = HD ** (-0.5)
    for head in range(lanes // HD):
        cols = slice(head * HD, (head + 1) * HD)
        for i in range(length // block):
            rows = slice(i * block, (i + 1) * block)
            end = (i + 1) * block
            q = q_ref[rows, cols]
            o = o_ref[rows, cols]
            k = k_ref[:end, cols]
            v = v_ref[:end, cols]
            scores = dot_nt(q, k) * scale
            row = i * block + lax.broadcasted_iota(jnp.int32, (block, end), 0)
            col = lax.broadcasted_iota(jnp.int32, (block, end), 1)
            scores = jnp.where(col <= row, scores, masked_score)
            top = jnp.max(scores, axis=-1, keepdims=True)
            weights = jnp.exp(scores - top)
            probs = weights * (1.0 / jnp.sum(weights, axis=-1, keepdims=True))
            probs_low = probs.astype(low)
            ctx_ref[rows, cols] = dot_nn(probs_low, v).astype(low)
            prob_grads = dot_nt(o, v)
            middle = jnp.sum(probs * prob_grads, axis=-1, keepdims=True)
            score_grads = (probs * (prob_grads - middle)).astype(low)
            dq[rows, cols] = dot_nn(score_grads, k) * scale
            key_part = dot_tn(score_grads, q) * scale
            value_part = dot_tn(probs_low, o)
            if i == 0:
                dk[:end, cols] = key_part
                dv[:end, cols] = value_part
                if end < length:
                    dk[end:, cols] = jnp.zeros((length - end, HD), full)
                    dv[end:, cols] = jnp.zeros((length - end, HD), full)
            else:
                dk[:end, cols] += key_part
                dv[:end, cols] += value_part
    cosine, sine = cos_ref[...], -sin_ref[...]
    half = ROT // 2
    sums = []
    for part, grads in enumerate(
        (turn(dq[...], cosine, sine, half), turn(dk[...], cosine, sine, half), dv[...])
    ):
        rounded = grads.astype(low)
        mg_ref[part] = rounded
        sums.append(jnp.sum(rounded.astype(full), axis=0, keepdims=True))
    total = jnp.concatenate(sums, axis=0)

    @pl.when(pl.program_id(1) == 0)
    def _():
        bias_ref[...] = total

    @pl.when(pl.program_id(1) > 0)
    def _():
        bias_ref[...] += total


def attend(batch, q, k, v, o, cosine, sine):
    rows, cols = q.shape
    length = rows // batch
    lanes = 128
    spec = pl.BlockSpec((length, lanes), lambda p, b: (b, p))
    angle_spec = pl.BlockSpec((length, 128), lambda p, b: (b, 0))
    return pl.pallas_call(
        functools.partial(attend_kernel, min(512, length)),
        grid=(cols // lanes, batch),
        in_specs=[spec] * 4 + [angle_spec] * 2,
        out_specs=[
            spec,
            pl.BlockSpec((3, length, lanes), lambda p, b: (0, b, p)),
            pl.BlockSpec((3, lanes), lambda p, b: (0, p)),
        ],
        out_shape=[
            shape((rows, cols), low),
            shape((3, rows, cols), low),
            shape((3, cols), full),
        ],
        scratch_shapes=[pltpu.VMEM((length, lanes), full)] * 3,
        compiler_params=params(),
        cost_estimate=cost(
            40 * rows * length * cols, 20 * rows * cols, rows * length * cols // HD
        ),
        name="attend",
    )(q, k, v, o, cosine, sine)


def attend_grads_kernel(n, me_ref, h_ref, c_ref, mg_ref, ctx_ref, *refs):
    own_ref, *slot_refs = refs[:n]
    wide = refs[n]
    step = pl.program_id(0)
    cols = ctx_ref.shape[1]

    @pl.when(step == 0)
    def _():
        for part in range(3):
            wide[:, part * cols : (part + 1) * cols] = mg_ref[part]

    grad = dot_tn(h_ref[...], wide[...])
    grads = [grad[:, part * cols : (part + 1) * cols] for part in range(3)]
    grads.append(dot_tn(c_ref[...], ctx_ref[...]))
    for j in range(n):

        @pl.when(step == j)
        def _(j=j):
            for part in range(4):
                if j == 0:
                    own_ref[part] = grads[part]
                else:
                    slot_refs[j - 1][part] = grads[part].astype(low)


def attend_grads(n, me, hidden, cot, mixed_grad, context):
    rows, width = hidden.shape
    cols = context.shape[1]
    piece = width // n
    whole3 = pl.BlockSpec((4, piece, cols), lambda i, m: (0, 0, 0))
    cut_spec = pl.BlockSpec((rows, piece), lambda i, m: (0, lax.rem(m[0] + i, n)))
    return pl.pallas_call(
        functools.partial(attend_grads_kernel, n),
        grid_spec=pltpu.PrefetchScalarGridSpec(
            num_scalar_prefetch=1,
            grid=(n,),
            in_specs=[
                cut_spec,
                cut_spec,
                pl.BlockSpec((3, rows, cols), lambda i, m: (0, 0, 0)),
                pl.BlockSpec((rows, cols), lambda i, m: (0, 0)),
            ],
            out_specs=[whole3] * n,
            scratch_shapes=[pltpu.VMEM((rows, 3 * cols), low)],
        ),
        out_shape=[shape((4, piece, cols), full)] + [shape((4, piece, cols), low)] * (n - 1),
        compiler_params=params(),
        cost_estimate=cost(8 * rows * width * cols, 4 * rows * width + 16 * width * cols),
        name="attend_grads",
    )(me, hidden, cot, mixed_grad, context)


def early_kernel(ctx_ref, mg_ref, act_ref, grad_ref, wa_ref, wf_ref, hid_ref, out_ref):
    hid = dot_nt(mg_ref[0], wa_ref[0]) + dot_nt(mg_ref[1], wa_ref[1]) + dot_nt(mg_ref[2], wa_ref[2])
    hid += dot_tn(grad_ref[...], wf_ref[0:2].reshape(grad_ref.shape[0], wf_ref.shape[2]))
    hid_ref[...] = hid.astype(low)
    out_ref[...] = (dot_nt(ctx_ref[...], wa_ref[3]) + dot_tn(act_ref[...], wf_ref[2])).astype(low)


def early_parts(context, mixed_grad, active, gates_grad, w_attend, w_feed):
    rows, cols = context.shape
    units, width = w_feed.shape[1:]
    block = min(256, rows)
    out_spec = pl.BlockSpec((block, width), lambda i: (i, 0))
    return pl.pallas_call(
        early_kernel,
        grid=(rows // block,),
        in_specs=[
            pl.BlockSpec((block, cols), lambda i: (i, 0)),
            pl.BlockSpec((3, block, cols), lambda i: (0, i, 0)),
            pl.BlockSpec((units, block), lambda i: (0, i)),
            pl.BlockSpec((2 * units, block), lambda i: (0, i)),
            pl.BlockSpec((4, width, cols), lambda i: (0, 0, 0)),
            pl.BlockSpec((3, units, width), lambda i: (0, 0, 0)),
        ],
        out_specs=[out_spec, out_spec],
        out_shape=[shape((rows, width), low)] * 2,
        compiler_params=params(),
        cost_estimate=cost(
            2 * rows * width * (4 * cols + 3 * units),
            4 * rows * width + 2 * (rows + width) * (4 * cols + 3 * units),
        ),
        name="early_parts",
    )(context, mixed_grad, active, gates_grad, w_attend, w_feed)


def sixteenth(which, m):
    return m[0] * 8 + (m[1] * 2 + m[2] if which == 0 else 4 + m[2] * 2 + m[1])


def back_kernel(info_ref, *refs):
    p_ref = refs[6]
    sums_ref = refs[9]
    total = 0.0
    for x_ref, near_ref, far_ref, back_ref in zip(refs[0:2], refs[2:4], refs[4:6], refs[7:9]):
        x = x_ref[...].astype(full)
        centred = x - jnp.mean(x, axis=-1, keepdims=True)
        inv = lax.rsqrt(jnp.mean(centred * centred, axis=-1, keepdims=True) + epsilon)
        normal = centred * inv
        grad = near_ref[...].astype(full) + far_ref[...].astype(full)
        scaled = grad * p_ref[0:1]
        back = inv * (
            scaled
            - jnp.mean(scaled, axis=-1, keepdims=True)
            - normal * jnp.mean(scaled * normal, axis=-1, keepdims=True)
        )
        back_ref[...] = back.astype(low)
        total += jnp.concatenate(
            [jnp.sum(grad * normal, axis=0, keepdims=True), jnp.sum(grad, axis=0, keepdims=True)],
            axis=0,
        )
    sums_ref[...] = total


def back_rows(info, rows, near, far, norm_params):
    count, width = near[0].shape
    spec = pl.BlockSpec((count, width), lambda i, m: (0, 0))
    pair = pl.BlockSpec((2, width), lambda i, m: (0, 0))
    return pl.pallas_call(
        back_kernel,
        grid_spec=pltpu.PrefetchScalarGridSpec(
            num_scalar_prefetch=1,
            grid=(1,),
            in_specs=[
                pl.BlockSpec((count, width), lambda i, m: (sixteenth(0, m), 0)),
                pl.BlockSpec((count, width), lambda i, m: (sixteenth(1, m), 0)),
            ]
            + [spec] * 4
            + [pair],
            out_specs=[spec, spec, pair],
        ),
        out_shape=[shape((count, width), low)] * 2 + [shape((2, width), full)],
        compiler_params=params(),
        cost_estimate=cost(40 * count * width, 16 * count * width),
        name="back_rows",
    )(info, rows, rows, *near, *far, norm_params)


def add_kernel(info_ref, *refs):
    for x_ref, near_ref, far_ref, out_ref in zip(refs[0:2], refs[2:4], refs[4:6], refs[6:8]):
        total = x_ref[...].astype(full) + near_ref[...].astype(full) + far_ref[...].astype(full)
        out_ref[...] = total.astype(low)


def add_rows(info, rows, near, far):
    count, width = near[0].shape
    spec = pl.BlockSpec((count, width), lambda i, m: (0, 0))
    return pl.pallas_call(
        add_kernel,
        grid_spec=pltpu.PrefetchScalarGridSpec(
            num_scalar_prefetch=1,
            grid=(1,),
            in_specs=[
                pl.BlockSpec((count, width), lambda i, m: (sixteenth(0, m), 0)),
                pl.BlockSpec((count, width), lambda i, m: (sixteenth(1, m), 0)),
            ]
            + [spec] * 4,
            out_specs=[spec, spec],
        ),
        out_shape=[shape((count, width), low)] * 2,
        compiler_params=params(),
        cost_estimate=cost(4 * count * width, 16 * count * width),
        name="add_rows",
    )(info, rows, rows, *near, *far)


def pack_kernel(info_ref, *refs):
    pieces, out_ref, sems = refs[:8], refs[8], refs[9]
    block = pieces[0].shape[0]
    x, y = info_ref[1], info_ref[2]
    copies = []
    for i, piece in enumerate(pieces):
        high, small = (i // 2) % 2, i % 2
        if i < 4:
            at = (x ^ high) * 2 + (y ^ small)
        else:
            at = 4 + (y ^ high) * 2 + (x ^ small)
        place = out_ref.at[pl.ds(pl.multiple_of(at * block, block), block), :]
        copies.append(pltpu.make_async_copy(piece, place, sems.at[i]))
    for copy in copies:
        copy.start()
    for copy in copies:
        copy.wait()


def pack_rows(info, pieces):
    block, width = pieces[0].shape
    return pl.pallas_call(
        pack_kernel,
        grid_spec=pltpu.PrefetchScalarGridSpec(
            num_scalar_prefetch=1,
            grid=(1,),
            in_specs=[pl.BlockSpec((block, width), lambda i, m: (0, 0))] * 8,
            out_specs=pl.BlockSpec(memory_space=pl.ANY),
            scratch_shapes=[pltpu.SemaphoreType.DMA((8,))],
        ),
        out_shape=shape((8 * block, width), low),
        compiler_params=params(),
        cost_estimate=cost(0, 32 * block * width),
        name="pack_rows",
    )(info, *pieces)


def finish_kernel(info_ref, *refs):
    own_ref, other_ref, out_ref = refs[-3:]
    mine = (pl.program_id(0) // 4) == info_ref[0]

    def store(value):
        if len(refs) == 4:
            value = refs[0][...].astype(full) + value.astype(full)
        out_ref[...] = value

    @pl.when(mine)
    def _():
        store(own_ref[...])

    @pl.when(jnp.logical_not(mine))
    def _():
        store(other_ref[...])


def finish_rows(info, own, other, cot=None):
    rows, width = 2 * own.shape[0], own.shape[1]
    extra = () if cot is None else (cot,)
    block = rows // 8
    spec = pl.BlockSpec((block, width), lambda i, m: (i, 0))
    edge = lambda i: jnp.where(i < 4, 0, 3)
    return pl.pallas_call(
        finish_kernel,
        grid_spec=pltpu.PrefetchScalarGridSpec(
            num_scalar_prefetch=1,
            grid=(8,),
            in_specs=[spec] * len(extra)
            + [
                pl.BlockSpec((block, width), lambda i, m: (jnp.where(i // 4 == m[0], i % 4, edge(i)), 0)),
                pl.BlockSpec((block, width), lambda i, m: (jnp.where(i // 4 == m[0], edge(i), i % 4), 0)),
            ],
            out_specs=spec,
        ),
        out_shape=shape((rows, width), low if cot is None else full),
        compiler_params=params(),
        cost_estimate=cost(2 * rows * width, 8 * rows * width),
        name="finish_rows",
    )(info, *extra, own, other)


def update_kernel(rates, count, *refs):
    g_ref = refs[0]
    ins = refs[1:7]
    outs = refs[7 + count :]
    for which, rate in enumerate(rates):
        grad = g_ref[:2] if which == 0 else g_ref[2]
        grad = grad.astype(full)
        w, m, a = (ref[...] for ref in ins[3 * which : 3 * which + 3])
        g_out, w_out, m_out, a_out = outs[4 * which : 4 * which + 4]
        g_out[...] = grad
        w_out[...], m_out[...], a_out[...] = advance(w, grad, m, a, rate)


def update_feed(start, grads, states, rates, begun=()):
    _, units, piece = grads.shape
    block = math.gcd(start, units)
    while block > 128 and block % 16 == 0:
        block //= 2
    at = start // block
    pair = pl.BlockSpec((2, block, piece), lambda i: (0, at + i, 0))
    single = pl.BlockSpec((block, piece), lambda i: (at + i, 0))
    total = states[0].shape[1]
    return pl.pallas_call(
        functools.partial(update_kernel, rates, len(begun)),
        grid=(units // block,),
        in_specs=[pl.BlockSpec((3, block, piece), lambda i: (0, i, 0))]
        + [pair] * 3
        + [single] * 3
        + [pl.BlockSpec(memory_space=pl.ANY)] * len(begun),
        out_specs=[pair] * 4 + [single] * 4,
        out_shape=[shape((2, total, piece), full)] * 4 + [shape((total, piece), full)] * 4,
        input_output_aliases={7 + i: i for i in range(len(begun))},
        compiler_params=params(),
        cost_estimate=cost(30 * units * piece, 3 * 30 * units * piece),
        name="update_feed",
    )(grads, *states, *begun)


def body(
    inputs,
    positions,
    cotangent,
    w_attend_in,
    w_attend_out,
    w_expand,
    w_reduce,
    norm_params,
    attend_bias,
    moment_attend_in,
    moment_attend_out,
    moment_expand,
    moment_reduce,
    moment_norm,
    moment_bias,
    average_attend_in,
    average_attend_out,
    average_expand,
    average_reduce,
    average_norm,
    average_bias,
):
    batch, length, width = inputs.shape
    rows = batch * length
    units = w_expand.shape[2]
    n = lax.axis_size("dp")
    group = lax.axis_size("mp")
    me = lax.axis_index("dp").astype(jnp.int32).reshape(1)
    spot = lax.axis_index("mp").astype(jnp.int32)
    info = jnp.stack([spot & 1, (spot >> 1) & 1, (spot >> 2) & 1, me[0]])
    fast = group == 8

    expand_t = jnp.transpose(w_expand, (1, 2, 0))
    reduce_t = jnp.transpose(w_reduce)
    in_t = jnp.transpose(w_attend_in, (1, 0, 2))
    cut = units // 2 // 16 * 16
    shards = [
        jnp.concatenate([expand_t[:, a:b], reduce_t[None, a:b]], axis=0).astype(low)
        for a, b in ((0, cut), (cut, units))
    ]
    attend_shard = jnp.concatenate([in_t, w_attend_out[None]], axis=0).astype(low)
    attend_pieces = [lax.all_gather(attend_shard, "dp")]
    first_shard, _ = lax.optimization_barrier((shards[0], attend_shard))
    first_pieces = [lax.all_gather(first_shard, "dp")]

    tokens = inputs.reshape(rows, width)
    cot = cotangent.reshape(rows, width)
    hidden = layer_norm(tokens, norm_params)

    half = ROT // 2
    lane = jnp.arange(128, dtype=jnp.int32) % HD
    frequency = 10000.0 ** (-((lane % half).astype(full) * 2.0 / ROT))
    angles = positions.reshape(rows).astype(full)[:, None] * frequency[None, :]
    cosine = jnp.where(lane < ROT, jnp.cos(angles), 1.0)
    sine = jnp.where(lane < half, -jnp.sin(angles), jnp.where(lane < ROT, jnp.sin(angles), 0.0))

    q, k, v, o, w_attend = project(n, me, attend_pieces, hidden, cot, cosine, sine, attend_bias)
    context, mixed_grad, bias_part = attend(batch, q, k, v, o, cosine, sine)
    attend_slots = attend_grads(n, me, hidden, cot, mixed_grad, context)
    last_shard, first_piece, attend_slots = lax.optimization_barrier(
        (shards[1], first_pieces[0], attend_slots)
    )
    active, gates_grad, w_feed, first_grads = feed_chunk(n, me, [first_piece], hidden, cot)
    hid_early, out_early = early_parts(context, mixed_grad, active, gates_grad, w_attend, w_feed)
    bias_grad = small_sum(bias_part, "dp")
    gathering, scattering = gather_hops(last_shard), scatter_hops(attend_slots)
    arrived = lax.optimization_barrier((next(gathering), first_grads))
    gathering.send(arrived[0])
    first_grads = arrived[1]
    for k in range(2, n):
        beside = (hid_early, out_early, bias_grad) if k == 2 else ()
        arrived = lax.optimization_barrier((next(gathering), next(scattering), beside))
        gathering.send(arrived[0])
        scattering.send(arrived[1])
        if k == 2:
            hid_early, out_early, bias_grad = arrived[2]
    last_pieces = next(gathering)
    arrived, last_pieces = lax.optimization_barrier((next(scattering), last_pieces))
    scattering.send(arrived)
    attend_grad = next(scattering)

    def scatter(grads):
        return lax.psum_scatter(grads, "dp", scatter_dimension=0, tiled=False)

    first_grads, _ = lax.optimization_barrier((first_grads, last_pieces))
    first_grads = scatter(first_grads)

    if fast:
        other_hid, other_out, own_hid, own_out, active, gates_grad = feed_last(
            n, info, True, last_pieces, hidden, cot, hid_early, out_early
        )
        came_hid, came_out = swap(other_hid, 1), swap(other_out, 1)
        e = rows // 8
        s = e // 2

        def send_rows(own, came):
            own = [own[i * e : (i + 1) * e].astype(full) + came[i * e : (i + 1) * e].astype(full) for i in range(4)]
            to_x, to_y = own[1].astype(low), own[3].astype(low)
            return own, (to_x, to_y), (swap(to_x, 2), swap(to_y, 4))

        def reduce_rows(own, came):
            over_x, over_y = came
            first = own[0] + over_x.astype(full)
            second = own[2] + over_y.astype(full)
            far = [swap(first[s:].astype(low), 4), swap(second[s:].astype(low), 2)]
            return [first[:s].astype(low), second[:s].astype(low)], far

        def spread_rows(first, second):
            first_y, second_x = swap(first, 4), swap(second, 2)
            first_x, second_y = swap(first, 2), swap(second, 4)
            first_xy, second_xy = swap(first_y, 2), swap(second_x, 4)
            return [first, first_y, first_x, first_xy, second, second_x, second_y, second_xy]

        own_hid, sent, came_hid = send_rows(own_hid, came_hid)
        active, gates_grad, _ = lax.optimization_barrier((active, gates_grad, sent))
        last_grads = feed_grads(n, hidden, cot, active, gates_grad)
        came_hid, last_grads, came_out, own_out = lax.optimization_barrier(
            (came_hid, last_grads, came_out, own_out)
        )
        own_out, _, came_out = send_rows(own_out, came_out)
        near, far = reduce_rows(own_hid, came_hid)
        back_a, back_b, norm_part = back_rows(info, tokens, near, far, norm_params)
        near, far = reduce_rows(own_out, came_out)
        out_a, out_b = add_rows(info, tokens, near, far)
        hid_pieces = spread_rows(back_a, back_b)
        hid_pieces[1], hid_pieces[5], out_a, out_b = lax.optimization_barrier(
            (hid_pieces[1], hid_pieces[5], out_a, out_b)
        )
        out_pieces = spread_rows(out_a, out_b)
        norm_grad = small_sum(small_sum(norm_part, "mp"), "dp")
        last_grads = scatter(last_grads)
    else:
        hid_part, out_part, active, gates_grad = feed_last(
            n, info, False, last_pieces, hidden, cot, hid_early, out_early
        )
        last_grads = scatter(feed_grads(n, hidden, cot, active, gates_grad))
        hidden_grad = lax.psum(hid_part, "mp").astype(full)
        summed = lax.psum(out_part, "mp").astype(full)
        values = tokens.astype(full)
        output = (values + summed).astype(low)
        centred = values - jnp.mean(values, axis=-1, keepdims=True)
        inv = lax.rsqrt(jnp.mean(centred * centred, axis=-1, keepdims=True) + epsilon)
        normal = centred * inv
        scaled = hidden_grad * norm_params[0]
        back = inv * (
            scaled
            - jnp.mean(scaled, axis=-1, keepdims=True)
            - normal * jnp.mean(scaled * normal, axis=-1, keepdims=True)
        )
        input_grad = cot.astype(full) + back
        norm_part = jnp.stack([jnp.sum(hidden_grad * normal, axis=0), jnp.sum(hidden_grad, axis=0)])
        norm_grad = small_sum(norm_part, "dp")

    grad_in = jnp.transpose(attend_grad[:3], (1, 0, 2))
    grad_out = attend_grad[3]

    total_tokens = rows * n
    new_in, moment_in_new, average_in_new = advance(
        w_attend_in, grad_in, moment_attend_in, average_attend_in, 0.5 / math.sqrt(width * total_tokens)
    )
    new_out, moment_out_new, average_out_new = advance(
        w_attend_out, grad_out, moment_attend_out, average_attend_out, 1.8 / math.sqrt(width * batch * n)
    )
    rates = (1.6 / math.sqrt(width * total_tokens), 0.77 / math.sqrt(FF * total_tokens))
    states = [jnp.transpose(a, (1, 2, 0)) for a in (w_expand, moment_expand, average_expand)]
    states += [jnp.transpose(a) for a in (w_reduce, moment_reduce, average_reduce)]
    first_grads = first_grads.reshape(3, cut, -1)
    last_grads = last_grads.reshape(3, units - cut, -1)
    begun = update_feed(0, first_grads, states, rates)
    if fast:
        updated = (norm_grad, new_in, new_out, begun)
        hid_pieces, updated = lax.optimization_barrier((hid_pieces, updated))
        norm_grad, new_in, new_out, begun = updated
    done = update_feed(cut, last_grads, states, rates, begun)
    if fast:
        mine_hid = pack_rows(info, hid_pieces)
        mine_out = pack_rows(info, out_pieces)
        input_grad = finish_rows(info, mine_hid, swap(mine_hid, 1), cot)
        other_out, done = lax.optimization_barrier((swap(mine_out, 1), done))
        output = finish_rows(info, mine_out, other_out)
    grad_expand, new_expand, moment_expand_new, average_expand_new = (
        jnp.transpose(a, (2, 0, 1)) for a in done[:4]
    )
    grad_reduce, new_reduce, moment_reduce_new, average_reduce_new = (
        jnp.transpose(a) for a in done[4:]
    )
    input_grad = input_grad.reshape(batch, length, width)
    output = output.reshape(batch, length, width)
    new_norm, moment_norm_new, average_norm_new = advance(
        norm_params, norm_grad, moment_norm, average_norm, 0.06 / math.sqrt(total_tokens)
    )
    new_bias, moment_bias_new, average_bias_new = advance(
        attend_bias, bias_grad, moment_bias, average_bias, 0.25 / math.sqrt(total_tokens)
    )
    return (
        output,
        input_grad,
        grad_in,
        grad_out,
        grad_expand,
        grad_reduce,
        norm_grad,
        bias_grad,
        new_in,
        new_out,
        new_expand,
        new_reduce,
        new_norm,
        new_bias,
        moment_in_new,
        moment_out_new,
        moment_expand_new,
        moment_reduce_new,
        moment_norm_new,
        moment_bias_new,
        average_in_new,
        average_out_new,
        average_expand_new,
        average_reduce_new,
        average_norm_new,
        average_bias_new,
    )


def solution(mesh):
    rows3 = P("dp", None, None)
    in3 = P("dp", None, "mp")
    in2 = P("dp", "mp")
    bias = P(None, "mp")
    states = (in3, in2, in3, in2, P(), bias)
    return jax.shard_map(
        body,
        mesh=mesh,
        in_specs=(rows3, P("dp", None), rows3) + states * 3,
        out_specs=(rows3, rows3) + states * 4,
        check_vma=False,
    )
```

```python
import functools
import math

import jax
import jax.numpy as jnp
from jax import lax
from jax.experimental import pallas as pl
from jax.experimental.pallas import tpu as pltpu
from jax.sharding import PartitionSpec as P

HD = 64
ROT = 16
FF = 5632

epsilon = 1e-05
decay_moment = 0.9
decay_average = 0.9
masked_score = -1e30

low = jnp.bfloat16
full = jnp.float32
vmem_limit = 60 << 20
tail_rows = 16


def dot_nt(left, right):
    return lax.dot_general(left, right, (((1,), (1,)), ((), ())), preferred_element_type=full)


def dot_nn(left, right):
    return lax.dot_general(left, right, (((1,), (0,)), ((), ())), preferred_element_type=full)


def dot_tn(left, right):
    return lax.dot_general(left, right, (((0,), (0,)), ((), ())), preferred_element_type=full)


def params(**more):
    return pltpu.CompilerParams(vmem_limit_bytes=vmem_limit, **more)


def cost(flops, moved, trans=0):
    return pl.CostEstimate(flops=int(flops), bytes_accessed=int(moved), transcendentals=int(trans))


def shape(dims, kind):
    return jax.ShapeDtypeStruct(dims, kind)


def advance(weight, grad, moment, average, rate):
    moment_new = decay_moment * moment + grad
    weight_new = weight - rate * (grad + decay_moment * moment_new)
    average_new = decay_average * average + (1.0 - decay_average) * weight_new
    return (weight_new, moment_new, average_new)


def after(value, *others):
    return lax.optimization_barrier((value, others))[0]


def gather_hop(k, right, left):
    n = lax.axis_size("dp")
    right = lax.ppermute(right, "dp", [(a, a + 1) for a in range(k - 1, n - 1)])
    left = lax.ppermute(left, "dp", [(a, a - 1) for a in range(1, n - k + 1)])
    return right, left


def scatter_load(k, slots, right, left):
    n = lax.axis_size("dp")
    to_right, to_left = slots[n - k], slots[k]
    if k > 1:
        to_right = (to_right.astype(full) + right.astype(full)).astype(low)
        to_left = (to_left.astype(full) + left.astype(full)).astype(low)
    return to_right, to_left


def scatter_hop(k, to_right, to_left):
    n = lax.axis_size("dp")
    right = lax.ppermute(to_right, "dp", [(a, a + 1) for a in range(k)])
    left = lax.ppermute(to_left, "dp", [(a, a - 1) for a in range(n - 1, n - 1 - k, -1)])
    return right, left


def swap(value, mask, axis="mp"):
    n = lax.axis_size(axis)
    return lax.ppermute(value, axis, [(a, a ^ mask) for a in range(n)])


def small_sum(value, axis):
    n = lax.axis_size(axis)
    if n & (n - 1):
        return lax.psum(value, axis)
    mask = 1
    while mask < n:
        value = value + swap(value, mask, axis)
        mask *= 2
    return value


def join_sums(norm_part, bias_part):
    cols = bias_part.shape[1]
    return jnp.concatenate([norm_part.reshape(-1, cols), bias_part])


def split_sums(sums, norm_part, bias_part):
    count = sums.shape[0] - bias_part.shape[0]
    return sums[:count].reshape(norm_part.shape), sums[count:]


def norm_kernel(x_ref, p_ref, o_ref):
    x = x_ref[...].astype(full)
    centred = x - jnp.mean(x, axis=-1, keepdims=True)
    inv = lax.rsqrt(jnp.mean(centred * centred, axis=-1, keepdims=True) + epsilon)
    o_ref[...] = (centred * inv * p_ref[0:1] + p_ref[1:2]).astype(low)


def layer_norm(rows, norm_params):
    count, width = rows.shape
    block = min(256, count)
    return pl.pallas_call(
        norm_kernel,
        grid=(count // block,),
        in_specs=[
            pl.BlockSpec((block, width), lambda i: (i, 0)),
            pl.BlockSpec((2, width), lambda i: (0, 0)),
        ],
        out_specs=pl.BlockSpec((block, width), lambda i: (i, 0)),
        out_shape=shape((count, width), low),
        compiler_params=params(),
        cost_estimate=cost(8 * count * width, 4 * count * width),
        name="layer_norm",
    )(rows, norm_params)


def fetch(n, me, pieces, target_of, sems, action):
    def run(source, index, sem):
        copy = pltpu.make_async_copy(source, target_of(index), sem)
        if action == "start":
            copy.start()
        else:
            copy.wait()

    if len(pieces) == 1:
        for j in range(n):
            run(pieces[0].at[j], j, sems.at[j])
        return
    run(pieces[0], me, sems.at[0])
    for k in range(1, n):

        @pl.when(me >= k)
        def _(k=k):
            run(pieces[k], me - k, sems.at[k])

        @pl.when(me + k < n)
        def _(k=k):
            run(pieces[n - 1 + k], me + k, sems.at[n - 1 + k])


def gates_of(w_ref, h, c):
    units = w_ref.shape[1]
    both = dot_nt(w_ref[0:2].reshape(2 * units, w_ref.shape[2]), h)
    gate, upper = both[:units], both[units:]
    active_grad = dot_nt(w_ref[2], c)
    sigmoid = jax.nn.sigmoid(gate)
    swish = gate * sigmoid
    active = (swish * upper).astype(low)
    gate_grad = active_grad * upper * sigmoid * (1.0 + gate * (1.0 - sigmoid))
    return active, jnp.concatenate([gate_grad, active_grad * swish], axis=0).astype(low)


def add_grads(acc, step, active, gates_grad, h, c):
    units = active.shape[0]

    @pl.when(step == 0)
    def _():
        acc[: 2 * units] = dot_nn(gates_grad, h)
        acc[2 * units :] = dot_nn(active, c)

    @pl.when(step > 0)
    def _():
        acc[: 2 * units] += dot_nn(gates_grad, h)
        acc[2 * units :] += dot_nn(active, c)


def store_grads(n, acc, out_ref):
    piece = out_ref.shape[2]
    for j in range(n):
        out_ref[j] = acc[:, j * piece : (j + 1) * piece].astype(low)


def wide_target(w_ref, piece):
    return lambda index: w_ref.at[:, :, pl.ds(pl.multiple_of(index * piece, piece), piece)]


def feed_kernel(n, count, me_ref, *refs):
    pieces = refs[:count]
    h_ref, c_ref, act_ref, grad_ref, w_ref, sems = refs[count:]
    target_of = wide_target(w_ref, w_ref.shape[2] // n)

    @pl.when(pl.program_id(0) == 0)
    def _():
        fetch(n, me_ref[0], pieces, target_of, sems, "start")
        fetch(n, me_ref[0], pieces, target_of, sems, "wait")

    act_ref[...], grad_ref[...] = gates_of(w_ref, h_ref[...], c_ref[...])


def feed_chunk(n, me, pieces, hidden, cot):
    rows, width = hidden.shape
    units = pieces[0].shape[-2]
    count = len(pieces)
    block = min(512, rows)
    row_spec = pl.BlockSpec((block, width), lambda i, m: (i, 0))
    return pl.pallas_call(
        functools.partial(feed_kernel, n, count),
        grid_spec=pltpu.PrefetchScalarGridSpec(
            num_scalar_prefetch=1,
            grid=(rows // block,),
            in_specs=[pl.BlockSpec(memory_space=pl.ANY)] * count + [row_spec, row_spec],
            out_specs=[
                pl.BlockSpec((units, block), lambda i, m: (0, i)),
                pl.BlockSpec((2 * units, block), lambda i, m: (0, i)),
                pl.BlockSpec((3, units, width), lambda i, m: (0, 0, 0)),
            ],
            scratch_shapes=[pltpu.SemaphoreType.DMA((2 * n - 1,))],
        ),
        out_shape=[
            shape((units, rows), low),
            shape((2 * units, rows), low),
            shape((3, units, width), low),
        ],
        compiler_params=params(),
        cost_estimate=cost(
            6 * rows * width * units, 4 * rows * width + 12 * units * width, rows * units
        ),
        name="feed_chunk",
    )(me, *pieces, hidden, cot)


def last_kernel(n, count, split, info_ref, *refs):
    pieces = refs[:count]
    h_ref, c_ref, hid_ref, out_ref = refs[count : count + 4]
    w_ref, sems = refs[-2:]
    act_ref, grad_ref = refs[-4:-2]
    parts = refs[count + 4 : -4]
    target_of = wide_target(w_ref, w_ref.shape[2] // n)
    step = pl.program_id(0)

    @pl.when(step == 0)
    def _():
        fetch(n, info_ref[3], pieces, target_of, sems, "start")
        fetch(n, info_ref[3], pieces, target_of, sems, "wait")

    active, gates_grad = gates_of(w_ref, h_ref[...], c_ref[...])
    act_ref[...] = active
    grad_ref[...] = gates_grad
    joined = w_ref[0:2].reshape(gates_grad.shape[0], w_ref.shape[2])
    hid = (hid_ref[...].astype(full) + dot_tn(gates_grad, joined)).astype(low)
    out = (out_ref[...].astype(full) + dot_tn(active, w_ref[2])).astype(low)
    if not split:
        parts[0][...] = hid
        parts[1][...] = out
        return
    sub = hid.shape[0] // 4
    high = jnp.where(step % 2 == 0, info_ref[1], info_ref[2])
    small = jnp.where(step % 2 == 0, info_ref[2], info_ref[1])
    for half in range(2):

        @pl.when(step // 2 == half)
        def _(half=half):
            for ref, value in ((parts[2 * half], hid), (parts[2 * half + 1], out)):
                for i in range(4):
                    at = ((i // 2) ^ high) * 2 + ((i % 2) ^ small)
                    place = pl.ds(pl.multiple_of(at * sub, sub), sub)
                    ref[place, :] = value[i * sub : (i + 1) * sub]


def feed_last(n, info, split, pieces, hidden, cot, hid_early, out_early):
    rows, width = hidden.shape
    units = pieces[0].shape[-2]
    count = len(pieces)
    if split:
        block, steps = rows // 4, 4
        place = lambda i, m: (m[0] ^ (1 - i // 2)) * 2 + i % 2
        part_specs = [pl.BlockSpec((block, width), lambda i, m: (jnp.minimum(i, 1), 0))] * 2
        part_specs += [pl.BlockSpec((block, width), lambda i, m: (jnp.maximum(i, 2) - 2, 0))] * 2
        part_shapes = [shape((rows // 2, width), low)] * 4
    else:
        block = min(256, rows)
        steps = rows // block
        place = lambda i, m: i
        part_specs = [pl.BlockSpec((block, width), lambda i, m: (i, 0))] * 2
        part_shapes = [shape((rows, width), low)] * 2
    row_spec = pl.BlockSpec((block, width), lambda i, m: (place(i, m), 0))
    return pl.pallas_call(
        functools.partial(last_kernel, n, count, split),
        grid_spec=pltpu.PrefetchScalarGridSpec(
            num_scalar_prefetch=1,
            grid=(steps,),
            in_specs=[pl.BlockSpec(memory_space=pl.ANY)] * count + [row_spec] * 4,
            out_specs=part_specs
            + [
                pl.BlockSpec((units, block), lambda i, m: (0, place(i, m))),
                pl.BlockSpec((2 * units, block), lambda i, m: (0, place(i, m))),
            ],
            scratch_shapes=[
                pltpu.VMEM((3, units, width), low),
                pltpu.SemaphoreType.DMA((2 * n - 1,)),
            ],
        ),
        out_shape=part_shapes + [shape((units, rows), low), shape((2 * units, rows), low)],
        compiler_params=params(),
        cost_estimate=cost(12 * rows * width * units, 12 * rows * width, rows * units),
        name="feed_last",
    )(info, *pieces, hidden, cot, hid_early, out_early)


def feed_grads_kernel(n, steps, h_ref, c_ref, act_ref, grad_ref, out_ref, acc):
    step = pl.program_id(0)
    add_grads(acc, step, act_ref[...], grad_ref[...], h_ref[...], c_ref[...])

    @pl.when(step == steps - 1)
    def _():
        store_grads(n, acc, out_ref)


def feed_grads(n, hidden, cot, active, gates_grad):
    rows, width = hidden.shape
    units = active.shape[0]
    piece = width // n
    block = min(512, rows)
    steps = rows // block
    row_spec = pl.BlockSpec((block, width), lambda i: (i, 0))
    return pl.pallas_call(
        functools.partial(feed_grads_kernel, n, steps),
        grid=(steps,),
        in_specs=[
            row_spec,
            row_spec,
            pl.BlockSpec((units, block), lambda i: (0, i)),
            pl.BlockSpec((2 * units, block), lambda i: (0, i)),
        ],
        out_specs=pl.BlockSpec((n, 3 * units, piece), lambda i: (0, 0, 0)),
        out_shape=shape((n, 3 * units, piece), low),
        scratch_shapes=[pltpu.VMEM((3 * units, width), full)],
        compiler_params=params(),
        cost_estimate=cost(6 * rows * width * units, 4 * rows * width + 12 * units * width),
        name="feed_grads",
    )(hidden, cot, active, gates_grad)


def turn(values, cosine, sine, half):
    cols = values.shape[1]
    lane = lax.broadcasted_iota(jnp.int32, (1, cols), 1) % HD
    other = jnp.where(
        lane < half, pltpu.roll(values, cols - half, 1), pltpu.roll(values, half, 1)
    )
    repeat = cols // cosine.shape[1]
    if repeat > 1:
        cosine = jnp.concatenate([cosine] * repeat, axis=1)
        sine = jnp.concatenate([sine] * repeat, axis=1)
    return values * cosine + other * sine


def project_kernel(n, count, me_ref, *refs):
    pieces = refs[:count]
    h_ref, c_ref, cos_ref, sin_ref, bias_ref, q_ref, k_ref, v_ref, o_ref, w_ref, sems = refs[
        count:
    ]
    piece = pieces[0].shape[-2]

    def target_of(index):
        return w_ref.at[:, pl.ds(pl.multiple_of(index * piece, piece), piece), :]

    @pl.when(pl.program_id(0) == 0)
    def _():
        fetch(n, me_ref[0], pieces, target_of, sems, "start")
        fetch(n, me_ref[0], pieces, target_of, sems, "wait")

    h = h_ref[...]
    cosine, sine = cos_ref[...], sin_ref[...]
    half = ROT // 2
    q_ref[...] = turn(dot_nn(h, w_ref[0]) + bias_ref[0:1], cosine, sine, half).astype(low)
    k_ref[...] = turn(dot_nn(h, w_ref[1]) + bias_ref[1:2], cosine, sine, half).astype(low)
    v_ref[...] = (dot_nn(h, w_ref[2]) + bias_ref[2:3]).astype(low)
    o_ref[...] = dot_nn(c_ref[...], w_ref[3]).astype(low)


def project(n, me, pieces, hidden, cot, cosine, sine, bias):
    rows, width = hidden.shape
    piece, cols = pieces[0].shape[-2:]
    count = len(pieces)
    block = min(512, rows)
    row_spec = pl.BlockSpec((block, width), lambda i, m: (i, 0))
    angle_spec = pl.BlockSpec((block, 128), lambda i, m: (i, 0))
    out_spec = pl.BlockSpec((block, cols), lambda i, m: (i, 0))
    return pl.pallas_call(
        functools.partial(project_kernel, n, count),
        grid_spec=pltpu.PrefetchScalarGridSpec(
            num_scalar_prefetch=1,
            grid=(rows // block,),
            in_specs=[pl.BlockSpec(memory_space=pl.ANY)] * count
            + [row_spec, row_spec, angle_spec, angle_spec]
            + [pl.BlockSpec((3, cols), lambda i, m: (0, 0))],
            out_specs=[out_spec] * 4 + [pl.BlockSpec((4, width, cols), lambda i, m: (0, 0, 0))],
            scratch_shapes=[pltpu.SemaphoreType.DMA((2 * n - 1,))],
        ),
        out_shape=[shape((rows, cols), low)] * 4 + [shape((4, width, cols), low)],
        compiler_params=params(),
        cost_estimate=cost(8 * rows * width * cols, 4 * rows * width + 16 * width * cols),
        name="project",
    )(me, *pieces, hidden, cot, cosine, sine, bias)


def attend_kernel(block, q_ref, k_ref, v_ref, o_ref, cos_ref, sin_ref, ctx_ref, mg_ref, bias_ref, dq, dk, dv):
    length, lanes = q_ref.shape
    scale = HD ** (-0.5)
    for head in range(lanes // HD):
        cols = slice(head * HD, (head + 1) * HD)
        for i in range(length // block):
            rows = slice(i * block, (i + 1) * block)
            end = (i + 1) * block
            q = q_ref[rows, cols]
            o = o_ref[rows, cols]
            k = k_ref[:end, cols]
            v = v_ref[:end, cols]
            scores = dot_nt(q, k) * scale
            row = i * block + lax.broadcasted_iota(jnp.int32, (block, end), 0)
            col = lax.broadcasted_iota(jnp.int32, (block, end), 1)
            scores = jnp.where(col <= row, scores, masked_score)
            top = jnp.max(scores, axis=-1, keepdims=True)
            weights = jnp.exp(scores - top)
            probs = weights * (1.0 / jnp.sum(weights, axis=-1, keepdims=True))
            probs_low = probs.astype(low)
            ctx_ref[rows, cols] = dot_nn(probs_low, v).astype(low)
            prob_grads = dot_nt(o, v)
            middle = jnp.sum(probs * prob_grads, axis=-1, keepdims=True)
            score_grads = (probs * (prob_grads - middle)).astype(low)
            dq[rows, cols] = dot_nn(score_grads, k) * scale
            key_part = dot_tn(score_grads, q) * scale
            value_part = dot_tn(probs_low, o)
            if i == 0:
                dk[:end, cols] = key_part
                dv[:end, cols] = value_part
                if end < length:
                    dk[end:, cols] = jnp.zeros((length - end, HD), full)
                    dv[end:, cols] = jnp.zeros((length - end, HD), full)
            else:
                dk[:end, cols] += key_part
                dv[:end, cols] += value_part
    cosine, sine = cos_ref[...], -sin_ref[...]
    half = ROT // 2
    sums = []
    for part, grads in enumerate(
        (turn(dq[...], cosine, sine, half), turn(dk[...], cosine, sine, half), dv[...])
    ):
        rounded = grads.astype(low)
        mg_ref[part] = rounded
        sums.append(jnp.sum(rounded.astype(full), axis=0, keepdims=True))
    total = jnp.concatenate(sums, axis=0)

    @pl.when(pl.program_id(1) == 0)
    def _():
        bias_ref[...] = total

    @pl.when(pl.program_id(1) > 0)
    def _():
        bias_ref[...] += total


def attend(batch, q, k, v, o, cosine, sine):
    rows, cols = q.shape
    length = rows // batch
    lanes = 128
    spec = pl.BlockSpec((length, lanes), lambda p, b: (b, p))
    angle_spec = pl.BlockSpec((length, 128), lambda p, b: (b, 0))
    return pl.pallas_call(
        functools.partial(attend_kernel, min(512, length)),
        grid=(cols // lanes, batch),
        in_specs=[spec] * 4 + [angle_spec] * 2,
        out_specs=[
            spec,
            pl.BlockSpec((3, length, lanes), lambda p, b: (0, b, p)),
            pl.BlockSpec((3, lanes), lambda p, b: (0, p)),
        ],
        out_shape=[
            shape((rows, cols), low),
            shape((3, rows, cols), low),
            shape((3, cols), full),
        ],
        scratch_shapes=[pltpu.VMEM((length, lanes), full)] * 3,
        compiler_params=params(),
        cost_estimate=cost(
            40 * rows * length * cols, 20 * rows * cols, rows * length * cols // HD
        ),
        name="attend",
    )(q, k, v, o, cosine, sine)


def attend_grads_kernel(n, me_ref, h_ref, c_ref, mg_ref, ctx_ref, *refs):
    own_ref, *slot_refs = refs[:n]
    wide = refs[n]
    step = pl.program_id(0)
    cols = ctx_ref.shape[1]

    @pl.when(step == 0)
    def _():
        for part in range(3):
            wide[:, part * cols : (part + 1) * cols] = mg_ref[part]

    grad = dot_tn(h_ref[...], wide[...])
    grads = [grad[:, part * cols : (part + 1) * cols] for part in range(3)]
    grads.append(dot_tn(c_ref[...], ctx_ref[...]))
    for j in range(n):

        @pl.when(step == j)
        def _(j=j):
            for part in range(4):
                if j == 0:
                    own_ref[part] = grads[part]
                else:
                    slot_refs[j - 1][part] = grads[part].astype(low)


def attend_grads(n, me, hidden, cot, mixed_grad, context):
    rows, width = hidden.shape
    cols = context.shape[1]
    piece = width // n
    whole3 = pl.BlockSpec((4, piece, cols), lambda i, m: (0, 0, 0))
    cut_spec = pl.BlockSpec((rows, piece), lambda i, m: (0, lax.rem(m[0] + i, n)))
    return pl.pallas_call(
        functools.partial(attend_grads_kernel, n),
        grid_spec=pltpu.PrefetchScalarGridSpec(
            num_scalar_prefetch=1,
            grid=(n,),
            in_specs=[
                cut_spec,
                cut_spec,
                pl.BlockSpec((3, rows, cols), lambda i, m: (0, 0, 0)),
                pl.BlockSpec((rows, cols), lambda i, m: (0, 0)),
            ],
            out_specs=[whole3] * n,
            scratch_shapes=[pltpu.VMEM((rows, 3 * cols), low)],
        ),
        out_shape=[shape((4, piece, cols), full)] + [shape((4, piece, cols), low)] * (n - 1),
        compiler_params=params(),
        cost_estimate=cost(8 * rows * width * cols, 4 * rows * width + 16 * width * cols),
        name="attend_grads",
    )(me, hidden, cot, mixed_grad, context)


def early_kernel(ctx_ref, mg_ref, act_ref, grad_ref, wa_ref, wf_ref, hid_ref, out_ref):
    hid = dot_nt(mg_ref[0], wa_ref[0]) + dot_nt(mg_ref[1], wa_ref[1]) + dot_nt(mg_ref[2], wa_ref[2])
    hid += dot_tn(grad_ref[...], wf_ref[0:2].reshape(grad_ref.shape[0], wf_ref.shape[2]))
    hid_ref[...] = hid.astype(low)
    out_ref[...] = (dot_nt(ctx_ref[...], wa_ref[3]) + dot_tn(act_ref[...], wf_ref[2])).astype(low)


def early_parts(context, mixed_grad, active, gates_grad, w_attend, w_feed):
    rows, cols = context.shape
    units, width = w_feed.shape[1:]
    block = min(256, rows)
    out_spec = pl.BlockSpec((block, width), lambda i: (i, 0))
    return pl.pallas_call(
        early_kernel,
        grid=(rows // block,),
        in_specs=[
            pl.BlockSpec((block, cols), lambda i: (i, 0)),
            pl.BlockSpec((3, block, cols), lambda i: (0, i, 0)),
            pl.BlockSpec((units, block), lambda i: (0, i)),
            pl.BlockSpec((2 * units, block), lambda i: (0, i)),
            pl.BlockSpec((4, width, cols), lambda i: (0, 0, 0)),
            pl.BlockSpec((3, units, width), lambda i: (0, 0, 0)),
        ],
        out_specs=[out_spec, out_spec],
        out_shape=[shape((rows, width), low)] * 2,
        compiler_params=params(),
        cost_estimate=cost(
            2 * rows * width * (4 * cols + 3 * units),
            4 * rows * width + 2 * (rows + width) * (4 * cols + 3 * units),
        ),
        name="early_parts",
    )(context, mixed_grad, active, gates_grad, w_attend, w_feed)


def sixteenth(which, m):
    return m[0] * 8 + (m[1] * 2 + m[2] if which == 0 else 4 + m[2] * 2 + m[1])


def back_kernel(info_ref, *refs):
    p_ref = refs[6]
    total = 0.0
    for x_ref, near_ref, far_ref, back_ref in zip(refs[0:2], refs[2:4], refs[4:6], refs[7:9]):
        x = x_ref[...].astype(full)
        centred = x - jnp.mean(x, axis=-1, keepdims=True)
        inv = lax.rsqrt(jnp.mean(centred * centred, axis=-1, keepdims=True) + epsilon)
        normal = centred * inv
        grad = near_ref[...].astype(full) + far_ref[...].astype(full)
        scaled = grad * p_ref[0:1]
        back = inv * (
            scaled
            - jnp.mean(scaled, axis=-1, keepdims=True)
            - normal * jnp.mean(scaled * normal, axis=-1, keepdims=True)
        )
        back_ref[: x.shape[0]] = back.astype(low)
        total += jnp.concatenate(
            [jnp.sum(grad * normal, axis=0, keepdims=True), jnp.sum(grad, axis=0, keepdims=True)],
            axis=0,
        )
    high = total.astype(low)
    rest = total - high.astype(full)
    middle = rest.astype(low)
    small = (rest - middle.astype(full)).astype(low)
    zeros = jnp.zeros((tail_rows - 6, total.shape[1]), full)
    terms = [high.astype(full), middle.astype(full), small.astype(full), zeros]
    refs[7][refs[0].shape[0] :] = jnp.concatenate(terms, axis=0).astype(low)


def back_rows(info, rows, near, far, norm_params):
    count, width = near[0].shape
    spec = pl.BlockSpec((count, width), lambda i, m: (0, 0))
    pair = pl.BlockSpec((2, width), lambda i, m: (0, 0))
    return pl.pallas_call(
        back_kernel,
        grid_spec=pltpu.PrefetchScalarGridSpec(
            num_scalar_prefetch=1,
            grid=(1,),
            in_specs=[
                pl.BlockSpec((count, width), lambda i, m: (sixteenth(0, m), 0)),
                pl.BlockSpec((count, width), lambda i, m: (sixteenth(1, m), 0)),
            ]
            + [spec] * 4
            + [pair],
            out_specs=[pl.BlockSpec((count + tail_rows, width), lambda i, m: (0, 0)), spec],
        ),
        out_shape=[shape((count + tail_rows, width), low), shape((count, width), low)],
        compiler_params=params(),
        cost_estimate=cost(40 * count * width, 16 * count * width),
        name="back_rows",
    )(info, rows, rows, *near, *far, norm_params)


def add_kernel(info_ref, *refs):
    for x_ref, near_ref, far_ref, out_ref in zip(refs[0:2], refs[2:4], refs[4:6], refs[6:8]):
        total = x_ref[...].astype(full) + near_ref[...].astype(full) + far_ref[...].astype(full)
        out_ref[...] = total.astype(low)


def add_rows(info, rows, near, far):
    count, width = near[0].shape
    spec = pl.BlockSpec((count, width), lambda i, m: (0, 0))
    return pl.pallas_call(
        add_kernel,
        grid_spec=pltpu.PrefetchScalarGridSpec(
            num_scalar_prefetch=1,
            grid=(1,),
            in_specs=[
                pl.BlockSpec((count, width), lambda i, m: (sixteenth(0, m), 0)),
                pl.BlockSpec((count, width), lambda i, m: (sixteenth(1, m), 0)),
            ]
            + [spec] * 4,
            out_specs=[spec, spec],
        ),
        out_shape=[shape((count, width), low)] * 2,
        compiler_params=params(),
        cost_estimate=cost(4 * count * width, 16 * count * width),
        name="add_rows",
    )(info, rows, rows, *near, *far)


def pack_kernel(block, info_ref, *refs):
    pieces, out_ref, sems = refs[:8], refs[8], refs[9]
    x, y = info_ref[1], info_ref[2]
    copies = []

    def move(source, at, size):
        place = out_ref.at[pl.ds(pl.multiple_of(at, 16), size), :]
        copies.append(pltpu.make_async_copy(source, place, sems.at[len(copies)]))

    for i, piece in enumerate(pieces):
        high, small = (i // 2) % 2, i % 2
        if i < 4:
            at = (x ^ high) * 2 + (y ^ small)
        else:
            at = 4 + (y ^ high) * 2 + (x ^ small)
        extra = piece.shape[0] - block
        move(piece.at[pl.ds(0, block), :], at * block, block)
        if extra:
            move(piece.at[pl.ds(block, extra), :], 8 * block + at * extra, extra)
    for copy in copies:
        copy.start()
    for copy in copies:
        copy.wait()


def pack_rows(info, pieces):
    block, width = pieces[-1].shape
    extra = pieces[0].shape[0] - block
    return pl.pallas_call(
        functools.partial(pack_kernel, block),
        grid_spec=pltpu.PrefetchScalarGridSpec(
            num_scalar_prefetch=1,
            grid=(1,),
            in_specs=[pl.BlockSpec(piece.shape, lambda i, m: (0, 0)) for piece in pieces],
            out_specs=pl.BlockSpec(memory_space=pl.ANY),
            scratch_shapes=[pltpu.SemaphoreType.DMA((12,))],
        ),
        out_shape=shape((8 * block + 4 * extra, width), low),
        compiler_params=params(),
        cost_estimate=cost(0, 32 * block * width),
        name="pack_rows",
    )(info, *pieces)


def tail_kernel(own_ref, other_ref, out_ref):
    def total(ref):
        values = ref[...].astype(full)
        sums = 0.0
        for i in range(4):
            at = i * tail_rows
            sums += values[at : at + 2] + values[at + 2 : at + 4] + values[at + 4 : at + 6]
        return sums

    out_ref[...] = total(own_ref) + total(other_ref)


def tail_sums(own, other):
    count, width = own.shape
    size = 4 * tail_rows
    spec = pl.BlockSpec((size, width), lambda i: (count // size - 1, 0))
    return pl.pallas_call(
        tail_kernel,
        grid=(1,),
        in_specs=[spec, spec],
        out_specs=pl.BlockSpec((2, width), lambda i: (0, 0)),
        out_shape=shape((2, width), full),
        compiler_params=params(),
        cost_estimate=cost(20 * width, 512 * width),
        name="tail_sums",
    )(own, other)


def finish_kernel(info_ref, *refs):
    own_ref, other_ref, out_ref = refs[-3:]
    mine = (pl.program_id(0) // 4) == info_ref[0]

    def store(value):
        if len(refs) == 4:
            value = refs[0][...].astype(full) + value.astype(full)
        out_ref[...] = value

    @pl.when(mine)
    def _():
        store(own_ref[...])

    @pl.when(jnp.logical_not(mine))
    def _():
        store(other_ref[...])


def finish_rows(info, rows, own, other, cot=None):
    width = own.shape[1]
    extra = () if cot is None else (cot,)
    block = rows // 8
    spec = pl.BlockSpec((block, width), lambda i, m: (i, 0))
    edge = lambda i: jnp.where(i < 4, 0, 3)
    return pl.pallas_call(
        finish_kernel,
        grid_spec=pltpu.PrefetchScalarGridSpec(
            num_scalar_prefetch=1,
            grid=(8,),
            in_specs=[spec] * len(extra)
            + [
                pl.BlockSpec((block, width), lambda i, m: (jnp.where(i // 4 == m[0], i % 4, edge(i)), 0)),
                pl.BlockSpec((block, width), lambda i, m: (jnp.where(i // 4 == m[0], edge(i), i % 4), 0)),
            ],
            out_specs=spec,
        ),
        out_shape=shape((rows, width), low if cot is None else full),
        compiler_params=params(),
        cost_estimate=cost(2 * rows * width, 8 * rows * width),
        name="finish_rows",
    )(info, *extra, own, other)


def update_kernel(rates, count, *refs):
    g_ref = refs[0]
    ins = refs[1:7]
    outs = refs[7 + count :]
    for which, rate in enumerate(rates):
        grad = g_ref[:2] if which == 0 else g_ref[2]
        grad = grad.astype(full)
        w, m, a = (ref[...] for ref in ins[3 * which : 3 * which + 3])
        g_out, w_out, m_out, a_out = outs[4 * which : 4 * which + 4]
        g_out[...] = grad
        w_out[...], m_out[...], a_out[...] = advance(w, grad, m, a, rate)


def update_feed(start, grads, states, rates, begun=()):
    _, units, piece = grads.shape
    block = math.gcd(start, units)
    while block > 128 and block % 16 == 0:
        block //= 2
    at = start // block
    pair = pl.BlockSpec((2, block, piece), lambda i: (0, at + i, 0))
    single = pl.BlockSpec((block, piece), lambda i: (at + i, 0))
    total = states[0].shape[1]
    return pl.pallas_call(
        functools.partial(update_kernel, rates, len(begun)),
        grid=(units // block,),
        in_specs=[pl.BlockSpec((3, block, piece), lambda i: (0, i, 0))]
        + [pair] * 3
        + [single] * 3
        + [pl.BlockSpec(memory_space=pl.ANY)] * len(begun),
        out_specs=[pair] * 4 + [single] * 4,
        out_shape=[shape((2, total, piece), full)] * 4 + [shape((total, piece), full)] * 4,
        input_output_aliases={7 + i: i for i in range(len(begun))},
        compiler_params=params(),
        cost_estimate=cost(30 * units * piece, 3 * 30 * units * piece),
        name="update_feed",
    )(grads, *states, *begun)


def body(
    inputs,
    positions,
    cotangent,
    w_attend_in,
    w_attend_out,
    w_expand,
    w_reduce,
    norm_params,
    attend_bias,
    moment_attend_in,
    moment_attend_out,
    moment_expand,
    moment_reduce,
    moment_norm,
    moment_bias,
    average_attend_in,
    average_attend_out,
    average_expand,
    average_reduce,
    average_norm,
    average_bias,
):
    batch, length, width = inputs.shape
    rows = batch * length
    units = w_expand.shape[2]
    n = lax.axis_size("dp")
    group = lax.axis_size("mp")
    me = lax.axis_index("dp").astype(jnp.int32).reshape(1)
    spot = lax.axis_index("mp").astype(jnp.int32)
    info = jnp.stack([spot & 1, (spot >> 1) & 1, (spot >> 2) & 1, me[0]])
    fast = group == 8

    expand_t = jnp.transpose(w_expand, (1, 2, 0))
    reduce_t = jnp.transpose(w_reduce)
    in_t = jnp.transpose(w_attend_in, (1, 0, 2))
    cut = units // 2 // 16 * 16
    shards = [
        jnp.concatenate([expand_t[:, a:b], reduce_t[None, a:b]], axis=0).astype(low)
        for a, b in ((0, cut), (cut, units))
    ]
    attend_shard = jnp.concatenate([in_t, w_attend_out[None]], axis=0).astype(low)
    attend_pieces = [lax.all_gather(attend_shard, "dp")]
    first_shard, _ = lax.optimization_barrier((shards[0], attend_shard))
    first_pieces = [lax.all_gather(first_shard, "dp")]

    tokens = inputs.reshape(rows, width)
    cot = cotangent.reshape(rows, width)
    hidden = layer_norm(tokens, norm_params)

    half = ROT // 2
    lane = jnp.arange(128, dtype=jnp.int32) % HD
    frequency = 10000.0 ** (-((lane % half).astype(full) * 2.0 / ROT))
    angles = positions.reshape(rows).astype(full)[:, None] * frequency[None, :]
    cosine = jnp.where(lane < ROT, jnp.cos(angles), 1.0)
    sine = jnp.where(lane < half, -jnp.sin(angles), jnp.where(lane < ROT, jnp.sin(angles), 0.0))

    q, k, v, o, w_attend = project(n, me, attend_pieces, hidden, cot, cosine, sine, attend_bias)
    context, mixed_grad, bias_part = attend(batch, q, k, v, o, cosine, sine)
    attend_slots = attend_grads(n, me, hidden, cot, mixed_grad, context)
    last_shard, first_piece, attend_slots = lax.optimization_barrier(
        (shards[1], first_pieces[0], attend_slots)
    )

    rights, lefts = [last_shard], [last_shard]
    came, beside = (None, None), None
    for k in range(1, n):
        right, left = gather_hop(k, rights[-1], lefts[-1])
        if k > 1:
            slots = after(attend_slots, (rights[-1], lefts[-1]))
            coming = scatter_hop(k - 1, *scatter_load(k - 1, slots, *came))
        if k == 1:
            active, gates_grad, w_feed = feed_chunk(n, me, [first_piece], hidden, cot)
            beside = (active, gates_grad, w_feed)
        elif k == 2:
            hid_early, out_early = early_parts(
                context, mixed_grad, active, gates_grad, w_attend, w_feed
            )
            beside = (hid_early, out_early)
        elif k == 3:
            first_grads = feed_grads(n, hidden, cot, active, gates_grad)
            beside = (first_grads,)
        if k > 1:
            right, left, came = lax.optimization_barrier((right, left, coming, beside))[:3]
        else:
            right, left = lax.optimization_barrier((right, left, beside))[:2]
        rights.append(right)
        lefts.append(left)
    load = scatter_load(n - 1, attend_slots, *came)
    came = scatter_hop(n - 1, *load)
    attend_grad = attend_slots[0] + came[0].astype(full) + came[1].astype(full)
    last_pieces = after([last_shard] + rights[1:] + lefts[1:], load)

    def scatter(grads):
        return lax.psum_scatter(grads, "dp", scatter_dimension=0, tiled=False)

    first_grads = scatter(first_grads).reshape(3, cut, -1)

    grad_in = jnp.transpose(attend_grad[:3], (1, 0, 2))
    grad_out = attend_grad[3]
    total_tokens = rows * n
    attend_new = advance(
        w_attend_in, grad_in, moment_attend_in, average_attend_in, 0.5 / math.sqrt(width * total_tokens)
    ) + advance(
        w_attend_out, grad_out, moment_attend_out, average_attend_out, 1.8 / math.sqrt(width * batch * n)
    )
    rates = (1.6 / math.sqrt(width * total_tokens), 0.77 / math.sqrt(FF * total_tokens))
    states = [jnp.transpose(a, (1, 2, 0)) for a in (w_expand, moment_expand, average_expand)]
    states += [jnp.transpose(a) for a in (w_reduce, moment_reduce, average_reduce)]

    if fast:
        other_hid, other_out, own_hid, own_out, active, gates_grad = feed_last(
            n, info, True, last_pieces, hidden, cot, hid_early, out_early
        )
        e = rows // 8
        s = e // 2

        def sum_cores(own, came):
            own = [own[i * e : (i + 1) * e].astype(full) + came[i * e : (i + 1) * e].astype(full) for i in range(4)]
            return own, (own[1].astype(low), own[3].astype(low))

        def sum_first(own, came):
            first = own[0] + came[0].astype(full)
            second = own[2] + came[1].astype(full)
            near = [first[:s].astype(low), second[:s].astype(low)]
            return near, (first[s:].astype(low), second[s:].astype(low))

        def both_ways(pair, masks):
            return [swap(pair[0], masks[0]), swap(pair[1], masks[1])]

        came_hid = swap(other_hid, 1)
        came_out = swap(after(other_out, came_hid), 1)
        own_hid, load_hid = sum_cores(own_hid, came_hid)
        one_hid = both_ways(load_hid, (2, 4))
        active, gates_grad = after((active, gates_grad), load_hid)
        last_grads = feed_grads(n, hidden, cot, active, gates_grad)
        own_out, load_out = sum_cores(own_out, came_out)
        one_hid = after(one_hid, last_grads, load_out)
        last_grads = scatter(last_grads).reshape(3, units - cut, -1)
        near_hid, load_hid = sum_first(own_hid, one_hid)
        two_hid = both_ways(load_hid, (4, 2))
        load_out = after(load_out, load_hid)
        one_out = both_ways(load_out, (2, 4))
        two_hid = after(two_hid, attend_new)
        back = back_rows(info, tokens, near_hid, two_hid, norm_params)
        hid_one = both_ways(back, (4, 2))
        hid_two = both_ways(back, (2, 4))
        one_out = after(one_out, back)
        near_out, load_out = sum_first(own_out, one_out)
        two_out = both_ways(load_out, (4, 2))
        begun = update_feed(0, after(first_grads, load_out), states, rates)
        hid_one = after(hid_one, begun)
        hid_three = both_ways(hid_one, (2, 4))
        two_out = after(two_out, hid_one)
        add = add_rows(info, tokens, near_out, two_out)
        out_one = both_ways(add, (4, 2))
        out_two = both_ways(add, (2, 4))
        hid_two, hid_three = after((hid_two, hid_three), add)
        mine_hid = pack_rows(
            info, [back[0], hid_one[0], hid_two[0], hid_three[0], back[1], hid_one[1], hid_two[1], hid_three[1]]
        )
        out_one = after(out_one, mine_hid)
        out_three = both_ways(out_one, (2, 4))
        other_hid = after(swap(mine_hid, 1), out_one)
        norm_part = tail_sums(mine_hid, other_hid)
        sums = small_sum(join_sums(norm_part, bias_part), "dp")
        input_grad = finish_rows(info, rows, mine_hid, after(other_hid, norm_part), cot)
        done = update_feed(cut, after(last_grads, input_grad), states, rates, begun)
        out_two, out_three = after((out_two, out_three), done)
        mine_out = pack_rows(
            info, [add[0], out_one[0], out_two[0], out_three[0], add[1], out_one[1], out_two[1], out_three[1]]
        )
        output = finish_rows(info, rows, mine_out, swap(mine_out, 1))
        norm_grad, bias_grad = split_sums(sums, norm_part, bias_part)
    else:
        hid_part, out_part, active, gates_grad = feed_last(
            n, info, False, last_pieces, hidden, cot, hid_early, out_early
        )
        last_grads = scatter(feed_grads(n, hidden, cot, active, gates_grad)).reshape(3, units - cut, -1)
        hidden_grad = lax.psum(hid_part, "mp").astype(full)
        summed = lax.psum(out_part, "mp").astype(full)
        values = tokens.astype(full)
        output = (values + summed).astype(low)
        centred = values - jnp.mean(values, axis=-1, keepdims=True)
        inv = lax.rsqrt(jnp.mean(centred * centred, axis=-1, keepdims=True) + epsilon)
        normal = centred * inv
        scaled = hidden_grad * norm_params[0]
        back = inv * (
            scaled
            - jnp.mean(scaled, axis=-1, keepdims=True)
            - normal * jnp.mean(scaled * normal, axis=-1, keepdims=True)
        )
        input_grad = cot.astype(full) + back
        norm_part = jnp.stack([jnp.sum(hidden_grad * normal, axis=0), jnp.sum(hidden_grad, axis=0)])
        sums = small_sum(join_sums(norm_part, bias_part), "dp")
        norm_grad, bias_grad = split_sums(sums, norm_part, bias_part)
        begun = update_feed(0, first_grads, states, rates)
        done = update_feed(cut, last_grads, states, rates, begun)
    new_in, moment_in_new, average_in_new, new_out, moment_out_new, average_out_new = attend_new
    grad_expand, new_expand, moment_expand_new, average_expand_new = (
        jnp.transpose(a, (2, 0, 1)) for a in done[:4]
    )
    grad_reduce, new_reduce, moment_reduce_new, average_reduce_new = (
        jnp.transpose(a) for a in done[4:]
    )
    input_grad = input_grad.reshape(batch, length, width)
    output = output.reshape(batch, length, width)
    new_norm, moment_norm_new, average_norm_new = advance(
        norm_params, norm_grad, moment_norm, average_norm, 0.06 / math.sqrt(total_tokens)
    )
    new_bias, moment_bias_new, average_bias_new = advance(
        attend_bias, bias_grad, moment_bias, average_bias, 0.25 / math.sqrt(total_tokens)
    )
    return (
        output,
        input_grad,
        grad_in,
        grad_out,
        grad_expand,
        grad_reduce,
        norm_grad,
        bias_grad,
        new_in,
        new_out,
        new_expand,
        new_reduce,
        new_norm,
        new_bias,
        moment_in_new,
        moment_out_new,
        moment_expand_new,
        moment_reduce_new,
        moment_norm_new,
        moment_bias_new,
        average_in_new,
        average_out_new,
        average_expand_new,
        average_reduce_new,
        average_norm_new,
        average_bias_new,
    )


def solution(mesh):
    rows3 = P("dp", None, None)
    in3 = P("dp", None, "mp")
    in2 = P("dp", "mp")
    bias = P(None, "mp")
    states = (in3, in2, in3, in2, P(), bias)
    return jax.shard_map(
        body,
        mesh=mesh,
        in_specs=(rows3, P("dp", None), rows3) + states * 3,
        out_specs=(rows3, rows3) + states * 4,
        check_vma=False,
    )
```

```python
import functools
import math

import jax
import jax.numpy as jnp
from jax import lax
from jax.experimental import pallas as pl
from jax.experimental.pallas import tpu as pltpu
from jax.sharding import PartitionSpec as P

HD = 64
ROT = 16
FF = 5632

epsilon = 1e-05
decay_moment = 0.9
decay_average = 0.9
masked_score = -1e30

low = jnp.bfloat16
full = jnp.float32
vmem_limit = 60 << 20
tail_rows = 16


def dot_nt(left, right):
    return lax.dot_general(left, right, (((1,), (1,)), ((), ())), preferred_element_type=full)


def dot_nn(left, right):
    return lax.dot_general(left, right, (((1,), (0,)), ((), ())), preferred_element_type=full)


def dot_tn(left, right):
    return lax.dot_general(left, right, (((0,), (0,)), ((), ())), preferred_element_type=full)


def params(**more):
    return pltpu.CompilerParams(vmem_limit_bytes=vmem_limit, **more)


def cost(flops, moved, trans=0):
    return pl.CostEstimate(flops=int(flops), bytes_accessed=int(moved), transcendentals=int(trans))


def shape(dims, kind):
    return jax.ShapeDtypeStruct(dims, kind)


def advance(weight, grad, moment, average, rate):
    moment_new = decay_moment * moment + grad
    weight_new = weight - rate * (grad + decay_moment * moment_new)
    average_new = decay_average * average + (1.0 - decay_average) * weight_new
    return (weight_new, moment_new, average_new)


def after(value, *others):
    return lax.optimization_barrier((value, others))[0]


def gather_hop(k, right, left, me):
    n = lax.axis_size("dp")
    to_right = [(a, a + 1) for a in range(k - 1, n - 1)]
    to_left = [(a, a - 1) for a in range(1, n - k + 1)]
    if k == n - 1 and n != 3:
        both = lax.ppermute(jnp.where(me == 1, left, right), "dp", to_right + to_left)
        return both, both
    return lax.ppermute(right, "dp", to_right), lax.ppermute(left, "dp", to_left)


def scatter_load(k, slots, right, left):
    n = lax.axis_size("dp")
    to_right, to_left = slots[n - k], slots[k]
    if k > 1:
        to_right = (to_right.astype(full) + right.astype(full)).astype(low)
        to_left = (to_left.astype(full) + left.astype(full)).astype(low)
    return to_right, to_left


def scatter_hop(k, to_right, to_left):
    n = lax.axis_size("dp")
    rights = [(a, a + 1) for a in range(k)]
    lefts = [(a, a - 1) for a in range(n - 1, n - 1 - k, -1)]
    if k == 1 and n != 3:
        both = lax.ppermute(to_right, "dp", rights + lefts)
        return both, both
    return lax.ppermute(to_right, "dp", rights), lax.ppermute(to_left, "dp", lefts)


def swap(value, mask, axis="mp"):
    n = lax.axis_size(axis)
    return lax.ppermute(value, axis, [(a, a ^ mask) for a in range(n)])


def small_sum(value, axis):
    n = lax.axis_size(axis)
    if n & (n - 1):
        return lax.psum(value, axis)
    mask = 1
    while mask < n:
        value = value + swap(value, mask, axis)
        mask *= 2
    return value


def join_sums(norm_part, bias_part):
    cols = bias_part.shape[1]
    return jnp.concatenate([norm_part.reshape(-1, cols), bias_part])


def split_sums(sums, norm_part, bias_part):
    count = sums.shape[0] - bias_part.shape[0]
    return sums[:count].reshape(norm_part.shape), sums[count:]


def norm_kernel(x_ref, p_ref, o_ref):
    x = x_ref[...].astype(full)
    centred = x - jnp.mean(x, axis=-1, keepdims=True)
    inv = lax.rsqrt(jnp.mean(centred * centred, axis=-1, keepdims=True) + epsilon)
    o_ref[...] = (centred * inv * p_ref[0:1] + p_ref[1:2]).astype(low)


def layer_norm(rows, norm_params):
    count, width = rows.shape
    block = min(256, count)
    return pl.pallas_call(
        norm_kernel,
        grid=(count // block,),
        in_specs=[
            pl.BlockSpec((block, width), lambda i: (i, 0)),
            pl.BlockSpec((2, width), lambda i: (0, 0)),
        ],
        out_specs=pl.BlockSpec((block, width), lambda i: (i, 0)),
        out_shape=shape((count, width), low),
        compiler_params=params(),
        cost_estimate=cost(8 * count * width, 4 * count * width),
        name="layer_norm",
    )(rows, norm_params)


def fetch(n, me, pieces, target_of, sems, action):
    def run(source, index, sem):
        copy = pltpu.make_async_copy(source, target_of(index), sem)
        if action == "start":
            copy.start()
        else:
            copy.wait()

    if len(pieces) == 1:
        for j in range(n):
            run(pieces[0].at[j], j, sems.at[j])
        return
    run(pieces[0], me, sems.at[0])
    for k in range(1, n):

        @pl.when(me >= k)
        def _(k=k):
            run(pieces[k], me - k, sems.at[k])

        @pl.when(me + k < n)
        def _(k=k):
            run(pieces[n - 1 + k], me + k, sems.at[n - 1 + k])


def swish_of(both):
    units = both.shape[0] // 2
    gate, upper = both[:units], both[units:]
    sigmoid = jax.nn.sigmoid(gate)
    return gate, upper, sigmoid, gate * sigmoid


def join_gates(w_ref):
    return w_ref[0:2].reshape(2 * w_ref.shape[1], w_ref.shape[2])


def gates_grad_of(both, active_grad):
    gate, upper, sigmoid, swish = swish_of(both)
    gate_grad = active_grad * upper * sigmoid * (1.0 + gate * (1.0 - sigmoid))
    return jnp.concatenate([gate_grad, active_grad * swish], axis=0).astype(low)


def gates_of(w_ref, h, c):
    both = dot_nt(join_gates(w_ref), h)
    _, upper, _, swish = swish_of(both)
    return (swish * upper).astype(low), gates_grad_of(both, dot_nt(w_ref[2], c))


def add_grads(acc, step, active, gates_grad, h, c):
    units = active.shape[0]

    @pl.when(step == 0)
    def _():
        acc[: 2 * units] = dot_nn(gates_grad, h)
        acc[2 * units :] = dot_nn(active, c)

    @pl.when(step > 0)
    def _():
        acc[: 2 * units] += dot_nn(gates_grad, h)
        acc[2 * units :] += dot_nn(active, c)


def store_grads(n, acc, out_ref):
    piece = out_ref.shape[2]
    for j in range(n):
        out_ref[j] = acc[:, j * piece : (j + 1) * piece].astype(low)


def wide_target(w_ref, piece):
    return lambda index: w_ref.at[:, :, pl.ds(pl.multiple_of(index * piece, piece), piece)]


def feed_kernel(n, count, me_ref, *refs):
    pieces = refs[:count]
    h_ref, c_ref, act_ref, grad_ref, w_ref, sems = refs[count:]
    target_of = wide_target(w_ref, w_ref.shape[2] // n)

    @pl.when(pl.program_id(0) == 0)
    def _():
        fetch(n, me_ref[0], pieces, target_of, sems, "start")
        fetch(n, me_ref[0], pieces, target_of, sems, "wait")

    act_ref[...], grad_ref[...] = gates_of(w_ref, h_ref[...], c_ref[...])


def feed_chunk(n, me, pieces, hidden, cot):
    rows, width = hidden.shape
    units = pieces[0].shape[-2]
    count = len(pieces)
    block = min(512, rows)
    row_spec = pl.BlockSpec((block, width), lambda i, m: (i, 0))
    return pl.pallas_call(
        functools.partial(feed_kernel, n, count),
        grid_spec=pltpu.PrefetchScalarGridSpec(
            num_scalar_prefetch=1,
            grid=(rows // block,),
            in_specs=[pl.BlockSpec(memory_space=pl.ANY)] * count + [row_spec, row_spec],
            out_specs=[
                pl.BlockSpec((units, block), lambda i, m: (0, i)),
                pl.BlockSpec((2 * units, block), lambda i, m: (0, i)),
                pl.BlockSpec((3, units, width), lambda i, m: (0, 0, 0)),
            ],
            scratch_shapes=[pltpu.SemaphoreType.DMA((2 * n - 1,))],
        ),
        out_shape=[
            shape((units, rows), low),
            shape((2 * units, rows), low),
            shape((3, units, width), low),
        ],
        compiler_params=params(),
        cost_estimate=cost(
            6 * rows * width * units, 4 * rows * width + 12 * units * width, rows * units
        ),
        name="feed_chunk",
    )(me, *pieces, hidden, cot)


def put_part(split, info_ref, parts, value):
    if not split:
        parts[0][...] = value
        return
    step = pl.program_id(0)
    sub = value.shape[0] // 4
    high = jnp.where(step % 2 == 0, info_ref[1], info_ref[2])
    small = jnp.where(step % 2 == 0, info_ref[2], info_ref[1])
    for half in range(2):

        @pl.when(step // 2 == half)
        def _(half=half):
            for i in range(4):
                at = ((i // 2) ^ high) * 2 + ((i % 2) ^ small)
                place = pl.ds(pl.multiple_of(at * sub, sub), sub)
                parts[half][place, :] = value[i * sub : (i + 1) * sub]


def last_blocks(split, rows, width):
    if split:
        block, steps = rows // 4, 4
        place = lambda i, m: (m[0] ^ (1 - i // 2)) * 2 + i % 2
        part_specs = [
            pl.BlockSpec((block, width), lambda i, m: (jnp.minimum(i, 1), 0)),
            pl.BlockSpec((block, width), lambda i, m: (jnp.maximum(i, 2) - 2, 0)),
        ]
        part_shapes = [shape((rows // 2, width), low)] * 2
    else:
        block = min(256, rows)
        steps = rows // block
        place = lambda i, m: i
        part_specs = [pl.BlockSpec((block, width), lambda i, m: (i, 0))]
        part_shapes = [shape((rows, width), low)]
    return block, steps, place, part_specs, part_shapes


def out_last_kernel(n, count, split, info_ref, *refs):
    pieces = refs[:count]
    h_ref, early_ref = refs[count : count + 2]
    parts = refs[count + 2 : -4]
    act_ref, both_ref, w_ref, sems = refs[-4:]
    target_of = wide_target(w_ref, w_ref.shape[2] // n)

    @pl.when(pl.program_id(0) == 0)
    def _():
        fetch(n, info_ref[3], pieces, target_of, sems, "start")
        fetch(n, info_ref[3], pieces, target_of, sems, "wait")

    both = dot_nt(join_gates(w_ref), h_ref[...])
    both_ref[...] = both
    _, upper, _, swish = swish_of(both)
    active = (swish * upper).astype(low)
    act_ref[...] = active
    put_part(split, info_ref, parts, (early_ref[...].astype(full) + dot_tn(active, w_ref[2])).astype(low))


def out_last(n, info, split, pieces, hidden, early):
    rows, width = hidden.shape
    units = pieces[0].shape[-2]
    count = len(pieces)
    block, steps, place, part_specs, part_shapes = last_blocks(split, rows, width)
    row_spec = pl.BlockSpec((block, width), lambda i, m: (place(i, m), 0))
    return pl.pallas_call(
        functools.partial(out_last_kernel, n, count, split),
        grid_spec=pltpu.PrefetchScalarGridSpec(
            num_scalar_prefetch=1,
            grid=(steps,),
            in_specs=[pl.BlockSpec(memory_space=pl.ANY)] * count + [row_spec] * 2,
            out_specs=part_specs
            + [
                pl.BlockSpec((units, block), lambda i, m: (0, place(i, m))),
                pl.BlockSpec((2 * units, block), lambda i, m: (0, place(i, m))),
                pl.BlockSpec((3, units, width), lambda i, m: (0, 0, 0)),
            ],
            scratch_shapes=[pltpu.SemaphoreType.DMA((2 * n - 1,))],
        ),
        out_shape=part_shapes
        + [shape((units, rows), low), shape((2 * units, rows), full), shape((3, units, width), low)],
        compiler_params=params(),
        cost_estimate=cost(6 * rows * width * units, 8 * rows * width, rows * units),
        name="out_last",
    )(info, *pieces, hidden, early)


def hid_last_kernel(split, info_ref, w_ref, both_ref, c_ref, early_ref, *refs):
    grad_ref = refs[-1]
    gates_grad = gates_grad_of(both_ref[...], dot_nt(w_ref[2], c_ref[...]))
    grad_ref[...] = gates_grad
    hid = early_ref[...].astype(full) + dot_tn(gates_grad, join_gates(w_ref))
    put_part(split, info_ref, refs[:-1], hid.astype(low))


def hid_last(info, split, weights, both, cot, early):
    rows, width = cot.shape
    units = weights.shape[1]
    block, steps, place, part_specs, part_shapes = last_blocks(split, rows, width)
    row_spec = pl.BlockSpec((block, width), lambda i, m: (place(i, m), 0))
    both_spec = pl.BlockSpec((2 * units, block), lambda i, m: (0, place(i, m)))
    return pl.pallas_call(
        functools.partial(hid_last_kernel, split),
        grid_spec=pltpu.PrefetchScalarGridSpec(
            num_scalar_prefetch=1,
            grid=(steps,),
            in_specs=[pl.BlockSpec((3, units, width), lambda i, m: (0, 0, 0)), both_spec]
            + [row_spec] * 2,
            out_specs=part_specs + [both_spec],
        ),
        out_shape=part_shapes + [shape((2 * units, rows), low)],
        compiler_params=params(),
        cost_estimate=cost(6 * rows * width * units, 8 * rows * width, rows * units),
        name="hid_last",
    )(info, weights, both, cot, early)


def feed_grads_kernel(n, steps, h_ref, c_ref, act_ref, grad_ref, out_ref, acc):
    step = pl.program_id(0)
    add_grads(acc, step, act_ref[...], grad_ref[...], h_ref[...], c_ref[...])

    @pl.when(step == steps - 1)
    def _():
        store_grads(n, acc, out_ref)


def feed_grads(n, hidden, cot, active, gates_grad):
    rows, width = hidden.shape
    units = active.shape[0]
    piece = width // n
    block = min(512, rows)
    steps = rows // block
    row_spec = pl.BlockSpec((block, width), lambda i: (i, 0))
    return pl.pallas_call(
        functools.partial(feed_grads_kernel, n, steps),
        grid=(steps,),
        in_specs=[
            row_spec,
            row_spec,
            pl.BlockSpec((units, block), lambda i: (0, i)),
            pl.BlockSpec((2 * units, block), lambda i: (0, i)),
        ],
        out_specs=pl.BlockSpec((n, 3 * units, piece), lambda i: (0, 0, 0)),
        out_shape=shape((n, 3 * units, piece), low),
        scratch_shapes=[pltpu.VMEM((3 * units, width), full)],
        compiler_params=params(),
        cost_estimate=cost(6 * rows * width * units, 4 * rows * width + 12 * units * width),
        name="feed_grads",
    )(hidden, cot, active, gates_grad)


def turn(values, cosine, sine, half):
    cols = values.shape[1]
    lane = lax.broadcasted_iota(jnp.int32, (1, cols), 1) % HD
    other = jnp.where(
        lane < half, pltpu.roll(values, cols - half, 1), pltpu.roll(values, half, 1)
    )
    repeat = cols // cosine.shape[1]
    if repeat > 1:
        cosine = jnp.concatenate([cosine] * repeat, axis=1)
        sine = jnp.concatenate([sine] * repeat, axis=1)
    return values * cosine + other * sine


def project_kernel(n, count, me_ref, *refs):
    pieces = refs[:count]
    h_ref, c_ref, cos_ref, sin_ref, bias_ref, q_ref, k_ref, v_ref, o_ref, w_ref, sems = refs[
        count:
    ]
    piece = pieces[0].shape[-2]

    def target_of(index):
        return w_ref.at[:, pl.ds(pl.multiple_of(index * piece, piece), piece), :]

    @pl.when(pl.program_id(0) == 0)
    def _():
        fetch(n, me_ref[0], pieces, target_of, sems, "start")
        fetch(n, me_ref[0], pieces, target_of, sems, "wait")

    h = h_ref[...]
    cosine, sine = cos_ref[...], sin_ref[...]
    half = ROT // 2
    q_ref[...] = turn(dot_nn(h, w_ref[0]) + bias_ref[0:1], cosine, sine, half).astype(low)
    k_ref[...] = turn(dot_nn(h, w_ref[1]) + bias_ref[1:2], cosine, sine, half).astype(low)
    v_ref[...] = (dot_nn(h, w_ref[2]) + bias_ref[2:3]).astype(low)
    o_ref[...] = dot_nn(c_ref[...], w_ref[3]).astype(low)


def project(n, me, pieces, hidden, cot, cosine, sine, bias):
    rows, width = hidden.shape
    piece, cols = pieces[0].shape[-2:]
    count = len(pieces)
    block = min(512, rows)
    row_spec = pl.BlockSpec((block, width), lambda i, m: (i, 0))
    angle_spec = pl.BlockSpec((block, 128), lambda i, m: (i, 0))
    out_spec = pl.BlockSpec((block, cols), lambda i, m: (i, 0))
    return pl.pallas_call(
        functools.partial(project_kernel, n, count),
        grid_spec=pltpu.PrefetchScalarGridSpec(
            num_scalar_prefetch=1,
            grid=(rows // block,),
            in_specs=[pl.BlockSpec(memory_space=pl.ANY)] * count
            + [row_spec, row_spec, angle_spec, angle_spec]
            + [pl.BlockSpec((3, cols), lambda i, m: (0, 0))],
            out_specs=[out_spec] * 4 + [pl.BlockSpec((4, width, cols), lambda i, m: (0, 0, 0))],
            scratch_shapes=[pltpu.SemaphoreType.DMA((2 * n - 1,))],
        ),
        out_shape=[shape((rows, cols), low)] * 4 + [shape((4, width, cols), low)],
        compiler_params=params(),
        cost_estimate=cost(8 * rows * width * cols, 4 * rows * width + 16 * width * cols),
        name="project",
    )(me, *pieces, hidden, cot, cosine, sine, bias)


def attend_kernel(block, q_ref, k_ref, v_ref, o_ref, cos_ref, sin_ref, ctx_ref, mg_ref, bias_ref, dq, dk, dv):
    length, lanes = q_ref.shape
    scale = HD ** (-0.5)
    for head in range(lanes // HD):
        cols = slice(head * HD, (head + 1) * HD)
        for i in range(length // block):
            rows = slice(i * block, (i + 1) * block)
            end = (i + 1) * block
            q = q_ref[rows, cols]
            o = o_ref[rows, cols]
            k = k_ref[:end, cols]
            v = v_ref[:end, cols]
            scores = dot_nt(q, k) * scale
            row = i * block + lax.broadcasted_iota(jnp.int32, (block, end), 0)
            col = lax.broadcasted_iota(jnp.int32, (block, end), 1)
            scores = jnp.where(col <= row, scores, masked_score)
            top = jnp.max(scores, axis=-1, keepdims=True)
            weights = jnp.exp(scores - top)
            probs = weights * (1.0 / jnp.sum(weights, axis=-1, keepdims=True))
            probs_low = probs.astype(low)
            ctx_ref[rows, cols] = dot_nn(probs_low, v).astype(low)
            prob_grads = dot_nt(o, v)
            middle = jnp.sum(probs * prob_grads, axis=-1, keepdims=True)
            score_grads = (probs * (prob_grads - middle)).astype(low)
            dq[rows, cols] = dot_nn(score_grads, k) * scale
            key_part = dot_tn(score_grads, q) * scale
            value_part = dot_tn(probs_low, o)
            if i == 0:
                dk[:end, cols] = key_part
                dv[:end, cols] = value_part
                if end < length:
                    dk[end:, cols] = jnp.zeros((length - end, HD), full)
                    dv[end:, cols] = jnp.zeros((length - end, HD), full)
            else:
                dk[:end, cols] += key_part
                dv[:end, cols] += value_part
    cosine, sine = cos_ref[...], -sin_ref[...]
    half = ROT // 2
    sums = []
    for part, grads in enumerate(
        (turn(dq[...], cosine, sine, half), turn(dk[...], cosine, sine, half), dv[...])
    ):
        rounded = grads.astype(low)
        mg_ref[part] = rounded
        sums.append(jnp.sum(rounded.astype(full), axis=0, keepdims=True))
    total = jnp.concatenate(sums, axis=0)

    @pl.when(pl.program_id(1) == 0)
    def _():
        bias_ref[...] = total

    @pl.when(pl.program_id(1) > 0)
    def _():
        bias_ref[...] += total


def attend(batch, q, k, v, o, cosine, sine):
    rows, cols = q.shape
    length = rows // batch
    lanes = 128
    spec = pl.BlockSpec((length, lanes), lambda p, b: (b, p))
    angle_spec = pl.BlockSpec((length, 128), lambda p, b: (b, 0))
    return pl.pallas_call(
        functools.partial(attend_kernel, min(512, length)),
        grid=(cols // lanes, batch),
        in_specs=[spec] * 4 + [angle_spec] * 2,
        out_specs=[
            spec,
            pl.BlockSpec((3, length, lanes), lambda p, b: (0, b, p)),
            pl.BlockSpec((3, lanes), lambda p, b: (0, p)),
        ],
        out_shape=[
            shape((rows, cols), low),
            shape((3, rows, cols), low),
            shape((3, cols), full),
        ],
        scratch_shapes=[pltpu.VMEM((length, lanes), full)] * 3,
        compiler_params=params(),
        cost_estimate=cost(
            40 * rows * length * cols, 20 * rows * cols, rows * length * cols // HD
        ),
        name="attend",
    )(q, k, v, o, cosine, sine)


def attend_grads_kernel(n, me_ref, h_ref, c_ref, mg_ref, ctx_ref, *refs):
    own_ref, *slot_refs = refs[:n]
    edge_ref, wide = refs[n:]
    step = pl.program_id(0)
    cols = ctx_ref.shape[1]

    @pl.when(step == 0)
    def _():
        for part in range(3):
            wide[:, part * cols : (part + 1) * cols] = mg_ref[part]

    grad = dot_tn(h_ref[...], wide[...])
    grads = [grad[:, part * cols : (part + 1) * cols] for part in range(3)]
    grads.append(dot_tn(c_ref[...], ctx_ref[...]))
    for j in range(n):

        @pl.when(step == j)
        def _(j=j):
            for part in range(4):
                if j == 0:
                    own_ref[part] = grads[part]
                else:
                    slot_refs[j - 1][part] = grads[part].astype(low)

    @pl.when(lax.rem(me_ref[0] + step, n) == n - 1 - me_ref[0])
    def _():
        for part in range(4):
            edge_ref[part] = grads[part].astype(low)


def attend_grads(n, me, hidden, cot, mixed_grad, context):
    rows, width = hidden.shape
    cols = context.shape[1]
    piece = width // n
    whole3 = pl.BlockSpec((4, piece, cols), lambda i, m: (0, 0, 0))
    cut_spec = pl.BlockSpec((rows, piece), lambda i, m: (0, lax.rem(m[0] + i, n)))
    return pl.pallas_call(
        functools.partial(attend_grads_kernel, n),
        grid_spec=pltpu.PrefetchScalarGridSpec(
            num_scalar_prefetch=1,
            grid=(n,),
            in_specs=[
                cut_spec,
                cut_spec,
                pl.BlockSpec((3, rows, cols), lambda i, m: (0, 0, 0)),
                pl.BlockSpec((rows, cols), lambda i, m: (0, 0)),
            ],
            out_specs=[whole3] * (n + 1),
            scratch_shapes=[pltpu.VMEM((rows, 3 * cols), low)],
        ),
        out_shape=[shape((4, piece, cols), full)] + [shape((4, piece, cols), low)] * n,
        compiler_params=params(),
        cost_estimate=cost(8 * rows * width * cols, 4 * rows * width + 16 * width * cols),
        name="attend_grads",
    )(me, hidden, cot, mixed_grad, context)


def heads_kernel(ctx_ref, mg_ref, wa_ref, hid_ref, out_ref):
    hid = dot_nt(mg_ref[0], wa_ref[0]) + dot_nt(mg_ref[1], wa_ref[1]) + dot_nt(mg_ref[2], wa_ref[2])
    hid_ref[...] = hid.astype(low)
    out_ref[...] = dot_nt(ctx_ref[...], wa_ref[3]).astype(low)


def heads_parts(context, mixed_grad, w_attend):
    rows, cols = context.shape
    width = w_attend.shape[1]
    block = min(256, rows)
    out_spec = pl.BlockSpec((block, width), lambda i: (i, 0))
    return pl.pallas_call(
        heads_kernel,
        grid=(rows // block,),
        in_specs=[
            pl.BlockSpec((block, cols), lambda i: (i, 0)),
            pl.BlockSpec((3, block, cols), lambda i: (0, i, 0)),
            pl.BlockSpec((4, width, cols), lambda i: (0, 0, 0)),
        ],
        out_specs=[out_spec, out_spec],
        out_shape=[shape((rows, width), low)] * 2,
        compiler_params=params(),
        cost_estimate=cost(8 * rows * width * cols, 4 * rows * width + 8 * (rows + width) * cols),
        name="heads_parts",
    )(context, mixed_grad, w_attend)


def early_kernel(act_ref, grad_ref, w_ref, hid_in_ref, out_in_ref, hid_ref, out_ref):
    hid = hid_in_ref[...].astype(full) + dot_tn(grad_ref[...], join_gates(w_ref))
    hid_ref[...] = hid.astype(low)
    out = out_in_ref[...].astype(full) + dot_tn(act_ref[...], w_ref[2])
    out_ref[...] = out.astype(low)


def early_parts(active, gates_grad, w_feed, hid, out):
    rows, width = hid.shape
    units = w_feed.shape[1]
    block = min(256, rows)
    row_spec = pl.BlockSpec((block, width), lambda i: (i, 0))
    return pl.pallas_call(
        early_kernel,
        grid=(rows // block,),
        in_specs=[
            pl.BlockSpec((units, block), lambda i: (0, i)),
            pl.BlockSpec((2 * units, block), lambda i: (0, i)),
            pl.BlockSpec((3, units, width), lambda i: (0, 0, 0)),
            row_spec,
            row_spec,
        ],
        out_specs=[row_spec, row_spec],
        out_shape=[shape((rows, width), low)] * 2,
        compiler_params=params(),
        cost_estimate=cost(6 * rows * width * units, 8 * rows * width + 6 * (rows + width) * units),
        name="early_parts",
    )(active, gates_grad, w_feed, hid, out)


def sixteenth(which, m):
    return m[0] * 8 + (m[1] * 2 + m[2] if which == 0 else 4 + m[2] * 2 + m[1])


def back_kernel(info_ref, *refs):
    p_ref = refs[6]
    total = 0.0
    for x_ref, near_ref, far_ref, back_ref in zip(refs[0:2], refs[2:4], refs[4:6], refs[7:9]):
        x = x_ref[...].astype(full)
        centred = x - jnp.mean(x, axis=-1, keepdims=True)
        inv = lax.rsqrt(jnp.mean(centred * centred, axis=-1, keepdims=True) + epsilon)
        normal = centred * inv
        grad = near_ref[...].astype(full) + far_ref[...].astype(full)
        scaled = grad * p_ref[0:1]
        back = inv * (
            scaled
            - jnp.mean(scaled, axis=-1, keepdims=True)
            - normal * jnp.mean(scaled * normal, axis=-1, keepdims=True)
        )
        back_ref[: x.shape[0]] = back.astype(low)
        total += jnp.concatenate(
            [jnp.sum(grad * normal, axis=0, keepdims=True), jnp.sum(grad, axis=0, keepdims=True)],
            axis=0,
        )
    high = total.astype(low)
    rest = total - high.astype(full)
    middle = rest.astype(low)
    small = (rest - middle.astype(full)).astype(low)
    zeros = jnp.zeros((tail_rows - 6, total.shape[1]), full)
    terms = [high.astype(full), middle.astype(full), small.astype(full), zeros]
    refs[7][refs[0].shape[0] :] = jnp.concatenate(terms, axis=0).astype(low)


def back_rows(info, rows, near, far, norm_params):
    count, width = near[0].shape
    spec = pl.BlockSpec((count, width), lambda i, m: (0, 0))
    pair = pl.BlockSpec((2, width), lambda i, m: (0, 0))
    return pl.pallas_call(
        back_kernel,
        grid_spec=pltpu.PrefetchScalarGridSpec(
            num_scalar_prefetch=1,
            grid=(1,),
            in_specs=[
                pl.BlockSpec((count, width), lambda i, m: (sixteenth(0, m), 0)),
                pl.BlockSpec((count, width), lambda i, m: (sixteenth(1, m), 0)),
            ]
            + [spec] * 4
            + [pair],
            out_specs=[pl.BlockSpec((count + tail_rows, width), lambda i, m: (0, 0)), spec],
        ),
        out_shape=[shape((count + tail_rows, width), low), shape((count, width), low)],
        compiler_params=params(),
        cost_estimate=cost(40 * count * width, 16 * count * width),
        name="back_rows",
    )(info, rows, rows, *near, *far, norm_params)


def add_kernel(info_ref, *refs):
    for x_ref, near_ref, far_ref, out_ref in zip(refs[0:2], refs[2:4], refs[4:6], refs[6:8]):
        total = x_ref[...].astype(full) + near_ref[...].astype(full) + far_ref[...].astype(full)
        out_ref[...] = total.astype(low)


def add_rows(info, rows, near, far):
    count, width = near[0].shape
    spec = pl.BlockSpec((count, width), lambda i, m: (0, 0))
    return pl.pallas_call(
        add_kernel,
        grid_spec=pltpu.PrefetchScalarGridSpec(
            num_scalar_prefetch=1,
            grid=(1,),
            in_specs=[
                pl.BlockSpec((count, width), lambda i, m: (sixteenth(0, m), 0)),
                pl.BlockSpec((count, width), lambda i, m: (sixteenth(1, m), 0)),
            ]
            + [spec] * 4,
            out_specs=[spec, spec],
        ),
        out_shape=[shape((count, width), low)] * 2,
        compiler_params=params(),
        cost_estimate=cost(4 * count * width, 16 * count * width),
        name="add_rows",
    )(info, rows, rows, *near, *far)


def pack_kernel(block, info_ref, *refs):
    pieces, out_ref, sems = refs[:8], refs[8], refs[9]
    x, y = info_ref[1], info_ref[2]
    copies = []

    def move(source, at, size):
        place = out_ref.at[pl.ds(pl.multiple_of(at, 16), size), :]
        copies.append(pltpu.make_async_copy(source, place, sems.at[len(copies)]))

    for i, piece in enumerate(pieces):
        high, small = (i // 2) % 2, i % 2
        if i < 4:
            at = (x ^ high) * 2 + (y ^ small)
        else:
            at = 4 + (y ^ high) * 2 + (x ^ small)
        extra = piece.shape[0] - block
        move(piece.at[pl.ds(0, block), :], at * block, block)
        if extra:
            move(piece.at[pl.ds(block, extra), :], 8 * block + at * extra, extra)
    for copy in copies:
        copy.start()
    for copy in copies:
        copy.wait()


def pack_rows(info, pieces):
    block, width = pieces[-1].shape
    extra = pieces[0].shape[0] - block
    return pl.pallas_call(
        functools.partial(pack_kernel, block),
        grid_spec=pltpu.PrefetchScalarGridSpec(
            num_scalar_prefetch=1,
            grid=(1,),
            in_specs=[pl.BlockSpec(piece.shape, lambda i, m: (0, 0)) for piece in pieces],
            out_specs=pl.BlockSpec(memory_space=pl.ANY),
            scratch_shapes=[pltpu.SemaphoreType.DMA((12,))],
        ),
        out_shape=shape((8 * block + 4 * extra, width), low),
        compiler_params=params(),
        cost_estimate=cost(0, 32 * block * width),
        name="pack_rows",
    )(info, *pieces)


def tail_kernel(own_ref, other_ref, out_ref):
    def total(ref):
        values = ref[...].astype(full)
        sums = 0.0
        for i in range(4):
            at = i * tail_rows
            sums += values[at : at + 2] + values[at + 2 : at + 4] + values[at + 4 : at + 6]
        return sums

    out_ref[...] = total(own_ref) + total(other_ref)


def tail_sums(own, other):
    count, width = own.shape
    size = 4 * tail_rows
    spec = pl.BlockSpec((size, width), lambda i: (count // size - 1, 0))
    return pl.pallas_call(
        tail_kernel,
        grid=(1,),
        in_specs=[spec, spec],
        out_specs=pl.BlockSpec((2, width), lambda i: (0, 0)),
        out_shape=shape((2, width), full),
        compiler_params=params(),
        cost_estimate=cost(20 * width, 512 * width),
        name="tail_sums",
    )(own, other)


def finish_kernel(info_ref, *refs):
    out_ref = refs[-1]
    value = refs[0][...]
    if len(refs) > 2 and refs[1].shape == out_ref.shape:
        value = refs[1][...].astype(full) + value.astype(full)
    out_ref[...] = value


def finish_rows(info, rows, half, part, cot=None, begun=None):
    width = part.shape[1]
    block = rows // 8
    place = lambda i, m: ((m[0] ^ half) * 4 + i, 0)
    ins, specs = [part], [pl.BlockSpec((block, width), lambda i, m: (i, 0))]
    if cot is not None:
        ins.append(cot)
        specs.append(pl.BlockSpec((block, width), place))
    if begun is not None:
        ins.append(begun)
        specs.append(pl.BlockSpec(memory_space=pl.ANY))
    return pl.pallas_call(
        finish_kernel,
        grid_spec=pltpu.PrefetchScalarGridSpec(
            num_scalar_prefetch=1,
            grid=(4,),
            in_specs=specs,
            out_specs=pl.BlockSpec((block, width), place),
        ),
        out_shape=shape((rows, width), low if cot is None else full),
        input_output_aliases={} if begun is None else {len(ins): 0},
        compiler_params=params(),
        cost_estimate=cost(rows * width, 4 * rows * width),
        name="finish_rows",
    )(info, *ins)


def update_kernel(rates, count, *refs):
    g_ref = refs[0]
    ins = refs[1:7]
    outs = refs[7 + count :]
    for which, rate in enumerate(rates):
        grad = g_ref[:2] if which == 0 else g_ref[2]
        grad = grad.astype(full)
        w, m, a = (ref[...] for ref in ins[3 * which : 3 * which + 3])
        g_out, w_out, m_out, a_out = outs[4 * which : 4 * which + 4]
        g_out[...] = grad
        w_out[...], m_out[...], a_out[...] = advance(w, grad, m, a, rate)


def update_feed(start, grads, states, rates, begun=()):
    _, units, piece = grads.shape
    block = math.gcd(start, units)
    while block > 128 and block % 16 == 0:
        block //= 2
    at = start // block
    pair = pl.BlockSpec((2, block, piece), lambda i: (0, at + i, 0))
    single = pl.BlockSpec((block, piece), lambda i: (at + i, 0))
    total = states[0].shape[1]
    return pl.pallas_call(
        functools.partial(update_kernel, rates, len(begun)),
        grid=(units // block,),
        in_specs=[pl.BlockSpec((3, block, piece), lambda i: (0, i, 0))]
        + [pair] * 3
        + [single] * 3
        + [pl.BlockSpec(memory_space=pl.ANY)] * len(begun),
        out_specs=[pair] * 4 + [single] * 4,
        out_shape=[shape((2, total, piece), full)] * 4 + [shape((total, piece), full)] * 4,
        input_output_aliases={7 + i: i for i in range(len(begun))},
        compiler_params=params(),
        cost_estimate=cost(30 * units * piece, 3 * 30 * units * piece),
        name="update_feed",
    )(grads, *states, *begun)


def body(
    inputs,
    positions,
    cotangent,
    w_attend_in,
    w_attend_out,
    w_expand,
    w_reduce,
    norm_params,
    attend_bias,
    moment_attend_in,
    moment_attend_out,
    moment_expand,
    moment_reduce,
    moment_norm,
    moment_bias,
    average_attend_in,
    average_attend_out,
    average_expand,
    average_reduce,
    average_norm,
    average_bias,
):
    batch, length, width = inputs.shape
    rows = batch * length
    units = w_expand.shape[2]
    n = lax.axis_size("dp")
    group = lax.axis_size("mp")
    me = lax.axis_index("dp").astype(jnp.int32).reshape(1)
    spot = lax.axis_index("mp").astype(jnp.int32)
    info = jnp.stack([spot & 1, (spot >> 1) & 1, (spot >> 2) & 1, me[0]])
    fast = group == 8

    expand_t = jnp.transpose(w_expand, (1, 2, 0))
    reduce_t = jnp.transpose(w_reduce)
    in_t = jnp.transpose(w_attend_in, (1, 0, 2))
    cut = units // 2 // 16 * 16
    shards = [
        jnp.concatenate([expand_t[:, a:b], reduce_t[None, a:b]], axis=0).astype(low)
        for a, b in ((0, cut), (cut, units))
    ]
    attend_shard = jnp.concatenate([in_t, w_attend_out[None]], axis=0).astype(low)
    attend_pieces = [lax.all_gather(attend_shard, "dp")]
    first_shard, _ = lax.optimization_barrier((shards[0], attend_shard))
    first_pieces = [lax.all_gather(first_shard, "dp")]

    tokens = inputs.reshape(rows, width)
    cot = cotangent.reshape(rows, width)
    hidden = layer_norm(tokens, norm_params)

    half = ROT // 2
    lane = jnp.arange(128, dtype=jnp.int32) % HD
    frequency = 10000.0 ** (-((lane % half).astype(full) * 2.0 / ROT))
    angles = positions.reshape(rows).astype(full)[:, None] * frequency[None, :]
    cosine = jnp.where(lane < ROT, jnp.cos(angles), 1.0)
    sine = jnp.where(lane < half, -jnp.sin(angles), jnp.where(lane < ROT, jnp.sin(angles), 0.0))

    q, k, v, o, w_attend = project(n, me, attend_pieces, hidden, cot, cosine, sine, attend_bias)
    context, mixed_grad, bias_part = attend(batch, q, k, v, o, cosine, sine)
    *attend_slots, edge = attend_grads(n, me, hidden, cot, mixed_grad, context)
    hid_early, out_early = heads_parts(context, mixed_grad, w_attend)
    last_shard, first_piece, attend_slots, edge, hid_early, out_early = lax.optimization_barrier(
        (shards[1], first_pieces[0], attend_slots, edge, hid_early, out_early)
    )

    rights, lefts = [last_shard], [last_shard]
    came = (None, None)
    for k in range(1, n):
        right, left = gather_hop(k, rights[-1], lefts[-1], me[0])
        if k > 1:
            if k == 2:
                load = (after(edge, (rights[-1], lefts[-1])),) * 2
            else:
                load = scatter_load(k - 1, attend_slots, *came)
            coming = scatter_hop(k - 1, *load)
        beside = ()
        if k == 1:
            active, gates_grad, w_feed = beside = feed_chunk(n, me, [first_piece], hidden, cot)
        elif k == 2:
            hid_early, out_early = beside = early_parts(
                active, gates_grad, w_feed, hid_early, out_early
            )
        elif k == 3:
            first_grads = beside = feed_grads(n, hidden, cot, active, gates_grad)
        if k > 1:
            (right, left), came = after(((right, left), coming), beside)
        else:
            right, left = after((right, left), beside)
        rights.append(right)
        lefts.append(left)
    last_pieces = [last_shard] + rights[1:] + lefts[1:]

    def scatter(grads):
        return lax.psum_scatter(grads, "dp", scatter_dimension=0, tiled=False)

    first_grads = scatter(first_grads).reshape(3, cut, -1)

    total_tokens = rows * n

    def update_attend(came):
        grad = attend_slots[0] + came[0].astype(full) + came[1].astype(full)
        grad_in, grad_out = jnp.transpose(grad[:3], (1, 0, 2)), grad[3]
        rate_in = 0.5 / math.sqrt(width * total_tokens)
        rate_out = 1.8 / math.sqrt(width * batch * n)
        new_in = advance(w_attend_in, grad_in, moment_attend_in, average_attend_in, rate_in)
        new_out = advance(w_attend_out, grad_out, moment_attend_out, average_attend_out, rate_out)
        return (grad_in, grad_out) + new_in + new_out

    rates = (1.6 / math.sqrt(width * total_tokens), 0.77 / math.sqrt(FF * total_tokens))
    states = [jnp.transpose(a, (1, 2, 0)) for a in (w_expand, moment_expand, average_expand)]
    states += [jnp.transpose(a) for a in (w_reduce, moment_reduce, average_reduce)]

    if fast:
        e = rows // 8
        s = e // 2

        def sum_cores(own, came):
            own = [own[i * e : (i + 1) * e].astype(full) + came[i * e : (i + 1) * e].astype(full) for i in range(4)]
            return own, (own[1].astype(low), own[3].astype(low))

        def sum_first(own, came):
            first = own[0] + came[0].astype(full)
            second = own[2] + came[1].astype(full)
            near = [first[:s].astype(low), second[:s].astype(low)]
            return near, (first[s:].astype(low), second[s:].astype(low))

        def both_ways(pair, masks):
            return [swap(pair[0], masks[0]), swap(pair[1], masks[1])]

        def join(one, first, second, third):
            pieces = (one, first, second, third)
            return pack_rows(info, [p[0] for p in pieces] + [p[1] for p in pieces])

        other_out, own_out, active, both, w_last = out_last(
            n, info, True, last_pieces, hidden, out_early
        )
        came_out = swap(other_out, 1)
        load = scatter_load(n - 1, after(attend_slots, other_out), *came)
        came_out = after(came_out, load)
        own_out, load_out = sum_cores(own_out, came_out)
        one_out = both_ways(load_out, (2, 4))
        other_hid, own_hid, gates_grad = hid_last(
            info, True, w_last, after(both, load_out), cot, hid_early
        )
        came_hid = swap(other_hid, 1)
        near_out, load_out = sum_first(own_out, after(one_out, other_hid))
        two_out = both_ways(load_out, (4, 2))
        own_hid, load_hid = sum_cores(own_hid, after(came_hid, load_out))
        one_hid = both_ways(load_hid, (2, 4))
        last_grads = feed_grads(n, hidden, cot, after(active, load_hid), gates_grad)
        two_out = after(two_out, last_grads)
        last_grads = scatter(last_grads).reshape(3, units - cut, -1)
        add = add_rows(info, tokens, near_out, two_out)
        out_one = both_ways(add, (4, 2))
        out_two = both_ways(add, (2, 4))
        near_hid, load_hid = sum_first(own_hid, after(one_hid, add))
        two_hid = both_ways(load_hid, (4, 2))
        came = scatter_hop(n - 1, *after(load, load_hid))
        out_one = after(out_one, load_hid)
        out_three = both_ways(out_one, (2, 4))
        two_hid = after(two_hid, out_one)
        back = back_rows(info, tokens, near_hid, two_hid, norm_params)
        hid_one = both_ways(back, (4, 2))
        hid_two = both_ways(back, (2, 4))
        begun = update_feed(0, after(first_grads, back), states, rates)
        hid_one = after(hid_one, begun)
        hid_three = both_ways(hid_one, (2, 4))
        attend_new = update_attend(after(came, hid_one))
        out_two, out_three = after((out_two, out_three), attend_new)
        mine_out = join(add, out_one, out_two, out_three)
        other_out = swap(mine_out, 1)
        output = finish_rows(info, rows, 0, mine_out)
        output = finish_rows(info, rows, 1, after(other_out, output), begun=output)
        done = update_feed(cut, after(last_grads, output), states, rates, begun)
        hid_two, hid_three = after((hid_two, hid_three), done)
        mine_hid = join(back, hid_one, hid_two, hid_three)
        other_hid = swap(mine_hid, 1)
        input_grad = finish_rows(info, rows, 0, mine_hid, cot)
        other_hid = after(other_hid, input_grad)
        norm_part = tail_sums(mine_hid, other_hid)
        sums = small_sum(join_sums(norm_part, bias_part), "dp")
        input_grad = finish_rows(info, rows, 1, after(other_hid, norm_part), cot, input_grad)
        norm_grad, bias_grad = split_sums(sums, norm_part, bias_part)
    else:
        out_part, active, both, w_last = out_last(n, info, False, last_pieces, hidden, out_early)
        hid_part, gates_grad = hid_last(info, False, w_last, both, cot, hid_early)
        came = scatter_hop(n - 1, *scatter_load(n - 1, attend_slots, *came))
        attend_new = update_attend(came)
        last_grads = scatter(feed_grads(n, hidden, cot, active, gates_grad)).reshape(3, units - cut, -1)
        hidden_grad = lax.psum(hid_part, "mp").astype(full)
        summed = lax.psum(out_part, "mp").astype(full)
        values = tokens.astype(full)
        output = (values + summed).astype(low)
        centred = values - jnp.mean(values, axis=-1, keepdims=True)
        inv = lax.rsqrt(jnp.mean(centred * centred, axis=-1, keepdims=True) + epsilon)
        normal = centred * inv
        scaled = hidden_grad * norm_params[0]
        back = inv * (
            scaled
            - jnp.mean(scaled, axis=-1, keepdims=True)
            - normal * jnp.mean(scaled * normal, axis=-1, keepdims=True)
        )
        input_grad = cot.astype(full) + back
        norm_part = jnp.stack([jnp.sum(hidden_grad * normal, axis=0), jnp.sum(hidden_grad, axis=0)])
        sums = small_sum(join_sums(norm_part, bias_part), "dp")
        norm_grad, bias_grad = split_sums(sums, norm_part, bias_part)
        begun = update_feed(0, first_grads, states, rates)
        done = update_feed(cut, last_grads, states, rates, begun)
    grad_in, grad_out = attend_new[:2]
    new_in, moment_in_new, average_in_new = attend_new[2:5]
    new_out, moment_out_new, average_out_new = attend_new[5:]
    grad_expand, new_expand, moment_expand_new, average_expand_new = (
        jnp.transpose(a, (2, 0, 1)) for a in done[:4]
    )
    grad_reduce, new_reduce, moment_reduce_new, average_reduce_new = (
        jnp.transpose(a) for a in done[4:]
    )
    input_grad = input_grad.reshape(batch, length, width)
    output = output.reshape(batch, length, width)
    new_norm, moment_norm_new, average_norm_new = advance(
        norm_params, norm_grad, moment_norm, average_norm, 0.06 / math.sqrt(total_tokens)
    )
    new_bias, moment_bias_new, average_bias_new = advance(
        attend_bias, bias_grad, moment_bias, average_bias, 0.25 / math.sqrt(total_tokens)
    )
    return (
        output,
        input_grad,
        grad_in,
        grad_out,
        grad_expand,
        grad_reduce,
        norm_grad,
        bias_grad,
        new_in,
        new_out,
        new_expand,
        new_reduce,
        new_norm,
        new_bias,
        moment_in_new,
        moment_out_new,
        moment_expand_new,
        moment_reduce_new,
        moment_norm_new,
        moment_bias_new,
        average_in_new,
        average_out_new,
        average_expand_new,
        average_reduce_new,
        average_norm_new,
        average_bias_new,
    )


def solution(mesh):
    rows3 = P("dp", None, None)
    in3 = P("dp", None, "mp")
    in2 = P("dp", "mp")
    bias = P(None, "mp")
    states = (in3, in2, in3, in2, P(), bias)
    return jax.shard_map(
        body,
        mesh=mesh,
        in_specs=(rows3, P("dp", None), rows3) + states * 3,
        out_specs=(rows3, rows3) + states * 4,
        check_vma=False,
    )
```

```python
import functools
import math

import jax
import jax.numpy as jnp
from jax import lax
from jax.experimental import pallas as pl
from jax.experimental.pallas import tpu as pltpu
from jax.sharding import PartitionSpec as P

HD = 64
ROT = 16
FF = 5632

epsilon = 1e-05
decay_moment = 0.9
decay_average = 0.9
masked_score = -1e30

low = jnp.bfloat16
full = jnp.float32
vmem_limit = 60 << 20
tail_rows = 16


def dot_nt(left, right):
    return lax.dot_general(left, right, (((1,), (1,)), ((), ())), preferred_element_type=full)


def dot_nn(left, right):
    return lax.dot_general(left, right, (((1,), (0,)), ((), ())), preferred_element_type=full)


def dot_tn(left, right):
    return lax.dot_general(left, right, (((0,), (0,)), ((), ())), preferred_element_type=full)


def params(**more):
    return pltpu.CompilerParams(vmem_limit_bytes=vmem_limit, **more)


def cost(flops, moved, trans=0):
    return pl.CostEstimate(flops=int(flops), bytes_accessed=int(moved), transcendentals=int(trans))


def shape(dims, kind):
    return jax.ShapeDtypeStruct(dims, kind)


def advance(weight, grad, moment, average, rate):
    moment_new = decay_moment * moment + grad
    weight_new = weight - rate * (grad + decay_moment * moment_new)
    average_new = decay_average * average + (1.0 - decay_average) * weight_new
    return (weight_new, moment_new, average_new)


def after(value, *others):
    return lax.optimization_barrier((value, others))[0]


def gather_hop(k, right, left, me):
    n = lax.axis_size("dp")
    to_right = [(a, a + 1) for a in range(k - 1, n - 1)]
    to_left = [(a, a - 1) for a in range(1, n - k + 1)]
    if k == n - 1 and n != 3:
        both = lax.ppermute(jnp.where(me == 1, left, right), "dp", to_right + to_left)
        return both, both
    return lax.ppermute(right, "dp", to_right), lax.ppermute(left, "dp", to_left)


def scatter_load(k, slots, right, left):
    n = lax.axis_size("dp")
    to_right, to_left = slots[n - k], slots[k]
    if k > 1:
        to_right = (to_right.astype(full) + right.astype(full)).astype(low)
        to_left = (to_left.astype(full) + left.astype(full)).astype(low)
    return to_right, to_left


def scatter_hop(k, to_right, to_left):
    n = lax.axis_size("dp")
    rights = [(a, a + 1) for a in range(k)]
    lefts = [(a, a - 1) for a in range(n - 1, n - 1 - k, -1)]
    if k == 1 and n != 3:
        both = lax.ppermute(to_right, "dp", rights + lefts)
        return both, both
    return lax.ppermute(to_right, "dp", rights), lax.ppermute(to_left, "dp", lefts)


def swap(value, mask, axis="mp"):
    n = lax.axis_size(axis)
    return lax.ppermute(value, axis, [(a, a ^ mask) for a in range(n)])


def small_sum(value, axis):
    n = lax.axis_size(axis)
    if n & (n - 1):
        return lax.psum(value, axis)
    mask = 1
    while mask < n:
        value = value + swap(value, mask, axis)
        mask *= 2
    return value


def join_sums(norm_part, bias_part):
    cols = bias_part.shape[1]
    return jnp.concatenate([norm_part.reshape(-1, cols), bias_part])


def split_sums(sums, norm_part, bias_part):
    count = sums.shape[0] - bias_part.shape[0]
    return sums[:count].reshape(norm_part.shape), sums[count:]


def norm_kernel(x_ref, p_ref, o_ref):
    x = x_ref[...].astype(full)
    centred = x - jnp.mean(x, axis=-1, keepdims=True)
    inv = lax.rsqrt(jnp.mean(centred * centred, axis=-1, keepdims=True) + epsilon)
    o_ref[...] = (centred * inv * p_ref[0:1] + p_ref[1:2]).astype(low)


def layer_norm(rows, norm_params):
    count, width = rows.shape
    block = min(256, count)
    return pl.pallas_call(
        norm_kernel,
        grid=(count // block,),
        in_specs=[
            pl.BlockSpec((block, width), lambda i: (i, 0)),
            pl.BlockSpec((2, width), lambda i: (0, 0)),
        ],
        out_specs=pl.BlockSpec((block, width), lambda i: (i, 0)),
        out_shape=shape((count, width), low),
        compiler_params=params(),
        cost_estimate=cost(8 * count * width, 4 * count * width),
        name="layer_norm",
    )(rows, norm_params)


def fetch(n, me, pieces, target_of, sems, action):
    def run(source, index, sem):
        copy = pltpu.make_async_copy(source, target_of(index), sem)
        if action == "start":
            copy.start()
        else:
            copy.wait()

    if len(pieces) == 1:
        for j in range(n):
            run(pieces[0].at[j], j, sems.at[j])
        return
    run(pieces[0], me, sems.at[0])
    for k in range(1, n):

        @pl.when(me >= k)
        def _(k=k):
            run(pieces[k], me - k, sems.at[k])

        @pl.when(me + k < n)
        def _(k=k):
            run(pieces[n - 1 + k], me + k, sems.at[n - 1 + k])


def swish_of(both):
    units = both.shape[0] // 2
    gate, upper = both[:units], both[units:]
    sigmoid = jax.nn.sigmoid(gate)
    return gate, upper, sigmoid, gate * sigmoid


def join_gates(w_ref):
    return w_ref[0:2].reshape(2 * w_ref.shape[1], w_ref.shape[2])


def gates_grad_of(both, active_grad):
    gate, upper, sigmoid, swish = swish_of(both)
    gate_grad = active_grad * upper * sigmoid * (1.0 + gate * (1.0 - sigmoid))
    return jnp.concatenate([gate_grad, active_grad * swish], axis=0).astype(low)


def gates_of(w_ref, h, c):
    both = dot_nt(join_gates(w_ref), h)
    _, upper, _, swish = swish_of(both)
    return (swish * upper).astype(low), gates_grad_of(both, dot_nt(w_ref[2], c))


def add_grads(acc, step, active, gates_grad, h, c):
    units = active.shape[0]

    @pl.when(step == 0)
    def _():
        acc[: 2 * units] = dot_nn(gates_grad, h)
        acc[2 * units :] = dot_nn(active, c)

    @pl.when(step > 0)
    def _():
        acc[: 2 * units] += dot_nn(gates_grad, h)
        acc[2 * units :] += dot_nn(active, c)


def store_grads(n, acc, out_ref):
    piece = out_ref.shape[2]
    for j in range(n):
        out_ref[j] = acc[:, j * piece : (j + 1) * piece].astype(low)


def wide_target(w_ref, piece):
    return lambda index: w_ref.at[:, :, pl.ds(pl.multiple_of(index * piece, piece), piece)]


def feed_kernel(n, count, me_ref, *refs):
    pieces = refs[:count]
    h_ref, c_ref, act_ref, grad_ref, w_ref, sems = refs[count:]
    target_of = wide_target(w_ref, w_ref.shape[2] // n)

    @pl.when(pl.program_id(0) == 0)
    def _():
        fetch(n, me_ref[0], pieces, target_of, sems, "start")
        fetch(n, me_ref[0], pieces, target_of, sems, "wait")

    act_ref[...], grad_ref[...] = gates_of(w_ref, h_ref[...], c_ref[...])


def feed_chunk(n, me, pieces, hidden, cot):
    rows, width = hidden.shape
    units = pieces[0].shape[-2]
    count = len(pieces)
    block = min(512, rows)
    row_spec = pl.BlockSpec((block, width), lambda i, m: (i, 0))
    return pl.pallas_call(
        functools.partial(feed_kernel, n, count),
        grid_spec=pltpu.PrefetchScalarGridSpec(
            num_scalar_prefetch=1,
            grid=(rows // block,),
            in_specs=[pl.BlockSpec(memory_space=pl.ANY)] * count + [row_spec, row_spec],
            out_specs=[
                pl.BlockSpec((units, block), lambda i, m: (0, i)),
                pl.BlockSpec((2 * units, block), lambda i, m: (0, i)),
                pl.BlockSpec((3, units, width), lambda i, m: (0, 0, 0)),
            ],
            scratch_shapes=[pltpu.SemaphoreType.DMA((2 * n - 1,))],
        ),
        out_shape=[
            shape((units, rows), low),
            shape((2 * units, rows), low),
            shape((3, units, width), low),
        ],
        compiler_params=params(),
        cost_estimate=cost(
            6 * rows * width * units, 4 * rows * width + 12 * units * width, rows * units
        ),
        name="feed_chunk",
    )(me, *pieces, hidden, cot)


def put_part(split, info_ref, parts, value):
    if not split:
        parts[0][...] = value.astype(low)
        return
    step = pl.program_id(0)
    sub = value.shape[0] // 4
    high = jnp.where(step % 2 == 0, info_ref[1], info_ref[2])
    small = jnp.where(step % 2 == 0, info_ref[2], info_ref[1])
    first, second = value[: 2 * sub], value[2 * sub :]
    near = jnp.where(high == 0, first, second).astype(low)
    far = jnp.where(high == 0, second, first).astype(low)
    for at in range(4):

        @pl.when(step == at)
        def _(at=at):
            for ref, pair in ((parts[2 * at], near), (parts[2 * at + 1], far)):
                for i in range(2):
                    place = pl.ds(pl.multiple_of((i ^ small) * sub, sub), sub)
                    ref[place, :] = pair[i * sub : (i + 1) * sub]


def last_blocks(split, rows, width):
    if split:
        block, steps = rows // 4, 4
        place = lambda i, m: (m[0] ^ (1 - i // 2)) * 2 + i % 2
        part_specs = [pl.BlockSpec((block // 2, width), lambda i, m: (0, 0))] * 8
        part_shapes = [shape((block // 2, width), low)] * 8
    else:
        block = min(256, rows)
        steps = rows // block
        place = lambda i, m: i
        part_specs = [pl.BlockSpec((block, width), lambda i, m: (i, 0))]
        part_shapes = [shape((rows, width), low)]
    return block, steps, place, part_specs, part_shapes


def out_last_kernel(n, count, split, info_ref, *refs):
    pieces = refs[:count]
    h_ref, early_ref = refs[count : count + 2]
    parts = refs[count + 2 : -4]
    act_ref, both_ref, w_ref, sems = refs[-4:]
    target_of = wide_target(w_ref, w_ref.shape[2] // n)

    @pl.when(pl.program_id(0) == 0)
    def _():
        fetch(n, info_ref[3], pieces, target_of, sems, "start")
        fetch(n, info_ref[3], pieces, target_of, sems, "wait")

    both = dot_nt(join_gates(w_ref), h_ref[...])
    both_ref[...] = both
    _, upper, _, swish = swish_of(both)
    active = (swish * upper).astype(low)
    act_ref[...] = active
    put_part(split, info_ref, parts, early_ref[...].astype(full) + dot_tn(active, w_ref[2]))


def out_last(n, info, split, pieces, hidden, early):
    rows, width = hidden.shape
    units = pieces[0].shape[-2]
    count = len(pieces)
    block, steps, place, part_specs, part_shapes = last_blocks(split, rows, width)
    row_spec = pl.BlockSpec((block, width), lambda i, m: (place(i, m), 0))
    return pl.pallas_call(
        functools.partial(out_last_kernel, n, count, split),
        grid_spec=pltpu.PrefetchScalarGridSpec(
            num_scalar_prefetch=1,
            grid=(steps,),
            in_specs=[pl.BlockSpec(memory_space=pl.ANY)] * count + [row_spec] * 2,
            out_specs=part_specs
            + [
                pl.BlockSpec((units, block), lambda i, m: (0, place(i, m))),
                pl.BlockSpec((2 * units, block), lambda i, m: (0, place(i, m))),
                pl.BlockSpec((3, units, width), lambda i, m: (0, 0, 0)),
            ],
            scratch_shapes=[pltpu.SemaphoreType.DMA((2 * n - 1,))],
        ),
        out_shape=part_shapes
        + [shape((units, rows), low), shape((2 * units, rows), full), shape((3, units, width), low)],
        compiler_params=params(),
        cost_estimate=cost(6 * rows * width * units, 8 * rows * width, rows * units),
        name="out_last",
    )(info, *pieces, hidden, early)


def hid_last_kernel(split, info_ref, w_ref, both_ref, c_ref, early_ref, *refs):
    grad_ref = refs[-1]
    gates_grad = gates_grad_of(both_ref[...], dot_nt(w_ref[2], c_ref[...]))
    grad_ref[...] = gates_grad
    hid = early_ref[...].astype(full) + dot_tn(gates_grad, join_gates(w_ref))
    put_part(split, info_ref, refs[:-1], hid)


def hid_last(info, split, weights, both, cot, early):
    rows, width = cot.shape
    units = weights.shape[1]
    block, steps, place, part_specs, part_shapes = last_blocks(split, rows, width)
    row_spec = pl.BlockSpec((block, width), lambda i, m: (place(i, m), 0))
    both_spec = pl.BlockSpec((2 * units, block), lambda i, m: (0, place(i, m)))
    return pl.pallas_call(
        functools.partial(hid_last_kernel, split),
        grid_spec=pltpu.PrefetchScalarGridSpec(
            num_scalar_prefetch=1,
            grid=(steps,),
            in_specs=[pl.BlockSpec((3, units, width), lambda i, m: (0, 0, 0)), both_spec]
            + [row_spec] * 2,
            out_specs=part_specs + [both_spec],
        ),
        out_shape=part_shapes + [shape((2 * units, rows), low)],
        compiler_params=params(),
        cost_estimate=cost(6 * rows * width * units, 8 * rows * width, rows * units),
        name="hid_last",
    )(info, weights, both, cot, early)


def feed_grads_kernel(n, steps, h_ref, c_ref, act_ref, grad_ref, out_ref, acc):
    step = pl.program_id(0)
    add_grads(acc, step, act_ref[...], grad_ref[...], h_ref[...], c_ref[...])

    @pl.when(step == steps - 1)
    def _():
        store_grads(n, acc, out_ref)


def feed_grads(n, hidden, cot, active, gates_grad):
    rows, width = hidden.shape
    units = active.shape[0]
    piece = width // n
    block = min(512, rows)
    steps = rows // block
    row_spec = pl.BlockSpec((block, width), lambda i: (i, 0))
    return pl.pallas_call(
        functools.partial(feed_grads_kernel, n, steps),
        grid=(steps,),
        in_specs=[
            row_spec,
            row_spec,
            pl.BlockSpec((units, block), lambda i: (0, i)),
            pl.BlockSpec((2 * units, block), lambda i: (0, i)),
        ],
        out_specs=pl.BlockSpec((n, 3 * units, piece), lambda i: (0, 0, 0)),
        out_shape=shape((n, 3 * units, piece), low),
        scratch_shapes=[pltpu.VMEM((3 * units, width), full)],
        compiler_params=params(),
        cost_estimate=cost(6 * rows * width * units, 4 * rows * width + 12 * units * width),
        name="feed_grads",
    )(hidden, cot, active, gates_grad)


def turn(values, cosine, sine, half):
    cols = values.shape[1]
    lane = lax.broadcasted_iota(jnp.int32, (1, cols), 1) % HD
    other = jnp.where(
        lane < half, pltpu.roll(values, cols - half, 1), pltpu.roll(values, half, 1)
    )
    repeat = cols // cosine.shape[1]
    if repeat > 1:
        cosine = jnp.concatenate([cosine] * repeat, axis=1)
        sine = jnp.concatenate([sine] * repeat, axis=1)
    return values * cosine + other * sine


def project_kernel(n, count, me_ref, *refs):
    pieces = refs[:count]
    h_ref, c_ref, cos_ref, sin_ref, bias_ref, q_ref, k_ref, v_ref, o_ref, w_ref, sems = refs[
        count:
    ]
    piece = pieces[0].shape[-2]

    def target_of(index):
        return w_ref.at[:, pl.ds(pl.multiple_of(index * piece, piece), piece), :]

    @pl.when(pl.program_id(0) == 0)
    def _():
        fetch(n, me_ref[0], pieces, target_of, sems, "start")
        fetch(n, me_ref[0], pieces, target_of, sems, "wait")

    h = h_ref[...]
    cosine, sine = cos_ref[...], sin_ref[...]
    half = ROT // 2
    q_ref[...] = turn(dot_nn(h, w_ref[0]) + bias_ref[0:1], cosine, sine, half).astype(low)
    k_ref[...] = turn(dot_nn(h, w_ref[1]) + bias_ref[1:2], cosine, sine, half).astype(low)
    v_ref[...] = (dot_nn(h, w_ref[2]) + bias_ref[2:3]).astype(low)
    o_ref[...] = dot_nn(c_ref[...], w_ref[3]).astype(low)


def project(n, me, pieces, hidden, cot, cosine, sine, bias):
    rows, width = hidden.shape
    piece, cols = pieces[0].shape[-2:]
    count = len(pieces)
    block = min(512, rows)
    row_spec = pl.BlockSpec((block, width), lambda i, m: (i, 0))
    angle_spec = pl.BlockSpec((block, 128), lambda i, m: (i, 0))
    out_spec = pl.BlockSpec((block, cols), lambda i, m: (i, 0))
    return pl.pallas_call(
        functools.partial(project_kernel, n, count),
        grid_spec=pltpu.PrefetchScalarGridSpec(
            num_scalar_prefetch=1,
            grid=(rows // block,),
            in_specs=[pl.BlockSpec(memory_space=pl.ANY)] * count
            + [row_spec, row_spec, angle_spec, angle_spec]
            + [pl.BlockSpec((3, cols), lambda i, m: (0, 0))],
            out_specs=[out_spec] * 4 + [pl.BlockSpec((4, width, cols), lambda i, m: (0, 0, 0))],
            scratch_shapes=[pltpu.SemaphoreType.DMA((2 * n - 1,))],
        ),
        out_shape=[shape((rows, cols), low)] * 4 + [shape((4, width, cols), low)],
        compiler_params=params(),
        cost_estimate=cost(8 * rows * width * cols, 4 * rows * width + 16 * width * cols),
        name="project",
    )(me, *pieces, hidden, cot, cosine, sine, bias)


def attend_kernel(block, q_ref, k_ref, v_ref, o_ref, cos_ref, sin_ref, ctx_ref, mg_ref, bias_ref, dq, dk, dv):
    length, lanes = q_ref.shape
    scale = HD ** (-0.5)
    for head in range(lanes // HD):
        cols = slice(head * HD, (head + 1) * HD)
        for i in range(length // block):
            rows = slice(i * block, (i + 1) * block)
            end = (i + 1) * block
            q = q_ref[rows, cols]
            o = o_ref[rows, cols]
            k = k_ref[:end, cols]
            v = v_ref[:end, cols]
            scores = dot_nt(q, k) * scale
            row = i * block + lax.broadcasted_iota(jnp.int32, (block, end), 0)
            col = lax.broadcasted_iota(jnp.int32, (block, end), 1)
            scores = jnp.where(col <= row, scores, masked_score)
            top = jnp.max(scores, axis=-1, keepdims=True)
            weights = jnp.exp(scores - top)
            probs = weights * (1.0 / jnp.sum(weights, axis=-1, keepdims=True))
            probs_low = probs.astype(low)
            ctx_ref[rows, cols] = dot_nn(probs_low, v).astype(low)
            prob_grads = dot_nt(o, v)
            middle = jnp.sum(probs * prob_grads, axis=-1, keepdims=True)
            score_grads = (probs * (prob_grads - middle)).astype(low)
            dq[rows, cols] = dot_nn(score_grads, k) * scale
            key_part = dot_tn(score_grads, q) * scale
            value_part = dot_tn(probs_low, o)
            if i == 0:
                dk[:end, cols] = key_part
                dv[:end, cols] = value_part
                if end < length:
                    dk[end:, cols] = jnp.zeros((length - end, HD), full)
                    dv[end:, cols] = jnp.zeros((length - end, HD), full)
            else:
                dk[:end, cols] += key_part
                dv[:end, cols] += value_part
    cosine, sine = cos_ref[...], -sin_ref[...]
    half = ROT // 2
    sums = []
    for part, grads in enumerate(
        (turn(dq[...], cosine, sine, half), turn(dk[...], cosine, sine, half), dv[...])
    ):
        rounded = grads.astype(low)
        mg_ref[part] = rounded
        sums.append(jnp.sum(rounded.astype(full), axis=0, keepdims=True))
    total = jnp.concatenate(sums, axis=0)

    @pl.when(pl.program_id(1) == 0)
    def _():
        bias_ref[...] = total

    @pl.when(pl.program_id(1) > 0)
    def _():
        bias_ref[...] += total


def attend(batch, q, k, v, o, cosine, sine):
    rows, cols = q.shape
    length = rows // batch
    lanes = 128
    spec = pl.BlockSpec((length, lanes), lambda p, b: (b, p))
    angle_spec = pl.BlockSpec((length, 128), lambda p, b: (b, 0))
    return pl.pallas_call(
        functools.partial(attend_kernel, min(512, length)),
        grid=(cols // lanes, batch),
        in_specs=[spec] * 4 + [angle_spec] * 2,
        out_specs=[
            spec,
            pl.BlockSpec((3, length, lanes), lambda p, b: (0, b, p)),
            pl.BlockSpec((3, lanes), lambda p, b: (0, p)),
        ],
        out_shape=[
            shape((rows, cols), low),
            shape((3, rows, cols), low),
            shape((3, cols), full),
        ],
        scratch_shapes=[pltpu.VMEM((length, lanes), full)] * 3,
        compiler_params=params(),
        cost_estimate=cost(
            40 * rows * length * cols, 20 * rows * cols, rows * length * cols // HD
        ),
        name="attend",
    )(q, k, v, o, cosine, sine)


def attend_grads_kernel(n, me_ref, h_ref, c_ref, mg_ref, ctx_ref, *refs):
    own_ref, *slot_refs = refs[:n]
    edge_ref, wide = refs[n:]
    step = pl.program_id(0)
    cols = ctx_ref.shape[1]

    @pl.when(step == 0)
    def _():
        for part in range(3):
            wide[:, part * cols : (part + 1) * cols] = mg_ref[part]

    grad = dot_tn(h_ref[...], wide[...])
    grads = [grad[:, part * cols : (part + 1) * cols] for part in range(3)]
    grads.append(dot_tn(c_ref[...], ctx_ref[...]))
    for j in range(n):

        @pl.when(step == j)
        def _(j=j):
            for part in range(4):
                if j == 0:
                    own_ref[part] = grads[part]
                else:
                    slot_refs[j - 1][part] = grads[part].astype(low)

    @pl.when(lax.rem(me_ref[0] + step, n) == n - 1 - me_ref[0])
    def _():
        for part in range(4):
            edge_ref[part] = grads[part].astype(low)


def attend_grads(n, me, hidden, cot, mixed_grad, context):
    rows, width = hidden.shape
    cols = context.shape[1]
    piece = width // n
    whole3 = pl.BlockSpec((4, piece, cols), lambda i, m: (0, 0, 0))
    cut_spec = pl.BlockSpec((rows, piece), lambda i, m: (0, lax.rem(m[0] + i, n)))
    return pl.pallas_call(
        functools.partial(attend_grads_kernel, n),
        grid_spec=pltpu.PrefetchScalarGridSpec(
            num_scalar_prefetch=1,
            grid=(n,),
            in_specs=[
                cut_spec,
                cut_spec,
                pl.BlockSpec((3, rows, cols), lambda i, m: (0, 0, 0)),
                pl.BlockSpec((rows, cols), lambda i, m: (0, 0)),
            ],
            out_specs=[whole3] * (n + 1),
            scratch_shapes=[pltpu.VMEM((rows, 3 * cols), low)],
        ),
        out_shape=[shape((4, piece, cols), full)] + [shape((4, piece, cols), low)] * n,
        compiler_params=params(),
        cost_estimate=cost(8 * rows * width * cols, 4 * rows * width + 16 * width * cols),
        name="attend_grads",
    )(me, hidden, cot, mixed_grad, context)


def heads_kernel(ctx_ref, mg_ref, wa_ref, hid_ref, out_ref):
    hid = dot_nt(mg_ref[0], wa_ref[0]) + dot_nt(mg_ref[1], wa_ref[1]) + dot_nt(mg_ref[2], wa_ref[2])
    hid_ref[...] = hid.astype(low)
    out_ref[...] = dot_nt(ctx_ref[...], wa_ref[3]).astype(low)


def heads_parts(context, mixed_grad, w_attend):
    rows, cols = context.shape
    width = w_attend.shape[1]
    block = min(256, rows)
    out_spec = pl.BlockSpec((block, width), lambda i: (i, 0))
    return pl.pallas_call(
        heads_kernel,
        grid=(rows // block,),
        in_specs=[
            pl.BlockSpec((block, cols), lambda i: (i, 0)),
            pl.BlockSpec((3, block, cols), lambda i: (0, i, 0)),
            pl.BlockSpec((4, width, cols), lambda i: (0, 0, 0)),
        ],
        out_specs=[out_spec, out_spec],
        out_shape=[shape((rows, width), low)] * 2,
        compiler_params=params(),
        cost_estimate=cost(8 * rows * width * cols, 4 * rows * width + 8 * (rows + width) * cols),
        name="heads_parts",
    )(context, mixed_grad, w_attend)


def early_kernel(act_ref, grad_ref, w_ref, hid_in_ref, out_in_ref, hid_ref, out_ref):
    hid = hid_in_ref[...].astype(full) + dot_tn(grad_ref[...], join_gates(w_ref))
    hid_ref[...] = hid.astype(low)
    out = out_in_ref[...].astype(full) + dot_tn(act_ref[...], w_ref[2])
    out_ref[...] = out.astype(low)


def early_parts(active, gates_grad, w_feed, hid, out):
    rows, width = hid.shape
    units = w_feed.shape[1]
    block = min(256, rows)
    row_spec = pl.BlockSpec((block, width), lambda i: (i, 0))
    return pl.pallas_call(
        early_kernel,
        grid=(rows // block,),
        in_specs=[
            pl.BlockSpec((units, block), lambda i: (0, i)),
            pl.BlockSpec((2 * units, block), lambda i: (0, i)),
            pl.BlockSpec((3, units, width), lambda i: (0, 0, 0)),
            row_spec,
            row_spec,
        ],
        out_specs=[row_spec, row_spec],
        out_shape=[shape((rows, width), low)] * 2,
        compiler_params=params(),
        cost_estimate=cost(6 * rows * width * units, 8 * rows * width + 6 * (rows + width) * units),
        name="early_parts",
    )(active, gates_grad, w_feed, hid, out)


def sixteenth(which, m):
    return m[0] * 8 + (m[1] * 2 + m[2] if which == 0 else 4 + m[2] * 2 + m[1])


def back_kernel(info_ref, *refs):
    p_ref = refs[6]
    total = 0.0
    for x_ref, near_ref, far_ref, back_ref in zip(refs[0:2], refs[2:4], refs[4:6], refs[7:9]):
        x = x_ref[...].astype(full)
        centred = x - jnp.mean(x, axis=-1, keepdims=True)
        inv = lax.rsqrt(jnp.mean(centred * centred, axis=-1, keepdims=True) + epsilon)
        normal = centred * inv
        grad = near_ref[...].astype(full) + far_ref[...].astype(full)
        scaled = grad * p_ref[0:1]
        back = inv * (
            scaled
            - jnp.mean(scaled, axis=-1, keepdims=True)
            - normal * jnp.mean(scaled * normal, axis=-1, keepdims=True)
        )
        back_ref[: x.shape[0]] = back.astype(low)
        total += jnp.concatenate(
            [jnp.sum(grad * normal, axis=0, keepdims=True), jnp.sum(grad, axis=0, keepdims=True)],
            axis=0,
        )
    high = total.astype(low)
    rest = total - high.astype(full)
    middle = rest.astype(low)
    small = (rest - middle.astype(full)).astype(low)
    zeros = jnp.zeros((tail_rows - 6, total.shape[1]), full)
    terms = [high.astype(full), middle.astype(full), small.astype(full), zeros]
    refs[7][refs[0].shape[0] :] = jnp.concatenate(terms, axis=0).astype(low)


def back_rows(info, rows, near, far, norm_params):
    count, width = near[0].shape
    spec = pl.BlockSpec((count, width), lambda i, m: (0, 0))
    pair = pl.BlockSpec((2, width), lambda i, m: (0, 0))
    return pl.pallas_call(
        back_kernel,
        grid_spec=pltpu.PrefetchScalarGridSpec(
            num_scalar_prefetch=1,
            grid=(1,),
            in_specs=[
                pl.BlockSpec((count, width), lambda i, m: (sixteenth(0, m), 0)),
                pl.BlockSpec((count, width), lambda i, m: (sixteenth(1, m), 0)),
            ]
            + [spec] * 4
            + [pair],
            out_specs=[pl.BlockSpec((count + tail_rows, width), lambda i, m: (0, 0)), spec],
        ),
        out_shape=[shape((count + tail_rows, width), low), shape((count, width), low)],
        compiler_params=params(),
        cost_estimate=cost(40 * count * width, 16 * count * width),
        name="back_rows",
    )(info, rows, rows, *near, *far, norm_params)


def add_kernel(info_ref, *refs):
    for x_ref, near_ref, far_ref, out_ref in zip(refs[0:2], refs[2:4], refs[4:6], refs[6:8]):
        total = x_ref[...].astype(full) + near_ref[...].astype(full) + far_ref[...].astype(full)
        out_ref[...] = total.astype(low)


def add_rows(info, rows, near, far):
    count, width = near[0].shape
    spec = pl.BlockSpec((count, width), lambda i, m: (0, 0))
    return pl.pallas_call(
        add_kernel,
        grid_spec=pltpu.PrefetchScalarGridSpec(
            num_scalar_prefetch=1,
            grid=(1,),
            in_specs=[
                pl.BlockSpec((count, width), lambda i, m: (sixteenth(0, m), 0)),
                pl.BlockSpec((count, width), lambda i, m: (sixteenth(1, m), 0)),
            ]
            + [spec] * 4,
            out_specs=[spec, spec],
        ),
        out_shape=[shape((count, width), low)] * 2,
        compiler_params=params(),
        cost_estimate=cost(4 * count * width, 16 * count * width),
        name="add_rows",
    )(info, rows, rows, *near, *far)


def pack_kernel(block, info_ref, *refs):
    pieces, out_ref, sems = refs[:8], refs[8], refs[9]
    x, y = info_ref[1], info_ref[2]
    copies = []

    def move(source, at, size):
        place = out_ref.at[pl.ds(pl.multiple_of(at, 16), size), :]
        copies.append(pltpu.make_async_copy(source, place, sems.at[len(copies)]))

    for i, piece in enumerate(pieces):
        high, small = (i // 2) % 2, i % 2
        if i < 4:
            at = (x ^ high) * 2 + (y ^ small)
        else:
            at = 4 + (y ^ high) * 2 + (x ^ small)
        extra = piece.shape[0] - block
        move(piece.at[pl.ds(0, block), :], at * block, block)
        if extra:
            move(piece.at[pl.ds(block, extra), :], 8 * block + at * extra, extra)
    for copy in copies:
        copy.start()
    for copy in copies:
        copy.wait()


def pack_rows(info, pieces):
    block, width = pieces[-1].shape
    extra = pieces[0].shape[0] - block
    return pl.pallas_call(
        functools.partial(pack_kernel, block),
        grid_spec=pltpu.PrefetchScalarGridSpec(
            num_scalar_prefetch=1,
            grid=(1,),
            in_specs=[pl.BlockSpec(piece.shape, lambda i, m: (0, 0)) for piece in pieces],
            out_specs=pl.BlockSpec(memory_space=pl.ANY),
            scratch_shapes=[pltpu.SemaphoreType.DMA((12,))],
        ),
        out_shape=shape((8 * block + 4 * extra, width), low),
        compiler_params=params(),
        cost_estimate=cost(0, 32 * block * width),
        name="pack_rows",
    )(info, *pieces)


def tail_kernel(own_ref, other_ref, out_ref):
    def total(ref):
        values = ref[...].astype(full)
        sums = 0.0
        for i in range(4):
            at = i * tail_rows
            sums += values[at : at + 2] + values[at + 2 : at + 4] + values[at + 4 : at + 6]
        return sums

    out_ref[...] = total(own_ref) + total(other_ref)


def tail_sums(own, other):
    count, width = own.shape
    size = 4 * tail_rows
    spec = pl.BlockSpec((size, width), lambda i: (count // size - 1, 0))
    return pl.pallas_call(
        tail_kernel,
        grid=(1,),
        in_specs=[spec, spec],
        out_specs=pl.BlockSpec((2, width), lambda i: (0, 0)),
        out_shape=shape((2, width), full),
        compiler_params=params(),
        cost_estimate=cost(20 * width, 512 * width),
        name="tail_sums",
    )(own, other)


def finish_kernel(info_ref, *refs):
    out_ref = refs[-1]
    value = refs[0][...]
    if len(refs) > 2 and refs[1].shape == out_ref.shape:
        value = refs[1][...].astype(full) + value.astype(full)
    out_ref[...] = value


def finish_rows(info, rows, half, part, cot=None, begun=None):
    width = part.shape[1]
    block = rows // 8
    place = lambda i, m: ((m[0] ^ half) * 4 + i, 0)
    ins, specs = [part], [pl.BlockSpec((block, width), lambda i, m: (i, 0))]
    if cot is not None:
        ins.append(cot)
        specs.append(pl.BlockSpec((block, width), place))
    if begun is not None:
        ins.append(begun)
        specs.append(pl.BlockSpec(memory_space=pl.ANY))
    return pl.pallas_call(
        finish_kernel,
        grid_spec=pltpu.PrefetchScalarGridSpec(
            num_scalar_prefetch=1,
            grid=(4,),
            in_specs=specs,
            out_specs=pl.BlockSpec((block, width), place),
        ),
        out_shape=shape((rows, width), low if cot is None else full),
        input_output_aliases={} if begun is None else {len(ins): 0},
        compiler_params=params(),
        cost_estimate=cost(rows * width, 4 * rows * width),
        name="finish_rows",
    )(info, *ins)


def update_kernel(rates, count, *refs):
    g_ref = refs[0]
    ins = refs[1:7]
    outs = refs[7 + count :]
    for which, rate in enumerate(rates):
        grad = g_ref[:2] if which == 0 else g_ref[2]
        grad = grad.astype(full)
        w, m, a = (ref[...] for ref in ins[3 * which : 3 * which + 3])
        g_out, w_out, m_out, a_out = outs[4 * which : 4 * which + 4]
        g_out[...] = grad
        w_out[...], m_out[...], a_out[...] = advance(w, grad, m, a, rate)


def update_feed(start, grads, states, rates, begun=()):
    _, units, piece = grads.shape
    block = math.gcd(start, units)
    while block > 128 and block % 16 == 0:
        block //= 2
    at = start // block
    pair = pl.BlockSpec((2, block, piece), lambda i: (0, at + i, 0))
    single = pl.BlockSpec((block, piece), lambda i: (at + i, 0))
    total = states[0].shape[1]
    return pl.pallas_call(
        functools.partial(update_kernel, rates, len(begun)),
        grid=(units // block,),
        in_specs=[pl.BlockSpec((3, block, piece), lambda i: (0, i, 0))]
        + [pair] * 3
        + [single] * 3
        + [pl.BlockSpec(memory_space=pl.ANY)] * len(begun),
        out_specs=[pair] * 4 + [single] * 4,
        out_shape=[shape((2, total, piece), full)] * 4 + [shape((total, piece), full)] * 4,
        input_output_aliases={7 + i: i for i in range(len(begun))},
        compiler_params=params(),
        cost_estimate=cost(30 * units * piece, 3 * 30 * units * piece),
        name="update_feed",
    )(grads, *states, *begun)


def body(
    inputs,
    positions,
    cotangent,
    w_attend_in,
    w_attend_out,
    w_expand,
    w_reduce,
    norm_params,
    attend_bias,
    moment_attend_in,
    moment_attend_out,
    moment_expand,
    moment_reduce,
    moment_norm,
    moment_bias,
    average_attend_in,
    average_attend_out,
    average_expand,
    average_reduce,
    average_norm,
    average_bias,
):
    batch, length, width = inputs.shape
    rows = batch * length
    units = w_expand.shape[2]
    n = lax.axis_size("dp")
    group = lax.axis_size("mp")
    me = lax.axis_index("dp").astype(jnp.int32).reshape(1)
    spot = lax.axis_index("mp").astype(jnp.int32)
    info = jnp.stack([spot & 1, (spot >> 1) & 1, (spot >> 2) & 1, me[0]])
    fast = group == 8

    expand_t = jnp.transpose(w_expand, (1, 2, 0))
    reduce_t = jnp.transpose(w_reduce)
    in_t = jnp.transpose(w_attend_in, (1, 0, 2))
    cut = units // 2 // 16 * 16
    shards = [
        jnp.concatenate([expand_t[:, a:b], reduce_t[None, a:b]], axis=0).astype(low)
        for a, b in ((0, cut), (cut, units))
    ]
    attend_shard = jnp.concatenate([in_t, w_attend_out[None]], axis=0).astype(low)
    attend_pieces = [lax.all_gather(attend_shard, "dp")]
    first_shard, _ = lax.optimization_barrier((shards[0], attend_shard))
    first_pieces = [lax.all_gather(first_shard, "dp")]

    tokens = inputs.reshape(rows, width)
    cot = cotangent.reshape(rows, width)
    hidden = layer_norm(tokens, norm_params)

    half = ROT // 2
    lane = jnp.arange(128, dtype=jnp.int32) % HD
    frequency = 10000.0 ** (-((lane % half).astype(full) * 2.0 / ROT))
    angles = positions.reshape(rows).astype(full)[:, None] * frequency[None, :]
    cosine = jnp.where(lane < ROT, jnp.cos(angles), 1.0)
    sine = jnp.where(lane < half, -jnp.sin(angles), jnp.where(lane < ROT, jnp.sin(angles), 0.0))

    q, k, v, o, w_attend = project(n, me, attend_pieces, hidden, cot, cosine, sine, attend_bias)
    context, mixed_grad, bias_part = attend(batch, q, k, v, o, cosine, sine)
    *attend_slots, edge = attend_grads(n, me, hidden, cot, mixed_grad, context)
    hid_early, out_early = heads_parts(context, mixed_grad, w_attend)
    last_shard, first_piece, attend_slots, edge, hid_early, out_early = lax.optimization_barrier(
        (shards[1], first_pieces[0], attend_slots, edge, hid_early, out_early)
    )

    rights, lefts = [last_shard], [last_shard]
    came = (None, None)
    for k in range(1, n):
        right, left = gather_hop(k, rights[-1], lefts[-1], me[0])
        if k > 1:
            if k == 2:
                load = (after(edge, (rights[-1], lefts[-1])),) * 2
            else:
                load = scatter_load(k - 1, attend_slots, *came)
            coming = scatter_hop(k - 1, *load)
        meanwhile = ()
        if k == 1:
            active, gates_grad, w_feed = meanwhile = feed_chunk(n, me, [first_piece], hidden, cot)
        elif k == 2:
            hid_early, out_early = meanwhile = early_parts(
                active, gates_grad, w_feed, hid_early, out_early
            )
        elif k == 3:
            first_grads = meanwhile = feed_grads(n, hidden, cot, active, gates_grad)
        if k > 1:
            (right, left), came = after(((right, left), coming), meanwhile)
        else:
            right, left = after((right, left), meanwhile)
        rights.append(right)
        lefts.append(left)
    last_pieces = [last_shard] + rights[1:] + lefts[1:]

    def scatter(grads):
        return lax.psum_scatter(grads, "dp", scatter_dimension=0, tiled=False)

    first_grads = scatter(first_grads).reshape(3, cut, -1)

    total_tokens = rows * n

    def update_attend(came):
        grad = attend_slots[0] + came[0].astype(full) + came[1].astype(full)
        grad_in, grad_out = jnp.transpose(grad[:3], (1, 0, 2)), grad[3]
        rate_in = 0.5 / math.sqrt(width * total_tokens)
        rate_out = 1.8 / math.sqrt(width * batch * n)
        new_in = advance(w_attend_in, grad_in, moment_attend_in, average_attend_in, rate_in)
        new_out = advance(w_attend_out, grad_out, moment_attend_out, average_attend_out, rate_out)
        return (grad_in, grad_out) + new_in + new_out

    rates = (1.6 / math.sqrt(width * total_tokens), 0.77 / math.sqrt(FF * total_tokens))
    states = [jnp.transpose(a, (1, 2, 0)) for a in (w_expand, moment_expand, average_expand)]
    states += [jnp.transpose(a) for a in (w_reduce, moment_reduce, average_reduce)]

    if fast:
        s = rows // 16

        def swap_cores(parts):
            came = {i: swap(parts[i], 1) for i in (1, 3, 0, 2)}
            return [came[i] for i in range(4)]

        def sum_cores(own, came):
            own = [a.astype(full) + b.astype(full) for a, b in zip(own, came)]
            return own, (own[1].astype(low), own[3].astype(low))

        def sum_first(own, came):
            first = own[0] + came[0].astype(full)
            second = own[2] + came[1].astype(full)
            near = [first[:s].astype(low), second[:s].astype(low)]
            return near, (first[s:].astype(low), second[s:].astype(low))

        def both_ways(pair, masks):
            return [swap(pair[0], masks[0]), swap(pair[1], masks[1])]

        def join(one, first, second, third):
            pieces = (one, first, second, third)
            return pack_rows(info, [p[0] for p in pieces] + [p[1] for p in pieces])

        *parts, active, both, w_last = out_last(n, info, True, last_pieces, hidden, out_early)
        own_out, load_out = sum_cores(parts[4:], swap_cores(parts[:4]))
        one_out = both_ways(load_out, (2, 4))
        *parts, gates_grad = hid_last(info, True, w_last, after(both, load_out), cot, hid_early)
        came_hid = swap_cores(parts[:4])
        near_out, load_out = sum_first(own_out, after(one_out, parts[0]))
        two_out = both_ways(load_out, (4, 2))
        own_hid, load_hid = sum_cores(parts[4:], after(came_hid, load_out))
        one_hid = both_ways(load_hid, (2, 4))
        last_grads = feed_grads(n, hidden, cot, after(active, load_hid), gates_grad)
        two_out = after(two_out, last_grads)
        last_grads = scatter(last_grads).reshape(3, units - cut, -1)
        add = add_rows(info, tokens, near_out, two_out)
        out_one = both_ways(add, (4, 2))
        out_two = both_ways(add, (2, 4))
        near_hid, load_hid = sum_first(own_hid, after(one_hid, add))
        two_hid = both_ways(load_hid, (4, 2))
        back = back_rows(info, tokens, near_hid, two_hid, norm_params)
        hid_one = both_ways(back, (4, 2))
        hid_two = both_ways(back, (2, 4))
        out_one, out_two = after((out_one, out_two), back)
        out_three = both_ways(out_one, (2, 4))
        begun = update_feed(0, after(first_grads, out_one), states, rates)
        hid_one, hid_two = after((hid_one, hid_two), begun)
        hid_three = both_ways(hid_one, (2, 4))
        out_three = after(out_three, hid_one)
        mine_out = join(add, out_one, out_two, out_three)
        other_out = swap(mine_out, 1)
        output = finish_rows(info, rows, 0, mine_out)
        output = finish_rows(info, rows, 1, after(other_out, output), begun=output)
        done = update_feed(cut, after(last_grads, output), states, rates, begun)
        came = scatter_hop(n - 1, *scatter_load(n - 1, after(attend_slots, done), *came))
        hid_three = after(hid_three, done)
        mine_hid = join(back, hid_one, hid_two, hid_three)
        other_hid = swap(mine_hid, 1)
        input_grad = finish_rows(info, rows, 0, mine_hid, cot)
        other_hid = after(other_hid, input_grad)
        norm_part = tail_sums(mine_hid, other_hid)
        sums = small_sum(join_sums(norm_part, bias_part), "dp")
        input_grad = finish_rows(info, rows, 1, after(other_hid, norm_part), cot, input_grad)
        attend_new = update_attend(after(came, input_grad))
        norm_grad, bias_grad = split_sums(sums, norm_part, bias_part)
    else:
        out_part, active, both, w_last = out_last(n, info, False, last_pieces, hidden, out_early)
        hid_part, gates_grad = hid_last(info, False, w_last, both, cot, hid_early)
        came = scatter_hop(n - 1, *scatter_load(n - 1, attend_slots, *came))
        attend_new = update_attend(came)
        last_grads = scatter(feed_grads(n, hidden, cot, active, gates_grad)).reshape(3, units - cut, -1)
        hidden_grad = lax.psum(hid_part, "mp").astype(full)
        summed = lax.psum(out_part, "mp").astype(full)
        values = tokens.astype(full)
        output = (values + summed).astype(low)
        centred = values - jnp.mean(values, axis=-1, keepdims=True)
        inv = lax.rsqrt(jnp.mean(centred * centred, axis=-1, keepdims=True) + epsilon)
        normal = centred * inv
        scaled = hidden_grad * norm_params[0]
        back = inv * (
            scaled
            - jnp.mean(scaled, axis=-1, keepdims=True)
            - normal * jnp.mean(scaled * normal, axis=-1, keepdims=True)
        )
        input_grad = cot.astype(full) + back
        norm_part = jnp.stack([jnp.sum(hidden_grad * normal, axis=0), jnp.sum(hidden_grad, axis=0)])
        sums = small_sum(join_sums(norm_part, bias_part), "dp")
        norm_grad, bias_grad = split_sums(sums, norm_part, bias_part)
        begun = update_feed(0, first_grads, states, rates)
        done = update_feed(cut, last_grads, states, rates, begun)
    grad_in, grad_out = attend_new[:2]
    new_in, moment_in_new, average_in_new = attend_new[2:5]
    new_out, moment_out_new, average_out_new = attend_new[5:]
    grad_expand, new_expand, moment_expand_new, average_expand_new = (
        jnp.transpose(a, (2, 0, 1)) for a in done[:4]
    )
    grad_reduce, new_reduce, moment_reduce_new, average_reduce_new = (
        jnp.transpose(a) for a in done[4:]
    )
    input_grad = input_grad.reshape(batch, length, width)
    output = output.reshape(batch, length, width)
    new_norm, moment_norm_new, average_norm_new = advance(
        norm_params, norm_grad, moment_norm, average_norm, 0.06 / math.sqrt(total_tokens)
    )
    new_bias, moment_bias_new, average_bias_new = advance(
        attend_bias, bias_grad, moment_bias, average_bias, 0.25 / math.sqrt(total_tokens)
    )
    return (
        output,
        input_grad,
        grad_in,
        grad_out,
        grad_expand,
        grad_reduce,
        norm_grad,
        bias_grad,
        new_in,
        new_out,
        new_expand,
        new_reduce,
        new_norm,
        new_bias,
        moment_in_new,
        moment_out_new,
        moment_expand_new,
        moment_reduce_new,
        moment_norm_new,
        moment_bias_new,
        average_in_new,
        average_out_new,
        average_expand_new,
        average_reduce_new,
        average_norm_new,
        average_bias_new,
    )


def solution(mesh):
    rows3 = P("dp", None, None)
    in3 = P("dp", None, "mp")
    in2 = P("dp", "mp")
    bias = P(None, "mp")
    states = (in3, in2, in3, in2, P(), bias)
    return jax.shard_map(
        body,
        mesh=mesh,
        in_specs=(rows3, P("dp", None), rows3) + states * 3,
        out_specs=(rows3, rows3) + states * 4,
        check_vma=False,
    )
```

```python
import functools
import math

import jax
import jax.numpy as jnp
from jax import lax
from jax.experimental import pallas as pl
from jax.experimental.pallas import tpu as pltpu
from jax.sharding import PartitionSpec as P

HD = 64
ROT = 16
FF = 5632

epsilon = 1e-05
decay_moment = 0.9
decay_average = 0.9
masked_score = -1e30

low = jnp.bfloat16
full = jnp.float32
vmem_limit = 60 << 20
tail_rows = 16


def dot_nt(left, right):
    return lax.dot_general(left, right, (((1,), (1,)), ((), ())), preferred_element_type=full)


def dot_nn(left, right):
    return lax.dot_general(left, right, (((1,), (0,)), ((), ())), preferred_element_type=full)


def dot_tn(left, right):
    return lax.dot_general(left, right, (((0,), (0,)), ((), ())), preferred_element_type=full)


def params(**more):
    return pltpu.CompilerParams(vmem_limit_bytes=vmem_limit, **more)


def cost(flops, moved, trans=0):
    return pl.CostEstimate(flops=int(flops), bytes_accessed=int(moved), transcendentals=int(trans))


def shape(dims, kind):
    return jax.ShapeDtypeStruct(dims, kind)


def advance(weight, grad, moment, average, rate):
    moment_new = decay_moment * moment + grad
    weight_new = weight - rate * (grad + decay_moment * moment_new)
    average_new = decay_average * average + (1.0 - decay_average) * weight_new
    return (weight_new, moment_new, average_new)


def after(value, *others):
    return lax.optimization_barrier((value, others))[0]


def gather_hop(k, right, left, me):
    n = lax.axis_size("dp")
    to_right = [(a, a + 1) for a in range(k - 1, n - 1)]
    to_left = [(a, a - 1) for a in range(1, n - k + 1)]
    if k == n - 1 and n != 3:
        both = lax.ppermute(jnp.where(me == 1, left, right), "dp", to_right + to_left)
        return both, both
    return lax.ppermute(right, "dp", to_right), lax.ppermute(left, "dp", to_left)


def scatter_load(k, slots, right, left):
    n = lax.axis_size("dp")
    to_right, to_left = slots[n - k], slots[k]
    if k > 1:
        to_right = (to_right.astype(full) + right.astype(full)).astype(low)
        to_left = (to_left.astype(full) + left.astype(full)).astype(low)
    return to_right, to_left


def scatter_hop(k, to_right, to_left):
    n = lax.axis_size("dp")
    rights = [(a, a + 1) for a in range(k)]
    lefts = [(a, a - 1) for a in range(n - 1, n - 1 - k, -1)]
    if k == 1 and n != 3:
        both = lax.ppermute(to_right, "dp", rights + lefts)
        return both, both
    return lax.ppermute(to_right, "dp", rights), lax.ppermute(to_left, "dp", lefts)


def swap(value, mask, axis="mp"):
    n = lax.axis_size(axis)
    return lax.ppermute(value, axis, [(a, a ^ mask) for a in range(n)])


def small_sum(value, axis):
    n = lax.axis_size(axis)
    if n & (n - 1):
        return lax.psum(value, axis)
    mask = 1
    while mask < n:
        value = value + swap(value, mask, axis)
        mask *= 2
    return value


def join_sums(norm_part, bias_part):
    cols = bias_part.shape[1]
    return jnp.concatenate([norm_part.reshape(-1, cols), bias_part])


def split_sums(sums, norm_part, bias_part):
    count = sums.shape[0] - bias_part.shape[0]
    return sums[:count].reshape(norm_part.shape), sums[count:]


def norm_kernel(x_ref, p_ref, o_ref):
    x = x_ref[...].astype(full)
    centred = x - jnp.mean(x, axis=-1, keepdims=True)
    inv = lax.rsqrt(jnp.mean(centred * centred, axis=-1, keepdims=True) + epsilon)
    o_ref[...] = (centred * inv * p_ref[0:1] + p_ref[1:2]).astype(low)


def layer_norm(rows, norm_params):
    count, width = rows.shape
    block = min(256, count)
    return pl.pallas_call(
        norm_kernel,
        grid=(count // block,),
        in_specs=[
            pl.BlockSpec((block, width), lambda i: (i, 0)),
            pl.BlockSpec((2, width), lambda i: (0, 0)),
        ],
        out_specs=pl.BlockSpec((block, width), lambda i: (i, 0)),
        out_shape=shape((count, width), low),
        compiler_params=params(),
        cost_estimate=cost(8 * count * width, 4 * count * width),
        name="layer_norm",
    )(rows, norm_params)


def fetch(n, me, pieces, target_of, sems, action):
    def run(source, index, sem):
        copy = pltpu.make_async_copy(source, target_of(index), sem)
        if action == "start":
            copy.start()
        else:
            copy.wait()

    if len(pieces) == 1:
        for j in range(n):
            run(pieces[0].at[j], j, sems.at[j])
        return
    run(pieces[0], me, sems.at[0])
    for k in range(1, n):

        @pl.when(me >= k)
        def _(k=k):
            run(pieces[k], me - k, sems.at[k])

        @pl.when(me + k < n)
        def _(k=k):
            run(pieces[n - 1 + k], me + k, sems.at[n - 1 + k])


def swish_of(both):
    units = both.shape[0] // 2
    gate, upper = both[:units], both[units:]
    sigmoid = jax.nn.sigmoid(gate)
    return gate, upper, sigmoid, gate * sigmoid


def join_gates(w_ref):
    return w_ref[0:2].reshape(2 * w_ref.shape[1], w_ref.shape[2])


def gates_grad_of(both, active_grad):
    gate, upper, sigmoid, swish = swish_of(both)
    gate_grad = active_grad * upper * sigmoid * (1.0 + gate * (1.0 - sigmoid))
    return jnp.concatenate([gate_grad, active_grad * swish], axis=0).astype(low)


def gates_of(w_ref, h, c):
    both = dot_nt(join_gates(w_ref), h)
    _, upper, _, swish = swish_of(both)
    return (swish * upper).astype(low), gates_grad_of(both, dot_nt(w_ref[2], c))


def add_grads(acc, step, active, gates_grad, h, c):
    units = active.shape[0]

    @pl.when(step == 0)
    def _():
        acc[: 2 * units] = dot_nn(gates_grad, h)
        acc[2 * units :] = dot_nn(active, c)

    @pl.when(step > 0)
    def _():
        acc[: 2 * units] += dot_nn(gates_grad, h)
        acc[2 * units :] += dot_nn(active, c)


def store_grads(n, acc, out_ref):
    piece = out_ref.shape[2]
    for j in range(n):
        out_ref[j] = acc[:, j * piece : (j + 1) * piece].astype(low)


def wide_target(w_ref, piece):
    return lambda index: w_ref.at[:, :, pl.ds(pl.multiple_of(index * piece, piece), piece)]


def feed_kernel(n, count, me_ref, *refs):
    pieces = refs[:count]
    h_ref, c_ref, act_ref, grad_ref, w_ref, sems = refs[count:]
    target_of = wide_target(w_ref, w_ref.shape[2] // n)

    @pl.when(pl.program_id(0) == 0)
    def _():
        fetch(n, me_ref[0], pieces, target_of, sems, "start")
        fetch(n, me_ref[0], pieces, target_of, sems, "wait")

    act_ref[...], grad_ref[...] = gates_of(w_ref, h_ref[...], c_ref[...])


def feed_chunk(n, me, pieces, hidden, cot):
    rows, width = hidden.shape
    units = pieces[0].shape[-2]
    count = len(pieces)
    block = min(512, rows)
    row_spec = pl.BlockSpec((block, width), lambda i, m: (i, 0))
    return pl.pallas_call(
        functools.partial(feed_kernel, n, count),
        grid_spec=pltpu.PrefetchScalarGridSpec(
            num_scalar_prefetch=1,
            grid=(rows // block,),
            in_specs=[pl.BlockSpec(memory_space=pl.ANY)] * count + [row_spec, row_spec],
            out_specs=[
                pl.BlockSpec((units, block), lambda i, m: (0, i)),
                pl.BlockSpec((2 * units, block), lambda i, m: (0, i)),
                pl.BlockSpec((3, units, width), lambda i, m: (0, 0, 0)),
            ],
            scratch_shapes=[pltpu.SemaphoreType.DMA((2 * n - 1,))],
        ),
        out_shape=[
            shape((units, rows), low),
            shape((2 * units, rows), low),
            shape((3, units, width), low),
        ],
        compiler_params=params(),
        cost_estimate=cost(
            6 * rows * width * units, 4 * rows * width + 12 * units * width, rows * units
        ),
        name="feed_chunk",
    )(me, *pieces, hidden, cot)


def put_part(split, info_ref, parts, value):
    if not split:
        parts[0][...] = value.astype(low)
        return
    step = pl.program_id(0)
    sub = value.shape[0] // 4
    high = jnp.where(step % 2 == 0, info_ref[1], info_ref[2])
    small = jnp.where(step % 2 == 0, info_ref[2], info_ref[1])
    first, second = value[: 2 * sub], value[2 * sub :]
    near = jnp.where(high == 0, first, second).astype(low)
    far = jnp.where(high == 0, second, first).astype(low)
    for at in range(4):

        @pl.when(step == at)
        def _(at=at):
            for ref, pair in ((parts[2 * at], near), (parts[2 * at + 1], far)):
                for i in range(2):
                    place = pl.ds(pl.multiple_of((i ^ small) * sub, sub), sub)
                    ref[place, :] = pair[i * sub : (i + 1) * sub]


def last_blocks(split, rows, width):
    if split:
        block, steps = rows // 4, 4
        place = lambda i, m: (m[0] ^ (1 - i // 2)) * 2 + i % 2
        part_specs = [pl.BlockSpec((block // 2, width), lambda i, m: (0, 0))] * 8
        part_shapes = [shape((block // 2, width), low)] * 8
    else:
        block = min(256, rows)
        steps = rows // block
        place = lambda i, m: i
        part_specs = [pl.BlockSpec((block, width), lambda i, m: (i, 0))]
        part_shapes = [shape((rows, width), low)]
    return block, steps, place, part_specs, part_shapes


def out_last_kernel(n, count, split, info_ref, *refs):
    pieces = refs[:count]
    h_ref, early_ref = refs[count : count + 2]
    parts = refs[count + 2 : -4]
    act_ref, both_ref, w_ref, sems = refs[-4:]
    target_of = wide_target(w_ref, w_ref.shape[2] // n)

    @pl.when(pl.program_id(0) == 0)
    def _():
        fetch(n, info_ref[3], pieces, target_of, sems, "start")
        fetch(n, info_ref[3], pieces, target_of, sems, "wait")

    both = dot_nt(join_gates(w_ref), h_ref[...])
    both_ref[...] = both
    _, upper, _, swish = swish_of(both)
    active = (swish * upper).astype(low)
    act_ref[...] = active
    put_part(split, info_ref, parts, early_ref[...].astype(full) + dot_tn(active, w_ref[2]))


def out_last(n, info, split, pieces, hidden, early):
    rows, width = hidden.shape
    units = pieces[0].shape[-2]
    count = len(pieces)
    block, steps, place, part_specs, part_shapes = last_blocks(split, rows, width)
    row_spec = pl.BlockSpec((block, width), lambda i, m: (place(i, m), 0))
    return pl.pallas_call(
        functools.partial(out_last_kernel, n, count, split),
        grid_spec=pltpu.PrefetchScalarGridSpec(
            num_scalar_prefetch=1,
            grid=(steps,),
            in_specs=[pl.BlockSpec(memory_space=pl.ANY)] * count + [row_spec] * 2,
            out_specs=part_specs
            + [
                pl.BlockSpec((units, block), lambda i, m: (0, place(i, m))),
                pl.BlockSpec((2 * units, block), lambda i, m: (0, place(i, m))),
                pl.BlockSpec((3, units, width), lambda i, m: (0, 0, 0)),
            ],
            scratch_shapes=[pltpu.SemaphoreType.DMA((2 * n - 1,))],
        ),
        out_shape=part_shapes
        + [shape((units, rows), low), shape((2 * units, rows), full), shape((3, units, width), low)],
        compiler_params=params(),
        cost_estimate=cost(6 * rows * width * units, 8 * rows * width, rows * units),
        name="out_last",
    )(info, *pieces, hidden, early)


def hid_last_kernel(split, info_ref, w_ref, both_ref, c_ref, early_ref, *refs):
    grad_ref = refs[-1]
    gates_grad = gates_grad_of(both_ref[...], dot_nt(w_ref[2], c_ref[...]))
    grad_ref[...] = gates_grad
    hid = early_ref[...].astype(full) + dot_tn(gates_grad, join_gates(w_ref))
    put_part(split, info_ref, refs[:-1], hid)


def hid_last(info, split, weights, both, cot, early):
    rows, width = cot.shape
    units = weights.shape[1]
    block, steps, place, part_specs, part_shapes = last_blocks(split, rows, width)
    row_spec = pl.BlockSpec((block, width), lambda i, m: (place(i, m), 0))
    both_spec = pl.BlockSpec((2 * units, block), lambda i, m: (0, place(i, m)))
    return pl.pallas_call(
        functools.partial(hid_last_kernel, split),
        grid_spec=pltpu.PrefetchScalarGridSpec(
            num_scalar_prefetch=1,
            grid=(steps,),
            in_specs=[pl.BlockSpec((3, units, width), lambda i, m: (0, 0, 0)), both_spec]
            + [row_spec] * 2,
            out_specs=part_specs + [both_spec],
        ),
        out_shape=part_shapes + [shape((2 * units, rows), low)],
        compiler_params=params(),
        cost_estimate=cost(6 * rows * width * units, 8 * rows * width, rows * units),
        name="hid_last",
    )(info, weights, both, cot, early)


def feed_grads_kernel(n, steps, h_ref, c_ref, act_ref, grad_ref, out_ref, acc):
    step = pl.program_id(0)
    add_grads(acc, step, act_ref[...], grad_ref[...], h_ref[...], c_ref[...])

    @pl.when(step == steps - 1)
    def _():
        store_grads(n, acc, out_ref)


def feed_grads(n, hidden, cot, active, gates_grad):
    rows, width = hidden.shape
    units = active.shape[0]
    piece = width // n
    block = min(512, rows)
    steps = rows // block
    row_spec = pl.BlockSpec((block, width), lambda i: (i, 0))
    return pl.pallas_call(
        functools.partial(feed_grads_kernel, n, steps),
        grid=(steps,),
        in_specs=[
            row_spec,
            row_spec,
            pl.BlockSpec((units, block), lambda i: (0, i)),
            pl.BlockSpec((2 * units, block), lambda i: (0, i)),
        ],
        out_specs=pl.BlockSpec((n, 3 * units, piece), lambda i: (0, 0, 0)),
        out_shape=shape((n, 3 * units, piece), low),
        scratch_shapes=[pltpu.VMEM((3 * units, width), full)],
        compiler_params=params(),
        cost_estimate=cost(6 * rows * width * units, 4 * rows * width + 12 * units * width),
        name="feed_grads",
    )(hidden, cot, active, gates_grad)


def turn(values, cosine, sine, half):
    cols = values.shape[1]
    lane = lax.broadcasted_iota(jnp.int32, (1, cols), 1) % HD
    other = jnp.where(
        lane < half, pltpu.roll(values, cols - half, 1), pltpu.roll(values, half, 1)
    )
    repeat = cols // cosine.shape[1]
    if repeat > 1:
        cosine = jnp.concatenate([cosine] * repeat, axis=1)
        sine = jnp.concatenate([sine] * repeat, axis=1)
    return values * cosine + other * sine


def project_kernel(n, count, me_ref, *refs):
    pieces = refs[:count]
    h_ref, c_ref, cos_ref, sin_ref, bias_ref, q_ref, k_ref, v_ref, o_ref, w_ref, sems = refs[
        count:
    ]
    piece = pieces[0].shape[-2]

    def target_of(index):
        return w_ref.at[:, pl.ds(pl.multiple_of(index * piece, piece), piece), :]

    @pl.when(pl.program_id(0) == 0)
    def _():
        fetch(n, me_ref[0], pieces, target_of, sems, "start")
        fetch(n, me_ref[0], pieces, target_of, sems, "wait")

    h = h_ref[...]
    cosine, sine = cos_ref[...], sin_ref[...]
    half = ROT // 2
    q_ref[...] = turn(dot_nn(h, w_ref[0]) + bias_ref[0:1], cosine, sine, half).astype(low)
    k_ref[...] = turn(dot_nn(h, w_ref[1]) + bias_ref[1:2], cosine, sine, half).astype(low)
    v_ref[...] = (dot_nn(h, w_ref[2]) + bias_ref[2:3]).astype(low)
    o_ref[...] = dot_nn(c_ref[...], w_ref[3]).astype(low)


def project(n, me, pieces, hidden, cot, cosine, sine, bias):
    rows, width = hidden.shape
    piece, cols = pieces[0].shape[-2:]
    count = len(pieces)
    block = min(512, rows)
    row_spec = pl.BlockSpec((block, width), lambda i, m: (i, 0))
    angle_spec = pl.BlockSpec((block, 128), lambda i, m: (i, 0))
    out_spec = pl.BlockSpec((block, cols), lambda i, m: (i, 0))
    return pl.pallas_call(
        functools.partial(project_kernel, n, count),
        grid_spec=pltpu.PrefetchScalarGridSpec(
            num_scalar_prefetch=1,
            grid=(rows // block,),
            in_specs=[pl.BlockSpec(memory_space=pl.ANY)] * count
            + [row_spec, row_spec, angle_spec, angle_spec]
            + [pl.BlockSpec((3, cols), lambda i, m: (0, 0))],
            out_specs=[out_spec] * 4 + [pl.BlockSpec((4, width, cols), lambda i, m: (0, 0, 0))],
            scratch_shapes=[pltpu.SemaphoreType.DMA((2 * n - 1,))],
        ),
        out_shape=[shape((rows, cols), low)] * 4 + [shape((4, width, cols), low)],
        compiler_params=params(),
        cost_estimate=cost(8 * rows * width * cols, 4 * rows * width + 16 * width * cols),
        name="project",
    )(me, *pieces, hidden, cot, cosine, sine, bias)


def attend_kernel(block, q_ref, k_ref, v_ref, o_ref, cos_ref, sin_ref, ctx_ref, mg_ref, bias_ref, dq, dk, dv):
    length, lanes = q_ref.shape
    scale = HD ** (-0.5)
    for head in range(lanes // HD):
        cols = slice(head * HD, (head + 1) * HD)
        for i in range(length // block):
            rows = slice(i * block, (i + 1) * block)
            end = (i + 1) * block
            q = q_ref[rows, cols]
            o = o_ref[rows, cols]
            k = k_ref[:end, cols]
            v = v_ref[:end, cols]
            scores = dot_nt(q, k) * scale
            row = i * block + lax.broadcasted_iota(jnp.int32, (block, end), 0)
            col = lax.broadcasted_iota(jnp.int32, (block, end), 1)
            scores = jnp.where(col <= row, scores, masked_score)
            top = jnp.max(scores, axis=-1, keepdims=True)
            weights = jnp.exp(scores - top)
            probs = weights * (1.0 / jnp.sum(weights, axis=-1, keepdims=True))
            probs_low = probs.astype(low)
            ctx_ref[rows, cols] = dot_nn(probs_low, v).astype(low)
            prob_grads = dot_nt(o, v)
            middle = jnp.sum(probs * prob_grads, axis=-1, keepdims=True)
            score_grads = (probs * (prob_grads - middle)).astype(low)
            dq[rows, cols] = dot_nn(score_grads, k) * scale
            key_part = dot_tn(score_grads, q) * scale
            value_part = dot_tn(probs_low, o)
            if i == 0:
                dk[:end, cols] = key_part
                dv[:end, cols] = value_part
                if end < length:
                    dk[end:, cols] = jnp.zeros((length - end, HD), full)
                    dv[end:, cols] = jnp.zeros((length - end, HD), full)
            else:
                dk[:end, cols] += key_part
                dv[:end, cols] += value_part
    cosine, sine = cos_ref[...], -sin_ref[...]
    half = ROT // 2
    sums = []
    for part, grads in enumerate(
        (turn(dq[...], cosine, sine, half), turn(dk[...], cosine, sine, half), dv[...])
    ):
        rounded = grads.astype(low)
        mg_ref[part] = rounded
        sums.append(jnp.sum(rounded.astype(full), axis=0, keepdims=True))
    total = jnp.concatenate(sums, axis=0)

    @pl.when(pl.program_id(1) == 0)
    def _():
        bias_ref[...] = total

    @pl.when(pl.program_id(1) > 0)
    def _():
        bias_ref[...] += total


def attend(batch, q, k, v, o, cosine, sine):
    rows, cols = q.shape
    length = rows // batch
    lanes = 128
    spec = pl.BlockSpec((length, lanes), lambda p, b: (b, p))
    angle_spec = pl.BlockSpec((length, 128), lambda p, b: (b, 0))
    return pl.pallas_call(
        functools.partial(attend_kernel, min(512, length)),
        grid=(cols // lanes, batch),
        in_specs=[spec] * 4 + [angle_spec] * 2,
        out_specs=[
            spec,
            pl.BlockSpec((3, length, lanes), lambda p, b: (0, b, p)),
            pl.BlockSpec((3, lanes), lambda p, b: (0, p)),
        ],
        out_shape=[
            shape((rows, cols), low),
            shape((3, rows, cols), low),
            shape((3, cols), full),
        ],
        scratch_shapes=[pltpu.VMEM((length, lanes), full)] * 3,
        compiler_params=params(),
        cost_estimate=cost(
            40 * rows * length * cols, 20 * rows * cols, rows * length * cols // HD
        ),
        name="attend",
    )(q, k, v, o, cosine, sine)


def attend_grads_kernel(n, me_ref, h_ref, c_ref, mg_ref, ctx_ref, *refs):
    own_ref, *slot_refs = refs[:n]
    edge_ref, wide = refs[n:]
    step = pl.program_id(0)
    cols = ctx_ref.shape[1]

    @pl.when(step == 0)
    def _():
        for part in range(3):
            wide[:, part * cols : (part + 1) * cols] = mg_ref[part]

    grad = dot_tn(h_ref[...], wide[...])
    grads = [grad[:, part * cols : (part + 1) * cols] for part in range(3)]
    grads.append(dot_tn(c_ref[...], ctx_ref[...]))
    for j in range(n):

        @pl.when(step == j)
        def _(j=j):
            for part in range(4):
                if j == 0:
                    own_ref[part] = grads[part]
                else:
                    slot_refs[j - 1][part] = grads[part].astype(low)

    @pl.when(lax.rem(me_ref[0] + step, n) == n - 1 - me_ref[0])
    def _():
        for part in range(4):
            edge_ref[part] = grads[part].astype(low)


def attend_grads(n, me, hidden, cot, mixed_grad, context):
    rows, width = hidden.shape
    cols = context.shape[1]
    piece = width // n
    whole3 = pl.BlockSpec((4, piece, cols), lambda i, m: (0, 0, 0))
    cut_spec = pl.BlockSpec((rows, piece), lambda i, m: (0, lax.rem(m[0] + i, n)))
    return pl.pallas_call(
        functools.partial(attend_grads_kernel, n),
        grid_spec=pltpu.PrefetchScalarGridSpec(
            num_scalar_prefetch=1,
            grid=(n,),
            in_specs=[
                cut_spec,
                cut_spec,
                pl.BlockSpec((3, rows, cols), lambda i, m: (0, 0, 0)),
                pl.BlockSpec((rows, cols), lambda i, m: (0, 0)),
            ],
            out_specs=[whole3] * (n + 1),
            scratch_shapes=[pltpu.VMEM((rows, 3 * cols), low)],
        ),
        out_shape=[shape((4, piece, cols), full)] + [shape((4, piece, cols), low)] * n,
        compiler_params=params(),
        cost_estimate=cost(8 * rows * width * cols, 4 * rows * width + 16 * width * cols),
        name="attend_grads",
    )(me, hidden, cot, mixed_grad, context)


def heads_kernel(ctx_ref, mg_ref, wa_ref, hid_ref, out_ref):
    hid = dot_nt(mg_ref[0], wa_ref[0]) + dot_nt(mg_ref[1], wa_ref[1]) + dot_nt(mg_ref[2], wa_ref[2])
    hid_ref[...] = hid.astype(low)
    out_ref[...] = dot_nt(ctx_ref[...], wa_ref[3]).astype(low)


def heads_parts(context, mixed_grad, w_attend):
    rows, cols = context.shape
    width = w_attend.shape[1]
    block = min(256, rows)
    out_spec = pl.BlockSpec((block, width), lambda i: (i, 0))
    return pl.pallas_call(
        heads_kernel,
        grid=(rows // block,),
        in_specs=[
            pl.BlockSpec((block, cols), lambda i: (i, 0)),
            pl.BlockSpec((3, block, cols), lambda i: (0, i, 0)),
            pl.BlockSpec((4, width, cols), lambda i: (0, 0, 0)),
        ],
        out_specs=[out_spec, out_spec],
        out_shape=[shape((rows, width), low)] * 2,
        compiler_params=params(),
        cost_estimate=cost(8 * rows * width * cols, 4 * rows * width + 8 * (rows + width) * cols),
        name="heads_parts",
    )(context, mixed_grad, w_attend)


def early_kernel(act_ref, grad_ref, w_ref, hid_in_ref, out_in_ref, hid_ref, out_ref):
    hid = hid_in_ref[...].astype(full) + dot_tn(grad_ref[...], join_gates(w_ref))
    hid_ref[...] = hid.astype(low)
    out = out_in_ref[...].astype(full) + dot_tn(act_ref[...], w_ref[2])
    out_ref[...] = out.astype(low)


def early_parts(active, gates_grad, w_feed, hid, out):
    rows, width = hid.shape
    units = w_feed.shape[1]
    block = min(256, rows)
    row_spec = pl.BlockSpec((block, width), lambda i: (i, 0))
    return pl.pallas_call(
        early_kernel,
        grid=(rows // block,),
        in_specs=[
            pl.BlockSpec((units, block), lambda i: (0, i)),
            pl.BlockSpec((2 * units, block), lambda i: (0, i)),
            pl.BlockSpec((3, units, width), lambda i: (0, 0, 0)),
            row_spec,
            row_spec,
        ],
        out_specs=[row_spec, row_spec],
        out_shape=[shape((rows, width), low)] * 2,
        compiler_params=params(),
        cost_estimate=cost(6 * rows * width * units, 8 * rows * width + 6 * (rows + width) * units),
        name="early_parts",
    )(active, gates_grad, w_feed, hid, out)


def sixteenth(which, m):
    return m[0] * 8 + (m[1] * 2 + m[2] if which == 0 else 4 + m[2] * 2 + m[1])


def back_kernel(info_ref, *refs):
    p_ref = refs[6]
    total = 0.0
    for x_ref, near_ref, far_ref, back_ref in zip(refs[0:2], refs[2:4], refs[4:6], refs[7:9]):
        x = x_ref[...].astype(full)
        centred = x - jnp.mean(x, axis=-1, keepdims=True)
        inv = lax.rsqrt(jnp.mean(centred * centred, axis=-1, keepdims=True) + epsilon)
        normal = centred * inv
        grad = near_ref[...].astype(full) + far_ref[...].astype(full)
        scaled = grad * p_ref[0:1]
        back = inv * (
            scaled
            - jnp.mean(scaled, axis=-1, keepdims=True)
            - normal * jnp.mean(scaled * normal, axis=-1, keepdims=True)
        )
        back_ref[: x.shape[0]] = back.astype(low)
        total += jnp.concatenate(
            [jnp.sum(grad * normal, axis=0, keepdims=True), jnp.sum(grad, axis=0, keepdims=True)],
            axis=0,
        )
    high = total.astype(low)
    rest = total - high.astype(full)
    middle = rest.astype(low)
    small = (rest - middle.astype(full)).astype(low)
    zeros = jnp.zeros((tail_rows - 6, total.shape[1]), full)
    terms = [high.astype(full), middle.astype(full), small.astype(full), zeros]
    refs[7][refs[0].shape[0] :] = jnp.concatenate(terms, axis=0).astype(low)


def back_rows(info, rows, near, far, norm_params):
    count, width = near[0].shape
    spec = pl.BlockSpec((count, width), lambda i, m: (0, 0))
    pair = pl.BlockSpec((2, width), lambda i, m: (0, 0))
    return pl.pallas_call(
        back_kernel,
        grid_spec=pltpu.PrefetchScalarGridSpec(
            num_scalar_prefetch=1,
            grid=(1,),
            in_specs=[
                pl.BlockSpec((count, width), lambda i, m: (sixteenth(0, m), 0)),
                pl.BlockSpec((count, width), lambda i, m: (sixteenth(1, m), 0)),
            ]
            + [spec] * 4
            + [pair],
            out_specs=[pl.BlockSpec((count + tail_rows, width), lambda i, m: (0, 0)), spec],
        ),
        out_shape=[shape((count + tail_rows, width), low), shape((count, width), low)],
        compiler_params=params(),
        cost_estimate=cost(40 * count * width, 16 * count * width),
        name="back_rows",
    )(info, rows, rows, *near, *far, norm_params)


def add_kernel(info_ref, *refs):
    for x_ref, near_ref, far_ref, out_ref in zip(refs[0:2], refs[2:4], refs[4:6], refs[6:8]):
        total = x_ref[...].astype(full) + near_ref[...].astype(full) + far_ref[...].astype(full)
        out_ref[...] = total.astype(low)


def add_rows(info, rows, near, far):
    count, width = near[0].shape
    spec = pl.BlockSpec((count, width), lambda i, m: (0, 0))
    return pl.pallas_call(
        add_kernel,
        grid_spec=pltpu.PrefetchScalarGridSpec(
            num_scalar_prefetch=1,
            grid=(1,),
            in_specs=[
                pl.BlockSpec((count, width), lambda i, m: (sixteenth(0, m), 0)),
                pl.BlockSpec((count, width), lambda i, m: (sixteenth(1, m), 0)),
            ]
            + [spec] * 4,
            out_specs=[spec, spec],
        ),
        out_shape=[shape((count, width), low)] * 2,
        compiler_params=params(),
        cost_estimate=cost(4 * count * width, 16 * count * width),
        name="add_rows",
    )(info, rows, rows, *near, *far)


def pack_kernel(block, info_ref, *refs):
    pieces, out_ref, sems = refs[:8], refs[8], refs[9]
    x, y = info_ref[1], info_ref[2]
    copies = []

    def move(source, at, size):
        place = out_ref.at[pl.ds(pl.multiple_of(at, 16), size), :]
        copies.append(pltpu.make_async_copy(source, place, sems.at[len(copies)]))

    for i, piece in enumerate(pieces):
        high, small = (i // 2) % 2, i % 2
        if i < 4:
            at = (x ^ high) * 2 + (y ^ small)
        else:
            at = 4 + (y ^ high) * 2 + (x ^ small)
        extra = piece.shape[0] - block
        move(piece.at[pl.ds(0, block), :], at * block, block)
        if extra:
            move(piece.at[pl.ds(block, extra), :], 8 * block + at * extra, extra)
    for copy in copies:
        copy.start()
    for copy in copies:
        copy.wait()


def pack_rows(info, pieces):
    block, width = pieces[-1].shape
    extra = pieces[0].shape[0] - block
    return pl.pallas_call(
        functools.partial(pack_kernel, block),
        grid_spec=pltpu.PrefetchScalarGridSpec(
            num_scalar_prefetch=1,
            grid=(1,),
            in_specs=[pl.BlockSpec(piece.shape, lambda i, m: (0, 0)) for piece in pieces],
            out_specs=pl.BlockSpec(memory_space=pl.ANY),
            scratch_shapes=[pltpu.SemaphoreType.DMA((12,))],
        ),
        out_shape=shape((8 * block + 4 * extra, width), low),
        compiler_params=params(),
        cost_estimate=cost(0, 32 * block * width),
        name="pack_rows",
    )(info, *pieces)


def tail_kernel(own_ref, other_ref, out_ref):
    def total(ref):
        values = ref[...].astype(full)
        sums = 0.0
        for i in range(4):
            at = i * tail_rows
            sums += values[at : at + 2] + values[at + 2 : at + 4] + values[at + 4 : at + 6]
        return sums

    out_ref[...] = total(own_ref) + total(other_ref)


def tail_sums(own, other):
    count, width = own.shape
    size = 4 * tail_rows
    spec = pl.BlockSpec((size, width), lambda i: (count // size - 1, 0))
    return pl.pallas_call(
        tail_kernel,
        grid=(1,),
        in_specs=[spec, spec],
        out_specs=pl.BlockSpec((2, width), lambda i: (0, 0)),
        out_shape=shape((2, width), full),
        compiler_params=params(),
        cost_estimate=cost(20 * width, 512 * width),
        name="tail_sums",
    )(own, other)


def finish_kernel(info_ref, *refs):
    out_ref = refs[-1]
    value = refs[0][...]
    if len(refs) > 2 and refs[1].shape == out_ref.shape:
        value = refs[1][...].astype(full) + value.astype(full)
    out_ref[...] = value


def finish_rows(info, rows, half, part, cot=None, begun=None):
    width = part.shape[1]
    block = rows // 8
    place = lambda i, m: ((m[0] ^ half) * 4 + i, 0)
    ins, specs = [part], [pl.BlockSpec((block, width), lambda i, m: (i, 0))]
    if cot is not None:
        ins.append(cot)
        specs.append(pl.BlockSpec((block, width), place))
    if begun is not None:
        ins.append(begun)
        specs.append(pl.BlockSpec(memory_space=pl.ANY))
    return pl.pallas_call(
        finish_kernel,
        grid_spec=pltpu.PrefetchScalarGridSpec(
            num_scalar_prefetch=1,
            grid=(4,),
            in_specs=specs,
            out_specs=pl.BlockSpec((block, width), place),
        ),
        out_shape=shape((rows, width), low if cot is None else full),
        input_output_aliases={} if begun is None else {len(ins): 0},
        compiler_params=params(),
        cost_estimate=cost(rows * width, 4 * rows * width),
        name="finish_rows",
    )(info, *ins)


def update_kernel(rates, count, *refs):
    g_ref = refs[0]
    ins = refs[1:7]
    outs = refs[7 + count :]
    for which, rate in enumerate(rates):
        grad = g_ref[:2] if which == 0 else g_ref[2]
        grad = grad.astype(full)
        w, m, a = (ref[...] for ref in ins[3 * which : 3 * which + 3])
        g_out, w_out, m_out, a_out = outs[4 * which : 4 * which + 4]
        g_out[...] = grad
        w_out[...], m_out[...], a_out[...] = advance(w, grad, m, a, rate)


def update_feed(start, grads, states, rates, begun=()):
    _, units, piece = grads.shape
    block = math.gcd(start, units)
    while block > 128 and block % 16 == 0:
        block //= 2
    at = start // block
    pair = pl.BlockSpec((2, block, piece), lambda i: (0, at + i, 0))
    single = pl.BlockSpec((block, piece), lambda i: (at + i, 0))
    total = states[0].shape[1]
    return pl.pallas_call(
        functools.partial(update_kernel, rates, len(begun)),
        grid=(units // block,),
        in_specs=[pl.BlockSpec((3, block, piece), lambda i: (0, i, 0))]
        + [pair] * 3
        + [single] * 3
        + [pl.BlockSpec(memory_space=pl.ANY)] * len(begun),
        out_specs=[pair] * 4 + [single] * 4,
        out_shape=[shape((2, total, piece), full)] * 4 + [shape((total, piece), full)] * 4,
        input_output_aliases={7 + i: i for i in range(len(begun))},
        compiler_params=params(),
        cost_estimate=cost(30 * units * piece, 3 * 30 * units * piece),
        name="update_feed",
    )(grads, *states, *begun)


def body(
    inputs,
    positions,
    cotangent,
    w_attend_in,
    w_attend_out,
    w_expand,
    w_reduce,
    norm_params,
    attend_bias,
    moment_attend_in,
    moment_attend_out,
    moment_expand,
    moment_reduce,
    moment_norm,
    moment_bias,
    average_attend_in,
    average_attend_out,
    average_expand,
    average_reduce,
    average_norm,
    average_bias,
):
    batch, length, width = inputs.shape
    rows = batch * length
    units = w_expand.shape[2]
    n = lax.axis_size("dp")
    group = lax.axis_size("mp")
    me = lax.axis_index("dp").astype(jnp.int32).reshape(1)
    spot = lax.axis_index("mp").astype(jnp.int32)
    info = jnp.stack([spot & 1, (spot >> 1) & 1, (spot >> 2) & 1, me[0]])
    fast = group == 8

    expand_t = jnp.transpose(w_expand, (1, 2, 0))
    reduce_t = jnp.transpose(w_reduce)
    in_t = jnp.transpose(w_attend_in, (1, 0, 2))
    cut = units // 2 // 16 * 16
    shards = [
        jnp.concatenate([expand_t[:, a:b], reduce_t[None, a:b]], axis=0).astype(low)
        for a, b in ((0, cut), (cut, units))
    ]
    attend_shard = jnp.concatenate([in_t, w_attend_out[None]], axis=0).astype(low)
    attend_pieces = [lax.all_gather(attend_shard, "dp")]
    first_shard, _ = lax.optimization_barrier((shards[0], attend_shard))
    first_pieces = [lax.all_gather(first_shard, "dp")]

    tokens = inputs.reshape(rows, width)
    cot = cotangent.reshape(rows, width)
    hidden = layer_norm(tokens, norm_params)

    half = ROT // 2
    lane = jnp.arange(128, dtype=jnp.int32) % HD
    frequency = 10000.0 ** (-((lane % half).astype(full) * 2.0 / ROT))
    angles = positions.reshape(rows).astype(full)[:, None] * frequency[None, :]
    cosine = jnp.where(lane < ROT, jnp.cos(angles), 1.0)
    sine = jnp.where(lane < half, -jnp.sin(angles), jnp.where(lane < ROT, jnp.sin(angles), 0.0))

    q, k, v, o, w_attend = project(n, me, attend_pieces, hidden, cot, cosine, sine, attend_bias)
    context, mixed_grad, bias_part = attend(batch, q, k, v, o, cosine, sine)
    *attend_slots, edge = attend_grads(n, me, hidden, cot, mixed_grad, context)
    hid_early, out_early = heads_parts(context, mixed_grad, w_attend)
    last_shard, first_piece, attend_slots, edge, hid_early, out_early = lax.optimization_barrier(
        (shards[1], first_pieces[0], attend_slots, edge, hid_early, out_early)
    )

    rights, lefts = [last_shard], [last_shard]
    came = (None, None)
    for k in range(1, n):
        right, left = gather_hop(k, rights[-1], lefts[-1], me[0])
        if k > 1:
            if k == 2:
                load = (after(edge, (rights[-1], lefts[-1])),) * 2
            else:
                load = scatter_load(k - 1, attend_slots, *came)
            coming = scatter_hop(k - 1, *load)
        meanwhile = ()
        if k == 1:
            active, gates_grad, w_feed = meanwhile = feed_chunk(n, me, [first_piece], hidden, cot)
        elif k == 2:
            hid_early, out_early = meanwhile = early_parts(
                active, gates_grad, w_feed, hid_early, out_early
            )
        elif k == 3:
            first_grads = meanwhile = feed_grads(n, hidden, cot, active, gates_grad)
        if k > 1:
            (right, left), came = after(((right, left), coming), meanwhile)
        else:
            right, left = after((right, left), meanwhile)
        rights.append(right)
        lefts.append(left)
    last_pieces = [last_shard] + rights[1:] + lefts[1:]

    def scatter(grads):
        return lax.psum_scatter(grads, "dp", scatter_dimension=0, tiled=False)

    first_grads = scatter(first_grads).reshape(3, cut, -1)

    total_tokens = rows * n

    def update_attend(came):
        grad = attend_slots[0] + came[0].astype(full) + came[1].astype(full)
        grad_in, grad_out = jnp.transpose(grad[:3], (1, 0, 2)), grad[3]
        rate_in = 0.5 / math.sqrt(width * total_tokens)
        rate_out = 1.8 / math.sqrt(width * batch * n)
        new_in = advance(w_attend_in, grad_in, moment_attend_in, average_attend_in, rate_in)
        new_out = advance(w_attend_out, grad_out, moment_attend_out, average_attend_out, rate_out)
        return (grad_in, grad_out) + new_in + new_out

    rates = (1.6 / math.sqrt(width * total_tokens), 0.77 / math.sqrt(FF * total_tokens))
    states = [jnp.transpose(a, (1, 2, 0)) for a in (w_expand, moment_expand, average_expand)]
    states += [jnp.transpose(a) for a in (w_reduce, moment_reduce, average_reduce)]

    if fast:
        s = rows // 16

        def swap_cores(parts):
            came = {i: swap(parts[i], 1) for i in (1, 3, 0, 2)}
            return [came[i] for i in range(4)]

        def sum_cores(own, came):
            own = [a.astype(full) + b.astype(full) for a, b in zip(own, came)]
            return own, (own[1].astype(low), own[3].astype(low))

        def sum_first(own, came):
            first = own[0] + came[0].astype(full)
            second = own[2] + came[1].astype(full)
            near = [first[:s].astype(low), second[:s].astype(low)]
            return near, (first[s:].astype(low), second[s:].astype(low))

        def both_ways(pair, masks):
            return [swap(pair[0], masks[0]), swap(pair[1], masks[1])]

        def join(one, first, second, third):
            pieces = (one, first, second, third)
            return pack_rows(info, [p[0] for p in pieces] + [p[1] for p in pieces])

        *parts, active, both, w_last = out_last(n, info, True, last_pieces, hidden, out_early)
        own_out, load_out = sum_cores(parts[4:], swap_cores(parts[:4]))
        one_out = both_ways(load_out, (2, 4))
        *parts, gates_grad = hid_last(info, True, w_last, after(both, load_out), cot, hid_early)
        came_hid = swap_cores(parts[:4])
        near_out, load_out = sum_first(own_out, after(one_out, parts[0]))
        two_out = both_ways(load_out, (4, 2))
        own_hid, load_hid = sum_cores(parts[4:], after(came_hid, load_out))
        one_hid = both_ways(load_hid, (2, 4))
        last_grads = feed_grads(n, hidden, cot, after(active, load_hid), gates_grad)
        two_out = after(two_out, last_grads)
        add = add_rows(info, tokens, near_out, two_out)
        last_grads = scatter(last_grads).reshape(3, units - cut, -1)
        out_one = both_ways(add, (4, 2))
        out_two = both_ways(add, (2, 4))
        near_hid, load_hid = sum_first(own_hid, after(one_hid, add))
        two_hid = both_ways(load_hid, (4, 2))
        back = back_rows(info, tokens, near_hid, two_hid, norm_params)
        hid_one = both_ways(back, (4, 2))
        hid_two = both_ways(back, (2, 4))
        out_one, out_two = after((out_one, out_two), back)
        out_three = both_ways(out_one, (2, 4))
        begun = update_feed(0, after(first_grads, out_one), states, rates)
        hid_one, hid_two = after((hid_one, hid_two), begun)
        hid_three = both_ways(hid_one, (2, 4))
        out_three = after(out_three, hid_one)
        mine_out = join(add, out_one, out_two, out_three)
        other_out = swap(mine_out, 1)
        load = scatter_load(n - 1, after(attend_slots, mine_out), *came)
        came = scatter_hop(n - 1, *load)
        output = finish_rows(info, rows, 0, after(mine_out, load))
        output = finish_rows(info, rows, 1, after(other_out, output), begun=output)
        done = update_feed(cut, after(last_grads, output), states, rates, begun)
        attend_new = update_attend(after(came, done))
        hid_three = after(hid_three, attend_new)
        mine_hid = join(back, hid_one, hid_two, hid_three)
        other_hid = swap(mine_hid, 1)
        input_grad = finish_rows(info, rows, 0, mine_hid, cot)
        other_hid = after(other_hid, input_grad)
        norm_part = tail_sums(mine_hid, other_hid)
        sums = small_sum(join_sums(norm_part, bias_part), "dp")
        input_grad = finish_rows(info, rows, 1, after(other_hid, norm_part), cot, input_grad)
        norm_grad, bias_grad = split_sums(sums, norm_part, bias_part)
    else:
        out_part, active, both, w_last = out_last(n, info, False, last_pieces, hidden, out_early)
        hid_part, gates_grad = hid_last(info, False, w_last, both, cot, hid_early)
        came = scatter_hop(n - 1, *scatter_load(n - 1, attend_slots, *came))
        attend_new = update_attend(came)
        last_grads = scatter(feed_grads(n, hidden, cot, active, gates_grad)).reshape(3, units - cut, -1)
        hidden_grad = lax.psum(hid_part, "mp").astype(full)
        summed = lax.psum(out_part, "mp").astype(full)
        values = tokens.astype(full)
        output = (values + summed).astype(low)
        centred = values - jnp.mean(values, axis=-1, keepdims=True)
        inv = lax.rsqrt(jnp.mean(centred * centred, axis=-1, keepdims=True) + epsilon)
        normal = centred * inv
        scaled = hidden_grad * norm_params[0]
        back = inv * (
            scaled
            - jnp.mean(scaled, axis=-1, keepdims=True)
            - normal * jnp.mean(scaled * normal, axis=-1, keepdims=True)
        )
        input_grad = cot.astype(full) + back
        norm_part = jnp.stack([jnp.sum(hidden_grad * normal, axis=0), jnp.sum(hidden_grad, axis=0)])
        sums = small_sum(join_sums(norm_part, bias_part), "dp")
        norm_grad, bias_grad = split_sums(sums, norm_part, bias_part)
        begun = update_feed(0, first_grads, states, rates)
        done = update_feed(cut, last_grads, states, rates, begun)
    grad_in, grad_out = attend_new[:2]
    new_in, moment_in_new, average_in_new = attend_new[2:5]
    new_out, moment_out_new, average_out_new = attend_new[5:]
    grad_expand, new_expand, moment_expand_new, average_expand_new = (
        jnp.transpose(a, (2, 0, 1)) for a in done[:4]
    )
    grad_reduce, new_reduce, moment_reduce_new, average_reduce_new = (
        jnp.transpose(a) for a in done[4:]
    )
    input_grad = input_grad.reshape(batch, length, width)
    output = output.reshape(batch, length, width)
    new_norm, moment_norm_new, average_norm_new = advance(
        norm_params, norm_grad, moment_norm, average_norm, 0.06 / math.sqrt(total_tokens)
    )
    new_bias, moment_bias_new, average_bias_new = advance(
        attend_bias, bias_grad, moment_bias, average_bias, 0.25 / math.sqrt(total_tokens)
    )
    return (
        output,
        input_grad,
        grad_in,
        grad_out,
        grad_expand,
        grad_reduce,
        norm_grad,
        bias_grad,
        new_in,
        new_out,
        new_expand,
        new_reduce,
        new_norm,
        new_bias,
        moment_in_new,
        moment_out_new,
        moment_expand_new,
        moment_reduce_new,
        moment_norm_new,
        moment_bias_new,
        average_in_new,
        average_out_new,
        average_expand_new,
        average_reduce_new,
        average_norm_new,
        average_bias_new,
    )


def solution(mesh):
    rows3 = P("dp", None, None)
    in3 = P("dp", None, "mp")
    in2 = P("dp", "mp")
    bias = P(None, "mp")
    states = (in3, in2, in3, in2, P(), bias)
    return jax.shard_map(
        body,
        mesh=mesh,
        in_specs=(rows3, P("dp", None), rows3) + states * 3,
        out_specs=(rows3, rows3) + states * 4,
        check_vma=False,
    )
```

```python
import functools
import math

import jax
import jax.numpy as jnp
from jax import lax
from jax.experimental import pallas as pl
from jax.experimental.pallas import tpu as pltpu
from jax.sharding import PartitionSpec as P

HD = 64
ROT = 16
FF = 5632

epsilon = 1e-05
decay_moment = 0.9
decay_average = 0.9
masked_score = -1e30

low = jnp.bfloat16
full = jnp.float32
vmem_limit = 60 << 20
tail_rows = 16


def dot_nt(left, right):
    return lax.dot_general(left, right, (((1,), (1,)), ((), ())), preferred_element_type=full)


def dot_nn(left, right):
    return lax.dot_general(left, right, (((1,), (0,)), ((), ())), preferred_element_type=full)


def dot_tn(left, right):
    return lax.dot_general(left, right, (((0,), (0,)), ((), ())), preferred_element_type=full)


def params(**more):
    return pltpu.CompilerParams(vmem_limit_bytes=vmem_limit, **more)


def cost(flops, moved, trans=0):
    return pl.CostEstimate(flops=int(flops), bytes_accessed=int(moved), transcendentals=int(trans))


def shape(dims, kind):
    return jax.ShapeDtypeStruct(dims, kind)


def advance(weight, grad, moment, average, rate):
    moment_new = decay_moment * moment + grad
    weight_new = weight - rate * (grad + decay_moment * moment_new)
    average_new = decay_average * average + (1.0 - decay_average) * weight_new
    return (weight_new, moment_new, average_new)


def after(value, *others):
    return lax.optimization_barrier((value, others))[0]


def swap(value, mask, axis="mp"):
    n = lax.axis_size(axis)
    return lax.ppermute(value, axis, [(a, a ^ mask) for a in range(n)])


def small_sum(value, axis):
    n = lax.axis_size(axis)
    if n & (n - 1):
        return lax.psum(value, axis)
    mask = 1
    while mask < n:
        value = value + swap(value, mask, axis)
        mask *= 2
    return value


def join_sums(norm_part, bias_part):
    cols = bias_part.shape[1]
    return jnp.concatenate([norm_part.reshape(-1, cols), bias_part])


def split_sums(sums, norm_part, bias_part):
    count = sums.shape[0] - bias_part.shape[0]
    return sums[:count].reshape(norm_part.shape), sums[count:]


def norm_kernel(x_ref, p_ref, o_ref):
    x = x_ref[...].astype(full)
    centred = x - jnp.mean(x, axis=-1, keepdims=True)
    inv = lax.rsqrt(jnp.mean(centred * centred, axis=-1, keepdims=True) + epsilon)
    o_ref[...] = (centred * inv * p_ref[0:1] + p_ref[1:2]).astype(low)


def layer_norm(rows, norm_params):
    count, width = rows.shape
    block = min(256, count)
    return pl.pallas_call(
        norm_kernel,
        grid=(count // block,),
        in_specs=[
            pl.BlockSpec((block, width), lambda i: (i, 0)),
            pl.BlockSpec((2, width), lambda i: (0, 0)),
        ],
        out_specs=pl.BlockSpec((block, width), lambda i: (i, 0)),
        out_shape=shape((count, width), low),
        compiler_params=params(),
        cost_estimate=cost(8 * count * width, 4 * count * width),
        name="layer_norm",
    )(rows, norm_params)


def fetch(gathered, target_of, sems):
    copies = [
        pltpu.make_async_copy(gathered.at[j], target_of(j), sems.at[j]) for j in range(gathered.shape[0])
    ]
    for copy in copies:
        copy.start()
    for copy in copies:
        copy.wait()


def swish_of(both):
    units = both.shape[0] // 2
    gate, upper = both[:units], both[units:]
    sigmoid = jax.nn.sigmoid(gate)
    return gate, upper, sigmoid, gate * sigmoid


def join_gates(w_ref):
    return w_ref[0:2].reshape(2 * w_ref.shape[1], w_ref.shape[2])


def gates_grad_of(both, active_grad):
    gate, upper, sigmoid, swish = swish_of(both)
    gate_grad = active_grad * upper * sigmoid * (1.0 + gate * (1.0 - sigmoid))
    return jnp.concatenate([gate_grad, active_grad * swish], axis=0).astype(low)


def gates_of(w_ref, h, c):
    both = dot_nt(join_gates(w_ref), h)
    _, upper, _, swish = swish_of(both)
    return (swish * upper).astype(low), gates_grad_of(both, dot_nt(w_ref[2], c))


def add_grads(acc, step, active, gates_grad, h, c):
    units = active.shape[0]

    @pl.when(step == 0)
    def _():
        acc[: 2 * units] = dot_nn(gates_grad, h)
        acc[2 * units :] = dot_nn(active, c)

    @pl.when(step > 0)
    def _():
        acc[: 2 * units] += dot_nn(gates_grad, h)
        acc[2 * units :] += dot_nn(active, c)


def store_grads(n, acc, out_ref):
    piece = out_ref.shape[2]
    for j in range(n):
        out_ref[j] = acc[:, j * piece : (j + 1) * piece].astype(low)


def wide_target(w_ref, piece):
    return lambda index: w_ref.at[:, :, pl.ds(index * piece, piece)]


def feed_kernel(shards_ref, h_ref, c_ref, act_ref, grad_ref, w_ref, sems):
    @pl.when(pl.program_id(0) == 0)
    def _():
        fetch(shards_ref, wide_target(w_ref, shards_ref.shape[3]), sems)

    act_ref[...], grad_ref[...] = gates_of(w_ref, h_ref[...], c_ref[...])


def feed_chunk(shards, hidden, cot):
    rows, width = hidden.shape
    n, _, units, _ = shards.shape
    block = min(512, rows)
    row_spec = pl.BlockSpec((block, width), lambda i: (i, 0))
    return pl.pallas_call(
        feed_kernel,
        grid=(rows // block,),
        in_specs=[pl.BlockSpec(memory_space=pl.ANY), row_spec, row_spec],
        out_specs=[
            pl.BlockSpec((units, block), lambda i: (0, i)),
            pl.BlockSpec((2 * units, block), lambda i: (0, i)),
            pl.BlockSpec((3, units, width), lambda i: (0, 0, 0)),
        ],
        out_shape=[
            shape((units, rows), low),
            shape((2 * units, rows), low),
            shape((3, units, width), low),
        ],
        scratch_shapes=[pltpu.SemaphoreType.DMA((n,))],
        compiler_params=params(),
        cost_estimate=cost(
            6 * rows * width * units, 4 * rows * width + 12 * units * width, rows * units
        ),
        name="feed_chunk",
    )(shards, hidden, cot)


def put_part(split, info_ref, parts, value):
    if not split:
        parts[0][...] = value.astype(low)
        return
    step = pl.program_id(0)
    sub = value.shape[0] // 4
    high = jnp.where(step % 2 == 0, info_ref[1], info_ref[2])
    small = jnp.where(step % 2 == 0, info_ref[2], info_ref[1])
    first, second = value[: 2 * sub], value[2 * sub :]
    near = jnp.where(high == 0, first, second).astype(low)
    far = jnp.where(high == 0, second, first).astype(low)
    for at in range(4):

        @pl.when(step == at)
        def _(at=at):
            for ref, pair in ((parts[2 * at], near), (parts[2 * at + 1], far)):
                for i in range(2):
                    place = pl.ds(pl.multiple_of((i ^ small) * sub, sub), sub)
                    ref[place, :] = pair[i * sub : (i + 1) * sub]


def last_blocks(split, rows, width):
    if split:
        block, steps = rows // 4, 4
        place = lambda i, m: (m[0] ^ (1 - i // 2)) * 2 + i % 2
        part_specs = [pl.BlockSpec((block // 2, width), lambda i, m: (0, 0))] * 8
        part_shapes = [shape((block // 2, width), low)] * 8
    else:
        block = min(256, rows)
        steps = rows // block
        place = lambda i, m: i
        part_specs = [pl.BlockSpec((block, width), lambda i, m: (i, 0))]
        part_shapes = [shape((rows, width), low)]
    return block, steps, place, part_specs, part_shapes


def out_last_kernel(split, info_ref, shards_ref, h_ref, early_ref, *refs):
    parts = refs[:-4]
    act_ref, both_ref, w_ref, sems = refs[-4:]

    @pl.when(pl.program_id(0) == 0)
    def _():
        fetch(shards_ref, wide_target(w_ref, shards_ref.shape[3]), sems)

    both = dot_nt(join_gates(w_ref), h_ref[...])
    both_ref[...] = both
    _, upper, _, swish = swish_of(both)
    active = (swish * upper).astype(low)
    act_ref[...] = active
    put_part(split, info_ref, parts, early_ref[...].astype(full) + dot_tn(active, w_ref[2]))


def out_last(info, split, shards, hidden, early):
    rows, width = hidden.shape
    n, _, units, _ = shards.shape
    block, steps, place, part_specs, part_shapes = last_blocks(split, rows, width)
    row_spec = pl.BlockSpec((block, width), lambda i, m: (place(i, m), 0))
    return pl.pallas_call(
        functools.partial(out_last_kernel, split),
        grid_spec=pltpu.PrefetchScalarGridSpec(
            num_scalar_prefetch=1,
            grid=(steps,),
            in_specs=[pl.BlockSpec(memory_space=pl.ANY)] + [row_spec] * 2,
            out_specs=part_specs
            + [
                pl.BlockSpec((units, block), lambda i, m: (0, place(i, m))),
                pl.BlockSpec((2 * units, block), lambda i, m: (0, place(i, m))),
                pl.BlockSpec((3, units, width), lambda i, m: (0, 0, 0)),
            ],
            scratch_shapes=[pltpu.SemaphoreType.DMA((n,))],
        ),
        out_shape=part_shapes
        + [shape((units, rows), low), shape((2 * units, rows), full), shape((3, units, width), low)],
        compiler_params=params(),
        cost_estimate=cost(6 * rows * width * units, 8 * rows * width, rows * units),
        name="out_last",
    )(info, shards, hidden, early)


def hid_last_kernel(split, info_ref, w_ref, both_ref, c_ref, early_ref, *refs):
    grad_ref = refs[-1]
    gates_grad = gates_grad_of(both_ref[...], dot_nt(w_ref[2], c_ref[...]))
    grad_ref[...] = gates_grad
    hid = early_ref[...].astype(full) + dot_tn(gates_grad, join_gates(w_ref))
    put_part(split, info_ref, refs[:-1], hid)


def hid_last(info, split, weights, both, cot, early):
    rows, width = cot.shape
    units = weights.shape[1]
    block, steps, place, part_specs, part_shapes = last_blocks(split, rows, width)
    row_spec = pl.BlockSpec((block, width), lambda i, m: (place(i, m), 0))
    both_spec = pl.BlockSpec((2 * units, block), lambda i, m: (0, place(i, m)))
    return pl.pallas_call(
        functools.partial(hid_last_kernel, split),
        grid_spec=pltpu.PrefetchScalarGridSpec(
            num_scalar_prefetch=1,
            grid=(steps,),
            in_specs=[pl.BlockSpec((3, units, width), lambda i, m: (0, 0, 0)), both_spec]
            + [row_spec] * 2,
            out_specs=part_specs + [both_spec],
        ),
        out_shape=part_shapes + [shape((2 * units, rows), low)],
        compiler_params=params(),
        cost_estimate=cost(6 * rows * width * units, 8 * rows * width, rows * units),
        name="hid_last",
    )(info, weights, both, cot, early)


def feed_grads_kernel(n, steps, h_ref, c_ref, act_ref, grad_ref, out_ref, acc):
    step = pl.program_id(0)
    add_grads(acc, step, act_ref[...], grad_ref[...], h_ref[...], c_ref[...])

    @pl.when(step == steps - 1)
    def _():
        store_grads(n, acc, out_ref)


def feed_grads(n, hidden, cot, active, gates_grad):
    rows, width = hidden.shape
    units = active.shape[0]
    piece = width // n
    block = min(512, rows)
    steps = rows // block
    row_spec = pl.BlockSpec((block, width), lambda i: (i, 0))
    return pl.pallas_call(
        functools.partial(feed_grads_kernel, n, steps),
        grid=(steps,),
        in_specs=[
            row_spec,
            row_spec,
            pl.BlockSpec((units, block), lambda i: (0, i)),
            pl.BlockSpec((2 * units, block), lambda i: (0, i)),
        ],
        out_specs=pl.BlockSpec((n, 3 * units, piece), lambda i: (0, 0, 0)),
        out_shape=shape((n, 3 * units, piece), low),
        scratch_shapes=[pltpu.VMEM((3 * units, width), full)],
        compiler_params=params(),
        cost_estimate=cost(6 * rows * width * units, 4 * rows * width + 12 * units * width),
        name="feed_grads",
    )(hidden, cot, active, gates_grad)


def turn(values, cosine, sine, half):
    cols = values.shape[1]
    lane = lax.broadcasted_iota(jnp.int32, (1, cols), 1) % HD
    other = jnp.where(
        lane < half, pltpu.roll(values, cols - half, 1), pltpu.roll(values, half, 1)
    )
    repeat = cols // cosine.shape[1]
    if repeat > 1:
        cosine = jnp.concatenate([cosine] * repeat, axis=1)
        sine = jnp.concatenate([sine] * repeat, axis=1)
    return values * cosine + other * sine


def project_kernel(shards_ref, h_ref, c_ref, cos_ref, sin_ref, bias_ref, q_ref, k_ref, v_ref, o_ref, w_ref, sems):
    piece = shards_ref.shape[2]

    @pl.when(pl.program_id(0) == 0)
    def _():
        fetch(shards_ref, lambda index: w_ref.at[:, pl.ds(index * piece, piece), :], sems)

    h = h_ref[...]
    cosine, sine = cos_ref[...], sin_ref[...]
    half = ROT // 2
    q_ref[...] = turn(dot_nn(h, w_ref[0]) + bias_ref[0:1], cosine, sine, half).astype(low)
    k_ref[...] = turn(dot_nn(h, w_ref[1]) + bias_ref[1:2], cosine, sine, half).astype(low)
    v_ref[...] = (dot_nn(h, w_ref[2]) + bias_ref[2:3]).astype(low)
    o_ref[...] = dot_nn(c_ref[...], w_ref[3]).astype(low)


def project(shards, hidden, cot, cosine, sine, bias):
    rows, width = hidden.shape
    n, _, _, cols = shards.shape
    block = min(512, rows)
    row_spec = pl.BlockSpec((block, width), lambda i: (i, 0))
    angle_spec = pl.BlockSpec((block, 128), lambda i: (i, 0))
    out_spec = pl.BlockSpec((block, cols), lambda i: (i, 0))
    return pl.pallas_call(
        project_kernel,
        grid=(rows // block,),
        in_specs=[pl.BlockSpec(memory_space=pl.ANY), row_spec, row_spec, angle_spec, angle_spec]
        + [pl.BlockSpec((3, cols), lambda i: (0, 0))],
        out_specs=[out_spec] * 4 + [pl.BlockSpec((4, width, cols), lambda i: (0, 0, 0))],
        out_shape=[shape((rows, cols), low)] * 4 + [shape((4, width, cols), low)],
        scratch_shapes=[pltpu.SemaphoreType.DMA((n,))],
        compiler_params=params(),
        cost_estimate=cost(8 * rows * width * cols, 4 * rows * width + 16 * width * cols),
        name="project",
    )(shards, hidden, cot, cosine, sine, bias)


def attend_kernel(block, q_ref, k_ref, v_ref, o_ref, cos_ref, sin_ref, ctx_ref, mg_ref, bias_ref, dq, dk, dv):
    length, lanes = q_ref.shape
    scale = HD ** (-0.5)
    for head in range(lanes // HD):
        cols = slice(head * HD, (head + 1) * HD)
        for i in range(length // block):
            rows = slice(i * block, (i + 1) * block)
            end = (i + 1) * block
            q = q_ref[rows, cols]
            o = o_ref[rows, cols]
            k = k_ref[:end, cols]
            v = v_ref[:end, cols]
            scores = dot_nt(q, k) * scale
            row = i * block + lax.broadcasted_iota(jnp.int32, (block, end), 0)
            col = lax.broadcasted_iota(jnp.int32, (block, end), 1)
            scores = jnp.where(col <= row, scores, masked_score)
            top = jnp.max(scores, axis=-1, keepdims=True)
            weights = jnp.exp(scores - top)
            probs = weights * (1.0 / jnp.sum(weights, axis=-1, keepdims=True))
            probs_low = probs.astype(low)
            ctx_ref[rows, cols] = dot_nn(probs_low, v).astype(low)
            prob_grads = dot_nt(o, v)
            middle = jnp.sum(probs * prob_grads, axis=-1, keepdims=True)
            score_grads = (probs * (prob_grads - middle)).astype(low)
            dq[rows, cols] = dot_nn(score_grads, k) * scale
            key_part = dot_tn(score_grads, q) * scale
            value_part = dot_tn(probs_low, o)
            if i == 0:
                dk[:end, cols] = key_part
                dv[:end, cols] = value_part
                if end < length:
                    dk[end:, cols] = jnp.zeros((length - end, HD), full)
                    dv[end:, cols] = jnp.zeros((length - end, HD), full)
            else:
                dk[:end, cols] += key_part
                dv[:end, cols] += value_part
    cosine, sine = cos_ref[...], -sin_ref[...]
    half = ROT // 2
    sums = []
    for part, grads in enumerate(
        (turn(dq[...], cosine, sine, half), turn(dk[...], cosine, sine, half), dv[...])
    ):
        rounded = grads.astype(low)
        mg_ref[part] = rounded
        sums.append(jnp.sum(rounded.astype(full), axis=0, keepdims=True))
    total = jnp.concatenate(sums, axis=0)

    @pl.when(pl.program_id(1) == 0)
    def _():
        bias_ref[...] = total

    @pl.when(pl.program_id(1) > 0)
    def _():
        bias_ref[...] += total


def attend(batch, q, k, v, o, cosine, sine):
    rows, cols = q.shape
    length = rows // batch
    lanes = 128
    spec = pl.BlockSpec((length, lanes), lambda p, b: (b, p))
    angle_spec = pl.BlockSpec((length, 128), lambda p, b: (b, 0))
    return pl.pallas_call(
        functools.partial(attend_kernel, min(512, length)),
        grid=(cols // lanes, batch),
        in_specs=[spec] * 4 + [angle_spec] * 2,
        out_specs=[
            spec,
            pl.BlockSpec((3, length, lanes), lambda p, b: (0, b, p)),
            pl.BlockSpec((3, lanes), lambda p, b: (0, p)),
        ],
        out_shape=[
            shape((rows, cols), low),
            shape((3, rows, cols), low),
            shape((3, cols), full),
        ],
        scratch_shapes=[pltpu.VMEM((length, lanes), full)] * 3,
        compiler_params=params(),
        cost_estimate=cost(
            40 * rows * length * cols, 20 * rows * cols, rows * length * cols // HD
        ),
        name="attend",
    )(q, k, v, o, cosine, sine)


def attend_grads_kernel(h_ref, c_ref, mg_ref, ctx_ref, out_ref, wide):
    cols = ctx_ref.shape[1]

    @pl.when(pl.program_id(0) == 0)
    def _():
        for part in range(3):
            wide[:, part * cols : (part + 1) * cols] = mg_ref[part]

    grad = dot_tn(h_ref[...], wide[...])
    for part in range(3):
        out_ref[0, part] = grad[:, part * cols : (part + 1) * cols].astype(low)
    out_ref[0, 3] = dot_tn(c_ref[...], ctx_ref[...]).astype(low)


def attend_grads(n, hidden, cot, mixed_grad, context):
    rows, width = hidden.shape
    cols = context.shape[1]
    piece = width // n
    cut_spec = pl.BlockSpec((rows, piece), lambda i: (0, i))
    return pl.pallas_call(
        attend_grads_kernel,
        grid=(n,),
        in_specs=[
            cut_spec,
            cut_spec,
            pl.BlockSpec((3, rows, cols), lambda i: (0, 0, 0)),
            pl.BlockSpec((rows, cols), lambda i: (0, 0)),
        ],
        out_specs=pl.BlockSpec((1, 4, piece, cols), lambda i: (i, 0, 0, 0)),
        out_shape=shape((n, 4, piece, cols), low),
        scratch_shapes=[pltpu.VMEM((rows, 3 * cols), low)],
        compiler_params=params(),
        cost_estimate=cost(8 * rows * width * cols, 4 * rows * width + 16 * width * cols),
        name="attend_grads",
    )(hidden, cot, mixed_grad, context)


def heads_kernel(ctx_ref, mg_ref, wa_ref, hid_ref, out_ref):
    hid = dot_nt(mg_ref[0], wa_ref[0]) + dot_nt(mg_ref[1], wa_ref[1]) + dot_nt(mg_ref[2], wa_ref[2])
    hid_ref[...] = hid.astype(low)
    out_ref[...] = dot_nt(ctx_ref[...], wa_ref[3]).astype(low)


def heads_parts(context, mixed_grad, w_attend):
    rows, cols = context.shape
    width = w_attend.shape[1]
    block = min(256, rows)
    out_spec = pl.BlockSpec((block, width), lambda i: (i, 0))
    return pl.pallas_call(
        heads_kernel,
        grid=(rows // block,),
        in_specs=[
            pl.BlockSpec((block, cols), lambda i: (i, 0)),
            pl.BlockSpec((3, block, cols), lambda i: (0, i, 0)),
            pl.BlockSpec((4, width, cols), lambda i: (0, 0, 0)),
        ],
        out_specs=[out_spec, out_spec],
        out_shape=[shape((rows, width), low)] * 2,
        compiler_params=params(),
        cost_estimate=cost(8 * rows * width * cols, 4 * rows * width + 8 * (rows + width) * cols),
        name="heads_parts",
    )(context, mixed_grad, w_attend)


def early_kernel(act_ref, grad_ref, w_ref, hid_in_ref, out_in_ref, hid_ref, out_ref):
    hid = hid_in_ref[...].astype(full) + dot_tn(grad_ref[...], join_gates(w_ref))
    hid_ref[...] = hid.astype(low)
    out = out_in_ref[...].astype(full) + dot_tn(act_ref[...], w_ref[2])
    out_ref[...] = out.astype(low)


def early_parts(active, gates_grad, w_feed, hid, out):
    rows, width = hid.shape
    units = w_feed.shape[1]
    block = min(256, rows)
    row_spec = pl.BlockSpec((block, width), lambda i: (i, 0))
    return pl.pallas_call(
        early_kernel,
        grid=(rows // block,),
        in_specs=[
            pl.BlockSpec((units, block), lambda i: (0, i)),
            pl.BlockSpec((2 * units, block), lambda i: (0, i)),
            pl.BlockSpec((3, units, width), lambda i: (0, 0, 0)),
            row_spec,
            row_spec,
        ],
        out_specs=[row_spec, row_spec],
        out_shape=[shape((rows, width), low)] * 2,
        compiler_params=params(),
        cost_estimate=cost(6 * rows * width * units, 8 * rows * width + 6 * (rows + width) * units),
        name="early_parts",
    )(active, gates_grad, w_feed, hid, out)


def sixteenth(which, m):
    return m[0] * 8 + (m[1] * 2 + m[2] if which == 0 else 4 + m[2] * 2 + m[1])


def back_kernel(info_ref, *refs):
    p_ref = refs[6]
    total = 0.0
    for x_ref, near_ref, far_ref, back_ref in zip(refs[0:2], refs[2:4], refs[4:6], refs[7:9]):
        x = x_ref[...].astype(full)
        centred = x - jnp.mean(x, axis=-1, keepdims=True)
        inv = lax.rsqrt(jnp.mean(centred * centred, axis=-1, keepdims=True) + epsilon)
        normal = centred * inv
        grad = near_ref[...].astype(full) + far_ref[...].astype(full)
        scaled = grad * p_ref[0:1]
        back = inv * (
            scaled
            - jnp.mean(scaled, axis=-1, keepdims=True)
            - normal * jnp.mean(scaled * normal, axis=-1, keepdims=True)
        )
        back_ref[: x.shape[0]] = back.astype(low)
        total += jnp.concatenate(
            [jnp.sum(grad * normal, axis=0, keepdims=True), jnp.sum(grad, axis=0, keepdims=True)],
            axis=0,
        )
    high = total.astype(low)
    rest = total - high.astype(full)
    middle = rest.astype(low)
    small = (rest - middle.astype(full)).astype(low)
    zeros = jnp.zeros((tail_rows - 6, total.shape[1]), full)
    terms = [high.astype(full), middle.astype(full), small.astype(full), zeros]
    refs[7][refs[0].shape[0] :] = jnp.concatenate(terms, axis=0).astype(low)


def back_rows(info, rows, near, far, norm_params):
    count, width = near[0].shape
    spec = pl.BlockSpec((count, width), lambda i, m: (0, 0))
    pair = pl.BlockSpec((2, width), lambda i, m: (0, 0))
    return pl.pallas_call(
        back_kernel,
        grid_spec=pltpu.PrefetchScalarGridSpec(
            num_scalar_prefetch=1,
            grid=(1,),
            in_specs=[
                pl.BlockSpec((count, width), lambda i, m: (sixteenth(0, m), 0)),
                pl.BlockSpec((count, width), lambda i, m: (sixteenth(1, m), 0)),
            ]
            + [spec] * 4
            + [pair],
            out_specs=[pl.BlockSpec((count + tail_rows, width), lambda i, m: (0, 0)), spec],
        ),
        out_shape=[shape((count + tail_rows, width), low), shape((count, width), low)],
        compiler_params=params(),
        cost_estimate=cost(40 * count * width, 16 * count * width),
        name="back_rows",
    )(info, rows, rows, *near, *far, norm_params)


def add_kernel(info_ref, *refs):
    for x_ref, near_ref, far_ref, out_ref in zip(refs[0:2], refs[2:4], refs[4:6], refs[6:8]):
        total = x_ref[...].astype(full) + near_ref[...].astype(full) + far_ref[...].astype(full)
        out_ref[...] = total.astype(low)


def add_rows(info, rows, near, far):
    count, width = near[0].shape
    spec = pl.BlockSpec((count, width), lambda i, m: (0, 0))
    return pl.pallas_call(
        add_kernel,
        grid_spec=pltpu.PrefetchScalarGridSpec(
            num_scalar_prefetch=1,
            grid=(1,),
            in_specs=[
                pl.BlockSpec((count, width), lambda i, m: (sixteenth(0, m), 0)),
                pl.BlockSpec((count, width), lambda i, m: (sixteenth(1, m), 0)),
            ]
            + [spec] * 4,
            out_specs=[spec, spec],
        ),
        out_shape=[shape((count, width), low)] * 2,
        compiler_params=params(),
        cost_estimate=cost(4 * count * width, 16 * count * width),
        name="add_rows",
    )(info, rows, rows, *near, *far)


def pack_kernel(block, info_ref, *refs):
    pieces, out_ref, sems = refs[:8], refs[8], refs[9]
    x, y = info_ref[1], info_ref[2]
    copies = []

    def move(source, at, size):
        place = out_ref.at[pl.ds(pl.multiple_of(at, 16), size), :]
        copies.append(pltpu.make_async_copy(source, place, sems.at[len(copies)]))

    for i, piece in enumerate(pieces):
        high, small = (i // 2) % 2, i % 2
        if i < 4:
            at = (x ^ high) * 2 + (y ^ small)
        else:
            at = 4 + (y ^ high) * 2 + (x ^ small)
        extra = piece.shape[0] - block
        move(piece.at[pl.ds(0, block), :], at * block, block)
        if extra:
            move(piece.at[pl.ds(block, extra), :], 8 * block + at * extra, extra)
    for copy in copies:
        copy.start()
    for copy in copies:
        copy.wait()


def pack_rows(info, pieces):
    block, width = pieces[-1].shape
    extra = pieces[0].shape[0] - block
    return pl.pallas_call(
        functools.partial(pack_kernel, block),
        grid_spec=pltpu.PrefetchScalarGridSpec(
            num_scalar_prefetch=1,
            grid=(1,),
            in_specs=[pl.BlockSpec(piece.shape, lambda i, m: (0, 0)) for piece in pieces],
            out_specs=pl.BlockSpec(memory_space=pl.ANY),
            scratch_shapes=[pltpu.SemaphoreType.DMA((12,))],
        ),
        out_shape=shape((8 * block + 4 * extra, width), low),
        compiler_params=params(),
        cost_estimate=cost(0, 32 * block * width),
        name="pack_rows",
    )(info, *pieces)


def tail_total(ref):
    values = ref[...].astype(full)
    sums = 0.0
    for i in range(4):
        at = i * tail_rows
        sums += values[at : at + 2] + values[at + 2 : at + 4] + values[at + 4 : at + 6]
    return sums


def finish_kernel(info_ref, *refs):
    mine = (pl.program_id(0) // 4) == info_ref[0]
    own_ref, other_ref = refs[:2]
    summed = len(refs) > 3
    out_ref = refs[5] if summed else refs[2]

    def store(value):
        if summed:
            value = refs[2][...].astype(full) + value.astype(full)
        out_ref[...] = value

    @pl.when(mine)
    def _():
        store(own_ref[...])

    @pl.when(jnp.logical_not(mine))
    def _():
        store(other_ref[...])

    if summed:

        @pl.when(pl.program_id(0) == 0)
        def _():
            refs[6][...] = tail_total(refs[3]) + tail_total(refs[4])


def finish_rows(info, rows, own, other, cot=None):
    width = own.shape[1]
    block = rows // 8
    spec = pl.BlockSpec((block, width), lambda i, m: (i, 0))
    edge = lambda i: jnp.where(i < 4, 0, 3)
    ins = [own, other]
    specs = [
        pl.BlockSpec((block, width), lambda i, m: (jnp.where(i // 4 == m[0], i % 4, edge(i)), 0)),
        pl.BlockSpec((block, width), lambda i, m: (jnp.where(i // 4 == m[0], edge(i), i % 4), 0)),
    ]
    out_specs, out_shape = [spec], [shape((rows, width), low if cot is None else full)]
    if cot is not None:
        size = 4 * tail_rows
        last = own.shape[0] // size - 1
        ins += [cot, own, other]
        specs += [spec] + [pl.BlockSpec((size, width), lambda i, m: (last, 0))] * 2
        out_specs.append(pl.BlockSpec((2, width), lambda i, m: (0, 0)))
        out_shape.append(shape((2, width), full))
    return pl.pallas_call(
        finish_kernel,
        grid_spec=pltpu.PrefetchScalarGridSpec(
            num_scalar_prefetch=1,
            grid=(8,),
            in_specs=specs,
            out_specs=out_specs,
        ),
        out_shape=out_shape,
        compiler_params=params(),
        cost_estimate=cost(2 * rows * width, 8 * rows * width),
        name="finish_rows",
    )(info, *ins)


def update_kernel(rates, count, *refs):
    g_ref = refs[0]
    ins = refs[1:7]
    outs = refs[7 + count :]
    for which, rate in enumerate(rates):
        grad = g_ref[:2] if which == 0 else g_ref[2]
        grad = grad.astype(full)
        w, m, a = (ref[...] for ref in ins[3 * which : 3 * which + 3])
        g_out, w_out, m_out, a_out = outs[4 * which : 4 * which + 4]
        g_out[...] = grad
        w_out[...], m_out[...], a_out[...] = advance(w, grad, m, a, rate)


def update_feed(start, grads, states, rates, begun=()):
    _, units, piece = grads.shape
    block = math.gcd(start, units)
    while block > 128 and block % 16 == 0:
        block //= 2
    at = start // block
    pair = pl.BlockSpec((2, block, piece), lambda i: (0, at + i, 0))
    single = pl.BlockSpec((block, piece), lambda i: (at + i, 0))
    total = states[0].shape[1]
    return pl.pallas_call(
        functools.partial(update_kernel, rates, len(begun)),
        grid=(units // block,),
        in_specs=[pl.BlockSpec((3, block, piece), lambda i: (0, i, 0))]
        + [pair] * 3
        + [single] * 3
        + [pl.BlockSpec(memory_space=pl.ANY)] * len(begun),
        out_specs=[pair] * 4 + [single] * 4,
        out_shape=[shape((2, total, piece), full)] * 4 + [shape((total, piece), full)] * 4,
        input_output_aliases={7 + i: i for i in range(len(begun))},
        compiler_params=params(),
        cost_estimate=cost(30 * units * piece, 3 * 30 * units * piece),
        name="update_feed",
    )(grads, *states, *begun)


def body(
    inputs,
    positions,
    cotangent,
    w_attend_in,
    w_attend_out,
    w_expand,
    w_reduce,
    norm_params,
    attend_bias,
    moment_attend_in,
    moment_attend_out,
    moment_expand,
    moment_reduce,
    moment_norm,
    moment_bias,
    average_attend_in,
    average_attend_out,
    average_expand,
    average_reduce,
    average_norm,
    average_bias,
):
    batch, length, width = inputs.shape
    rows = batch * length
    units = w_expand.shape[2]
    n = lax.axis_size("dp")
    group = lax.axis_size("mp")
    spot = lax.axis_index("mp").astype(jnp.int32)
    info = jnp.stack([spot & 1, (spot >> 1) & 1, (spot >> 2) & 1])
    fast = group == 8

    expand_t = jnp.transpose(w_expand, (1, 2, 0))
    reduce_t = jnp.transpose(w_reduce)
    in_t = jnp.transpose(w_attend_in, (1, 0, 2))
    cut = units // 2 // 16 * 16
    shards = [
        jnp.concatenate([expand_t[:, a:b], reduce_t[None, a:b]], axis=0).astype(low)
        for a, b in ((0, cut), (cut, units))
    ]
    attend_shard = jnp.concatenate([in_t, w_attend_out[None]], axis=0).astype(low)
    attend_all = lax.all_gather(attend_shard, "dp")
    first_all = lax.all_gather(after(shards[0], attend_shard), "dp")
    last_all = lax.all_gather(after(shards[1], shards[0]), "dp")

    tokens = inputs.reshape(rows, width)
    cot = cotangent.reshape(rows, width)
    hidden = layer_norm(tokens, norm_params)

    half = ROT // 2
    lane = jnp.arange(128, dtype=jnp.int32) % HD
    frequency = 10000.0 ** (-((lane % half).astype(full) * 2.0 / ROT))
    angles = positions.reshape(rows).astype(full)[:, None] * frequency[None, :]
    cosine = jnp.where(lane < ROT, jnp.cos(angles), 1.0)
    sine = jnp.where(lane < half, -jnp.sin(angles), jnp.where(lane < ROT, jnp.sin(angles), 0.0))

    def scatter(grads):
        return lax.psum_scatter(grads, "dp", scatter_dimension=0, tiled=False)

    q, k, v, o, w_attend = project(attend_all, hidden, cot, cosine, sine, attend_bias)
    context, mixed_grad, bias_part = attend(batch, q, k, v, o, cosine, sine)
    attend_grad = attend_grads(n, hidden, cot, mixed_grad, context)
    hid_early, out_early = heads_parts(context, mixed_grad, w_attend)
    first_all = after(first_all, attend_grad, hid_early, out_early)
    active, gates_grad, w_feed = feed_chunk(first_all, hidden, cot)
    hid_early, out_early = early_parts(active, gates_grad, w_feed, hid_early, out_early)
    first_grads = feed_grads(n, hidden, cot, active, gates_grad)
    last_all = after(last_all, first_grads, hid_early, out_early)
    attend_grad = scatter(after(attend_grad, last_all))
    first_grads = scatter(after(first_grads, last_all)).reshape(3, cut, -1)

    total_tokens = rows * n

    def update_attend(grad):
        grad = grad.astype(full)
        grad_in, grad_out = jnp.transpose(grad[:3], (1, 0, 2)), grad[3]
        rate_in = 0.5 / math.sqrt(width * total_tokens)
        rate_out = 1.8 / math.sqrt(width * batch * n)
        new_in = advance(w_attend_in, grad_in, moment_attend_in, average_attend_in, rate_in)
        new_out = advance(w_attend_out, grad_out, moment_attend_out, average_attend_out, rate_out)
        return (grad_in, grad_out) + new_in + new_out

    rates = (1.6 / math.sqrt(width * total_tokens), 0.77 / math.sqrt(FF * total_tokens))
    states = [jnp.transpose(a, (1, 2, 0)) for a in (w_expand, moment_expand, average_expand)]
    states += [jnp.transpose(a) for a in (w_reduce, moment_reduce, average_reduce)]

    if fast:
        s = rows // 16

        def swap_cores(parts):
            came = {i: swap(parts[i], 1) for i in (1, 3, 0, 2)}
            return [came[i] for i in range(4)]

        def sum_cores(own, came):
            own = [a.astype(full) + b.astype(full) for a, b in zip(own, came)]
            return own, (own[1].astype(low), own[3].astype(low))

        def sum_first(own, came):
            first = own[0] + came[0].astype(full)
            second = own[2] + came[1].astype(full)
            near = [first[:s].astype(low), second[:s].astype(low)]
            return near, (first[s:].astype(low), second[s:].astype(low))

        def both_ways(pair, masks):
            return [swap(pair[0], masks[0]), swap(pair[1], masks[1])]

        def join(one, first, second, third):
            pieces = (one, first, second, third)
            return pack_rows(info, [p[0] for p in pieces] + [p[1] for p in pieces])

        *parts, active, both, w_last = out_last(info, True, last_all, hidden, out_early)
        own_out, load_out = sum_cores(parts[4:], swap_cores(parts[:4]))
        one_out = both_ways(load_out, (2, 4))
        *parts, gates_grad = hid_last(info, True, w_last, after(both, load_out), cot, hid_early)
        came_hid = swap_cores(parts[:4])
        near_out, load_out = sum_first(own_out, after(one_out, parts[0]))
        two_out = both_ways(load_out, (4, 2))
        own_hid, load_hid = sum_cores(parts[4:], after(came_hid, load_out))
        one_hid = both_ways(load_hid, (2, 4))
        last_grads = feed_grads(n, hidden, cot, after(active, load_hid), gates_grad)
        two_out = after(two_out, last_grads)
        add = add_rows(info, tokens, near_out, two_out)
        last_grads = scatter(last_grads).reshape(3, units - cut, -1)
        out_one = both_ways(add, (4, 2))
        out_two = both_ways(add, (2, 4))
        near_hid, load_hid = sum_first(own_hid, after(one_hid, add))
        two_hid = both_ways(load_hid, (4, 2))
        back = back_rows(info, tokens, near_hid, two_hid, norm_params)
        hid_one = both_ways(back, (4, 2))
        hid_two = both_ways(back, (2, 4))
        out_one, out_two = after((out_one, out_two), back)
        out_three = both_ways(out_one, (2, 4))
        attend_new = update_attend(after(attend_grad, out_one))
        hid_one, hid_two = after((hid_one, hid_two), attend_new)
        hid_three = both_ways(hid_one, (2, 4))
        begun = update_feed(0, after(first_grads, hid_one), states, rates)
        out_three = after(out_three, begun)
        mine_out = join(add, out_one, out_two, out_three)
        other_out = swap(mine_out, 1)
        hid_three = after(hid_three, other_out)
        mine_hid = join(back, hid_one, hid_two, hid_three)
        other_hid = swap(mine_hid, 1)
        (output,) = finish_rows(info, rows, after(mine_out, mine_hid), other_out)
        input_grad, norm_part = finish_rows(info, rows, mine_hid, after(other_hid, output), cot)
        sums = small_sum(join_sums(norm_part, bias_part), "dp")
        done = update_feed(cut, after(last_grads, input_grad), states, rates, begun)
        norm_grad, bias_grad = split_sums(sums, norm_part, bias_part)
    else:
        out_part, active, both, w_last = out_last(info, False, last_all, hidden, out_early)
        hid_part, gates_grad = hid_last(info, False, w_last, both, cot, hid_early)
        attend_new = update_attend(attend_grad)
        last_grads = scatter(feed_grads(n, hidden, cot, active, gates_grad)).reshape(3, units - cut, -1)
        hidden_grad = lax.psum(hid_part, "mp").astype(full)
        summed = lax.psum(out_part, "mp").astype(full)
        values = tokens.astype(full)
        output = (values + summed).astype(low)
        centred = values - jnp.mean(values, axis=-1, keepdims=True)
        inv = lax.rsqrt(jnp.mean(centred * centred, axis=-1, keepdims=True) + epsilon)
        normal = centred * inv
        scaled = hidden_grad * norm_params[0]
        back = inv * (
            scaled
            - jnp.mean(scaled, axis=-1, keepdims=True)
            - normal * jnp.mean(scaled * normal, axis=-1, keepdims=True)
        )
        input_grad = cot.astype(full) + back
        norm_part = jnp.stack([jnp.sum(hidden_grad * normal, axis=0), jnp.sum(hidden_grad, axis=0)])
        sums = small_sum(join_sums(norm_part, bias_part), "dp")
        norm_grad, bias_grad = split_sums(sums, norm_part, bias_part)
        begun = update_feed(0, first_grads, states, rates)
        done = update_feed(cut, last_grads, states, rates, begun)
    grad_in, grad_out = attend_new[:2]
    new_in, moment_in_new, average_in_new = attend_new[2:5]
    new_out, moment_out_new, average_out_new = attend_new[5:]
    grad_expand, new_expand, moment_expand_new, average_expand_new = (
        jnp.transpose(a, (2, 0, 1)) for a in done[:4]
    )
    grad_reduce, new_reduce, moment_reduce_new, average_reduce_new = (
        jnp.transpose(a) for a in done[4:]
    )
    input_grad = input_grad.reshape(batch, length, width)
    output = output.reshape(batch, length, width)
    new_norm, moment_norm_new, average_norm_new = advance(
        norm_params, norm_grad, moment_norm, average_norm, 0.06 / math.sqrt(total_tokens)
    )
    new_bias, moment_bias_new, average_bias_new = advance(
        attend_bias, bias_grad, moment_bias, average_bias, 0.25 / math.sqrt(total_tokens)
    )
    return (
        output,
        input_grad,
        grad_in,
        grad_out,
        grad_expand,
        grad_reduce,
        norm_grad,
        bias_grad,
        new_in,
        new_out,
        new_expand,
        new_reduce,
        new_norm,
        new_bias,
        moment_in_new,
        moment_out_new,
        moment_expand_new,
        moment_reduce_new,
        moment_norm_new,
        moment_bias_new,
        average_in_new,
        average_out_new,
        average_expand_new,
        average_reduce_new,
        average_norm_new,
        average_bias_new,
    )


def solution(mesh):
    rows3 = P("dp", None, None)
    in3 = P("dp", None, "mp")
    in2 = P("dp", "mp")
    bias = P(None, "mp")
    states = (in3, in2, in3, in2, P(), bias)
    return jax.shard_map(
        body,
        mesh=mesh,
        in_specs=(rows3, P("dp", None), rows3) + states * 3,
        out_specs=(rows3, rows3) + states * 4,
        check_vma=False,
    )
```

```python
import functools
import math

import jax
import jax.numpy as jnp
from jax import lax
from jax.experimental import pallas as pl
from jax.experimental.pallas import tpu as pltpu
from jax.sharding import PartitionSpec as P

HD = 64
ROT = 16
FF = 5632

epsilon = 1e-05
decay_moment = 0.9
decay_average = 0.9
masked_score = -1e30

low = jnp.bfloat16
full = jnp.float32
vmem_limit = 60 << 20
tail_rows = 16


def dot_nt(left, right):
    return lax.dot_general(left, right, (((1,), (1,)), ((), ())), preferred_element_type=full)


def dot_nn(left, right):
    return lax.dot_general(left, right, (((1,), (0,)), ((), ())), preferred_element_type=full)


def dot_tn(left, right):
    return lax.dot_general(left, right, (((0,), (0,)), ((), ())), preferred_element_type=full)


def params(**more):
    return pltpu.CompilerParams(vmem_limit_bytes=vmem_limit, **more)


def cost(flops, moved, trans=0):
    return pl.CostEstimate(flops=int(flops), bytes_accessed=int(moved), transcendentals=int(trans))


def shape(dims, kind):
    return jax.ShapeDtypeStruct(dims, kind)


def advance(weight, grad, moment, average, rate):
    moment_new = decay_moment * moment + grad
    weight_new = weight - rate * (grad + decay_moment * moment_new)
    average_new = decay_average * average + (1.0 - decay_average) * weight_new
    return (weight_new, moment_new, average_new)


def after(value, *others):
    return lax.optimization_barrier((value, others))[0]


def swap(value, mask, axis="mp"):
    n = lax.axis_size(axis)
    return lax.ppermute(value, axis, [(a, a ^ mask) for a in range(n)])


def small_sum(value, axis):
    n = lax.axis_size(axis)
    if n & (n - 1):
        return lax.psum(value, axis)
    mask = 1
    while mask < n:
        value = value + swap(value, mask, axis)
        mask *= 2
    return value


def join_sums(norm_part, bias_part):
    cols = bias_part.shape[1]
    return jnp.concatenate([norm_part.reshape(-1, cols), bias_part])


def split_sums(sums, norm_part, bias_part):
    count = sums.shape[0] - bias_part.shape[0]
    return sums[:count].reshape(norm_part.shape), sums[count:]


def norm_kernel(x_ref, p_ref, o_ref):
    x = x_ref[...].astype(full)
    centred = x - jnp.mean(x, axis=-1, keepdims=True)
    inv = lax.rsqrt(jnp.mean(centred * centred, axis=-1, keepdims=True) + epsilon)
    o_ref[...] = (centred * inv * p_ref[0:1] + p_ref[1:2]).astype(low)


def layer_norm(rows, norm_params):
    count, width = rows.shape
    block = min(256, count)
    return pl.pallas_call(
        norm_kernel,
        grid=(count // block,),
        in_specs=[
            pl.BlockSpec((block, width), lambda i: (i, 0)),
            pl.BlockSpec((2, width), lambda i: (0, 0)),
        ],
        out_specs=pl.BlockSpec((block, width), lambda i: (i, 0)),
        out_shape=shape((count, width), low),
        compiler_params=params(),
        cost_estimate=cost(8 * count * width, 4 * count * width),
        name="layer_norm",
    )(rows, norm_params)


def fetch(gathered, target_of, sems):
    copies = [
        pltpu.make_async_copy(gathered.at[j], target_of(j), sems.at[j]) for j in range(gathered.shape[0])
    ]
    for copy in copies:
        copy.start()
    for copy in copies:
        copy.wait()


def swish_of(both):
    units = both.shape[0] // 2
    gate, upper = both[:units], both[units:]
    sigmoid = jax.nn.sigmoid(gate)
    return gate, upper, sigmoid, gate * sigmoid


def join_gates(w_ref):
    return w_ref[0:2].reshape(2 * w_ref.shape[1], w_ref.shape[2])


def gates_grad_of(both, active_grad):
    gate, upper, sigmoid, swish = swish_of(both)
    gate_grad = active_grad * upper * sigmoid * (1.0 + gate * (1.0 - sigmoid))
    return jnp.concatenate([gate_grad, active_grad * swish], axis=0).astype(low)


def gates_of(w_ref, h, c):
    both = dot_nt(join_gates(w_ref), h)
    _, upper, _, swish = swish_of(both)
    return (swish * upper).astype(low), gates_grad_of(both, dot_nt(w_ref[2], c))


def add_grads(acc, step, active, gates_grad, h, c):
    units = active.shape[0]

    @pl.when(step == 0)
    def _():
        acc[: 2 * units] = dot_nn(gates_grad, h)
        acc[2 * units :] = dot_nn(active, c)

    @pl.when(step > 0)
    def _():
        acc[: 2 * units] += dot_nn(gates_grad, h)
        acc[2 * units :] += dot_nn(active, c)


def store_grads(n, acc, out_ref):
    piece = out_ref.shape[2]
    for j in range(n):
        out_ref[j] = acc[:, j * piece : (j + 1) * piece].astype(low)


def wide_target(w_ref, piece):
    return lambda index: w_ref.at[:, :, pl.ds(index * piece, piece)]


def feed_kernel(shards_ref, h_ref, c_ref, act_ref, grad_ref, w_ref, sems):
    @pl.when(pl.program_id(0) == 0)
    def _():
        fetch(shards_ref, wide_target(w_ref, shards_ref.shape[3]), sems)

    act_ref[...], grad_ref[...] = gates_of(w_ref, h_ref[...], c_ref[...])


def feed_chunk(shards, hidden, cot):
    rows, width = hidden.shape
    n, _, units, _ = shards.shape
    block = min(512, rows)
    row_spec = pl.BlockSpec((block, width), lambda i: (i, 0))
    return pl.pallas_call(
        feed_kernel,
        grid=(rows // block,),
        in_specs=[pl.BlockSpec(memory_space=pl.ANY), row_spec, row_spec],
        out_specs=[
            pl.BlockSpec((units, block), lambda i: (0, i)),
            pl.BlockSpec((2 * units, block), lambda i: (0, i)),
            pl.BlockSpec((3, units, width), lambda i: (0, 0, 0)),
        ],
        out_shape=[
            shape((units, rows), low),
            shape((2 * units, rows), low),
            shape((3, units, width), low),
        ],
        scratch_shapes=[pltpu.SemaphoreType.DMA((n,))],
        compiler_params=params(),
        cost_estimate=cost(
            6 * rows * width * units, 4 * rows * width + 12 * units * width, rows * units
        ),
        name="feed_chunk",
    )(shards, hidden, cot)


def put_part(split, info_ref, parts, value):
    if not split:
        parts[0][...] = value.astype(low)
        return
    step = pl.program_id(0)
    sub = value.shape[0] // 4
    high = jnp.where(step % 2 == 0, info_ref[1], info_ref[2])
    small = jnp.where(step % 2 == 0, info_ref[2], info_ref[1])
    first, second = value[: 2 * sub], value[2 * sub :]
    near = jnp.where(high == 0, first, second).astype(low)
    far = jnp.where(high == 0, second, first).astype(low)
    for at in range(4):

        @pl.when(step == at)
        def _(at=at):
            for ref, pair in ((parts[2 * at], near), (parts[2 * at + 1], far)):
                for i in range(2):
                    place = pl.ds(pl.multiple_of((i ^ small) * sub, sub), sub)
                    ref[place, :] = pair[i * sub : (i + 1) * sub]


def last_blocks(split, rows, width):
    if split:
        block, steps = rows // 4, 4
        place = lambda i, m: (m[0] ^ (1 - i // 2)) * 2 + i % 2
        part_specs = [pl.BlockSpec((block // 2, width), lambda i, m: (0, 0))] * 8
        part_shapes = [shape((block // 2, width), low)] * 8
    else:
        block = min(256, rows)
        steps = rows // block
        place = lambda i, m: i
        part_specs = [pl.BlockSpec((block, width), lambda i, m: (i, 0))]
        part_shapes = [shape((rows, width), low)]
    return block, steps, place, part_specs, part_shapes


def out_last_kernel(split, info_ref, shards_ref, h_ref, early_ref, *refs):
    parts = refs[:-4]
    act_ref, both_ref, w_ref, sems = refs[-4:]

    @pl.when(pl.program_id(0) == 0)
    def _():
        fetch(shards_ref, wide_target(w_ref, shards_ref.shape[3]), sems)

    both = dot_nt(join_gates(w_ref), h_ref[...])
    both_ref[...] = both
    _, upper, _, swish = swish_of(both)
    active = (swish * upper).astype(low)
    act_ref[...] = active
    put_part(split, info_ref, parts, early_ref[...].astype(full) + dot_tn(active, w_ref[2]))


def out_last(info, split, shards, hidden, early):
    rows, width = hidden.shape
    n, _, units, _ = shards.shape
    block, steps, place, part_specs, part_shapes = last_blocks(split, rows, width)
    row_spec = pl.BlockSpec((block, width), lambda i, m: (place(i, m), 0))
    return pl.pallas_call(
        functools.partial(out_last_kernel, split),
        grid_spec=pltpu.PrefetchScalarGridSpec(
            num_scalar_prefetch=1,
            grid=(steps,),
            in_specs=[pl.BlockSpec(memory_space=pl.ANY)] + [row_spec] * 2,
            out_specs=part_specs
            + [
                pl.BlockSpec((units, block), lambda i, m: (0, place(i, m))),
                pl.BlockSpec((2 * units, block), lambda i, m: (0, place(i, m))),
                pl.BlockSpec((3, units, width), lambda i, m: (0, 0, 0)),
            ],
            scratch_shapes=[pltpu.SemaphoreType.DMA((n,))],
        ),
        out_shape=part_shapes
        + [shape((units, rows), low), shape((2 * units, rows), full), shape((3, units, width), low)],
        compiler_params=params(),
        cost_estimate=cost(6 * rows * width * units, 8 * rows * width, rows * units),
        name="out_last",
    )(info, shards, hidden, early)


def hid_last_kernel(split, info_ref, w_ref, both_ref, c_ref, early_ref, *refs):
    grad_ref = refs[-1]
    gates_grad = gates_grad_of(both_ref[...], dot_nt(w_ref[2], c_ref[...]))
    grad_ref[...] = gates_grad
    hid = early_ref[...].astype(full) + dot_tn(gates_grad, join_gates(w_ref))
    put_part(split, info_ref, refs[:-1], hid)


def hid_last(info, split, weights, both, cot, early):
    rows, width = cot.shape
    units = weights.shape[1]
    block, steps, place, part_specs, part_shapes = last_blocks(split, rows, width)
    row_spec = pl.BlockSpec((block, width), lambda i, m: (place(i, m), 0))
    both_spec = pl.BlockSpec((2 * units, block), lambda i, m: (0, place(i, m)))
    return pl.pallas_call(
        functools.partial(hid_last_kernel, split),
        grid_spec=pltpu.PrefetchScalarGridSpec(
            num_scalar_prefetch=1,
            grid=(steps,),
            in_specs=[pl.BlockSpec((3, units, width), lambda i, m: (0, 0, 0)), both_spec]
            + [row_spec] * 2,
            out_specs=part_specs + [both_spec],
        ),
        out_shape=part_shapes + [shape((2 * units, rows), low)],
        compiler_params=params(),
        cost_estimate=cost(6 * rows * width * units, 8 * rows * width, rows * units),
        name="hid_last",
    )(info, weights, both, cot, early)


def feed_grads_kernel(n, steps, h_ref, c_ref, act_ref, grad_ref, out_ref, acc):
    step = pl.program_id(0)
    add_grads(acc, step, act_ref[...], grad_ref[...], h_ref[...], c_ref[...])

    @pl.when(step == steps - 1)
    def _():
        store_grads(n, acc, out_ref)


def feed_grads(n, hidden, cot, active, gates_grad):
    rows, width = hidden.shape
    units = active.shape[0]
    piece = width // n
    block = min(512, rows)
    steps = rows // block
    row_spec = pl.BlockSpec((block, width), lambda i: (i, 0))
    return pl.pallas_call(
        functools.partial(feed_grads_kernel, n, steps),
        grid=(steps,),
        in_specs=[
            row_spec,
            row_spec,
            pl.BlockSpec((units, block), lambda i: (0, i)),
            pl.BlockSpec((2 * units, block), lambda i: (0, i)),
        ],
        out_specs=pl.BlockSpec((n, 3 * units, piece), lambda i: (0, 0, 0)),
        out_shape=shape((n, 3 * units, piece), low),
        scratch_shapes=[pltpu.VMEM((3 * units, width), full)],
        compiler_params=params(),
        cost_estimate=cost(6 * rows * width * units, 4 * rows * width + 12 * units * width),
        name="feed_grads",
    )(hidden, cot, active, gates_grad)


def turn(values, cosine, sine, half):
    cols = values.shape[1]
    lane = lax.broadcasted_iota(jnp.int32, (1, cols), 1) % HD
    other = jnp.where(
        lane < half, pltpu.roll(values, cols - half, 1), pltpu.roll(values, half, 1)
    )
    repeat = cols // cosine.shape[1]
    if repeat > 1:
        cosine = jnp.concatenate([cosine] * repeat, axis=1)
        sine = jnp.concatenate([sine] * repeat, axis=1)
    return values * cosine + other * sine


def project_kernel(shards_ref, h_ref, c_ref, cos_ref, sin_ref, bias_ref, q_ref, k_ref, v_ref, o_ref, w_ref, sems):
    piece = shards_ref.shape[2]

    @pl.when(pl.program_id(0) == 0)
    def _():
        fetch(shards_ref, lambda index: w_ref.at[:, pl.ds(index * piece, piece), :], sems)

    h = h_ref[...]
    cosine, sine = cos_ref[...], sin_ref[...]
    half = ROT // 2
    q_ref[...] = turn(dot_nn(h, w_ref[0]) + bias_ref[0:1], cosine, sine, half).astype(low)
    k_ref[...] = turn(dot_nn(h, w_ref[1]) + bias_ref[1:2], cosine, sine, half).astype(low)
    v_ref[...] = (dot_nn(h, w_ref[2]) + bias_ref[2:3]).astype(low)
    o_ref[...] = dot_nn(c_ref[...], w_ref[3]).astype(low)


def project(shards, hidden, cot, cosine, sine, bias):
    rows, width = hidden.shape
    n, _, _, cols = shards.shape
    block = min(512, rows)
    row_spec = pl.BlockSpec((block, width), lambda i: (i, 0))
    angle_spec = pl.BlockSpec((block, 128), lambda i: (i, 0))
    out_spec = pl.BlockSpec((block, cols), lambda i: (i, 0))
    return pl.pallas_call(
        project_kernel,
        grid=(rows // block,),
        in_specs=[pl.BlockSpec(memory_space=pl.ANY), row_spec, row_spec, angle_spec, angle_spec]
        + [pl.BlockSpec((3, cols), lambda i: (0, 0))],
        out_specs=[out_spec] * 4 + [pl.BlockSpec((4, width, cols), lambda i: (0, 0, 0))],
        out_shape=[shape((rows, cols), low)] * 4 + [shape((4, width, cols), low)],
        scratch_shapes=[pltpu.SemaphoreType.DMA((n,))],
        compiler_params=params(),
        cost_estimate=cost(8 * rows * width * cols, 4 * rows * width + 16 * width * cols),
        name="project",
    )(shards, hidden, cot, cosine, sine, bias)


def attend_kernel(block, q_ref, k_ref, v_ref, o_ref, cos_ref, sin_ref, ctx_ref, mg_ref, bias_ref, dq, dk, dv):
    length, lanes = q_ref.shape
    scale = HD ** (-0.5)
    for head in range(lanes // HD):
        cols = slice(head * HD, (head + 1) * HD)
        for i in range(length // block):
            rows = slice(i * block, (i + 1) * block)
            end = (i + 1) * block
            q = q_ref[rows, cols]
            o = o_ref[rows, cols]
            k = k_ref[:end, cols]
            v = v_ref[:end, cols]
            scores = dot_nt(q, k) * scale
            row = i * block + lax.broadcasted_iota(jnp.int32, (block, end), 0)
            col = lax.broadcasted_iota(jnp.int32, (block, end), 1)
            scores = jnp.where(col <= row, scores, masked_score)
            top = jnp.max(scores, axis=-1, keepdims=True)
            weights = jnp.exp(scores - top)
            probs = weights * (1.0 / jnp.sum(weights, axis=-1, keepdims=True))
            probs_low = probs.astype(low)
            ctx_ref[rows, cols] = dot_nn(probs_low, v).astype(low)
            prob_grads = dot_nt(o, v)
            middle = jnp.sum(probs * prob_grads, axis=-1, keepdims=True)
            score_grads = (probs * (prob_grads - middle)).astype(low)
            dq[rows, cols] = dot_nn(score_grads, k) * scale
            key_part = dot_tn(score_grads, q) * scale
            value_part = dot_tn(probs_low, o)
            if i == 0:
                dk[:end, cols] = key_part
                dv[:end, cols] = value_part
                if end < length:
                    dk[end:, cols] = jnp.zeros((length - end, HD), full)
                    dv[end:, cols] = jnp.zeros((length - end, HD), full)
            else:
                dk[:end, cols] += key_part
                dv[:end, cols] += value_part
    cosine, sine = cos_ref[...], -sin_ref[...]
    half = ROT // 2
    sums = []
    for part, grads in enumerate(
        (turn(dq[...], cosine, sine, half), turn(dk[...], cosine, sine, half), dv[...])
    ):
        rounded = grads.astype(low)
        mg_ref[part] = rounded
        sums.append(jnp.sum(rounded.astype(full), axis=0, keepdims=True))
    total = jnp.concatenate(sums, axis=0)

    @pl.when(pl.program_id(1) == 0)
    def _():
        bias_ref[...] = total

    @pl.when(pl.program_id(1) > 0)
    def _():
        bias_ref[...] += total


def attend(batch, q, k, v, o, cosine, sine):
    rows, cols = q.shape
    length = rows // batch
    lanes = 128
    spec = pl.BlockSpec((length, lanes), lambda p, b: (b, p))
    angle_spec = pl.BlockSpec((length, 128), lambda p, b: (b, 0))
    return pl.pallas_call(
        functools.partial(attend_kernel, min(512, length)),
        grid=(cols // lanes, batch),
        in_specs=[spec] * 4 + [angle_spec] * 2,
        out_specs=[
            spec,
            pl.BlockSpec((3, length, lanes), lambda p, b: (0, b, p)),
            pl.BlockSpec((3, lanes), lambda p, b: (0, p)),
        ],
        out_shape=[
            shape((rows, cols), low),
            shape((3, rows, cols), low),
            shape((3, cols), full),
        ],
        scratch_shapes=[pltpu.VMEM((length, lanes), full)] * 3,
        compiler_params=params(),
        cost_estimate=cost(
            40 * rows * length * cols, 20 * rows * cols, rows * length * cols // HD
        ),
        name="attend",
    )(q, k, v, o, cosine, sine)


def attend_grads_kernel(h_ref, c_ref, mg_ref, ctx_ref, out_ref, wide):
    cols = ctx_ref.shape[1]

    @pl.when(pl.program_id(0) == 0)
    def _():
        for part in range(3):
            wide[:, part * cols : (part + 1) * cols] = mg_ref[part]

    grad = dot_tn(h_ref[...], wide[...])
    for part in range(3):
        out_ref[0, part] = grad[:, part * cols : (part + 1) * cols].astype(low)
    out_ref[0, 3] = dot_tn(c_ref[...], ctx_ref[...]).astype(low)


def attend_grads(n, hidden, cot, mixed_grad, context):
    rows, width = hidden.shape
    cols = context.shape[1]
    piece = width // n
    cut_spec = pl.BlockSpec((rows, piece), lambda i: (0, i))
    return pl.pallas_call(
        attend_grads_kernel,
        grid=(n,),
        in_specs=[
            cut_spec,
            cut_spec,
            pl.BlockSpec((3, rows, cols), lambda i: (0, 0, 0)),
            pl.BlockSpec((rows, cols), lambda i: (0, 0)),
        ],
        out_specs=pl.BlockSpec((1, 4, piece, cols), lambda i: (i, 0, 0, 0)),
        out_shape=shape((n, 4, piece, cols), low),
        scratch_shapes=[pltpu.VMEM((rows, 3 * cols), low)],
        compiler_params=params(),
        cost_estimate=cost(8 * rows * width * cols, 4 * rows * width + 16 * width * cols),
        name="attend_grads",
    )(hidden, cot, mixed_grad, context)


def heads_kernel(ctx_ref, mg_ref, wa_ref, hid_ref, out_ref):
    hid = dot_nt(mg_ref[0], wa_ref[0]) + dot_nt(mg_ref[1], wa_ref[1]) + dot_nt(mg_ref[2], wa_ref[2])
    hid_ref[...] = hid.astype(low)
    out_ref[...] = dot_nt(ctx_ref[...], wa_ref[3]).astype(low)


def heads_parts(context, mixed_grad, w_attend):
    rows, cols = context.shape
    width = w_attend.shape[1]
    block = min(256, rows)
    out_spec = pl.BlockSpec((block, width), lambda i: (i, 0))
    return pl.pallas_call(
        heads_kernel,
        grid=(rows // block,),
        in_specs=[
            pl.BlockSpec((block, cols), lambda i: (i, 0)),
            pl.BlockSpec((3, block, cols), lambda i: (0, i, 0)),
            pl.BlockSpec((4, width, cols), lambda i: (0, 0, 0)),
        ],
        out_specs=[out_spec, out_spec],
        out_shape=[shape((rows, width), low)] * 2,
        compiler_params=params(),
        cost_estimate=cost(8 * rows * width * cols, 4 * rows * width + 8 * (rows + width) * cols),
        name="heads_parts",
    )(context, mixed_grad, w_attend)


def early_kernel(act_ref, grad_ref, w_ref, hid_in_ref, out_in_ref, hid_ref, out_ref):
    hid = hid_in_ref[...].astype(full) + dot_tn(grad_ref[...], join_gates(w_ref))
    hid_ref[...] = hid.astype(low)
    out = out_in_ref[...].astype(full) + dot_tn(act_ref[...], w_ref[2])
    out_ref[...] = out.astype(low)


def early_parts(active, gates_grad, w_feed, hid, out):
    rows, width = hid.shape
    units = w_feed.shape[1]
    block = min(256, rows)
    row_spec = pl.BlockSpec((block, width), lambda i: (i, 0))
    return pl.pallas_call(
        early_kernel,
        grid=(rows // block,),
        in_specs=[
            pl.BlockSpec((units, block), lambda i: (0, i)),
            pl.BlockSpec((2 * units, block), lambda i: (0, i)),
            pl.BlockSpec((3, units, width), lambda i: (0, 0, 0)),
            row_spec,
            row_spec,
        ],
        out_specs=[row_spec, row_spec],
        out_shape=[shape((rows, width), low)] * 2,
        compiler_params=params(),
        cost_estimate=cost(6 * rows * width * units, 8 * rows * width + 6 * (rows + width) * units),
        name="early_parts",
    )(active, gates_grad, w_feed, hid, out)


def sixteenth(which, m):
    return m[0] * 8 + (m[1] * 2 + m[2] if which == 0 else 4 + m[2] * 2 + m[1])


def back_kernel(info_ref, *refs):
    p_ref = refs[6]
    total = 0.0
    for x_ref, near_ref, far_ref, back_ref in zip(refs[0:2], refs[2:4], refs[4:6], refs[7:9]):
        x = x_ref[...].astype(full)
        centred = x - jnp.mean(x, axis=-1, keepdims=True)
        inv = lax.rsqrt(jnp.mean(centred * centred, axis=-1, keepdims=True) + epsilon)
        normal = centred * inv
        grad = near_ref[...].astype(full) + far_ref[...].astype(full)
        scaled = grad * p_ref[0:1]
        back = inv * (
            scaled
            - jnp.mean(scaled, axis=-1, keepdims=True)
            - normal * jnp.mean(scaled * normal, axis=-1, keepdims=True)
        )
        back_ref[: x.shape[0]] = back.astype(low)
        total += jnp.concatenate(
            [jnp.sum(grad * normal, axis=0, keepdims=True), jnp.sum(grad, axis=0, keepdims=True)],
            axis=0,
        )
    high = total.astype(low)
    rest = total - high.astype(full)
    middle = rest.astype(low)
    small = (rest - middle.astype(full)).astype(low)
    zeros = jnp.zeros((tail_rows - 6, total.shape[1]), full)
    terms = [high.astype(full), middle.astype(full), small.astype(full), zeros]
    refs[7][refs[0].shape[0] :] = jnp.concatenate(terms, axis=0).astype(low)


def back_rows(info, rows, near, far, norm_params):
    count, width = near[0].shape
    spec = pl.BlockSpec((count, width), lambda i, m: (0, 0))
    pair = pl.BlockSpec((2, width), lambda i, m: (0, 0))
    return pl.pallas_call(
        back_kernel,
        grid_spec=pltpu.PrefetchScalarGridSpec(
            num_scalar_prefetch=1,
            grid=(1,),
            in_specs=[
                pl.BlockSpec((count, width), lambda i, m: (sixteenth(0, m), 0)),
                pl.BlockSpec((count, width), lambda i, m: (sixteenth(1, m), 0)),
            ]
            + [spec] * 4
            + [pair],
            out_specs=[pl.BlockSpec((count + tail_rows, width), lambda i, m: (0, 0)), spec],
        ),
        out_shape=[shape((count + tail_rows, width), low), shape((count, width), low)],
        compiler_params=params(),
        cost_estimate=cost(40 * count * width, 16 * count * width),
        name="back_rows",
    )(info, rows, rows, *near, *far, norm_params)


def add_kernel(info_ref, *refs):
    for x_ref, near_ref, far_ref, out_ref in zip(refs[0:2], refs[2:4], refs[4:6], refs[6:8]):
        total = x_ref[...].astype(full) + near_ref[...].astype(full) + far_ref[...].astype(full)
        out_ref[...] = total.astype(low)


def add_rows(info, rows, near, far):
    count, width = near[0].shape
    spec = pl.BlockSpec((count, width), lambda i, m: (0, 0))
    return pl.pallas_call(
        add_kernel,
        grid_spec=pltpu.PrefetchScalarGridSpec(
            num_scalar_prefetch=1,
            grid=(1,),
            in_specs=[
                pl.BlockSpec((count, width), lambda i, m: (sixteenth(0, m), 0)),
                pl.BlockSpec((count, width), lambda i, m: (sixteenth(1, m), 0)),
            ]
            + [spec] * 4,
            out_specs=[spec, spec],
        ),
        out_shape=[shape((count, width), low)] * 2,
        compiler_params=params(),
        cost_estimate=cost(4 * count * width, 16 * count * width),
        name="add_rows",
    )(info, rows, rows, *near, *far)


def pack_kernel(block, info_ref, *refs):
    pieces, out_ref, sems = refs[:8], refs[8], refs[9]
    x, y = info_ref[1], info_ref[2]
    copies = []

    def move(source, at, size):
        place = out_ref.at[pl.ds(pl.multiple_of(at, 16), size), :]
        copies.append(pltpu.make_async_copy(source, place, sems.at[len(copies)]))

    for i, piece in enumerate(pieces):
        high, small = (i // 2) % 2, i % 2
        if i < 4:
            at = (x ^ high) * 2 + (y ^ small)
        else:
            at = 4 + (y ^ high) * 2 + (x ^ small)
        extra = piece.shape[0] - block
        move(piece.at[pl.ds(0, block), :], at * block, block)
        if extra:
            move(piece.at[pl.ds(block, extra), :], 8 * block + at * extra, extra)
    for copy in copies:
        copy.start()
    for copy in copies:
        copy.wait()


def pack_rows(info, pieces):
    block, width = pieces[-1].shape
    extra = pieces[0].shape[0] - block
    return pl.pallas_call(
        functools.partial(pack_kernel, block),
        grid_spec=pltpu.PrefetchScalarGridSpec(
            num_scalar_prefetch=1,
            grid=(1,),
            in_specs=[pl.BlockSpec(piece.shape, lambda i, m: (0, 0)) for piece in pieces],
            out_specs=pl.BlockSpec(memory_space=pl.ANY),
            scratch_shapes=[pltpu.SemaphoreType.DMA((12,))],
        ),
        out_shape=shape((8 * block + 4 * extra, width), low),
        compiler_params=params(),
        cost_estimate=cost(0, 32 * block * width),
        name="pack_rows",
    )(info, *pieces)


def tail_total(ref):
    values = ref[...].astype(full)
    sums = 0.0
    for i in range(4):
        at = i * tail_rows
        sums += values[at : at + 2] + values[at + 2 : at + 4] + values[at + 4 : at + 6]
    return sums


def finish_kernel(info_ref, *refs):
    mine = (pl.program_id(0) // 4) == info_ref[0]
    own_ref, other_ref = refs[:2]
    summed = len(refs) > 3
    out_ref = refs[5] if summed else refs[2]

    def store(value):
        if summed:
            value = refs[2][...].astype(full) + value.astype(full)
        out_ref[...] = value

    @pl.when(mine)
    def _():
        store(own_ref[...])

    @pl.when(jnp.logical_not(mine))
    def _():
        store(other_ref[...])

    if summed:

        @pl.when(pl.program_id(0) == 0)
        def _():
            refs[6][...] = tail_total(refs[3]) + tail_total(refs[4])


def finish_rows(info, rows, own, other, cot=None):
    width = own.shape[1]
    block = rows // 8
    spec = pl.BlockSpec((block, width), lambda i, m: (i, 0))
    edge = lambda i: jnp.where(i < 4, 0, 3)
    ins = [own, other]
    specs = [
        pl.BlockSpec((block, width), lambda i, m: (jnp.where(i // 4 == m[0], i % 4, edge(i)), 0)),
        pl.BlockSpec((block, width), lambda i, m: (jnp.where(i // 4 == m[0], edge(i), i % 4), 0)),
    ]
    out_specs, out_shape = [spec], [shape((rows, width), low if cot is None else full)]
    if cot is not None:
        size = 4 * tail_rows
        last = own.shape[0] // size - 1
        ins += [cot, own, other]
        specs += [spec] + [pl.BlockSpec((size, width), lambda i, m: (last, 0))] * 2
        out_specs.append(pl.BlockSpec((2, width), lambda i, m: (0, 0)))
        out_shape.append(shape((2, width), full))
    return pl.pallas_call(
        finish_kernel,
        grid_spec=pltpu.PrefetchScalarGridSpec(
            num_scalar_prefetch=1,
            grid=(8,),
            in_specs=specs,
            out_specs=out_specs,
        ),
        out_shape=out_shape,
        compiler_params=params(),
        cost_estimate=cost(2 * rows * width, 8 * rows * width),
        name="finish_rows",
    )(info, *ins)


def update_kernel(rates, count, *refs):
    g_ref = refs[0]
    ins = refs[1:7]
    outs = refs[7 + count :]
    for which, rate in enumerate(rates):
        grad = g_ref[:2] if which == 0 else g_ref[2]
        grad = grad.astype(full)
        w, m, a = (ref[...] for ref in ins[3 * which : 3 * which + 3])
        g_out, w_out, m_out, a_out = outs[4 * which : 4 * which + 4]
        g_out[...] = grad
        w_out[...], m_out[...], a_out[...] = advance(w, grad, m, a, rate)


def update_feed(start, grads, states, rates, begun=()):
    _, units, piece = grads.shape
    block = math.gcd(start, units)
    while block > 128 and block % 16 == 0:
        block //= 2
    at = start // block
    pair = pl.BlockSpec((2, block, piece), lambda i: (0, at + i, 0))
    single = pl.BlockSpec((block, piece), lambda i: (at + i, 0))
    total = states[0].shape[1]
    return pl.pallas_call(
        functools.partial(update_kernel, rates, len(begun)),
        grid=(units // block,),
        in_specs=[pl.BlockSpec((3, block, piece), lambda i: (0, i, 0))]
        + [pair] * 3
        + [single] * 3
        + [pl.BlockSpec(memory_space=pl.ANY)] * len(begun),
        out_specs=[pair] * 4 + [single] * 4,
        out_shape=[shape((2, total, piece), full)] * 4 + [shape((total, piece), full)] * 4,
        input_output_aliases={7 + i: i for i in range(len(begun))},
        compiler_params=params(),
        cost_estimate=cost(30 * units * piece, 3 * 30 * units * piece),
        name="update_feed",
    )(grads, *states, *begun)


def body(
    inputs,
    positions,
    cotangent,
    w_attend_in,
    w_attend_out,
    w_expand,
    w_reduce,
    norm_params,
    attend_bias,
    moment_attend_in,
    moment_attend_out,
    moment_expand,
    moment_reduce,
    moment_norm,
    moment_bias,
    average_attend_in,
    average_attend_out,
    average_expand,
    average_reduce,
    average_norm,
    average_bias,
):
    batch, length, width = inputs.shape
    rows = batch * length
    units = w_expand.shape[2]
    n = lax.axis_size("dp")
    group = lax.axis_size("mp")
    spot = lax.axis_index("mp").astype(jnp.int32)
    info = jnp.stack([spot & 1, (spot >> 1) & 1, (spot >> 2) & 1])
    fast = group == 8

    expand_t = jnp.transpose(w_expand, (1, 2, 0))
    reduce_t = jnp.transpose(w_reduce)
    in_t = jnp.transpose(w_attend_in, (1, 0, 2))
    cut = units // 2 // 16 * 16
    shards = [
        jnp.concatenate([expand_t[:, a:b], reduce_t[None, a:b]], axis=0).astype(low)
        for a, b in ((0, cut), (cut, units))
    ]
    attend_shard = jnp.concatenate([in_t, w_attend_out[None]], axis=0).astype(low)
    attend_all = lax.all_gather(attend_shard, "dp")
    first_all = lax.all_gather(after(shards[0], attend_shard), "dp")
    last_all = lax.all_gather(after(shards[1], shards[0]), "dp")

    tokens = inputs.reshape(rows, width)
    cot = cotangent.reshape(rows, width)
    hidden = layer_norm(tokens, norm_params)

    half = ROT // 2
    lane = jnp.arange(128, dtype=jnp.int32) % HD
    frequency = 10000.0 ** (-((lane % half).astype(full) * 2.0 / ROT))
    angles = positions.reshape(rows).astype(full)[:, None] * frequency[None, :]
    cosine = jnp.where(lane < ROT, jnp.cos(angles), 1.0)
    sine = jnp.where(lane < half, -jnp.sin(angles), jnp.where(lane < ROT, jnp.sin(angles), 0.0))

    def scatter(grads):
        return lax.psum_scatter(grads, "dp", scatter_dimension=0, tiled=False)

    q, k, v, o, w_attend = project(attend_all, hidden, cot, cosine, sine, attend_bias)
    context, mixed_grad, bias_part = attend(batch, q, k, v, o, cosine, sine)
    attend_grad = attend_grads(n, hidden, cot, mixed_grad, context)
    hid_early, out_early = heads_parts(context, mixed_grad, w_attend)
    first_all = after(first_all, attend_grad, hid_early, out_early)
    active, gates_grad, w_feed = feed_chunk(first_all, hidden, cot)
    hid_early, out_early = early_parts(active, gates_grad, w_feed, hid_early, out_early)
    first_grads = feed_grads(n, hidden, cot, active, gates_grad)
    last_all = after(last_all, first_grads, hid_early, out_early)
    first_grads = scatter(after(first_grads, last_all)).reshape(3, cut, -1)

    total_tokens = rows * n

    def update_attend(grad):
        grad = grad.astype(full)
        grad_in, grad_out = jnp.transpose(grad[:3], (1, 0, 2)), grad[3]
        rate_in = 0.5 / math.sqrt(width * total_tokens)
        rate_out = 1.8 / math.sqrt(width * batch * n)
        new_in = advance(w_attend_in, grad_in, moment_attend_in, average_attend_in, rate_in)
        new_out = advance(w_attend_out, grad_out, moment_attend_out, average_attend_out, rate_out)
        return (grad_in, grad_out) + new_in + new_out

    rates = (1.6 / math.sqrt(width * total_tokens), 0.77 / math.sqrt(FF * total_tokens))
    states = [jnp.transpose(a, (1, 2, 0)) for a in (w_expand, moment_expand, average_expand)]
    states += [jnp.transpose(a) for a in (w_reduce, moment_reduce, average_reduce)]

    if fast:
        s = rows // 16

        def swap_cores(parts):
            came = {i: swap(parts[i], 1) for i in (1, 3, 0, 2)}
            return [came[i] for i in range(4)]

        def sum_cores(own, came):
            own = [a.astype(full) + b.astype(full) for a, b in zip(own, came)]
            return own, (own[1].astype(low), own[3].astype(low))

        def sum_first(own, came):
            first = own[0] + came[0].astype(full)
            second = own[2] + came[1].astype(full)
            near = [first[:s].astype(low), second[:s].astype(low)]
            return near, (first[s:].astype(low), second[s:].astype(low))

        def both_ways(pair, masks):
            return [swap(pair[0], masks[0]), swap(pair[1], masks[1])]

        def join(one, first, second, third):
            pieces = (one, first, second, third)
            return pack_rows(info, [p[0] for p in pieces] + [p[1] for p in pieces])

        *parts, active, both, w_last = out_last(info, True, last_all, hidden, out_early)
        own_out, load_out = sum_cores(parts[4:], swap_cores(parts[:4]))
        one_out = both_ways(load_out, (2, 4))
        attend_grad = scatter(after(attend_grad, load_out))
        *parts, gates_grad = hid_last(info, True, w_last, after(both, load_out), cot, hid_early)
        came_hid = swap_cores(parts[:4])
        near_out, load_out = sum_first(own_out, after(one_out, parts[0]))
        two_out = both_ways(load_out, (4, 2))
        own_hid, load_hid = sum_cores(parts[4:], after(came_hid, load_out))
        one_hid = both_ways(load_hid, (2, 4))
        last_grads = feed_grads(n, hidden, cot, after(active, load_hid), gates_grad)
        two_out = after(two_out, last_grads)
        add = add_rows(info, tokens, near_out, two_out)
        last_grads = scatter(last_grads).reshape(3, units - cut, -1)
        out_one = both_ways(add, (4, 2))
        out_two = both_ways(add, (2, 4))
        near_hid, load_hid = sum_first(own_hid, after(one_hid, add))
        two_hid = both_ways(load_hid, (4, 2))
        back = back_rows(info, tokens, near_hid, two_hid, norm_params)
        hid_one = both_ways(back, (4, 2))
        hid_two = both_ways(back, (2, 4))
        out_one, out_two = after((out_one, out_two), back)
        out_three = both_ways(out_one, (2, 4))
        begun = update_feed(0, after(first_grads, out_one), states, rates)
        hid_one, hid_two = after((hid_one, hid_two), begun)
        hid_three = both_ways(hid_one, (2, 4))
        out_three = after(out_three, hid_one)
        mine_out = join(add, out_one, out_two, out_three)
        other_out = swap(mine_out, 1)
        hid_three = after(hid_three, mine_out)
        mine_hid = join(back, hid_one, hid_two, hid_three)
        other_hid = swap(mine_hid, 1)
        attend_new = update_attend(after(attend_grad, mine_hid))
        (output,) = finish_rows(info, rows, mine_out, after(other_out, attend_new))
        input_grad, norm_part = finish_rows(info, rows, mine_hid, after(other_hid, output), cot)
        sums = small_sum(join_sums(norm_part, bias_part), "dp")
        done = update_feed(cut, after(last_grads, input_grad), states, rates, begun)
        norm_grad, bias_grad = split_sums(sums, norm_part, bias_part)
    else:
        out_part, active, both, w_last = out_last(info, False, last_all, hidden, out_early)
        hid_part, gates_grad = hid_last(info, False, w_last, both, cot, hid_early)
        attend_new = update_attend(scatter(attend_grad))
        last_grads = scatter(feed_grads(n, hidden, cot, active, gates_grad)).reshape(3, units - cut, -1)
        hidden_grad = lax.psum(hid_part, "mp").astype(full)
        summed = lax.psum(out_part, "mp").astype(full)
        values = tokens.astype(full)
        output = (values + summed).astype(low)
        centred = values - jnp.mean(values, axis=-1, keepdims=True)
        inv = lax.rsqrt(jnp.mean(centred * centred, axis=-1, keepdims=True) + epsilon)
        normal = centred * inv
        scaled = hidden_grad * norm_params[0]
        back = inv * (
            scaled
            - jnp.mean(scaled, axis=-1, keepdims=True)
            - normal * jnp.mean(scaled * normal, axis=-1, keepdims=True)
        )
        input_grad = cot.astype(full) + back
        norm_part = jnp.stack([jnp.sum(hidden_grad * normal, axis=0), jnp.sum(hidden_grad, axis=0)])
        sums = small_sum(join_sums(norm_part, bias_part), "dp")
        norm_grad, bias_grad = split_sums(sums, norm_part, bias_part)
        begun = update_feed(0, first_grads, states, rates)
        done = update_feed(cut, last_grads, states, rates, begun)
    grad_in, grad_out = attend_new[:2]
    new_in, moment_in_new, average_in_new = attend_new[2:5]
    new_out, moment_out_new, average_out_new = attend_new[5:]
    grad_expand, new_expand, moment_expand_new, average_expand_new = (
        jnp.transpose(a, (2, 0, 1)) for a in done[:4]
    )
    grad_reduce, new_reduce, moment_reduce_new, average_reduce_new = (
        jnp.transpose(a) for a in done[4:]
    )
    input_grad = input_grad.reshape(batch, length, width)
    output = output.reshape(batch, length, width)
    new_norm, moment_norm_new, average_norm_new = advance(
        norm_params, norm_grad, moment_norm, average_norm, 0.06 / math.sqrt(total_tokens)
    )
    new_bias, moment_bias_new, average_bias_new = advance(
        attend_bias, bias_grad, moment_bias, average_bias, 0.25 / math.sqrt(total_tokens)
    )
    return (
        output,
        input_grad,
        grad_in,
        grad_out,
        grad_expand,
        grad_reduce,
        norm_grad,
        bias_grad,
        new_in,
        new_out,
        new_expand,
        new_reduce,
        new_norm,
        new_bias,
        moment_in_new,
        moment_out_new,
        moment_expand_new,
        moment_reduce_new,
        moment_norm_new,
        moment_bias_new,
        average_in_new,
        average_out_new,
        average_expand_new,
        average_reduce_new,
        average_norm_new,
        average_bias_new,
    )


def solution(mesh):
    rows3 = P("dp", None, None)
    in3 = P("dp", None, "mp")
    in2 = P("dp", "mp")
    bias = P(None, "mp")
    states = (in3, in2, in3, in2, P(), bias)
    return jax.shard_map(
        body,
        mesh=mesh,
        in_specs=(rows3, P("dp", None), rows3) + states * 3,
        out_specs=(rows3, rows3) + states * 4,
        check_vma=False,
    )
```

```python
import functools
import math

import jax
import jax.numpy as jnp
from jax import lax
from jax.experimental import pallas as pl
from jax.experimental.pallas import tpu as pltpu
from jax.sharding import PartitionSpec as P

HD = 64
ROT = 16
FF = 5632

epsilon = 1e-05
decay_moment = 0.9
decay_average = 0.9
masked_score = -1e30

low = jnp.bfloat16
full = jnp.float32
vmem_limit = 60 << 20
tail_rows = 16


def dot_nt(left, right):
    return lax.dot_general(left, right, (((1,), (1,)), ((), ())), preferred_element_type=full)


def dot_nn(left, right):
    return lax.dot_general(left, right, (((1,), (0,)), ((), ())), preferred_element_type=full)


def dot_tn(left, right):
    return lax.dot_general(left, right, (((0,), (0,)), ((), ())), preferred_element_type=full)


def params(**more):
    return pltpu.CompilerParams(vmem_limit_bytes=vmem_limit, **more)


def cost(flops, moved, trans=0):
    return pl.CostEstimate(flops=int(flops), bytes_accessed=int(moved), transcendentals=int(trans))


def shape(dims, kind):
    return jax.ShapeDtypeStruct(dims, kind)


def advance(weight, grad, moment, average, rate):
    moment_new = decay_moment * moment + grad
    weight_new = weight - rate * (grad + decay_moment * moment_new)
    average_new = decay_average * average + (1.0 - decay_average) * weight_new
    return (weight_new, moment_new, average_new)


def after(value, *others):
    return lax.optimization_barrier((value, others))[0]


def swap(value, mask, axis="mp"):
    n = lax.axis_size(axis)
    return lax.ppermute(value, axis, [(a, a ^ mask) for a in range(n)])


def small_sum(value, axis):
    n = lax.axis_size(axis)
    if n & (n - 1):
        return lax.psum(value, axis)
    mask = 1
    while mask < n:
        value = value + swap(value, mask, axis)
        mask *= 2
    return value


def join_sums(norm_part, bias_part):
    cols = bias_part.shape[1]
    return jnp.concatenate([norm_part.reshape(-1, cols), bias_part])


def split_sums(sums, norm_part, bias_part):
    count = sums.shape[0] - bias_part.shape[0]
    return sums[:count].reshape(norm_part.shape), sums[count:]


def norm_kernel(x_ref, p_ref, o_ref):
    x = x_ref[...].astype(full)
    centred = x - jnp.mean(x, axis=-1, keepdims=True)
    inv = lax.rsqrt(jnp.mean(centred * centred, axis=-1, keepdims=True) + epsilon)
    o_ref[...] = (centred * inv * p_ref[0:1] + p_ref[1:2]).astype(low)


def layer_norm(rows, norm_params):
    count, width = rows.shape
    block = min(256, count)
    return pl.pallas_call(
        norm_kernel,
        grid=(count // block,),
        in_specs=[
            pl.BlockSpec((block, width), lambda i: (i, 0)),
            pl.BlockSpec((2, width), lambda i: (0, 0)),
        ],
        out_specs=pl.BlockSpec((block, width), lambda i: (i, 0)),
        out_shape=shape((count, width), low),
        compiler_params=params(),
        cost_estimate=cost(8 * count * width, 4 * count * width),
        name="layer_norm",
    )(rows, norm_params)


def fetch(gathered, target_of, sems):
    copies = [
        pltpu.make_async_copy(gathered.at[j], target_of(j), sems.at[j]) for j in range(gathered.shape[0])
    ]
    for copy in copies:
        copy.start()
    for copy in copies:
        copy.wait()


def swish_of(both):
    units = both.shape[0] // 2
    gate, upper = both[:units], both[units:]
    sigmoid = jax.nn.sigmoid(gate)
    return gate, upper, sigmoid, gate * sigmoid


def join_gates(w_ref):
    return w_ref[0:2].reshape(2 * w_ref.shape[1], w_ref.shape[2])


def gates_grad_of(both, active_grad):
    gate, upper, sigmoid, swish = swish_of(both)
    gate_grad = active_grad * upper * sigmoid * (1.0 + gate * (1.0 - sigmoid))
    return jnp.concatenate([gate_grad, active_grad * swish], axis=0).astype(low)


def gates_of(w_ref, h, c):
    both = dot_nt(join_gates(w_ref), h)
    _, upper, _, swish = swish_of(both)
    return (swish * upper).astype(low), gates_grad_of(both, dot_nt(w_ref[2], c))


def add_grads(acc, step, active, gates_grad, h, c):
    units = active.shape[0]

    @pl.when(step == 0)
    def _():
        acc[: 2 * units] = dot_nn(gates_grad, h)
        acc[2 * units :] = dot_nn(active, c)

    @pl.when(step > 0)
    def _():
        acc[: 2 * units] += dot_nn(gates_grad, h)
        acc[2 * units :] += dot_nn(active, c)


def store_grads(n, acc, out_ref):
    piece = out_ref.shape[2]
    for j in range(n):
        out_ref[j] = acc[:, j * piece : (j + 1) * piece].astype(low)


def wide_target(w_ref, piece):
    return lambda index: w_ref.at[:, :, pl.ds(index * piece, piece)]


def feed_kernel(shards_ref, h_ref, c_ref, act_ref, grad_ref, w_ref, sems):
    @pl.when(pl.program_id(0) == 0)
    def _():
        fetch(shards_ref, wide_target(w_ref, shards_ref.shape[3]), sems)

    act_ref[...], grad_ref[...] = gates_of(w_ref, h_ref[...], c_ref[...])


def feed_chunk(shards, hidden, cot):
    rows, width = hidden.shape
    n, _, units, _ = shards.shape
    block = min(512, rows)
    row_spec = pl.BlockSpec((block, width), lambda i: (i, 0))
    return pl.pallas_call(
        feed_kernel,
        grid=(rows // block,),
        in_specs=[pl.BlockSpec(memory_space=pl.ANY), row_spec, row_spec],
        out_specs=[
            pl.BlockSpec((units, block), lambda i: (0, i)),
            pl.BlockSpec((2 * units, block), lambda i: (0, i)),
            pl.BlockSpec((3, units, width), lambda i: (0, 0, 0)),
        ],
        out_shape=[
            shape((units, rows), low),
            shape((2 * units, rows), low),
            shape((3, units, width), low),
        ],
        scratch_shapes=[pltpu.SemaphoreType.DMA((n,))],
        compiler_params=params(),
        cost_estimate=cost(
            6 * rows * width * units, 4 * rows * width + 12 * units * width, rows * units
        ),
        name="feed_chunk",
    )(shards, hidden, cot)


def put_part(split, info_ref, parts, value):
    if not split:
        parts[0][...] = value.astype(low)
        return
    step = pl.program_id(0)
    sub = value.shape[0] // 4
    high = jnp.where(step % 2 == 0, info_ref[1], info_ref[2])
    small = jnp.where(step % 2 == 0, info_ref[2], info_ref[1])
    first, second = value[: 2 * sub], value[2 * sub :]
    near = jnp.where(high == 0, first, second).astype(low)
    far = jnp.where(high == 0, second, first).astype(low)
    for at in range(4):

        @pl.when(step == at)
        def _(at=at):
            for ref, pair in ((parts[2 * at], near), (parts[2 * at + 1], far)):
                for i in range(2):
                    place = pl.ds(pl.multiple_of((i ^ small) * sub, sub), sub)
                    ref[place, :] = pair[i * sub : (i + 1) * sub]


def last_blocks(split, rows, width):
    if split:
        block, steps = rows // 4, 4
        place = lambda i, m: (m[0] ^ (1 - i // 2)) * 2 + i % 2
        part_specs = [pl.BlockSpec((block // 2, width), lambda i, m: (0, 0))] * 8
        part_shapes = [shape((block // 2, width), low)] * 8
    else:
        block = min(256, rows)
        steps = rows // block
        place = lambda i, m: i
        part_specs = [pl.BlockSpec((block, width), lambda i, m: (i, 0))]
        part_shapes = [shape((rows, width), low)]
    return block, steps, place, part_specs, part_shapes


def out_last_kernel(split, info_ref, shards_ref, h_ref, early_ref, *refs):
    parts = refs[:-4]
    act_ref, both_ref, w_ref, sems = refs[-4:]

    @pl.when(pl.program_id(0) == 0)
    def _():
        fetch(shards_ref, wide_target(w_ref, shards_ref.shape[3]), sems)

    both = dot_nt(join_gates(w_ref), h_ref[...])
    both_ref[...] = both
    _, upper, _, swish = swish_of(both)
    active = (swish * upper).astype(low)
    act_ref[...] = active
    put_part(split, info_ref, parts, early_ref[...].astype(full) + dot_tn(active, w_ref[2]))


def out_last(info, split, shards, hidden, early):
    rows, width = hidden.shape
    n, _, units, _ = shards.shape
    block, steps, place, part_specs, part_shapes = last_blocks(split, rows, width)
    row_spec = pl.BlockSpec((block, width), lambda i, m: (place(i, m), 0))
    return pl.pallas_call(
        functools.partial(out_last_kernel, split),
        grid_spec=pltpu.PrefetchScalarGridSpec(
            num_scalar_prefetch=1,
            grid=(steps,),
            in_specs=[pl.BlockSpec(memory_space=pl.ANY)] + [row_spec] * 2,
            out_specs=part_specs
            + [
                pl.BlockSpec((units, block), lambda i, m: (0, place(i, m))),
                pl.BlockSpec((2 * units, block), lambda i, m: (0, place(i, m))),
                pl.BlockSpec((3, units, width), lambda i, m: (0, 0, 0)),
            ],
            scratch_shapes=[pltpu.SemaphoreType.DMA((n,))],
        ),
        out_shape=part_shapes
        + [shape((units, rows), low), shape((2 * units, rows), full), shape((3, units, width), low)],
        compiler_params=params(),
        cost_estimate=cost(6 * rows * width * units, 8 * rows * width, rows * units),
        name="out_last",
    )(info, shards, hidden, early)


def hid_last_kernel(split, info_ref, w_ref, both_ref, c_ref, early_ref, *refs):
    grad_ref = refs[-1]
    gates_grad = gates_grad_of(both_ref[...], dot_nt(w_ref[2], c_ref[...]))
    grad_ref[...] = gates_grad
    hid = early_ref[...].astype(full) + dot_tn(gates_grad, join_gates(w_ref))
    put_part(split, info_ref, refs[:-1], hid)


def hid_last(info, split, weights, both, cot, early):
    rows, width = cot.shape
    units = weights.shape[1]
    block, steps, place, part_specs, part_shapes = last_blocks(split, rows, width)
    row_spec = pl.BlockSpec((block, width), lambda i, m: (place(i, m), 0))
    both_spec = pl.BlockSpec((2 * units, block), lambda i, m: (0, place(i, m)))
    return pl.pallas_call(
        functools.partial(hid_last_kernel, split),
        grid_spec=pltpu.PrefetchScalarGridSpec(
            num_scalar_prefetch=1,
            grid=(steps,),
            in_specs=[pl.BlockSpec((3, units, width), lambda i, m: (0, 0, 0)), both_spec]
            + [row_spec] * 2,
            out_specs=part_specs + [both_spec],
        ),
        out_shape=part_shapes + [shape((2 * units, rows), low)],
        compiler_params=params(),
        cost_estimate=cost(6 * rows * width * units, 8 * rows * width, rows * units),
        name="hid_last",
    )(info, weights, both, cot, early)


def feed_grads_kernel(n, steps, h_ref, c_ref, act_ref, grad_ref, out_ref, acc):
    step = pl.program_id(0)
    add_grads(acc, step, act_ref[...], grad_ref[...], h_ref[...], c_ref[...])

    @pl.when(step == steps - 1)
    def _():
        store_grads(n, acc, out_ref)


def feed_grads(n, hidden, cot, active, gates_grad):
    rows, width = hidden.shape
    units = active.shape[0]
    piece = width // n
    block = min(512, rows)
    steps = rows // block
    row_spec = pl.BlockSpec((block, width), lambda i: (i, 0))
    return pl.pallas_call(
        functools.partial(feed_grads_kernel, n, steps),
        grid=(steps,),
        in_specs=[
            row_spec,
            row_spec,
            pl.BlockSpec((units, block), lambda i: (0, i)),
            pl.BlockSpec((2 * units, block), lambda i: (0, i)),
        ],
        out_specs=pl.BlockSpec((n, 3 * units, piece), lambda i: (0, 0, 0)),
        out_shape=shape((n, 3 * units, piece), low),
        scratch_shapes=[pltpu.VMEM((3 * units, width), full)],
        compiler_params=params(),
        cost_estimate=cost(6 * rows * width * units, 4 * rows * width + 12 * units * width),
        name="feed_grads",
    )(hidden, cot, active, gates_grad)


def turn(values, cosine, sine, half):
    cols = values.shape[1]
    lane = lax.broadcasted_iota(jnp.int32, (1, cols), 1) % HD
    other = jnp.where(
        lane < half, pltpu.roll(values, cols - half, 1), pltpu.roll(values, half, 1)
    )
    repeat = cols // cosine.shape[1]
    if repeat > 1:
        cosine = jnp.concatenate([cosine] * repeat, axis=1)
        sine = jnp.concatenate([sine] * repeat, axis=1)
    return values * cosine + other * sine


def project_kernel(shards_ref, h_ref, c_ref, cos_ref, sin_ref, bias_ref, q_ref, k_ref, v_ref, o_ref, w_ref, sems):
    piece = shards_ref.shape[2]

    @pl.when(pl.program_id(0) == 0)
    def _():
        fetch(shards_ref, lambda index: w_ref.at[:, pl.ds(index * piece, piece), :], sems)

    h = h_ref[...]
    cosine, sine = cos_ref[...], sin_ref[...]
    half = ROT // 2
    q_ref[...] = turn(dot_nn(h, w_ref[0]) + bias_ref[0:1], cosine, sine, half).astype(low)
    k_ref[...] = turn(dot_nn(h, w_ref[1]) + bias_ref[1:2], cosine, sine, half).astype(low)
    v_ref[...] = (dot_nn(h, w_ref[2]) + bias_ref[2:3]).astype(low)
    o_ref[...] = dot_nn(c_ref[...], w_ref[3]).astype(low)


def project(shards, hidden, cot, cosine, sine, bias):
    rows, width = hidden.shape
    n, _, _, cols = shards.shape
    block = min(512, rows)
    row_spec = pl.BlockSpec((block, width), lambda i: (i, 0))
    angle_spec = pl.BlockSpec((block, 128), lambda i: (i, 0))
    out_spec = pl.BlockSpec((block, cols), lambda i: (i, 0))
    return pl.pallas_call(
        project_kernel,
        grid=(rows // block,),
        in_specs=[pl.BlockSpec(memory_space=pl.ANY), row_spec, row_spec, angle_spec, angle_spec]
        + [pl.BlockSpec((3, cols), lambda i: (0, 0))],
        out_specs=[out_spec] * 4 + [pl.BlockSpec((4, width, cols), lambda i: (0, 0, 0))],
        out_shape=[shape((rows, cols), low)] * 4 + [shape((4, width, cols), low)],
        scratch_shapes=[pltpu.SemaphoreType.DMA((n,))],
        compiler_params=params(),
        cost_estimate=cost(8 * rows * width * cols, 4 * rows * width + 16 * width * cols),
        name="project",
    )(shards, hidden, cot, cosine, sine, bias)


def attend_kernel(block, q_ref, k_ref, v_ref, o_ref, cos_ref, sin_ref, ctx_ref, mg_ref, bias_ref, dq, dk, dv):
    length, lanes = q_ref.shape
    scale = HD ** (-0.5)
    for head in range(lanes // HD):
        cols = slice(head * HD, (head + 1) * HD)
        for i in range(length // block):
            rows = slice(i * block, (i + 1) * block)
            end = (i + 1) * block
            q = q_ref[rows, cols]
            o = o_ref[rows, cols]
            k = k_ref[:end, cols]
            v = v_ref[:end, cols]
            scores = dot_nt(q, k) * scale
            row = i * block + lax.broadcasted_iota(jnp.int32, (block, end), 0)
            col = lax.broadcasted_iota(jnp.int32, (block, end), 1)
            scores = jnp.where(col <= row, scores, masked_score)
            top = jnp.max(scores, axis=-1, keepdims=True)
            weights = jnp.exp(scores - top)
            probs = weights * (1.0 / jnp.sum(weights, axis=-1, keepdims=True))
            probs_low = probs.astype(low)
            ctx_ref[rows, cols] = dot_nn(probs_low, v).astype(low)
            prob_grads = dot_nt(o, v)
            middle = jnp.sum(probs * prob_grads, axis=-1, keepdims=True)
            score_grads = (probs * (prob_grads - middle)).astype(low)
            dq[rows, cols] = dot_nn(score_grads, k) * scale
            key_part = dot_tn(score_grads, q) * scale
            value_part = dot_tn(probs_low, o)
            if i == 0:
                dk[:end, cols] = key_part
                dv[:end, cols] = value_part
                if end < length:
                    dk[end:, cols] = jnp.zeros((length - end, HD), full)
                    dv[end:, cols] = jnp.zeros((length - end, HD), full)
            else:
                dk[:end, cols] += key_part
                dv[:end, cols] += value_part
    cosine, sine = cos_ref[...], -sin_ref[...]
    half = ROT // 2
    sums = []
    for part, grads in enumerate(
        (turn(dq[...], cosine, sine, half), turn(dk[...], cosine, sine, half), dv[...])
    ):
        rounded = grads.astype(low)
        mg_ref[part] = rounded
        sums.append(jnp.sum(rounded.astype(full), axis=0, keepdims=True))
    total = jnp.concatenate(sums, axis=0)

    @pl.when(pl.program_id(1) == 0)
    def _():
        bias_ref[...] = total

    @pl.when(pl.program_id(1) > 0)
    def _():
        bias_ref[...] += total


def attend(batch, q, k, v, o, cosine, sine):
    rows, cols = q.shape
    length = rows // batch
    lanes = 128
    spec = pl.BlockSpec((length, lanes), lambda p, b: (b, p))
    angle_spec = pl.BlockSpec((length, 128), lambda p, b: (b, 0))
    return pl.pallas_call(
        functools.partial(attend_kernel, min(512, length)),
        grid=(cols // lanes, batch),
        in_specs=[spec] * 4 + [angle_spec] * 2,
        out_specs=[
            spec,
            pl.BlockSpec((3, length, lanes), lambda p, b: (0, b, p)),
            pl.BlockSpec((3, lanes), lambda p, b: (0, p)),
        ],
        out_shape=[
            shape((rows, cols), low),
            shape((3, rows, cols), low),
            shape((3, cols), full),
        ],
        scratch_shapes=[pltpu.VMEM((length, lanes), full)] * 3,
        compiler_params=params(),
        cost_estimate=cost(
            40 * rows * length * cols, 20 * rows * cols, rows * length * cols // HD
        ),
        name="attend",
    )(q, k, v, o, cosine, sine)


def attend_grads_kernel(h_ref, c_ref, mg_ref, ctx_ref, out_ref, wide):
    cols = ctx_ref.shape[1]

    @pl.when(pl.program_id(0) == 0)
    def _():
        for part in range(3):
            wide[:, part * cols : (part + 1) * cols] = mg_ref[part]

    grad = dot_tn(h_ref[...], wide[...])
    for part in range(3):
        out_ref[0, part] = grad[:, part * cols : (part + 1) * cols].astype(low)
    out_ref[0, 3] = dot_tn(c_ref[...], ctx_ref[...]).astype(low)


def attend_grads(n, hidden, cot, mixed_grad, context):
    rows, width = hidden.shape
    cols = context.shape[1]
    piece = width // n
    cut_spec = pl.BlockSpec((rows, piece), lambda i: (0, i))
    return pl.pallas_call(
        attend_grads_kernel,
        grid=(n,),
        in_specs=[
            cut_spec,
            cut_spec,
            pl.BlockSpec((3, rows, cols), lambda i: (0, 0, 0)),
            pl.BlockSpec((rows, cols), lambda i: (0, 0)),
        ],
        out_specs=pl.BlockSpec((1, 4, piece, cols), lambda i: (i, 0, 0, 0)),
        out_shape=shape((n, 4, piece, cols), low),
        scratch_shapes=[pltpu.VMEM((rows, 3 * cols), low)],
        compiler_params=params(),
        cost_estimate=cost(8 * rows * width * cols, 4 * rows * width + 16 * width * cols),
        name="attend_grads",
    )(hidden, cot, mixed_grad, context)


def heads_kernel(ctx_ref, mg_ref, wa_ref, hid_ref, out_ref):
    hid = dot_nt(mg_ref[0], wa_ref[0]) + dot_nt(mg_ref[1], wa_ref[1]) + dot_nt(mg_ref[2], wa_ref[2])
    hid_ref[...] = hid.astype(low)
    out_ref[...] = dot_nt(ctx_ref[...], wa_ref[3]).astype(low)


def heads_parts(context, mixed_grad, w_attend):
    rows, cols = context.shape
    width = w_attend.shape[1]
    block = min(256, rows)
    out_spec = pl.BlockSpec((block, width), lambda i: (i, 0))
    return pl.pallas_call(
        heads_kernel,
        grid=(rows // block,),
        in_specs=[
            pl.BlockSpec((block, cols), lambda i: (i, 0)),
            pl.BlockSpec((3, block, cols), lambda i: (0, i, 0)),
            pl.BlockSpec((4, width, cols), lambda i: (0, 0, 0)),
        ],
        out_specs=[out_spec, out_spec],
        out_shape=[shape((rows, width), low)] * 2,
        compiler_params=params(),
        cost_estimate=cost(8 * rows * width * cols, 4 * rows * width + 8 * (rows + width) * cols),
        name="heads_parts",
    )(context, mixed_grad, w_attend)


def early_kernel(act_ref, grad_ref, w_ref, hid_in_ref, out_in_ref, hid_ref, out_ref):
    hid = hid_in_ref[...].astype(full) + dot_tn(grad_ref[...], join_gates(w_ref))
    hid_ref[...] = hid.astype(low)
    out = out_in_ref[...].astype(full) + dot_tn(act_ref[...], w_ref[2])
    out_ref[...] = out.astype(low)


def early_parts(active, gates_grad, w_feed, hid, out):
    rows, width = hid.shape
    units = w_feed.shape[1]
    block = min(256, rows)
    row_spec = pl.BlockSpec((block, width), lambda i: (i, 0))
    return pl.pallas_call(
        early_kernel,
        grid=(rows // block,),
        in_specs=[
            pl.BlockSpec((units, block), lambda i: (0, i)),
            pl.BlockSpec((2 * units, block), lambda i: (0, i)),
            pl.BlockSpec((3, units, width), lambda i: (0, 0, 0)),
            row_spec,
            row_spec,
        ],
        out_specs=[row_spec, row_spec],
        out_shape=[shape((rows, width), low)] * 2,
        compiler_params=params(),
        cost_estimate=cost(6 * rows * width * units, 8 * rows * width + 6 * (rows + width) * units),
        name="early_parts",
    )(active, gates_grad, w_feed, hid, out)


def sixteenth(which, m):
    return m[0] * 8 + (m[1] * 2 + m[2] if which == 0 else 4 + m[2] * 2 + m[1])


def back_kernel(info_ref, *refs):
    p_ref = refs[6]
    total = 0.0
    for x_ref, near_ref, far_ref, back_ref in zip(refs[0:2], refs[2:4], refs[4:6], refs[7:9]):
        x = x_ref[...].astype(full)
        centred = x - jnp.mean(x, axis=-1, keepdims=True)
        inv = lax.rsqrt(jnp.mean(centred * centred, axis=-1, keepdims=True) + epsilon)
        normal = centred * inv
        grad = near_ref[...].astype(full) + far_ref[...].astype(full)
        scaled = grad * p_ref[0:1]
        back = inv * (
            scaled
            - jnp.mean(scaled, axis=-1, keepdims=True)
            - normal * jnp.mean(scaled * normal, axis=-1, keepdims=True)
        )
        back_ref[: x.shape[0]] = back.astype(low)
        total += jnp.concatenate(
            [jnp.sum(grad * normal, axis=0, keepdims=True), jnp.sum(grad, axis=0, keepdims=True)],
            axis=0,
        )
    high = total.astype(low)
    rest = total - high.astype(full)
    middle = rest.astype(low)
    small = (rest - middle.astype(full)).astype(low)
    zeros = jnp.zeros((tail_rows - 6, total.shape[1]), full)
    terms = [high.astype(full), middle.astype(full), small.astype(full), zeros]
    refs[7][refs[0].shape[0] :] = jnp.concatenate(terms, axis=0).astype(low)


def back_rows(info, rows, near, far, norm_params):
    count, width = near[0].shape
    spec = pl.BlockSpec((count, width), lambda i, m: (0, 0))
    pair = pl.BlockSpec((2, width), lambda i, m: (0, 0))
    return pl.pallas_call(
        back_kernel,
        grid_spec=pltpu.PrefetchScalarGridSpec(
            num_scalar_prefetch=1,
            grid=(1,),
            in_specs=[
                pl.BlockSpec((count, width), lambda i, m: (sixteenth(0, m), 0)),
                pl.BlockSpec((count, width), lambda i, m: (sixteenth(1, m), 0)),
            ]
            + [spec] * 4
            + [pair],
            out_specs=[pl.BlockSpec((count + tail_rows, width), lambda i, m: (0, 0)), spec],
        ),
        out_shape=[shape((count + tail_rows, width), low), shape((count, width), low)],
        compiler_params=params(),
        cost_estimate=cost(40 * count * width, 16 * count * width),
        name="back_rows",
    )(info, rows, rows, *near, *far, norm_params)


def add_kernel(info_ref, *refs):
    for x_ref, near_ref, far_ref, out_ref in zip(refs[0:2], refs[2:4], refs[4:6], refs[6:8]):
        total = x_ref[...].astype(full) + near_ref[...].astype(full) + far_ref[...].astype(full)
        out_ref[...] = total.astype(low)


def add_rows(info, rows, near, far):
    count, width = near[0].shape
    spec = pl.BlockSpec((count, width), lambda i, m: (0, 0))
    return pl.pallas_call(
        add_kernel,
        grid_spec=pltpu.PrefetchScalarGridSpec(
            num_scalar_prefetch=1,
            grid=(1,),
            in_specs=[
                pl.BlockSpec((count, width), lambda i, m: (sixteenth(0, m), 0)),
                pl.BlockSpec((count, width), lambda i, m: (sixteenth(1, m), 0)),
            ]
            + [spec] * 4,
            out_specs=[spec, spec],
        ),
        out_shape=[shape((count, width), low)] * 2,
        compiler_params=params(),
        cost_estimate=cost(4 * count * width, 16 * count * width),
        name="add_rows",
    )(info, rows, rows, *near, *far)


def pack_kernel(block, info_ref, *refs):
    pieces, out_ref, sems = refs[:8], refs[8], refs[9]
    x, y = info_ref[1], info_ref[2]
    copies = []

    def move(source, at, size):
        place = out_ref.at[pl.ds(pl.multiple_of(at, 16), size), :]
        copies.append(pltpu.make_async_copy(source, place, sems.at[len(copies)]))

    for i, piece in enumerate(pieces):
        high, small = (i // 2) % 2, i % 2
        if i < 4:
            at = (x ^ high) * 2 + (y ^ small)
        else:
            at = 4 + (y ^ high) * 2 + (x ^ small)
        extra = piece.shape[0] - block
        move(piece.at[pl.ds(0, block), :], at * block, block)
        if extra:
            move(piece.at[pl.ds(block, extra), :], 8 * block + at * extra, extra)
    for copy in copies:
        copy.start()
    for copy in copies:
        copy.wait()


def pack_rows(info, pieces):
    block, width = pieces[-1].shape
    extra = pieces[0].shape[0] - block
    return pl.pallas_call(
        functools.partial(pack_kernel, block),
        grid_spec=pltpu.PrefetchScalarGridSpec(
            num_scalar_prefetch=1,
            grid=(1,),
            in_specs=[pl.BlockSpec(piece.shape, lambda i, m: (0, 0)) for piece in pieces],
            out_specs=pl.BlockSpec(memory_space=pl.ANY),
            scratch_shapes=[pltpu.SemaphoreType.DMA((12,))],
        ),
        out_shape=shape((8 * block + 4 * extra, width), low),
        compiler_params=params(),
        cost_estimate=cost(0, 32 * block * width),
        name="pack_rows",
    )(info, *pieces)


def tail_total(ref):
    values = ref[...].astype(full)
    sums = 0.0
    for i in range(4):
        at = i * tail_rows
        sums += values[at : at + 2] + values[at + 2 : at + 4] + values[at + 4 : at + 6]
    return sums


def finish_kernel(info_ref, *refs):
    mine = (pl.program_id(0) // 4) == info_ref[0]
    own_ref, other_ref = refs[:2]
    summed = len(refs) > 3
    out_ref = refs[5] if summed else refs[2]

    def store(value):
        if summed:
            value = refs[2][...].astype(full) + value.astype(full)
        out_ref[...] = value

    @pl.when(mine)
    def _():
        store(own_ref[...])

    @pl.when(jnp.logical_not(mine))
    def _():
        store(other_ref[...])

    if summed:

        @pl.when(pl.program_id(0) == 0)
        def _():
            refs[6][...] = tail_total(refs[3]) + tail_total(refs[4])


def finish_rows(info, rows, own, other, cot=None):
    width = own.shape[1]
    block = rows // 8
    spec = pl.BlockSpec((block, width), lambda i, m: (i, 0))
    edge = lambda i: jnp.where(i < 4, 0, 3)
    ins = [own, other]
    specs = [
        pl.BlockSpec((block, width), lambda i, m: (jnp.where(i // 4 == m[0], i % 4, edge(i)), 0)),
        pl.BlockSpec((block, width), lambda i, m: (jnp.where(i // 4 == m[0], edge(i), i % 4), 0)),
    ]
    out_specs, out_shape = [spec], [shape((rows, width), low if cot is None else full)]
    if cot is not None:
        size = 4 * tail_rows
        last = own.shape[0] // size - 1
        ins += [cot, own, other]
        specs += [spec] + [pl.BlockSpec((size, width), lambda i, m: (last, 0))] * 2
        out_specs.append(pl.BlockSpec((2, width), lambda i, m: (0, 0)))
        out_shape.append(shape((2, width), full))
    return pl.pallas_call(
        finish_kernel,
        grid_spec=pltpu.PrefetchScalarGridSpec(
            num_scalar_prefetch=1,
            grid=(8,),
            in_specs=specs,
            out_specs=out_specs,
        ),
        out_shape=out_shape,
        compiler_params=params(),
        cost_estimate=cost(2 * rows * width, 8 * rows * width),
        name="finish_rows",
    )(info, *ins)


def update_kernel(rates, count, *refs):
    g_ref = refs[0]
    ins = refs[1:7]
    outs = refs[7 + count :]
    for which, rate in enumerate(rates):
        grad = g_ref[:2] if which == 0 else g_ref[2]
        grad = grad.astype(full)
        w, m, a = (ref[...] for ref in ins[3 * which : 3 * which + 3])
        g_out, w_out, m_out, a_out = outs[4 * which : 4 * which + 4]
        g_out[...] = grad
        w_out[...], m_out[...], a_out[...] = advance(w, grad, m, a, rate)


def update_feed(start, grads, states, rates, begun=()):
    _, units, piece = grads.shape
    block = math.gcd(start, units)
    while block > 128 and block % 16 == 0:
        block //= 2
    at = start // block
    pair = pl.BlockSpec((2, block, piece), lambda i: (0, at + i, 0))
    single = pl.BlockSpec((block, piece), lambda i: (at + i, 0))
    total = states[0].shape[1]
    return pl.pallas_call(
        functools.partial(update_kernel, rates, len(begun)),
        grid=(units // block,),
        in_specs=[pl.BlockSpec((3, block, piece), lambda i: (0, i, 0))]
        + [pair] * 3
        + [single] * 3
        + [pl.BlockSpec(memory_space=pl.ANY)] * len(begun),
        out_specs=[pair] * 4 + [single] * 4,
        out_shape=[shape((2, total, piece), full)] * 4 + [shape((total, piece), full)] * 4,
        input_output_aliases={7 + i: i for i in range(len(begun))},
        compiler_params=params(),
        cost_estimate=cost(30 * units * piece, 3 * 30 * units * piece),
        name="update_feed",
    )(grads, *states, *begun)


def body(
    inputs,
    positions,
    cotangent,
    w_attend_in,
    w_attend_out,
    w_expand,
    w_reduce,
    norm_params,
    attend_bias,
    moment_attend_in,
    moment_attend_out,
    moment_expand,
    moment_reduce,
    moment_norm,
    moment_bias,
    average_attend_in,
    average_attend_out,
    average_expand,
    average_reduce,
    average_norm,
    average_bias,
):
    batch, length, width = inputs.shape
    rows = batch * length
    units = w_expand.shape[2]
    n = lax.axis_size("dp")
    group = lax.axis_size("mp")
    spot = lax.axis_index("mp").astype(jnp.int32)
    info = jnp.stack([spot & 1, (spot >> 1) & 1, (spot >> 2) & 1])
    fast = group == 8

    expand_t = jnp.transpose(w_expand, (1, 2, 0))
    reduce_t = jnp.transpose(w_reduce)
    in_t = jnp.transpose(w_attend_in, (1, 0, 2))
    cut = units * 7 // 11 // 16 * 16
    shards = [
        jnp.concatenate([expand_t[:, a:b], reduce_t[None, a:b]], axis=0).astype(low)
        for a, b in ((0, cut), (cut, units))
    ]
    attend_shard = jnp.concatenate([in_t, w_attend_out[None]], axis=0).astype(low)
    attend_all = lax.all_gather(attend_shard, "dp")
    first_all = lax.all_gather(after(shards[0], attend_shard), "dp")
    last_all = lax.all_gather(after(shards[1], shards[0]), "dp")

    tokens = inputs.reshape(rows, width)
    cot = cotangent.reshape(rows, width)
    hidden = layer_norm(tokens, norm_params)

    half = ROT // 2
    lane = jnp.arange(128, dtype=jnp.int32) % HD
    frequency = 10000.0 ** (-((lane % half).astype(full) * 2.0 / ROT))
    angles = positions.reshape(rows).astype(full)[:, None] * frequency[None, :]
    cosine = jnp.where(lane < ROT, jnp.cos(angles), 1.0)
    sine = jnp.where(lane < half, -jnp.sin(angles), jnp.where(lane < ROT, jnp.sin(angles), 0.0))

    def scatter(grads):
        return lax.psum_scatter(grads, "dp", scatter_dimension=0, tiled=False)

    q, k, v, o, w_attend = project(attend_all, hidden, cot, cosine, sine, attend_bias)
    context, mixed_grad, bias_part = attend(batch, q, k, v, o, cosine, sine)
    attend_grad = attend_grads(n, hidden, cot, mixed_grad, context)
    hid_early, out_early = heads_parts(context, mixed_grad, w_attend)
    first_all = after(first_all, attend_grad, hid_early, out_early)
    active, gates_grad, w_feed = feed_chunk(first_all, hidden, cot)
    hid_early, out_early = early_parts(active, gates_grad, w_feed, hid_early, out_early)
    first_grads = feed_grads(n, hidden, cot, active, gates_grad)
    last_all = after(last_all, first_grads, hid_early, out_early)
    first_grads = scatter(after(first_grads, last_all)).reshape(3, cut, -1)

    total_tokens = rows * n

    def update_attend(grad):
        grad = grad.astype(full)
        grad_in, grad_out = jnp.transpose(grad[:3], (1, 0, 2)), grad[3]
        rate_in = 0.5 / math.sqrt(width * total_tokens)
        rate_out = 1.8 / math.sqrt(width * batch * n)
        new_in = advance(w_attend_in, grad_in, moment_attend_in, average_attend_in, rate_in)
        new_out = advance(w_attend_out, grad_out, moment_attend_out, average_attend_out, rate_out)
        return (grad_in, grad_out) + new_in + new_out

    rates = (1.6 / math.sqrt(width * total_tokens), 0.77 / math.sqrt(FF * total_tokens))
    states = [jnp.transpose(a, (1, 2, 0)) for a in (w_expand, moment_expand, average_expand)]
    states += [jnp.transpose(a) for a in (w_reduce, moment_reduce, average_reduce)]

    if fast:
        s = rows // 16

        def swap_cores(parts):
            came = {i: swap(parts[i], 1) for i in (1, 3, 0, 2)}
            return [came[i] for i in range(4)]

        def sum_cores(own, came):
            own = [a.astype(full) + b.astype(full) for a, b in zip(own, came)]
            return own, (own[1].astype(low), own[3].astype(low))

        def sum_first(own, came):
            first = own[0] + came[0].astype(full)
            second = own[2] + came[1].astype(full)
            near = [first[:s].astype(low), second[:s].astype(low)]
            return near, (first[s:].astype(low), second[s:].astype(low))

        def both_ways(pair, masks):
            return [swap(pair[0], masks[0]), swap(pair[1], masks[1])]

        def join(one, first, second, third):
            pieces = (one, first, second, third)
            return pack_rows(info, [p[0] for p in pieces] + [p[1] for p in pieces])

        *parts, active, both, w_last = out_last(info, True, last_all, hidden, out_early)
        own_out, load_out = sum_cores(parts[4:], swap_cores(parts[:4]))
        one_out = both_ways(load_out, (2, 4))
        attend_grad = scatter(after(attend_grad, load_out))
        *parts, gates_grad = hid_last(info, True, w_last, after(both, load_out), cot, hid_early)
        came_hid = swap_cores(parts[:4])
        near_out, load_out = sum_first(own_out, after(one_out, parts[0]))
        two_out = both_ways(load_out, (4, 2))
        own_hid, load_hid = sum_cores(parts[4:], after(came_hid, load_out))
        one_hid = both_ways(load_hid, (2, 4))
        last_grads = feed_grads(n, hidden, cot, after(active, load_hid), gates_grad)
        two_out = after(two_out, last_grads)
        add = add_rows(info, tokens, near_out, two_out)
        last_grads = scatter(last_grads).reshape(3, units - cut, -1)
        out_one = both_ways(add, (4, 2))
        out_two = both_ways(add, (2, 4))
        near_hid, load_hid = sum_first(own_hid, after(one_hid, add))
        two_hid = both_ways(load_hid, (4, 2))
        back = back_rows(info, tokens, near_hid, two_hid, norm_params)
        hid_one = both_ways(back, (4, 2))
        hid_two = both_ways(back, (2, 4))
        out_one, out_two = after((out_one, out_two), back)
        out_three = both_ways(out_one, (2, 4))
        begun = update_feed(0, after(first_grads, out_one), states, rates)
        out_two, out_three = after((out_two, out_three), begun)
        mine_out = join(add, out_one, out_two, out_three)
        other_out = swap(mine_out, 1)
        hid_one, hid_two = after((hid_one, hid_two), mine_out)
        hid_three = both_ways(hid_one, (2, 4))
        mine_hid = join(back, hid_one, hid_two, hid_three)
        other_hid = swap(mine_hid, 1)
        attend_new = update_attend(after(attend_grad, mine_hid))
        (output,) = finish_rows(info, rows, mine_out, after(other_out, attend_new))
        input_grad, norm_part = finish_rows(info, rows, mine_hid, after(other_hid, output), cot)
        sums = join_sums(norm_part, bias_part)
        done = update_feed(cut, after(last_grads, sums), states, rates, begun)
        sums = small_sum(sums, "dp")
        norm_grad, bias_grad = split_sums(sums, norm_part, bias_part)
    else:
        out_part, active, both, w_last = out_last(info, False, last_all, hidden, out_early)
        hid_part, gates_grad = hid_last(info, False, w_last, both, cot, hid_early)
        attend_new = update_attend(scatter(attend_grad))
        last_grads = scatter(feed_grads(n, hidden, cot, active, gates_grad)).reshape(3, units - cut, -1)
        hidden_grad = lax.psum(hid_part, "mp").astype(full)
        summed = lax.psum(out_part, "mp").astype(full)
        values = tokens.astype(full)
        output = (values + summed).astype(low)
        centred = values - jnp.mean(values, axis=-1, keepdims=True)
        inv = lax.rsqrt(jnp.mean(centred * centred, axis=-1, keepdims=True) + epsilon)
        normal = centred * inv
        scaled = hidden_grad * norm_params[0]
        back = inv * (
            scaled
            - jnp.mean(scaled, axis=-1, keepdims=True)
            - normal * jnp.mean(scaled * normal, axis=-1, keepdims=True)
        )
        input_grad = cot.astype(full) + back
        norm_part = jnp.stack([jnp.sum(hidden_grad * normal, axis=0), jnp.sum(hidden_grad, axis=0)])
        sums = small_sum(join_sums(norm_part, bias_part), "dp")
        norm_grad, bias_grad = split_sums(sums, norm_part, bias_part)
        begun = update_feed(0, first_grads, states, rates)
        done = update_feed(cut, last_grads, states, rates, begun)
    grad_in, grad_out = attend_new[:2]
    new_in, moment_in_new, average_in_new = attend_new[2:5]
    new_out, moment_out_new, average_out_new = attend_new[5:]
    grad_expand, new_expand, moment_expand_new, average_expand_new = (
        jnp.transpose(a, (2, 0, 1)) for a in done[:4]
    )
    grad_reduce, new_reduce, moment_reduce_new, average_reduce_new = (
        jnp.transpose(a) for a in done[4:]
    )
    input_grad = input_grad.reshape(batch, length, width)
    output = output.reshape(batch, length, width)
    new_norm, moment_norm_new, average_norm_new = advance(
        norm_params, norm_grad, moment_norm, average_norm, 0.06 / math.sqrt(total_tokens)
    )
    new_bias, moment_bias_new, average_bias_new = advance(
        attend_bias, bias_grad, moment_bias, average_bias, 0.25 / math.sqrt(total_tokens)
    )
    return (
        output,
        input_grad,
        grad_in,
        grad_out,
        grad_expand,
        grad_reduce,
        norm_grad,
        bias_grad,
        new_in,
        new_out,
        new_expand,
        new_reduce,
        new_norm,
        new_bias,
        moment_in_new,
        moment_out_new,
        moment_expand_new,
        moment_reduce_new,
        moment_norm_new,
        moment_bias_new,
        average_in_new,
        average_out_new,
        average_expand_new,
        average_reduce_new,
        average_norm_new,
        average_bias_new,
    )


def solution(mesh):
    rows3 = P("dp", None, None)
    in3 = P("dp", None, "mp")
    in2 = P("dp", "mp")
    bias = P(None, "mp")
    states = (in3, in2, in3, in2, P(), bias)
    return jax.shard_map(
        body,
        mesh=mesh,
        in_specs=(rows3, P("dp", None), rows3) + states * 3,
        out_specs=(rows3, rows3) + states * 4,
        check_vma=False,
    )
```

```python
import functools
import math

import jax
import jax.numpy as jnp
from jax import lax
from jax.experimental import pallas as pl
from jax.experimental.pallas import tpu as pltpu
from jax.sharding import PartitionSpec as P

HD = 64
ROT = 16
FF = 5632

epsilon = 1e-05
decay_moment = 0.9
decay_average = 0.9
masked_score = -1e30

low = jnp.bfloat16
full = jnp.float32
vmem_limit = 60 << 20
tail_rows = 16


def dot_nt(left, right):
    return lax.dot_general(left, right, (((1,), (1,)), ((), ())), preferred_element_type=full)


def dot_nn(left, right):
    return lax.dot_general(left, right, (((1,), (0,)), ((), ())), preferred_element_type=full)


def dot_tn(left, right):
    return lax.dot_general(left, right, (((0,), (0,)), ((), ())), preferred_element_type=full)


def params(**more):
    return pltpu.CompilerParams(vmem_limit_bytes=vmem_limit, **more)


def cost(flops, moved, trans=0):
    return pl.CostEstimate(flops=int(flops), bytes_accessed=int(moved), transcendentals=int(trans))


def shape(dims, kind):
    return jax.ShapeDtypeStruct(dims, kind)


def advance(weight, grad, moment, average, rate):
    moment_new = decay_moment * moment + grad
    weight_new = weight - rate * (grad + decay_moment * moment_new)
    average_new = decay_average * average + (1.0 - decay_average) * weight_new
    return (weight_new, moment_new, average_new)


def after(value, *others):
    return lax.optimization_barrier((value, others))[0]


def swap(value, mask, axis="mp"):
    n = lax.axis_size(axis)
    return lax.ppermute(value, axis, [(a, a ^ mask) for a in range(n)])


def small_sum(value, axis):
    n = lax.axis_size(axis)
    if n & (n - 1):
        return lax.psum(value, axis)
    mask = 1
    while mask < n:
        value = value + swap(value, mask, axis)
        mask *= 2
    return value


def join_sums(norm_part, bias_part):
    cols = bias_part.shape[1]
    return jnp.concatenate([norm_part.reshape(-1, cols), bias_part])


def split_sums(sums, norm_part, bias_part):
    count = sums.shape[0] - bias_part.shape[0]
    return sums[:count].reshape(norm_part.shape), sums[count:]


def norm_kernel(x_ref, p_ref, o_ref):
    x = x_ref[...].astype(full)
    centred = x - jnp.mean(x, axis=-1, keepdims=True)
    inv = lax.rsqrt(jnp.mean(centred * centred, axis=-1, keepdims=True) + epsilon)
    o_ref[...] = (centred * inv * p_ref[0:1] + p_ref[1:2]).astype(low)


def layer_norm(rows, norm_params):
    count, width = rows.shape
    block = min(256, count)
    return pl.pallas_call(
        norm_kernel,
        grid=(count // block,),
        in_specs=[
            pl.BlockSpec((block, width), lambda i: (i, 0)),
            pl.BlockSpec((2, width), lambda i: (0, 0)),
        ],
        out_specs=pl.BlockSpec((block, width), lambda i: (i, 0)),
        out_shape=shape((count, width), low),
        compiler_params=params(),
        cost_estimate=cost(8 * count * width, 4 * count * width),
        name="layer_norm",
    )(rows, norm_params)


def fetch(gathered, target_of, sems):
    copies = [
        pltpu.make_async_copy(gathered.at[j], target_of(j), sems.at[j]) for j in range(gathered.shape[0])
    ]
    for copy in copies:
        copy.start()
    for copy in copies:
        copy.wait()


def swish_of(both):
    units = both.shape[0] // 2
    gate, upper = both[:units], both[units:]
    sigmoid = jax.nn.sigmoid(gate)
    return gate, upper, sigmoid, gate * sigmoid


def join_gates(w_ref):
    return w_ref[0:2].reshape(2 * w_ref.shape[1], w_ref.shape[2])


def gates_grad_of(both, active_grad):
    gate, upper, sigmoid, swish = swish_of(both)
    gate_grad = active_grad * upper * sigmoid * (1.0 + gate * (1.0 - sigmoid))
    return jnp.concatenate([gate_grad, active_grad * swish], axis=0).astype(low)


def gates_of(w_ref, h, c):
    both = dot_nt(join_gates(w_ref), h)
    _, upper, _, swish = swish_of(both)
    return (swish * upper).astype(low), gates_grad_of(both, dot_nt(w_ref[2], c))


def add_grads(acc, step, active, gates_grad, h, c):
    units = active.shape[0]

    @pl.when(step == 0)
    def _():
        acc[: 2 * units] = dot_nn(gates_grad, h)
        acc[2 * units :] = dot_nn(active, c)

    @pl.when(step > 0)
    def _():
        acc[: 2 * units] += dot_nn(gates_grad, h)
        acc[2 * units :] += dot_nn(active, c)


def store_grads(n, acc, out_ref):
    piece = out_ref.shape[2]
    for j in range(n):
        out_ref[j] = acc[:, j * piece : (j + 1) * piece].astype(low)


def wide_target(w_ref, piece):
    return lambda index: w_ref.at[:, :, pl.ds(index * piece, piece)]


def feed_kernel(shards_ref, h_ref, c_ref, act_ref, grad_ref, w_ref, sems):
    @pl.when(pl.program_id(0) == 0)
    def _():
        fetch(shards_ref, wide_target(w_ref, shards_ref.shape[3]), sems)

    act_ref[...], grad_ref[...] = gates_of(w_ref, h_ref[...], c_ref[...])


def feed_chunk(shards, hidden, cot):
    rows, width = hidden.shape
    n, _, units, _ = shards.shape
    block = min(512, rows)
    row_spec = pl.BlockSpec((block, width), lambda i: (i, 0))
    return pl.pallas_call(
        feed_kernel,
        grid=(rows // block,),
        in_specs=[pl.BlockSpec(memory_space=pl.ANY), row_spec, row_spec],
        out_specs=[
            pl.BlockSpec((units, block), lambda i: (0, i)),
            pl.BlockSpec((2 * units, block), lambda i: (0, i)),
            pl.BlockSpec((3, units, width), lambda i: (0, 0, 0)),
        ],
        out_shape=[
            shape((units, rows), low),
            shape((2 * units, rows), low),
            shape((3, units, width), low),
        ],
        scratch_shapes=[pltpu.SemaphoreType.DMA((n,))],
        compiler_params=params(),
        cost_estimate=cost(
            6 * rows * width * units, 4 * rows * width + 12 * units * width, rows * units
        ),
        name="feed_chunk",
    )(shards, hidden, cot)


def put_part(split, info_ref, parts, value):
    if not split:
        parts[0][...] = value.astype(low)
        return
    step = pl.program_id(0)
    sub = value.shape[0] // 4
    high = jnp.where(step % 2 == 0, info_ref[1], info_ref[2])
    small = jnp.where(step % 2 == 0, info_ref[2], info_ref[1])
    first, second = value[: 2 * sub], value[2 * sub :]
    near = jnp.where(high == 0, first, second).astype(low)
    far = jnp.where(high == 0, second, first).astype(low)
    for at in range(4):

        @pl.when(step == at)
        def _(at=at):
            for ref, pair in ((parts[2 * at], near), (parts[2 * at + 1], far)):
                for i in range(2):
                    place = pl.ds(pl.multiple_of((i ^ small) * sub, sub), sub)
                    ref[place, :] = pair[i * sub : (i + 1) * sub]


def last_blocks(split, rows, width):
    if split:
        block, steps = rows // 4, 4
        place = lambda i, m: (m[0] ^ (1 - i // 2)) * 2 + i % 2
        part_specs = [pl.BlockSpec((block // 2, width), lambda i, m: (0, 0))] * 8
        part_shapes = [shape((block // 2, width), low)] * 8
    else:
        block = min(256, rows)
        steps = rows // block
        place = lambda i, m: i
        part_specs = [pl.BlockSpec((block, width), lambda i, m: (i, 0))]
        part_shapes = [shape((rows, width), low)]
    return block, steps, place, part_specs, part_shapes


def out_last_kernel(split, info_ref, shards_ref, h_ref, early_ref, *refs):
    parts = refs[:-4]
    act_ref, both_ref, w_ref, sems = refs[-4:]

    @pl.when(pl.program_id(0) == 0)
    def _():
        fetch(shards_ref, wide_target(w_ref, shards_ref.shape[3]), sems)

    both = dot_nt(join_gates(w_ref), h_ref[...])
    both_ref[...] = both
    _, upper, _, swish = swish_of(both)
    active = (swish * upper).astype(low)
    act_ref[...] = active
    put_part(split, info_ref, parts, early_ref[...].astype(full) + dot_tn(active, w_ref[2]))


def out_last(info, split, shards, hidden, early):
    rows, width = hidden.shape
    n, _, units, _ = shards.shape
    block, steps, place, part_specs, part_shapes = last_blocks(split, rows, width)
    row_spec = pl.BlockSpec((block, width), lambda i, m: (place(i, m), 0))
    return pl.pallas_call(
        functools.partial(out_last_kernel, split),
        grid_spec=pltpu.PrefetchScalarGridSpec(
            num_scalar_prefetch=1,
            grid=(steps,),
            in_specs=[pl.BlockSpec(memory_space=pl.ANY)] + [row_spec] * 2,
            out_specs=part_specs
            + [
                pl.BlockSpec((units, block), lambda i, m: (0, place(i, m))),
                pl.BlockSpec((2 * units, block), lambda i, m: (0, place(i, m))),
                pl.BlockSpec((3, units, width), lambda i, m: (0, 0, 0)),
            ],
            scratch_shapes=[pltpu.SemaphoreType.DMA((n,))],
        ),
        out_shape=part_shapes
        + [shape((units, rows), low), shape((2 * units, rows), full), shape((3, units, width), low)],
        compiler_params=params(),
        cost_estimate=cost(6 * rows * width * units, 8 * rows * width, rows * units),
        name="out_last",
    )(info, shards, hidden, early)


def hid_last_kernel(split, info_ref, w_ref, both_ref, c_ref, early_ref, *refs):
    grad_ref = refs[-1]
    gates_grad = gates_grad_of(both_ref[...], dot_nt(w_ref[2], c_ref[...]))
    grad_ref[...] = gates_grad
    hid = early_ref[...].astype(full) + dot_tn(gates_grad, join_gates(w_ref))
    put_part(split, info_ref, refs[:-1], hid)


def hid_last(info, split, weights, both, cot, early):
    rows, width = cot.shape
    units = weights.shape[1]
    block, steps, place, part_specs, part_shapes = last_blocks(split, rows, width)
    row_spec = pl.BlockSpec((block, width), lambda i, m: (place(i, m), 0))
    both_spec = pl.BlockSpec((2 * units, block), lambda i, m: (0, place(i, m)))
    return pl.pallas_call(
        functools.partial(hid_last_kernel, split),
        grid_spec=pltpu.PrefetchScalarGridSpec(
            num_scalar_prefetch=1,
            grid=(steps,),
            in_specs=[pl.BlockSpec((3, units, width), lambda i, m: (0, 0, 0)), both_spec]
            + [row_spec] * 2,
            out_specs=part_specs + [both_spec],
        ),
        out_shape=part_shapes + [shape((2 * units, rows), low)],
        compiler_params=params(),
        cost_estimate=cost(6 * rows * width * units, 8 * rows * width, rows * units),
        name="hid_last",
    )(info, weights, both, cot, early)


def feed_grads_kernel(n, steps, h_ref, c_ref, act_ref, grad_ref, out_ref, acc):
    step = pl.program_id(0)
    add_grads(acc, step, act_ref[...], grad_ref[...], h_ref[...], c_ref[...])

    @pl.when(step == steps - 1)
    def _():
        store_grads(n, acc, out_ref)


def feed_grads(n, hidden, cot, active, gates_grad):
    rows, width = hidden.shape
    units = active.shape[0]
    piece = width // n
    block = min(512, rows)
    steps = rows // block
    row_spec = pl.BlockSpec((block, width), lambda i: (i, 0))
    return pl.pallas_call(
        functools.partial(feed_grads_kernel, n, steps),
        grid=(steps,),
        in_specs=[
            row_spec,
            row_spec,
            pl.BlockSpec((units, block), lambda i: (0, i)),
            pl.BlockSpec((2 * units, block), lambda i: (0, i)),
        ],
        out_specs=pl.BlockSpec((n, 3 * units, piece), lambda i: (0, 0, 0)),
        out_shape=shape((n, 3 * units, piece), low),
        scratch_shapes=[pltpu.VMEM((3 * units, width), full)],
        compiler_params=params(),
        cost_estimate=cost(6 * rows * width * units, 4 * rows * width + 12 * units * width),
        name="feed_grads",
    )(hidden, cot, active, gates_grad)


def turn(values, cosine, sine, half):
    cols = values.shape[1]
    lane = lax.broadcasted_iota(jnp.int32, (1, cols), 1) % HD
    other = jnp.where(
        lane < half, pltpu.roll(values, cols - half, 1), pltpu.roll(values, half, 1)
    )
    repeat = cols // cosine.shape[1]
    if repeat > 1:
        cosine = jnp.concatenate([cosine] * repeat, axis=1)
        sine = jnp.concatenate([sine] * repeat, axis=1)
    return values * cosine + other * sine


def project_kernel(shards_ref, h_ref, c_ref, cos_ref, sin_ref, bias_ref, q_ref, k_ref, v_ref, o_ref, w_ref, sems):
    piece = shards_ref.shape[2]

    @pl.when(pl.program_id(0) == 0)
    def _():
        fetch(shards_ref, lambda index: w_ref.at[:, pl.ds(index * piece, piece), :], sems)

    h = h_ref[...]
    cosine, sine = cos_ref[...], sin_ref[...]
    half = ROT // 2
    q_ref[...] = turn(dot_nn(h, w_ref[0]) + bias_ref[0:1], cosine, sine, half).astype(low)
    k_ref[...] = turn(dot_nn(h, w_ref[1]) + bias_ref[1:2], cosine, sine, half).astype(low)
    v_ref[...] = (dot_nn(h, w_ref[2]) + bias_ref[2:3]).astype(low)
    o_ref[...] = dot_nn(c_ref[...], w_ref[3]).astype(low)


def project(shards, hidden, cot, cosine, sine, bias):
    rows, width = hidden.shape
    n, _, _, cols = shards.shape
    block = min(512, rows)
    row_spec = pl.BlockSpec((block, width), lambda i: (i, 0))
    angle_spec = pl.BlockSpec((block, 128), lambda i: (i, 0))
    out_spec = pl.BlockSpec((block, cols), lambda i: (i, 0))
    return pl.pallas_call(
        project_kernel,
        grid=(rows // block,),
        in_specs=[pl.BlockSpec(memory_space=pl.ANY), row_spec, row_spec, angle_spec, angle_spec]
        + [pl.BlockSpec((3, cols), lambda i: (0, 0))],
        out_specs=[out_spec] * 4 + [pl.BlockSpec((4, width, cols), lambda i: (0, 0, 0))],
        out_shape=[shape((rows, cols), low)] * 4 + [shape((4, width, cols), low)],
        scratch_shapes=[pltpu.SemaphoreType.DMA((n,))],
        compiler_params=params(),
        cost_estimate=cost(8 * rows * width * cols, 4 * rows * width + 16 * width * cols),
        name="project",
    )(shards, hidden, cot, cosine, sine, bias)


def attend_kernel(block, q_ref, k_ref, v_ref, o_ref, cos_ref, sin_ref, ctx_ref, mg_ref, bias_ref, dq, dk, dv):
    length, lanes = q_ref.shape
    scale = HD ** (-0.5)
    for head in range(lanes // HD):
        cols = slice(head * HD, (head + 1) * HD)
        for i in range(length // block):
            rows = slice(i * block, (i + 1) * block)
            end = (i + 1) * block
            q = q_ref[rows, cols]
            o = o_ref[rows, cols]
            k = k_ref[:end, cols]
            v = v_ref[:end, cols]
            scores = dot_nt(q, k) * scale
            row = i * block + lax.broadcasted_iota(jnp.int32, (block, end), 0)
            col = lax.broadcasted_iota(jnp.int32, (block, end), 1)
            scores = jnp.where(col <= row, scores, masked_score)
            top = jnp.max(scores, axis=-1, keepdims=True)
            weights = jnp.exp(scores - top)
            probs = weights * (1.0 / jnp.sum(weights, axis=-1, keepdims=True))
            probs_low = probs.astype(low)
            ctx_ref[rows, cols] = dot_nn(probs_low, v).astype(low)
            prob_grads = dot_nt(o, v)
            middle = jnp.sum(probs * prob_grads, axis=-1, keepdims=True)
            score_grads = (probs * (prob_grads - middle)).astype(low)
            dq[rows, cols] = dot_nn(score_grads, k) * scale
            key_part = dot_tn(score_grads, q) * scale
            value_part = dot_tn(probs_low, o)
            if i == 0:
                dk[:end, cols] = key_part
                dv[:end, cols] = value_part
                if end < length:
                    dk[end:, cols] = jnp.zeros((length - end, HD), full)
                    dv[end:, cols] = jnp.zeros((length - end, HD), full)
            else:
                dk[:end, cols] += key_part
                dv[:end, cols] += value_part
    cosine, sine = cos_ref[...], -sin_ref[...]
    half = ROT // 2
    sums = []
    for part, grads in enumerate(
        (turn(dq[...], cosine, sine, half), turn(dk[...], cosine, sine, half), dv[...])
    ):
        rounded = grads.astype(low)
        mg_ref[part] = rounded
        sums.append(jnp.sum(rounded.astype(full), axis=0, keepdims=True))
    total = jnp.concatenate(sums, axis=0)

    @pl.when(pl.program_id(1) == 0)
    def _():
        bias_ref[...] = total

    @pl.when(pl.program_id(1) > 0)
    def _():
        bias_ref[...] += total


def attend(batch, q, k, v, o, cosine, sine):
    rows, cols = q.shape
    length = rows // batch
    lanes = 128
    spec = pl.BlockSpec((length, lanes), lambda p, b: (b, p))
    angle_spec = pl.BlockSpec((length, 128), lambda p, b: (b, 0))
    return pl.pallas_call(
        functools.partial(attend_kernel, min(512, length)),
        grid=(cols // lanes, batch),
        in_specs=[spec] * 4 + [angle_spec] * 2,
        out_specs=[
            spec,
            pl.BlockSpec((3, length, lanes), lambda p, b: (0, b, p)),
            pl.BlockSpec((3, lanes), lambda p, b: (0, p)),
        ],
        out_shape=[
            shape((rows, cols), low),
            shape((3, rows, cols), low),
            shape((3, cols), full),
        ],
        scratch_shapes=[pltpu.VMEM((length, lanes), full)] * 3,
        compiler_params=params(),
        cost_estimate=cost(
            40 * rows * length * cols, 20 * rows * cols, rows * length * cols // HD
        ),
        name="attend",
    )(q, k, v, o, cosine, sine)


def attend_grads_kernel(h_ref, c_ref, mg_ref, ctx_ref, out_ref, wide):
    cols = ctx_ref.shape[1]

    @pl.when(pl.program_id(0) == 0)
    def _():
        for part in range(3):
            wide[:, part * cols : (part + 1) * cols] = mg_ref[part]

    grad = dot_tn(h_ref[...], wide[...])
    for part in range(3):
        out_ref[0, part] = grad[:, part * cols : (part + 1) * cols].astype(low)
    out_ref[0, 3] = dot_tn(c_ref[...], ctx_ref[...]).astype(low)


def attend_grads(n, hidden, cot, mixed_grad, context):
    rows, width = hidden.shape
    cols = context.shape[1]
    piece = width // n
    cut_spec = pl.BlockSpec((rows, piece), lambda i: (0, i))
    return pl.pallas_call(
        attend_grads_kernel,
        grid=(n,),
        in_specs=[
            cut_spec,
            cut_spec,
            pl.BlockSpec((3, rows, cols), lambda i: (0, 0, 0)),
            pl.BlockSpec((rows, cols), lambda i: (0, 0)),
        ],
        out_specs=pl.BlockSpec((1, 4, piece, cols), lambda i: (i, 0, 0, 0)),
        out_shape=shape((n, 4, piece, cols), low),
        scratch_shapes=[pltpu.VMEM((rows, 3 * cols), low)],
        compiler_params=params(),
        cost_estimate=cost(8 * rows * width * cols, 4 * rows * width + 16 * width * cols),
        name="attend_grads",
    )(hidden, cot, mixed_grad, context)


def heads_kernel(ctx_ref, mg_ref, wa_ref, hid_ref, out_ref):
    hid = dot_nt(mg_ref[0], wa_ref[0]) + dot_nt(mg_ref[1], wa_ref[1]) + dot_nt(mg_ref[2], wa_ref[2])
    hid_ref[...] = hid.astype(low)
    out_ref[...] = dot_nt(ctx_ref[...], wa_ref[3]).astype(low)


def heads_parts(context, mixed_grad, w_attend):
    rows, cols = context.shape
    width = w_attend.shape[1]
    block = min(256, rows)
    out_spec = pl.BlockSpec((block, width), lambda i: (i, 0))
    return pl.pallas_call(
        heads_kernel,
        grid=(rows // block,),
        in_specs=[
            pl.BlockSpec((block, cols), lambda i: (i, 0)),
            pl.BlockSpec((3, block, cols), lambda i: (0, i, 0)),
            pl.BlockSpec((4, width, cols), lambda i: (0, 0, 0)),
        ],
        out_specs=[out_spec, out_spec],
        out_shape=[shape((rows, width), low)] * 2,
        compiler_params=params(),
        cost_estimate=cost(8 * rows * width * cols, 4 * rows * width + 8 * (rows + width) * cols),
        name="heads_parts",
    )(context, mixed_grad, w_attend)


def early_kernel(act_ref, grad_ref, w_ref, hid_in_ref, out_in_ref, hid_ref, out_ref):
    hid = hid_in_ref[...].astype(full) + dot_tn(grad_ref[...], join_gates(w_ref))
    hid_ref[...] = hid.astype(low)
    out = out_in_ref[...].astype(full) + dot_tn(act_ref[...], w_ref[2])
    out_ref[...] = out.astype(low)


def early_parts(active, gates_grad, w_feed, hid, out):
    rows, width = hid.shape
    units = w_feed.shape[1]
    block = min(256, rows)
    row_spec = pl.BlockSpec((block, width), lambda i: (i, 0))
    return pl.pallas_call(
        early_kernel,
        grid=(rows // block,),
        in_specs=[
            pl.BlockSpec((units, block), lambda i: (0, i)),
            pl.BlockSpec((2 * units, block), lambda i: (0, i)),
            pl.BlockSpec((3, units, width), lambda i: (0, 0, 0)),
            row_spec,
            row_spec,
        ],
        out_specs=[row_spec, row_spec],
        out_shape=[shape((rows, width), low)] * 2,
        compiler_params=params(),
        cost_estimate=cost(6 * rows * width * units, 8 * rows * width + 6 * (rows + width) * units),
        name="early_parts",
    )(active, gates_grad, w_feed, hid, out)


def sixteenth(which, m):
    return m[0] * 8 + (m[1] * 2 + m[2] if which == 0 else 4 + m[2] * 2 + m[1])


def back_kernel(info_ref, *refs):
    p_ref = refs[6]
    total = 0.0
    for x_ref, near_ref, far_ref, back_ref in zip(refs[0:2], refs[2:4], refs[4:6], refs[7:9]):
        x = x_ref[...].astype(full)
        centred = x - jnp.mean(x, axis=-1, keepdims=True)
        inv = lax.rsqrt(jnp.mean(centred * centred, axis=-1, keepdims=True) + epsilon)
        normal = centred * inv
        grad = near_ref[...].astype(full) + far_ref[...].astype(full)
        scaled = grad * p_ref[0:1]
        back = inv * (
            scaled
            - jnp.mean(scaled, axis=-1, keepdims=True)
            - normal * jnp.mean(scaled * normal, axis=-1, keepdims=True)
        )
        back_ref[: x.shape[0]] = back.astype(low)
        total += jnp.concatenate(
            [jnp.sum(grad * normal, axis=0, keepdims=True), jnp.sum(grad, axis=0, keepdims=True)],
            axis=0,
        )
    high = total.astype(low)
    rest = total - high.astype(full)
    middle = rest.astype(low)
    small = (rest - middle.astype(full)).astype(low)
    zeros = jnp.zeros((tail_rows - 6, total.shape[1]), full)
    terms = [high.astype(full), middle.astype(full), small.astype(full), zeros]
    refs[7][refs[0].shape[0] :] = jnp.concatenate(terms, axis=0).astype(low)


def back_rows(info, rows, near, far, norm_params):
    count, width = near[0].shape
    spec = pl.BlockSpec((count, width), lambda i, m: (0, 0))
    pair = pl.BlockSpec((2, width), lambda i, m: (0, 0))
    return pl.pallas_call(
        back_kernel,
        grid_spec=pltpu.PrefetchScalarGridSpec(
            num_scalar_prefetch=1,
            grid=(1,),
            in_specs=[
                pl.BlockSpec((count, width), lambda i, m: (sixteenth(0, m), 0)),
                pl.BlockSpec((count, width), lambda i, m: (sixteenth(1, m), 0)),
            ]
            + [spec] * 4
            + [pair],
            out_specs=[pl.BlockSpec((count + tail_rows, width), lambda i, m: (0, 0)), spec],
        ),
        out_shape=[shape((count + tail_rows, width), low), shape((count, width), low)],
        compiler_params=params(),
        cost_estimate=cost(40 * count * width, 16 * count * width),
        name="back_rows",
    )(info, rows, rows, *near, *far, norm_params)


def add_kernel(info_ref, *refs):
    for x_ref, near_ref, far_ref, out_ref in zip(refs[0:2], refs[2:4], refs[4:6], refs[6:8]):
        total = x_ref[...].astype(full) + near_ref[...].astype(full) + far_ref[...].astype(full)
        out_ref[...] = total.astype(low)


def add_rows(info, rows, near, far):
    count, width = near[0].shape
    spec = pl.BlockSpec((count, width), lambda i, m: (0, 0))
    return pl.pallas_call(
        add_kernel,
        grid_spec=pltpu.PrefetchScalarGridSpec(
            num_scalar_prefetch=1,
            grid=(1,),
            in_specs=[
                pl.BlockSpec((count, width), lambda i, m: (sixteenth(0, m), 0)),
                pl.BlockSpec((count, width), lambda i, m: (sixteenth(1, m), 0)),
            ]
            + [spec] * 4,
            out_specs=[spec, spec],
        ),
        out_shape=[shape((count, width), low)] * 2,
        compiler_params=params(),
        cost_estimate=cost(4 * count * width, 16 * count * width),
        name="add_rows",
    )(info, rows, rows, *near, *far)


def pack_kernel(block, info_ref, *refs):
    pieces, out_ref, sems = refs[:8], refs[8], refs[9]
    x, y = info_ref[1], info_ref[2]
    copies = []

    def move(source, at, size):
        place = out_ref.at[pl.ds(pl.multiple_of(at, 16), size), :]
        copies.append(pltpu.make_async_copy(source, place, sems.at[len(copies)]))

    for i, piece in enumerate(pieces):
        high, small = (i // 2) % 2, i % 2
        if i < 4:
            at = (x ^ high) * 2 + (y ^ small)
        else:
            at = 4 + (y ^ high) * 2 + (x ^ small)
        extra = piece.shape[0] - block
        move(piece.at[pl.ds(0, block), :], at * block, block)
        if extra:
            move(piece.at[pl.ds(block, extra), :], 8 * block + at * extra, extra)
    for copy in copies:
        copy.start()
    for copy in copies:
        copy.wait()


def pack_rows(info, pieces):
    block, width = pieces[-1].shape
    extra = pieces[0].shape[0] - block
    return pl.pallas_call(
        functools.partial(pack_kernel, block),
        grid_spec=pltpu.PrefetchScalarGridSpec(
            num_scalar_prefetch=1,
            grid=(1,),
            in_specs=[pl.BlockSpec(piece.shape, lambda i, m: (0, 0)) for piece in pieces],
            out_specs=pl.BlockSpec(memory_space=pl.ANY),
            scratch_shapes=[pltpu.SemaphoreType.DMA((12,))],
        ),
        out_shape=shape((8 * block + 4 * extra, width), low),
        compiler_params=params(),
        cost_estimate=cost(0, 32 * block * width),
        name="pack_rows",
    )(info, *pieces)


def tail_total(ref):
    values = ref[...].astype(full)
    sums = 0.0
    for i in range(4):
        at = i * tail_rows
        sums += values[at : at + 2] + values[at + 2 : at + 4] + values[at + 4 : at + 6]
    return sums


def tail_kernel(own_ref, other_ref, out_ref):
    out_ref[...] = tail_total(own_ref) + tail_total(other_ref)


def tail_sums(own, other):
    count, width = own.shape
    size = 4 * tail_rows
    spec = pl.BlockSpec((size, width), lambda i: (count // size - 1, 0))
    return pl.pallas_call(
        tail_kernel,
        grid=(1,),
        in_specs=[spec, spec],
        out_specs=pl.BlockSpec((2, width), lambda i: (0, 0)),
        out_shape=shape((2, width), full),
        compiler_params=params(),
        cost_estimate=cost(20 * width, 512 * width),
        name="tail_sums",
    )(own, other)


def finish_kernel(info_ref, *refs):
    mine = (pl.program_id(0) // 4) == info_ref[0]
    out_ref = refs[-1]

    def store(value):
        if len(refs) > 3:
            value = refs[2][...].astype(full) + value.astype(full)
        out_ref[...] = value

    @pl.when(mine)
    def _():
        store(refs[0][...])

    @pl.when(jnp.logical_not(mine))
    def _():
        store(refs[1][...])


def finish_rows(info, rows, own, other, cot=None):
    width = own.shape[1]
    block = rows // 8
    spec = pl.BlockSpec((block, width), lambda i, m: (i, 0))
    edge = lambda i: jnp.where(i < 4, 0, 3)
    extra = () if cot is None else (cot,)
    return pl.pallas_call(
        finish_kernel,
        grid_spec=pltpu.PrefetchScalarGridSpec(
            num_scalar_prefetch=1,
            grid=(8,),
            in_specs=[
                pl.BlockSpec((block, width), lambda i, m: (jnp.where(i // 4 == m[0], i % 4, edge(i)), 0)),
                pl.BlockSpec((block, width), lambda i, m: (jnp.where(i // 4 == m[0], edge(i), i % 4), 0)),
            ]
            + [spec] * len(extra),
            out_specs=spec,
        ),
        out_shape=shape((rows, width), low if cot is None else full),
        compiler_params=params(),
        cost_estimate=cost(2 * rows * width, 8 * rows * width),
        name="finish_rows",
    )(info, own, other, *extra)


def update_kernel(rates, count, *refs):
    g_ref = refs[0]
    ins = refs[1:7]
    outs = refs[7 + count :]
    for which, rate in enumerate(rates):
        grad = g_ref[:2] if which == 0 else g_ref[2]
        grad = grad.astype(full)
        w, m, a = (ref[...] for ref in ins[3 * which : 3 * which + 3])
        g_out, w_out, m_out, a_out = outs[4 * which : 4 * which + 4]
        g_out[...] = grad
        w_out[...], m_out[...], a_out[...] = advance(w, grad, m, a, rate)


def update_feed(start, grads, states, rates, begun=()):
    _, units, piece = grads.shape
    block = math.gcd(start, units)
    while block > 128 and block % 16 == 0:
        block //= 2
    at = start // block
    pair = pl.BlockSpec((2, block, piece), lambda i: (0, at + i, 0))
    single = pl.BlockSpec((block, piece), lambda i: (at + i, 0))
    total = states[0].shape[1]
    return pl.pallas_call(
        functools.partial(update_kernel, rates, len(begun)),
        grid=(units // block,),
        in_specs=[pl.BlockSpec((3, block, piece), lambda i: (0, i, 0))]
        + [pair] * 3
        + [single] * 3
        + [pl.BlockSpec(memory_space=pl.ANY)] * len(begun),
        out_specs=[pair] * 4 + [single] * 4,
        out_shape=[shape((2, total, piece), full)] * 4 + [shape((total, piece), full)] * 4,
        input_output_aliases={7 + i: i for i in range(len(begun))},
        compiler_params=params(),
        cost_estimate=cost(30 * units * piece, 3 * 30 * units * piece),
        name="update_feed",
    )(grads, *states, *begun)


def body(
    inputs,
    positions,
    cotangent,
    w_attend_in,
    w_attend_out,
    w_expand,
    w_reduce,
    norm_params,
    attend_bias,
    moment_attend_in,
    moment_attend_out,
    moment_expand,
    moment_reduce,
    moment_norm,
    moment_bias,
    average_attend_in,
    average_attend_out,
    average_expand,
    average_reduce,
    average_norm,
    average_bias,
):
    batch, length, width = inputs.shape
    rows = batch * length
    units = w_expand.shape[2]
    n = lax.axis_size("dp")
    group = lax.axis_size("mp")
    spot = lax.axis_index("mp").astype(jnp.int32)
    info = jnp.stack([spot & 1, (spot >> 1) & 1, (spot >> 2) & 1])
    fast = group == 8 and n == 4

    expand_t = jnp.transpose(w_expand, (1, 2, 0))
    reduce_t = jnp.transpose(w_reduce)
    in_t = jnp.transpose(w_attend_in, (1, 0, 2))
    cut = units * 7 // 11 // 16 * 16
    shards = [
        jnp.concatenate([expand_t[:, a:b], reduce_t[None, a:b]], axis=0).astype(low)
        for a, b in ((0, cut), (cut, units))
    ]
    attend_shard = jnp.concatenate([in_t, w_attend_out[None]], axis=0).astype(low)
    attend_all = lax.all_gather(attend_shard, "dp")
    first_all = lax.all_gather(after(shards[0], attend_shard), "dp")
    last_all = lax.all_gather(after(shards[1], shards[0]), "dp")

    tokens = inputs.reshape(rows, width)
    cot = cotangent.reshape(rows, width)
    hidden = layer_norm(tokens, norm_params)

    half = ROT // 2
    lane = jnp.arange(128, dtype=jnp.int32) % HD
    frequency = 10000.0 ** (-((lane % half).astype(full) * 2.0 / ROT))
    angles = positions.reshape(rows).astype(full)[:, None] * frequency[None, :]
    cosine = jnp.where(lane < ROT, jnp.cos(angles), 1.0)
    sine = jnp.where(lane < half, -jnp.sin(angles), jnp.where(lane < ROT, jnp.sin(angles), 0.0))

    def scatter(grads):
        return lax.psum_scatter(grads, "dp", scatter_dimension=0, tiled=False)

    q, k, v, o, w_attend = project(attend_all, hidden, cot, cosine, sine, attend_bias)
    context, mixed_grad, bias_part = attend(batch, q, k, v, o, cosine, sine)
    attend_grad = attend_grads(n, hidden, cot, mixed_grad, context)
    hid_early, out_early = heads_parts(context, mixed_grad, w_attend)
    first_all = after(first_all, attend_grad, hid_early, out_early)
    active, gates_grad, w_feed = feed_chunk(first_all, hidden, cot)
    hid_early, out_early = early_parts(active, gates_grad, w_feed, hid_early, out_early)
    first_grads = feed_grads(n, hidden, cot, active, gates_grad)
    last_all = after(last_all, first_grads, hid_early, out_early)
    first_grads = scatter(after(first_grads, last_all)).reshape(3, cut, -1)

    total_tokens = rows * n

    def update_attend(grad):
        grad = grad.astype(full)
        grad_in, grad_out = jnp.transpose(grad[:3], (1, 0, 2)), grad[3]
        rate_in = 0.5 / math.sqrt(width * total_tokens)
        rate_out = 1.8 / math.sqrt(width * batch * n)
        new_in = advance(w_attend_in, grad_in, moment_attend_in, average_attend_in, rate_in)
        new_out = advance(w_attend_out, grad_out, moment_attend_out, average_attend_out, rate_out)
        return (grad_in, grad_out) + new_in + new_out

    rates = (1.6 / math.sqrt(width * total_tokens), 0.77 / math.sqrt(FF * total_tokens))
    states = [jnp.transpose(a, (1, 2, 0)) for a in (w_expand, moment_expand, average_expand)]
    states += [jnp.transpose(a) for a in (w_reduce, moment_reduce, average_reduce)]

    if fast:
        s = rows // 16

        def swap_cores(parts):
            came = {i: swap(parts[i], 1) for i in (1, 3, 0, 2)}
            return [came[i] for i in range(4)]

        def sum_cores(own, came):
            own = [a.astype(full) + b.astype(full) for a, b in zip(own, came)]
            return own, (own[1].astype(low), own[3].astype(low))

        def sum_first(own, came):
            first = own[0] + came[0].astype(full)
            second = own[2] + came[1].astype(full)
            near = [first[:s].astype(low), second[:s].astype(low)]
            return near, (first[s:].astype(low), second[s:].astype(low))

        def both_ways(pair, masks):
            return [swap(pair[0], masks[0]), swap(pair[1], masks[1])]

        def join(one, first, second, third):
            pieces = (one, first, second, third)
            return pack_rows(info, [p[0] for p in pieces] + [p[1] for p in pieces])

        *parts, active, both, w_last = out_last(info, True, last_all, hidden, out_early)
        own_out, load_out = sum_cores(parts[4:], swap_cores(parts[:4]))
        one_out = both_ways(load_out, (2, 4))
        attend_grad = scatter(after(attend_grad, load_out))
        *parts, gates_grad = hid_last(info, True, w_last, after(both, load_out), cot, hid_early)
        came_hid = swap_cores(parts[:4])
        near_out, load_out = sum_first(own_out, after(one_out, parts[0]))
        two_out = both_ways(load_out, (4, 2))
        own_hid, load_hid = sum_cores(parts[4:], after(came_hid, load_out))
        one_hid = both_ways(load_hid, (2, 4))
        last_grads = feed_grads(n, hidden, cot, after(active, load_hid), gates_grad)
        two_out = after(two_out, last_grads)
        add = add_rows(info, tokens, near_out, two_out)
        last_grads = scatter(last_grads).reshape(3, units - cut, -1)
        out_one = both_ways(add, (4, 2))
        out_two = both_ways(add, (2, 4))
        near_hid, load_hid = sum_first(own_hid, after(one_hid, add))
        two_hid = both_ways(load_hid, (4, 2))
        back = back_rows(info, tokens, near_hid, two_hid, norm_params)
        hid_one = both_ways(back, (4, 2))
        hid_two = both_ways(back, (2, 4))
        out_one, out_two = after((out_one, out_two), back)
        out_three = both_ways(out_one, (2, 4))
        begun = update_feed(0, after(first_grads, out_one), states, rates)
        out_two, out_three = after((out_two, out_three), begun)
        mine_out = join(add, out_one, out_two, out_three)
        other_out = swap(mine_out, 1)
        hid_one, hid_two = after((hid_one, hid_two), mine_out)
        hid_three = both_ways(hid_one, (2, 4))
        mine_hid = join(back, hid_one, hid_two, hid_three)
        other_hid = swap(mine_hid, 1)
        attend_new = update_attend(after(attend_grad, mine_hid))
        other_hid = after(other_hid, attend_new)
        norm_part = tail_sums(mine_hid, other_hid)
        sums = join_sums(norm_part, bias_part)
        near_sums = swap(sums, 1, "dp")
        output = finish_rows(info, rows, after(mine_out, sums), other_out)
        near_sums = after(near_sums, output)
        sums = sums + near_sums
        far_sums = swap(sums, 2, "dp")
        input_grad = finish_rows(info, rows, mine_hid, after(other_hid, sums), cot)
        sums = sums + after(far_sums, input_grad)
        done = update_feed(cut, after(last_grads, input_grad), states, rates, begun)
        norm_grad, bias_grad = split_sums(sums, norm_part, bias_part)
    else:
        out_part, active, both, w_last = out_last(info, False, last_all, hidden, out_early)
        hid_part, gates_grad = hid_last(info, False, w_last, both, cot, hid_early)
        attend_new = update_attend(scatter(attend_grad))
        last_grads = scatter(feed_grads(n, hidden, cot, active, gates_grad)).reshape(3, units - cut, -1)
        hidden_grad = lax.psum(hid_part, "mp").astype(full)
        summed = lax.psum(out_part, "mp").astype(full)
        values = tokens.astype(full)
        output = (values + summed).astype(low)
        centred = values - jnp.mean(values, axis=-1, keepdims=True)
        inv = lax.rsqrt(jnp.mean(centred * centred, axis=-1, keepdims=True) + epsilon)
        normal = centred * inv
        scaled = hidden_grad * norm_params[0]
        back = inv * (
            scaled
            - jnp.mean(scaled, axis=-1, keepdims=True)
            - normal * jnp.mean(scaled * normal, axis=-1, keepdims=True)
        )
        input_grad = cot.astype(full) + back
        norm_part = jnp.stack([jnp.sum(hidden_grad * normal, axis=0), jnp.sum(hidden_grad, axis=0)])
        sums = small_sum(join_sums(norm_part, bias_part), "dp")
        norm_grad, bias_grad = split_sums(sums, norm_part, bias_part)
        begun = update_feed(0, first_grads, states, rates)
        done = update_feed(cut, last_grads, states, rates, begun)
    grad_in, grad_out = attend_new[:2]
    new_in, moment_in_new, average_in_new = attend_new[2:5]
    new_out, moment_out_new, average_out_new = attend_new[5:]
    grad_expand, new_expand, moment_expand_new, average_expand_new = (
        jnp.transpose(a, (2, 0, 1)) for a in done[:4]
    )
    grad_reduce, new_reduce, moment_reduce_new, average_reduce_new = (
        jnp.transpose(a) for a in done[4:]
    )
    input_grad = input_grad.reshape(batch, length, width)
    output = output.reshape(batch, length, width)
    new_norm, moment_norm_new, average_norm_new = advance(
        norm_params, norm_grad, moment_norm, average_norm, 0.06 / math.sqrt(total_tokens)
    )
    new_bias, moment_bias_new, average_bias_new = advance(
        attend_bias, bias_grad, moment_bias, average_bias, 0.25 / math.sqrt(total_tokens)
    )
    return (
        output,
        input_grad,
        grad_in,
        grad_out,
        grad_expand,
        grad_reduce,
        norm_grad,
        bias_grad,
        new_in,
        new_out,
        new_expand,
        new_reduce,
        new_norm,
        new_bias,
        moment_in_new,
        moment_out_new,
        moment_expand_new,
        moment_reduce_new,
        moment_norm_new,
        moment_bias_new,
        average_in_new,
        average_out_new,
        average_expand_new,
        average_reduce_new,
        average_norm_new,
        average_bias_new,
    )


def solution(mesh):
    rows3 = P("dp", None, None)
    in3 = P("dp", None, "mp")
    in2 = P("dp", "mp")
    bias = P(None, "mp")
    states = (in3, in2, in3, in2, P(), bias)
    return jax.shard_map(
        body,
        mesh=mesh,
        in_specs=(rows3, P("dp", None), rows3) + states * 3,
        out_specs=(rows3, rows3) + states * 4,
        check_vma=False,
    )
```

```python
import functools
import math

import jax
import jax.numpy as jnp
from jax import lax
from jax.experimental import pallas as pl
from jax.experimental.pallas import tpu as pltpu
from jax.sharding import PartitionSpec as P

HD = 64
ROT = 16
FF = 5632

epsilon = 1e-05
decay_moment = 0.9
decay_average = 0.9
masked_score = -1e30

low = jnp.bfloat16
full = jnp.float32
vmem_limit = 60 << 20
tail_rows = 16


def dot_nt(left, right):
    return lax.dot_general(left, right, (((1,), (1,)), ((), ())), preferred_element_type=full)


def dot_nn(left, right):
    return lax.dot_general(left, right, (((1,), (0,)), ((), ())), preferred_element_type=full)


def dot_tn(left, right):
    return lax.dot_general(left, right, (((0,), (0,)), ((), ())), preferred_element_type=full)


def params(**more):
    return pltpu.CompilerParams(vmem_limit_bytes=vmem_limit, **more)


def cost(flops, moved, trans=0):
    return pl.CostEstimate(flops=int(flops), bytes_accessed=int(moved), transcendentals=int(trans))


def shape(dims, kind):
    return jax.ShapeDtypeStruct(dims, kind)


def advance(weight, grad, moment, average, rate):
    moment_new = decay_moment * moment + grad
    weight_new = weight - rate * (grad + decay_moment * moment_new)
    average_new = decay_average * average + (1.0 - decay_average) * weight_new
    return (weight_new, moment_new, average_new)


def after(value, *others):
    return lax.optimization_barrier((value, others))[0]


def swap(value, mask, axis="mp"):
    n = lax.axis_size(axis)
    return lax.ppermute(value, axis, [(a, a ^ mask) for a in range(n)])


def small_sum(value, axis):
    n = lax.axis_size(axis)
    if n & (n - 1):
        return lax.psum(value, axis)
    mask = 1
    while mask < n:
        value = value + swap(value, mask, axis)
        mask *= 2
    return value


def join_sums(norm_part, bias_part):
    cols = bias_part.shape[1]
    return jnp.concatenate([norm_part.reshape(-1, cols), bias_part])


def split_sums(sums, norm_part, bias_part):
    count = sums.shape[0] - bias_part.shape[0]
    return sums[:count].reshape(norm_part.shape), sums[count:]


def norm_kernel(x_ref, p_ref, o_ref):
    x = x_ref[...].astype(full)
    centred = x - jnp.mean(x, axis=-1, keepdims=True)
    inv = lax.rsqrt(jnp.mean(centred * centred, axis=-1, keepdims=True) + epsilon)
    o_ref[...] = (centred * inv * p_ref[0:1] + p_ref[1:2]).astype(low)


def layer_norm(rows, norm_params):
    count, width = rows.shape
    block = min(256, count)
    return pl.pallas_call(
        norm_kernel,
        grid=(count // block,),
        in_specs=[
            pl.BlockSpec((block, width), lambda i: (i, 0)),
            pl.BlockSpec((2, width), lambda i: (0, 0)),
        ],
        out_specs=pl.BlockSpec((block, width), lambda i: (i, 0)),
        out_shape=shape((count, width), low),
        compiler_params=params(),
        cost_estimate=cost(8 * count * width, 4 * count * width),
        name="layer_norm",
    )(rows, norm_params)


def fetch(gathered, target_of, sems):
    copies = [
        pltpu.make_async_copy(gathered.at[j], target_of(j), sems.at[j]) for j in range(gathered.shape[0])
    ]
    for copy in copies:
        copy.start()
    for copy in copies:
        copy.wait()


def swish_of(both):
    units = both.shape[0] // 2
    gate, upper = both[:units], both[units:]
    sigmoid = jax.nn.sigmoid(gate)
    return gate, upper, sigmoid, gate * sigmoid


def join_gates(w_ref):
    return w_ref[0:2].reshape(2 * w_ref.shape[1], w_ref.shape[2])


def gates_grad_of(both, active_grad):
    gate, upper, sigmoid, swish = swish_of(both)
    gate_grad = active_grad * upper * sigmoid * (1.0 + gate * (1.0 - sigmoid))
    return jnp.concatenate([gate_grad, active_grad * swish], axis=0).astype(low)


def gates_of(w_ref, h, c):
    both = dot_nt(join_gates(w_ref), h)
    _, upper, _, swish = swish_of(both)
    return (swish * upper).astype(low), gates_grad_of(both, dot_nt(w_ref[2], c))


def add_grads(acc, step, active, gates_grad, h, c):
    units = active.shape[0]

    @pl.when(step == 0)
    def _():
        acc[: 2 * units] = dot_nn(gates_grad, h)
        acc[2 * units :] = dot_nn(active, c)

    @pl.when(step > 0)
    def _():
        acc[: 2 * units] += dot_nn(gates_grad, h)
        acc[2 * units :] += dot_nn(active, c)


def store_grads(n, acc, out_ref):
    piece = out_ref.shape[2]
    for j in range(n):
        out_ref[j] = acc[:, j * piece : (j + 1) * piece].astype(low)


def wide_target(w_ref, piece):
    return lambda index: w_ref.at[:, :, pl.ds(index * piece, piece)]


def feed_kernel(shards_ref, h_ref, c_ref, act_ref, grad_ref, w_ref, sems):
    @pl.when(pl.program_id(0) == 0)
    def _():
        fetch(shards_ref, wide_target(w_ref, shards_ref.shape[3]), sems)

    act_ref[...], grad_ref[...] = gates_of(w_ref, h_ref[...], c_ref[...])


def feed_chunk(shards, hidden, cot):
    rows, width = hidden.shape
    n, _, units, _ = shards.shape
    block = min(512, rows)
    row_spec = pl.BlockSpec((block, width), lambda i: (i, 0))
    return pl.pallas_call(
        feed_kernel,
        grid=(rows // block,),
        in_specs=[pl.BlockSpec(memory_space=pl.ANY), row_spec, row_spec],
        out_specs=[
            pl.BlockSpec((units, block), lambda i: (0, i)),
            pl.BlockSpec((2 * units, block), lambda i: (0, i)),
            pl.BlockSpec((3, units, width), lambda i: (0, 0, 0)),
        ],
        out_shape=[
            shape((units, rows), low),
            shape((2 * units, rows), low),
            shape((3, units, width), low),
        ],
        scratch_shapes=[pltpu.SemaphoreType.DMA((n,))],
        compiler_params=params(),
        cost_estimate=cost(
            6 * rows * width * units, 4 * rows * width + 12 * units * width, rows * units
        ),
        name="feed_chunk",
    )(shards, hidden, cot)


def put_part(split, info_ref, parts, value):
    if not split:
        parts[0][...] = value.astype(low)
        return
    step = pl.program_id(0)
    sub = value.shape[0] // 4
    high = jnp.where(step % 2 == 0, info_ref[1], info_ref[2])
    small = jnp.where(step % 2 == 0, info_ref[2], info_ref[1])
    first, second = value[: 2 * sub], value[2 * sub :]
    near = jnp.where(high == 0, first, second).astype(low)
    far = jnp.where(high == 0, second, first).astype(low)
    for at in range(4):

        @pl.when(step == at)
        def _(at=at):
            for ref, pair in ((parts[2 * at], near), (parts[2 * at + 1], far)):
                for i in range(2):
                    place = pl.ds(pl.multiple_of((i ^ small) * sub, sub), sub)
                    ref[place, :] = pair[i * sub : (i + 1) * sub]


def last_blocks(split, rows, width):
    if split:
        block, steps = rows // 4, 4
        place = lambda i, m: (m[0] ^ (1 - i // 2)) * 2 + i % 2
        part_specs = [pl.BlockSpec((block // 2, width), lambda i, m: (0, 0))] * 8
        part_shapes = [shape((block // 2, width), low)] * 8
    else:
        block = min(256, rows)
        steps = rows // block
        place = lambda i, m: i
        part_specs = [pl.BlockSpec((block, width), lambda i, m: (i, 0))]
        part_shapes = [shape((rows, width), low)]
    return block, steps, place, part_specs, part_shapes


def out_last_kernel(split, info_ref, shards_ref, h_ref, early_ref, *refs):
    parts = refs[:-4]
    act_ref, both_ref, w_ref, sems = refs[-4:]

    @pl.when(pl.program_id(0) == 0)
    def _():
        fetch(shards_ref, wide_target(w_ref, shards_ref.shape[3]), sems)

    both = dot_nt(join_gates(w_ref), h_ref[...])
    both_ref[...] = both
    _, upper, _, swish = swish_of(both)
    active = (swish * upper).astype(low)
    act_ref[...] = active
    put_part(split, info_ref, parts, early_ref[...].astype(full) + dot_tn(active, w_ref[2]))


def out_last(info, split, shards, hidden, early):
    rows, width = hidden.shape
    n, _, units, _ = shards.shape
    block, steps, place, part_specs, part_shapes = last_blocks(split, rows, width)
    row_spec = pl.BlockSpec((block, width), lambda i, m: (place(i, m), 0))
    return pl.pallas_call(
        functools.partial(out_last_kernel, split),
        grid_spec=pltpu.PrefetchScalarGridSpec(
            num_scalar_prefetch=1,
            grid=(steps,),
            in_specs=[pl.BlockSpec(memory_space=pl.ANY)] + [row_spec] * 2,
            out_specs=part_specs
            + [
                pl.BlockSpec((units, block), lambda i, m: (0, place(i, m))),
                pl.BlockSpec((2 * units, block), lambda i, m: (0, place(i, m))),
                pl.BlockSpec((3, units, width), lambda i, m: (0, 0, 0)),
            ],
            scratch_shapes=[pltpu.SemaphoreType.DMA((n,))],
        ),
        out_shape=part_shapes
        + [shape((units, rows), low), shape((2 * units, rows), full), shape((3, units, width), low)],
        compiler_params=params(),
        cost_estimate=cost(6 * rows * width * units, 8 * rows * width, rows * units),
        name="out_last",
    )(info, shards, hidden, early)


def hid_last_kernel(split, info_ref, w_ref, both_ref, c_ref, early_ref, *refs):
    grad_ref = refs[-1]
    gates_grad = gates_grad_of(both_ref[...], dot_nt(w_ref[2], c_ref[...]))
    grad_ref[...] = gates_grad
    hid = early_ref[...].astype(full) + dot_tn(gates_grad, join_gates(w_ref))
    put_part(split, info_ref, refs[:-1], hid)


def hid_last(info, split, weights, both, cot, early):
    rows, width = cot.shape
    units = weights.shape[1]
    block, steps, place, part_specs, part_shapes = last_blocks(split, rows, width)
    row_spec = pl.BlockSpec((block, width), lambda i, m: (place(i, m), 0))
    both_spec = pl.BlockSpec((2 * units, block), lambda i, m: (0, place(i, m)))
    return pl.pallas_call(
        functools.partial(hid_last_kernel, split),
        grid_spec=pltpu.PrefetchScalarGridSpec(
            num_scalar_prefetch=1,
            grid=(steps,),
            in_specs=[pl.BlockSpec((3, units, width), lambda i, m: (0, 0, 0)), both_spec]
            + [row_spec] * 2,
            out_specs=part_specs + [both_spec],
        ),
        out_shape=part_shapes + [shape((2 * units, rows), low)],
        compiler_params=params(),
        cost_estimate=cost(6 * rows * width * units, 8 * rows * width, rows * units),
        name="hid_last",
    )(info, weights, both, cot, early)


def feed_grads_kernel(n, steps, h_ref, c_ref, act_ref, grad_ref, out_ref, acc):
    step = pl.program_id(0)
    add_grads(acc, step, act_ref[...], grad_ref[...], h_ref[...], c_ref[...])

    @pl.when(step == steps - 1)
    def _():
        store_grads(n, acc, out_ref)


def feed_grads(n, hidden, cot, active, gates_grad):
    rows, width = hidden.shape
    units = active.shape[0]
    piece = width // n
    block = min(512, rows)
    steps = rows // block
    row_spec = pl.BlockSpec((block, width), lambda i: (i, 0))
    return pl.pallas_call(
        functools.partial(feed_grads_kernel, n, steps),
        grid=(steps,),
        in_specs=[
            row_spec,
            row_spec,
            pl.BlockSpec((units, block), lambda i: (0, i)),
            pl.BlockSpec((2 * units, block), lambda i: (0, i)),
        ],
        out_specs=pl.BlockSpec((n, 3 * units, piece), lambda i: (0, 0, 0)),
        out_shape=shape((n, 3 * units, piece), low),
        scratch_shapes=[pltpu.VMEM((3 * units, width), full)],
        compiler_params=params(),
        cost_estimate=cost(6 * rows * width * units, 4 * rows * width + 12 * units * width),
        name="feed_grads",
    )(hidden, cot, active, gates_grad)


def turn(values, cosine, sine, half):
    cols = values.shape[1]
    lane = lax.broadcasted_iota(jnp.int32, (1, cols), 1) % HD
    other = jnp.where(
        lane < half, pltpu.roll(values, cols - half, 1), pltpu.roll(values, half, 1)
    )
    repeat = cols // cosine.shape[1]
    if repeat > 1:
        cosine = jnp.concatenate([cosine] * repeat, axis=1)
        sine = jnp.concatenate([sine] * repeat, axis=1)
    return values * cosine + other * sine


def project_kernel(shards_ref, h_ref, c_ref, cos_ref, sin_ref, bias_ref, q_ref, k_ref, v_ref, o_ref, w_ref, sems):
    piece = shards_ref.shape[2]

    @pl.when(pl.program_id(0) == 0)
    def _():
        fetch(shards_ref, lambda index: w_ref.at[:, pl.ds(index * piece, piece), :], sems)

    h = h_ref[...]
    cosine, sine = cos_ref[...], sin_ref[...]
    half = ROT // 2
    q_ref[...] = turn(dot_nn(h, w_ref[0]) + bias_ref[0:1], cosine, sine, half).astype(low)
    k_ref[...] = turn(dot_nn(h, w_ref[1]) + bias_ref[1:2], cosine, sine, half).astype(low)
    v_ref[...] = (dot_nn(h, w_ref[2]) + bias_ref[2:3]).astype(low)
    o_ref[...] = dot_nn(c_ref[...], w_ref[3]).astype(low)


def project(shards, hidden, cot, cosine, sine, bias):
    rows, width = hidden.shape
    n, _, _, cols = shards.shape
    block = min(512, rows)
    row_spec = pl.BlockSpec((block, width), lambda i: (i, 0))
    angle_spec = pl.BlockSpec((block, 128), lambda i: (i, 0))
    out_spec = pl.BlockSpec((block, cols), lambda i: (i, 0))
    return pl.pallas_call(
        project_kernel,
        grid=(rows // block,),
        in_specs=[pl.BlockSpec(memory_space=pl.ANY), row_spec, row_spec, angle_spec, angle_spec]
        + [pl.BlockSpec((3, cols), lambda i: (0, 0))],
        out_specs=[out_spec] * 4 + [pl.BlockSpec((4, width, cols), lambda i: (0, 0, 0))],
        out_shape=[shape((rows, cols), low)] * 4 + [shape((4, width, cols), low)],
        scratch_shapes=[pltpu.SemaphoreType.DMA((n,))],
        compiler_params=params(),
        cost_estimate=cost(8 * rows * width * cols, 4 * rows * width + 16 * width * cols),
        name="project",
    )(shards, hidden, cot, cosine, sine, bias)


def attend_kernel(block, q_ref, k_ref, v_ref, o_ref, cos_ref, sin_ref, ctx_ref, mg_ref, bias_ref, dq, dk, dv):
    length, lanes = q_ref.shape
    scale = HD ** (-0.5)
    for head in range(lanes // HD):
        cols = slice(head * HD, (head + 1) * HD)
        for i in range(length // block):
            rows = slice(i * block, (i + 1) * block)
            end = (i + 1) * block
            q = q_ref[rows, cols]
            o = o_ref[rows, cols]
            k = k_ref[:end, cols]
            v = v_ref[:end, cols]
            scores = dot_nt(q, k) * scale
            row = i * block + lax.broadcasted_iota(jnp.int32, (block, end), 0)
            col = lax.broadcasted_iota(jnp.int32, (block, end), 1)
            scores = jnp.where(col <= row, scores, masked_score)
            top = jnp.max(scores, axis=-1, keepdims=True)
            weights = jnp.exp(scores - top)
            probs = weights * (1.0 / jnp.sum(weights, axis=-1, keepdims=True))
            probs_low = probs.astype(low)
            ctx_ref[rows, cols] = dot_nn(probs_low, v).astype(low)
            prob_grads = dot_nt(o, v)
            middle = jnp.sum(probs * prob_grads, axis=-1, keepdims=True)
            score_grads = (probs * (prob_grads - middle)).astype(low)
            dq[rows, cols] = dot_nn(score_grads, k) * scale
            key_part = dot_tn(score_grads, q) * scale
            value_part = dot_tn(probs_low, o)
            if i == 0:
                dk[:end, cols] = key_part
                dv[:end, cols] = value_part
                if end < length:
                    dk[end:, cols] = jnp.zeros((length - end, HD), full)
                    dv[end:, cols] = jnp.zeros((length - end, HD), full)
            else:
                dk[:end, cols] += key_part
                dv[:end, cols] += value_part
    cosine, sine = cos_ref[...], -sin_ref[...]
    half = ROT // 2
    sums = []
    for part, grads in enumerate(
        (turn(dq[...], cosine, sine, half), turn(dk[...], cosine, sine, half), dv[...])
    ):
        rounded = grads.astype(low)
        mg_ref[part] = rounded
        sums.append(jnp.sum(rounded.astype(full), axis=0, keepdims=True))
    total = jnp.concatenate(sums, axis=0)

    @pl.when(pl.program_id(1) == 0)
    def _():
        bias_ref[...] = total

    @pl.when(pl.program_id(1) > 0)
    def _():
        bias_ref[...] += total


def attend(batch, q, k, v, o, cosine, sine):
    rows, cols = q.shape
    length = rows // batch
    lanes = 128
    spec = pl.BlockSpec((length, lanes), lambda p, b: (b, p))
    angle_spec = pl.BlockSpec((length, 128), lambda p, b: (b, 0))
    return pl.pallas_call(
        functools.partial(attend_kernel, min(512, length)),
        grid=(cols // lanes, batch),
        in_specs=[spec] * 4 + [angle_spec] * 2,
        out_specs=[
            spec,
            pl.BlockSpec((3, length, lanes), lambda p, b: (0, b, p)),
            pl.BlockSpec((3, lanes), lambda p, b: (0, p)),
        ],
        out_shape=[
            shape((rows, cols), low),
            shape((3, rows, cols), low),
            shape((3, cols), full),
        ],
        scratch_shapes=[pltpu.VMEM((length, lanes), full)] * 3,
        compiler_params=params(),
        cost_estimate=cost(
            40 * rows * length * cols, 20 * rows * cols, rows * length * cols // HD
        ),
        name="attend",
    )(q, k, v, o, cosine, sine)


def attend_grads_kernel(h_ref, c_ref, mg_ref, ctx_ref, out_ref, wide):
    cols = ctx_ref.shape[1]

    @pl.when(pl.program_id(0) == 0)
    def _():
        for part in range(3):
            wide[:, part * cols : (part + 1) * cols] = mg_ref[part]

    grad = dot_tn(h_ref[...], wide[...])
    for part in range(3):
        out_ref[0, part] = grad[:, part * cols : (part + 1) * cols].astype(low)
    out_ref[0, 3] = dot_tn(c_ref[...], ctx_ref[...]).astype(low)


def attend_grads(n, hidden, cot, mixed_grad, context):
    rows, width = hidden.shape
    cols = context.shape[1]
    piece = width // n
    cut_spec = pl.BlockSpec((rows, piece), lambda i: (0, i))
    return pl.pallas_call(
        attend_grads_kernel,
        grid=(n,),
        in_specs=[
            cut_spec,
            cut_spec,
            pl.BlockSpec((3, rows, cols), lambda i: (0, 0, 0)),
            pl.BlockSpec((rows, cols), lambda i: (0, 0)),
        ],
        out_specs=pl.BlockSpec((1, 4, piece, cols), lambda i: (i, 0, 0, 0)),
        out_shape=shape((n, 4, piece, cols), low),
        scratch_shapes=[pltpu.VMEM((rows, 3 * cols), low)],
        compiler_params=params(),
        cost_estimate=cost(8 * rows * width * cols, 4 * rows * width + 16 * width * cols),
        name="attend_grads",
    )(hidden, cot, mixed_grad, context)


def heads_kernel(ctx_ref, mg_ref, wa_ref, hid_ref, out_ref):
    hid = dot_nt(mg_ref[0], wa_ref[0]) + dot_nt(mg_ref[1], wa_ref[1]) + dot_nt(mg_ref[2], wa_ref[2])
    hid_ref[...] = hid.astype(low)
    out_ref[...] = dot_nt(ctx_ref[...], wa_ref[3]).astype(low)


def heads_parts(context, mixed_grad, w_attend):
    rows, cols = context.shape
    width = w_attend.shape[1]
    block = min(256, rows)
    out_spec = pl.BlockSpec((block, width), lambda i: (i, 0))
    return pl.pallas_call(
        heads_kernel,
        grid=(rows // block,),
        in_specs=[
            pl.BlockSpec((block, cols), lambda i: (i, 0)),
            pl.BlockSpec((3, block, cols), lambda i: (0, i, 0)),
            pl.BlockSpec((4, width, cols), lambda i: (0, 0, 0)),
        ],
        out_specs=[out_spec, out_spec],
        out_shape=[shape((rows, width), low)] * 2,
        compiler_params=params(),
        cost_estimate=cost(8 * rows * width * cols, 4 * rows * width + 8 * (rows + width) * cols),
        name="heads_parts",
    )(context, mixed_grad, w_attend)


def early_kernel(act_ref, grad_ref, w_ref, hid_in_ref, out_in_ref, hid_ref, out_ref):
    hid = hid_in_ref[...].astype(full) + dot_tn(grad_ref[...], join_gates(w_ref))
    hid_ref[...] = hid.astype(low)
    out = out_in_ref[...].astype(full) + dot_tn(act_ref[...], w_ref[2])
    out_ref[...] = out.astype(low)


def early_parts(active, gates_grad, w_feed, hid, out):
    rows, width = hid.shape
    units = w_feed.shape[1]
    block = min(256, rows)
    row_spec = pl.BlockSpec((block, width), lambda i: (i, 0))
    return pl.pallas_call(
        early_kernel,
        grid=(rows // block,),
        in_specs=[
            pl.BlockSpec((units, block), lambda i: (0, i)),
            pl.BlockSpec((2 * units, block), lambda i: (0, i)),
            pl.BlockSpec((3, units, width), lambda i: (0, 0, 0)),
            row_spec,
            row_spec,
        ],
        out_specs=[row_spec, row_spec],
        out_shape=[shape((rows, width), low)] * 2,
        compiler_params=params(),
        cost_estimate=cost(6 * rows * width * units, 8 * rows * width + 6 * (rows + width) * units),
        name="early_parts",
    )(active, gates_grad, w_feed, hid, out)


def sixteenth(which, m):
    return m[0] * 8 + (m[1] * 2 + m[2] if which == 0 else 4 + m[2] * 2 + m[1])


def back_kernel(info_ref, *refs):
    p_ref = refs[6]
    total = 0.0
    for x_ref, near_ref, far_ref, back_ref in zip(refs[0:2], refs[2:4], refs[4:6], refs[7:9]):
        x = x_ref[...].astype(full)
        centred = x - jnp.mean(x, axis=-1, keepdims=True)
        inv = lax.rsqrt(jnp.mean(centred * centred, axis=-1, keepdims=True) + epsilon)
        normal = centred * inv
        grad = near_ref[...].astype(full) + far_ref[...].astype(full)
        scaled = grad * p_ref[0:1]
        back = inv * (
            scaled
            - jnp.mean(scaled, axis=-1, keepdims=True)
            - normal * jnp.mean(scaled * normal, axis=-1, keepdims=True)
        )
        back_ref[: x.shape[0]] = back.astype(low)
        total += jnp.concatenate(
            [jnp.sum(grad * normal, axis=0, keepdims=True), jnp.sum(grad, axis=0, keepdims=True)],
            axis=0,
        )
    high = total.astype(low)
    rest = total - high.astype(full)
    middle = rest.astype(low)
    small = (rest - middle.astype(full)).astype(low)
    zeros = jnp.zeros((tail_rows - 6, total.shape[1]), full)
    terms = [high.astype(full), middle.astype(full), small.astype(full), zeros]
    refs[7][refs[0].shape[0] :] = jnp.concatenate(terms, axis=0).astype(low)


def back_rows(info, rows, near, far, norm_params):
    count, width = near[0].shape
    spec = pl.BlockSpec((count, width), lambda i, m: (0, 0))
    pair = pl.BlockSpec((2, width), lambda i, m: (0, 0))
    return pl.pallas_call(
        back_kernel,
        grid_spec=pltpu.PrefetchScalarGridSpec(
            num_scalar_prefetch=1,
            grid=(1,),
            in_specs=[
                pl.BlockSpec((count, width), lambda i, m: (sixteenth(0, m), 0)),
                pl.BlockSpec((count, width), lambda i, m: (sixteenth(1, m), 0)),
            ]
            + [spec] * 4
            + [pair],
            out_specs=[pl.BlockSpec((count + tail_rows, width), lambda i, m: (0, 0)), spec],
        ),
        out_shape=[shape((count + tail_rows, width), low), shape((count, width), low)],
        compiler_params=params(),
        cost_estimate=cost(40 * count * width, 16 * count * width),
        name="back_rows",
    )(info, rows, rows, *near, *far, norm_params)


def add_kernel(info_ref, *refs):
    for x_ref, near_ref, far_ref, out_ref in zip(refs[0:2], refs[2:4], refs[4:6], refs[6:8]):
        total = x_ref[...].astype(full) + near_ref[...].astype(full) + far_ref[...].astype(full)
        out_ref[...] = total.astype(low)


def add_rows(info, rows, near, far):
    count, width = near[0].shape
    spec = pl.BlockSpec((count, width), lambda i, m: (0, 0))
    return pl.pallas_call(
        add_kernel,
        grid_spec=pltpu.PrefetchScalarGridSpec(
            num_scalar_prefetch=1,
            grid=(1,),
            in_specs=[
                pl.BlockSpec((count, width), lambda i, m: (sixteenth(0, m), 0)),
                pl.BlockSpec((count, width), lambda i, m: (sixteenth(1, m), 0)),
            ]
            + [spec] * 4,
            out_specs=[spec, spec],
        ),
        out_shape=[shape((count, width), low)] * 2,
        compiler_params=params(),
        cost_estimate=cost(4 * count * width, 16 * count * width),
        name="add_rows",
    )(info, rows, rows, *near, *far)


def pack_kernel(block, info_ref, *refs):
    pieces, out_ref, sems = refs[:8], refs[8], refs[9]
    x, y = info_ref[1], info_ref[2]
    copies = []

    def move(source, at, size):
        place = out_ref.at[pl.ds(pl.multiple_of(at, 16), size), :]
        copies.append(pltpu.make_async_copy(source, place, sems.at[len(copies)]))

    for i, piece in enumerate(pieces):
        high, small = (i // 2) % 2, i % 2
        if i < 4:
            at = (x ^ high) * 2 + (y ^ small)
        else:
            at = 4 + (y ^ high) * 2 + (x ^ small)
        extra = piece.shape[0] - block
        move(piece.at[pl.ds(0, block), :], at * block, block)
        if extra:
            move(piece.at[pl.ds(block, extra), :], 8 * block + at * extra, extra)
    for copy in copies:
        copy.start()
    for copy in copies:
        copy.wait()


def pack_rows(info, pieces):
    block, width = pieces[-1].shape
    extra = pieces[0].shape[0] - block
    return pl.pallas_call(
        functools.partial(pack_kernel, block),
        grid_spec=pltpu.PrefetchScalarGridSpec(
            num_scalar_prefetch=1,
            grid=(1,),
            in_specs=[pl.BlockSpec(piece.shape, lambda i, m: (0, 0)) for piece in pieces],
            out_specs=pl.BlockSpec(memory_space=pl.ANY),
            scratch_shapes=[pltpu.SemaphoreType.DMA((12,))],
        ),
        out_shape=shape((8 * block + 4 * extra, width), low),
        compiler_params=params(),
        cost_estimate=cost(0, 32 * block * width),
        name="pack_rows",
    )(info, *pieces)


def tail_total(ref):
    values = ref[...].astype(full)
    sums = 0.0
    for i in range(4):
        at = i * tail_rows
        sums += values[at : at + 2] + values[at + 2 : at + 4] + values[at + 4 : at + 6]
    return sums


def tail_kernel(own_ref, other_ref, out_ref):
    out_ref[...] = tail_total(own_ref) + tail_total(other_ref)


def tail_sums(own, other):
    count, width = own.shape
    size = 4 * tail_rows
    spec = pl.BlockSpec((size, width), lambda i: (count // size - 1, 0))
    return pl.pallas_call(
        tail_kernel,
        grid=(1,),
        in_specs=[spec, spec],
        out_specs=pl.BlockSpec((2, width), lambda i: (0, 0)),
        out_shape=shape((2, width), full),
        compiler_params=params(),
        cost_estimate=cost(20 * width, 512 * width),
        name="tail_sums",
    )(own, other)


def finish_kernel(info_ref, *refs):
    mine = (pl.program_id(0) // 4) == info_ref[0]
    out_ref = refs[-1]

    def store(value):
        if len(refs) > 3:
            value = refs[2][...].astype(full) + value.astype(full)
        out_ref[...] = value

    @pl.when(mine)
    def _():
        store(refs[0][...])

    @pl.when(jnp.logical_not(mine))
    def _():
        store(refs[1][...])


def finish_rows(info, rows, own, other, cot=None):
    width = own.shape[1]
    block = rows // 8
    spec = pl.BlockSpec((block, width), lambda i, m: (i, 0))
    edge = lambda i: jnp.where(i < 4, 0, 3)
    extra = () if cot is None else (cot,)
    return pl.pallas_call(
        finish_kernel,
        grid_spec=pltpu.PrefetchScalarGridSpec(
            num_scalar_prefetch=1,
            grid=(8,),
            in_specs=[
                pl.BlockSpec((block, width), lambda i, m: (jnp.where(i // 4 == m[0], i % 4, edge(i)), 0)),
                pl.BlockSpec((block, width), lambda i, m: (jnp.where(i // 4 == m[0], edge(i), i % 4), 0)),
            ]
            + [spec] * len(extra),
            out_specs=spec,
        ),
        out_shape=shape((rows, width), low if cot is None else full),
        compiler_params=params(),
        cost_estimate=cost(2 * rows * width, 8 * rows * width),
        name="finish_rows",
    )(info, own, other, *extra)


def update_kernel(rates, count, *refs):
    g_ref = refs[0]
    ins = refs[1:7]
    outs = refs[7 + count :]
    for which, rate in enumerate(rates):
        grad = g_ref[:2] if which == 0 else g_ref[2]
        grad = grad.astype(full)
        w, m, a = (ref[...] for ref in ins[3 * which : 3 * which + 3])
        g_out, w_out, m_out, a_out = outs[4 * which : 4 * which + 4]
        g_out[...] = grad
        w_out[...], m_out[...], a_out[...] = advance(w, grad, m, a, rate)


def update_feed(start, grads, states, rates, begun=()):
    _, units, piece = grads.shape
    block = math.gcd(start, units)
    while block > 128 and block % 16 == 0:
        block //= 2
    at = start // block
    pair = pl.BlockSpec((2, block, piece), lambda i: (0, at + i, 0))
    single = pl.BlockSpec((block, piece), lambda i: (at + i, 0))
    total = states[0].shape[1]
    return pl.pallas_call(
        functools.partial(update_kernel, rates, len(begun)),
        grid=(units // block,),
        in_specs=[pl.BlockSpec((3, block, piece), lambda i: (0, i, 0))]
        + [pair] * 3
        + [single] * 3
        + [pl.BlockSpec(memory_space=pl.ANY)] * len(begun),
        out_specs=[pair] * 4 + [single] * 4,
        out_shape=[shape((2, total, piece), full)] * 4 + [shape((total, piece), full)] * 4,
        input_output_aliases={7 + i: i for i in range(len(begun))},
        compiler_params=params(),
        cost_estimate=cost(30 * units * piece, 3 * 30 * units * piece),
        name="update_feed",
    )(grads, *states, *begun)


def body(
    inputs,
    positions,
    cotangent,
    w_attend_in,
    w_attend_out,
    w_expand,
    w_reduce,
    norm_params,
    attend_bias,
    moment_attend_in,
    moment_attend_out,
    moment_expand,
    moment_reduce,
    moment_norm,
    moment_bias,
    average_attend_in,
    average_attend_out,
    average_expand,
    average_reduce,
    average_norm,
    average_bias,
):
    batch, length, width = inputs.shape
    rows = batch * length
    units = w_expand.shape[2]
    n = lax.axis_size("dp")
    group = lax.axis_size("mp")
    spot = lax.axis_index("mp").astype(jnp.int32)
    info = jnp.stack([spot & 1, (spot >> 1) & 1, (spot >> 2) & 1])
    fast = group == 8 and n == 4

    expand_t = jnp.transpose(w_expand, (1, 2, 0))
    reduce_t = jnp.transpose(w_reduce)
    in_t = jnp.transpose(w_attend_in, (1, 0, 2))
    cut = units * 7 // 11 // 16 * 16
    shards = [
        jnp.concatenate([expand_t[:, a:b], reduce_t[None, a:b]], axis=0).astype(low)
        for a, b in ((0, cut), (cut, units))
    ]
    attend_shard = jnp.concatenate([in_t, w_attend_out[None]], axis=0).astype(low)
    attend_all = lax.all_gather(attend_shard, "dp")
    first_all = lax.all_gather(after(shards[0], attend_shard), "dp")
    last_all = lax.all_gather(after(shards[1], shards[0]), "dp")

    tokens = inputs.reshape(rows, width)
    cot = cotangent.reshape(rows, width)
    hidden = layer_norm(tokens, norm_params)

    half = ROT // 2
    lane = jnp.arange(128, dtype=jnp.int32) % HD
    frequency = 10000.0 ** (-((lane % half).astype(full) * 2.0 / ROT))
    angles = positions.reshape(rows).astype(full)[:, None] * frequency[None, :]
    cosine = jnp.where(lane < ROT, jnp.cos(angles), 1.0)
    sine = jnp.where(lane < half, -jnp.sin(angles), jnp.where(lane < ROT, jnp.sin(angles), 0.0))

    def scatter(grads):
        return lax.psum_scatter(grads, "dp", scatter_dimension=0, tiled=False)

    q, k, v, o, w_attend = project(attend_all, hidden, cot, cosine, sine, attend_bias)
    context, mixed_grad, bias_part = attend(batch, q, k, v, o, cosine, sine)
    attend_grad = attend_grads(n, hidden, cot, mixed_grad, context)
    hid_early, out_early = heads_parts(context, mixed_grad, w_attend)
    first_all = after(first_all, attend_grad, hid_early, out_early)
    active, gates_grad, w_feed = feed_chunk(first_all, hidden, cot)
    hid_early, out_early = early_parts(active, gates_grad, w_feed, hid_early, out_early)
    first_grads = feed_grads(n, hidden, cot, after(active, hid_early), gates_grad)
    last_all = after(last_all, first_grads, hid_early, out_early)
    first_grads = scatter(after(first_grads, last_all)).reshape(3, cut, -1)

    total_tokens = rows * n

    def update_attend(grad):
        grad = grad.astype(full)
        grad_in, grad_out = jnp.transpose(grad[:3], (1, 0, 2)), grad[3]
        rate_in = 0.5 / math.sqrt(width * total_tokens)
        rate_out = 1.8 / math.sqrt(width * batch * n)
        new_in = advance(w_attend_in, grad_in, moment_attend_in, average_attend_in, rate_in)
        new_out = advance(w_attend_out, grad_out, moment_attend_out, average_attend_out, rate_out)
        return (grad_in, grad_out) + new_in + new_out

    rates = (1.6 / math.sqrt(width * total_tokens), 0.77 / math.sqrt(FF * total_tokens))
    states = [jnp.transpose(a, (1, 2, 0)) for a in (w_expand, moment_expand, average_expand)]
    states += [jnp.transpose(a) for a in (w_reduce, moment_reduce, average_reduce)]

    if fast:
        s = rows // 16

        def swap_cores(parts):
            came = {i: swap(parts[i], 1) for i in (1, 3, 0, 2)}
            return [came[i] for i in range(4)]

        def sum_cores(own, came):
            own = [a.astype(full) + b.astype(full) for a, b in zip(own, came)]
            return own, (own[1].astype(low), own[3].astype(low))

        def sum_first(own, came):
            first = own[0] + came[0].astype(full)
            second = own[2] + came[1].astype(full)
            near = [first[:s].astype(low), second[:s].astype(low)]
            return near, (first[s:].astype(low), second[s:].astype(low))

        def both_ways(pair, masks):
            return [swap(pair[0], masks[0]), swap(pair[1], masks[1])]

        def join(one, first, second, third):
            pieces = (one, first, second, third)
            return pack_rows(info, [p[0] for p in pieces] + [p[1] for p in pieces])

        *parts, active, both, w_last = out_last(info, True, last_all, hidden, out_early)
        own_out, load_out = sum_cores(parts[4:], swap_cores(parts[:4]))
        one_out = both_ways(load_out, (2, 4))
        attend_grad = scatter(after(attend_grad, load_out))
        *parts, gates_grad = hid_last(info, True, w_last, after(both, load_out), cot, hid_early)
        came_hid = swap_cores(parts[:4])
        near_out, load_out = sum_first(own_out, after(one_out, parts[0]))
        two_out = both_ways(load_out, (4, 2))
        own_hid, load_hid = sum_cores(parts[4:], after(came_hid, load_out))
        one_hid = both_ways(load_hid, (2, 4))
        last_grads = feed_grads(n, hidden, cot, after(active, load_hid), gates_grad)
        two_out = after(two_out, last_grads)
        add = add_rows(info, tokens, near_out, two_out)
        last_grads = scatter(last_grads).reshape(3, units - cut, -1)
        out_one = both_ways(add, (4, 2))
        out_two = both_ways(add, (2, 4))
        near_hid, load_hid = sum_first(own_hid, after(one_hid, add))
        two_hid = both_ways(load_hid, (4, 2))
        back = back_rows(info, tokens, near_hid, two_hid, norm_params)
        hid_one = both_ways(back, (4, 2))
        hid_two = both_ways(back, (2, 4))
        out_one, out_two = after((out_one, out_two), back)
        out_three = both_ways(out_one, (2, 4))
        begun = update_feed(0, after(first_grads, out_one), states, rates)
        out_two, out_three = after((out_two, out_three), begun)
        mine_out = join(add, out_one, out_two, out_three)
        other_out = swap(mine_out, 1)
        hid_one, hid_two = after((hid_one, hid_two), mine_out)
        hid_three = both_ways(hid_one, (2, 4))
        mine_hid = join(back, hid_one, hid_two, hid_three)
        other_hid = swap(mine_hid, 1)
        attend_new = update_attend(after(attend_grad, mine_hid))
        other_hid = after(other_hid, attend_new)
        norm_part = tail_sums(mine_hid, other_hid)
        sums = join_sums(norm_part, bias_part)
        near_sums = swap(sums, 1, "dp")
        output = finish_rows(info, rows, after(mine_out, sums), other_out)
        near_sums = after(near_sums, output)
        sums = sums + near_sums
        far_sums = swap(sums, 2, "dp")
        input_grad = finish_rows(info, rows, mine_hid, after(other_hid, sums), cot)
        sums = sums + after(far_sums, input_grad)
        done = update_feed(cut, after(last_grads, input_grad), states, rates, begun)
        norm_grad, bias_grad = split_sums(sums, norm_part, bias_part)
    else:
        out_part, active, both, w_last = out_last(info, False, last_all, hidden, out_early)
        hid_part, gates_grad = hid_last(info, False, w_last, both, cot, hid_early)
        attend_new = update_attend(scatter(attend_grad))
        last_grads = scatter(feed_grads(n, hidden, cot, active, gates_grad)).reshape(3, units - cut, -1)
        hidden_grad = lax.psum(hid_part, "mp").astype(full)
        summed = lax.psum(out_part, "mp").astype(full)
        values = tokens.astype(full)
        output = (values + summed).astype(low)
        centred = values - jnp.mean(values, axis=-1, keepdims=True)
        inv = lax.rsqrt(jnp.mean(centred * centred, axis=-1, keepdims=True) + epsilon)
        normal = centred * inv
        scaled = hidden_grad * norm_params[0]
        back = inv * (
            scaled
            - jnp.mean(scaled, axis=-1, keepdims=True)
            - normal * jnp.mean(scaled * normal, axis=-1, keepdims=True)
        )
        input_grad = cot.astype(full) + back
        norm_part = jnp.stack([jnp.sum(hidden_grad * normal, axis=0), jnp.sum(hidden_grad, axis=0)])
        sums = small_sum(join_sums(norm_part, bias_part), "dp")
        norm_grad, bias_grad = split_sums(sums, norm_part, bias_part)
        begun = update_feed(0, first_grads, states, rates)
        done = update_feed(cut, last_grads, states, rates, begun)
    grad_in, grad_out = attend_new[:2]
    new_in, moment_in_new, average_in_new = attend_new[2:5]
    new_out, moment_out_new, average_out_new = attend_new[5:]
    grad_expand, new_expand, moment_expand_new, average_expand_new = (
        jnp.transpose(a, (2, 0, 1)) for a in done[:4]
    )
    grad_reduce, new_reduce, moment_reduce_new, average_reduce_new = (
        jnp.transpose(a) for a in done[4:]
    )
    input_grad = input_grad.reshape(batch, length, width)
    output = output.reshape(batch, length, width)
    new_norm, moment_norm_new, average_norm_new = advance(
        norm_params, norm_grad, moment_norm, average_norm, 0.06 / math.sqrt(total_tokens)
    )
    new_bias, moment_bias_new, average_bias_new = advance(
        attend_bias, bias_grad, moment_bias, average_bias, 0.25 / math.sqrt(total_tokens)
    )
    return (
        output,
        input_grad,
        grad_in,
        grad_out,
        grad_expand,
        grad_reduce,
        norm_grad,
        bias_grad,
        new_in,
        new_out,
        new_expand,
        new_reduce,
        new_norm,
        new_bias,
        moment_in_new,
        moment_out_new,
        moment_expand_new,
        moment_reduce_new,
        moment_norm_new,
        moment_bias_new,
        average_in_new,
        average_out_new,
        average_expand_new,
        average_reduce_new,
        average_norm_new,
        average_bias_new,
    )


def solution(mesh):
    rows3 = P("dp", None, None)
    in3 = P("dp", None, "mp")
    in2 = P("dp", "mp")
    bias = P(None, "mp")
    states = (in3, in2, in3, in2, P(), bias)
    return jax.shard_map(
        body,
        mesh=mesh,
        in_specs=(rows3, P("dp", None), rows3) + states * 3,
        out_specs=(rows3, rows3) + states * 4,
        check_vma=False,
    )
```
